128 devices in a mesh: section: 2 (over x_hi), group: 16 (over z, y), replica: 4 (over x_lo, core).
Axes of the slice: x: 4 (x_hi: 2, x_lo: 2; x = x_hi * 2 + x_lo), y: 4, z: 4, core: 2. Of those that a mesh axis runs over, the one named last changes fastest.
Arguments:
- inputs: bfloat16 [4, 2, 1024, 896], P('replica', None, 'group'), may hold values from -6 to 6
- cotangent: bfloat16 [4, 2, 1024, 896], P('replica', None, 'group'), may hold values from -6 to 6
- segments: int32 [4, 2048], P('replica'), may hold values from 0 to 6, as said below
- w_qkv: bfloat16 [2, 896, 1152], P('section', 'group'), may hold values from -0.1875 to 0.1875
- b_qkv: bfloat16 [2, 1152], P('section', 'group'), may hold values from -3 to 3
- w_out: bfloat16 [2, 896, 896], P('section', 'group'), may hold values from -1.5 to 1.5
- w_gate: bfloat16 [2, 896, 4864], P('section', 'group'), may hold values from -0.1875 to 0.1875
- w_up: bfloat16 [2, 896, 4864], P('section', 'group'), may hold values from -0.1875 to 0.1875
- w_down: bfloat16 [2, 4864, 896], P('section', 'group'), may hold values from -0.15625 to 0.15625
- g_attn: bfloat16 [2, 896], P('section', 'group'), may hold values from 0.5 to 1.5
- g_mlp: bfloat16 [2, 896], P('section', 'group'), may hold values from 0.5 to 1.5
Outputs:
- block_out: bfloat16 [2, 4, 2, 1024, 896], P('section', 'replica', None, 'group')
- input_grad: bfloat16 [2, 4, 2, 1024, 896], P('section', 'replica', None, 'group')
- grad_qkv: float32 [2, 896, 1152], P('section', 'group')
- grad_bias: float32 [2, 1024], P('section', 'group')
- grad_value_bias: float32 [2, 128], P('section', 'group')
- grad_out: float32 [2, 896, 896], P('section', 'group')
- grad_gate: float32 [2, 896, 4864], P('section', 'group')
- grad_up: float32 [2, 896, 4864], P('section', 'group')
- grad_down: float32 [2, 4864, 896], P('section', 'group')
- grad_attn_gain: float32 [2, 896], P('section', 'group')
- grad_mlp_gain: float32 [2, 896], P('section', 'group')
The draws below stay inside these ranges and needn't reach their ends.
Inputs may be any that keep to these rules, and one draw needn't show every extreme that they name: `segments`: document numbers never fall along a sequence, and the last token of every sequence carries the largest; in each sequence one document covers a whole block of 1024 tokens that starts at a multiple of 1024.
All inputs are finite; a program needn't handle non-finite values.
Results may differ from the reference program's by a relative error of at most 0.035.
Values may be sent and summed in bfloat16 or wider, within the bound.
A program may use at most 192 MiB of HBM per device.

```python
import jax
import jax.numpy as jnp
from jax import lax

D = 896
HEADS = 14
KV_HEADS = 2
HEAD_DIM = 64
FF = 4864
LEN = 2048
MB = 2
QKV = 1152
SPAN = 1024
SEQS = 4
N_SECTION = 2


def draw_segments(key, part):
    key = jax.random.fold_in(key, 11)
    seq_keys = jax.random.split(key, SEQS)
    cut_count = max(LEN // 512, 2)

    def one_sequence(seq_key):
        key_chosen, key_before, key_after, key_cuts = jax.random.split(seq_key, 4)
        chosen = jax.random.randint(key_chosen, (), 0, MB)
        margin = SPAN // 4 + 1
        before = jax.random.randint(key_before, (), 0, margin)
        after = jax.random.randint(key_after, (), 0, margin)
        first = jnp.maximum(chosen * SPAN - before, 0)
        final = jnp.minimum((chosen + 1) * SPAN + after, LEN)
        cut_points = jax.random.randint(key_cuts, (cut_count,), 1, LEN)
        inside = (cut_points >= first) & (cut_points < final)
        cut_points = jnp.where(inside, first, cut_points)
        final = jnp.where(final >= LEN, 0, final)
        bounds = jnp.concatenate([cut_points, jnp.stack([first, final])])
        places = jnp.arange(LEN, dtype=jnp.int32)
        return jnp.sum((places[:, None] >= bounds[None, :]).astype(jnp.int32), axis=1)
    return jax.vmap(one_sequence)(seq_keys).astype(jnp.int32)


def shard_levels(own_key, extent, cuts, smallest, high):
    level = 1.0
    for axis_at, blocks in cuts:
        heights = jax.random.uniform(jax.random.fold_in(jax.random.fold_in(own_key, 6), axis_at), (blocks,), jnp.float32, smallest / len(cuts), high / len(cuts))
        level = level * jnp.repeat(jnp.exp(heights), extent[axis_at] // blocks).reshape((-1,) + (1,) * (len(extent) - 1 - axis_at))
    return level


def scatter_about(key, dims, deviation, bound, shards=(), held_as=jnp.bfloat16):
    loudness = shard_levels(key, dims, shards, -0.22, 0.18) if shards else 1.0
    values = jax.random.normal(key, dims, jnp.float32) * deviation * loudness
    return jnp.minimum(jnp.maximum(values, -bound), bound).astype(held_as)


def setup_inputs(seed: int = 0) -> dict:
    arg_keys = jax.random.split(jax.random.key(seed), 12)
    inputs = scatter_about(arg_keys[0], (SEQS, MB, SPAN, D), 1.0, 6.0, ((0, 4), (2, 16)))
    cotangent = scatter_about(arg_keys[1], (SEQS, MB, SPAN, D), 1.0, 6.0, ((0, 4), (2, 16)))
    segments = draw_segments(jax.random.fold_in(arg_keys[11], 71), 0)
    w_qkv = scatter_about(arg_keys[3], (N_SECTION, D, QKV), D ** -0.5, 0.1875, ((0, 2), (1, 16)))
    b_qkv = scatter_about(arg_keys[4], (N_SECTION, QKV), 0.5, 3.0, ((0, 2), (1, 16)))
    w_out = scatter_about(arg_keys[5], (N_SECTION, D, D), (D // 64) ** -0.5, 1.5, ((0, 2), (1, 16)))
    w_gate = scatter_about(arg_keys[6], (N_SECTION, D, FF), D ** -0.5, 0.1875, ((0, 2), (1, 16)))
    w_up = scatter_about(arg_keys[7], (N_SECTION, D, FF), D ** -0.5, 0.1875, ((0, 2), (1, 16)))
    w_down = scatter_about(arg_keys[8], (N_SECTION, FF, D), (FF // 4) ** -0.5, 0.15625, ((0, 2), (1, 16)))
    g_attn = jnp.clip(1.0 + 0.1 * jax.random.normal(arg_keys[9], (N_SECTION, D), jnp.float32), 0.5, 1.5).astype(jnp.bfloat16)
    g_mlp = jnp.clip(1.0 + 0.1 * jax.random.normal(arg_keys[10], (N_SECTION, D), jnp.float32), 0.5, 1.5).astype(jnp.bfloat16)
    return {"inputs": inputs, "cotangent": cotangent, "segments": segments, "w_qkv": w_qkv, "b_qkv": b_qkv, "w_out": w_out, "w_gate": w_gate, "w_up": w_up, "w_down": w_down, "g_attn": g_attn, "g_mlp": g_mlp}


EPSILON = 1e-06
THETA = 1000000.0
NEGATIVE = -1e+30
HIGHEST = lax.Precision.HIGHEST

@jax.custom_vjp
def low(v):
    return lax.optimization_barrier(v.astype(jnp.bfloat16)).astype(jnp.float32)

@jax.custom_vjp
def low_back(v):
    return v

def low_keep(v):
    return (low(v), None)

def low_pass(kept, grad):
    return (grad,)

def back_keep(v):
    return (v, None)

def back_low(kept, grad):
    return (low(grad),)
low.defvjp(low_keep, low_pass)
low_back.defvjp(back_keep, back_low)

def rotary(positions):
    half_dim = HEAD_DIM // 2
    steps_float = jnp.arange(half_dim, dtype=jnp.float32)
    frequency = THETA ** (-steps_float * 2.0 / HEAD_DIM)
    angles = positions.astype(jnp.float32)[:, None] * frequency[None, :]
    return (jnp.cos(angles), jnp.sin(angles))

def rotate(values, cosine, sine_table):
    half_dim = values.shape[-1] // 2
    first_half = values[..., :half_dim]
    second_half = values[..., half_dim:]
    cos_rows = cosine[:, None, :]
    sin_rows = sine_table[:, None, :]
    return jnp.concatenate([first_half * cos_rows - second_half * sin_rows, second_half * cos_rows + first_half * sin_rows], axis=-1)

def rms_norm(values, gain):
    return values * lax.rsqrt(lax.optimization_barrier(jnp.mean(values * values, axis=-1, keepdims=True)) + EPSILON) * gain

def attention(query_rows, key_rows, value_rows, segment_row):
    block_rows = min(512, LEN)
    positions = jnp.arange(LEN, dtype=jnp.int32)
    grouped = query_rows.reshape(LEN, KV_HEADS, HEADS // KV_HEADS, HEAD_DIM)

    def one_block(block_index):
        first_row = block_index * block_rows
        query_block = lax.dynamic_slice_in_dim(grouped, first_row, block_rows, 0)
        query_pos = lax.dynamic_slice_in_dim(positions, first_row, block_rows, 0)
        query_seg = lax.dynamic_slice_in_dim(segment_row, first_row, block_rows, 0)
        scores = jnp.einsum('rkgd,tkd->kgrt', query_block, key_rows, precision=HIGHEST) * HEAD_DIM ** (-0.5)
        scores = low_back(scores)
        allowed = (positions[None, :] <= query_pos[:, None]) & (segment_row[None, :] == query_seg[:, None])
        scores = jnp.where(allowed, scores, NEGATIVE)
        highest = lax.optimization_barrier(jnp.max(scores, axis=-1, keepdims=True))
        exponent = jnp.exp(scores - highest)
        weights_block = low(exponent / lax.optimization_barrier(jnp.sum(exponent, axis=-1, keepdims=True)))
        return jnp.einsum('kgrt,tkd->rkgd', weights_block, value_rows, precision=HIGHEST)
    blocks = lax.map(jax.checkpoint(one_block), jnp.arange(LEN // block_rows, dtype=jnp.int32))
    return blocks.reshape(LEN, HEADS * HEAD_DIM)

def layer(layer_input, segment_row, w_qkv, b_qkv, w_out, w_gate, w_up, w_down, g_attn, g_mlp):
    cosine, sine_table = rotary(jnp.arange(LEN, dtype=jnp.int32))
    kv_width = KV_HEADS * HEAD_DIM
    normed = low(rms_norm(layer_input, g_attn))
    projected = jnp.dot(normed, w_qkv, precision=HIGHEST) + b_qkv
    query_rows = low_back(projected[:, :D])
    key_rows = low_back(projected[:, D:D + kv_width])
    value_rows = low(low_back(projected[:, D + kv_width:]))
    query_rows = low(rotate(query_rows.reshape(LEN, HEADS, HEAD_DIM), cosine, sine_table))
    key_rows = low(rotate(key_rows.reshape(LEN, KV_HEADS, HEAD_DIM), cosine, sine_table))
    context = attention(query_rows, key_rows, value_rows.reshape(LEN, KV_HEADS, HEAD_DIM), segment_row)
    context = low_back(low(context))
    hidden = layer_input + low_back(jnp.dot(context, w_out, precision=HIGHEST))
    normed2 = low(rms_norm(hidden, g_mlp))
    gate_value = low_back(jnp.dot(normed2, w_gate, precision=HIGHEST))
    upward = low_back(jnp.dot(normed2, w_up, precision=HIGHEST))
    product = low(jax.nn.silu(gate_value) * upward)
    return low(hidden + jnp.dot(product, w_down, precision=HIGHEST))

def reference(inputs, cotangent, segments, w_qkv, b_qkv, w_out, w_gate, w_up, w_down, g_attn, g_mlp):
    params = tuple((member.astype(jnp.float32) for member in (w_qkv, b_qkv, w_out, w_gate, w_up, w_down, g_attn, g_mlp)))

    def one_sequence(totals, data):
        input_seq, grad_seq, segment_row = data
        current = input_seq.reshape(LEN, D).astype(jnp.float32)
        pullbacks = []
        outputs = []
        for layer_index in range(N_SECTION):
            layer_params = tuple((member[layer_index] for member in params))

            def apply_layer(layer_input, *layer_weights):
                return layer(layer_input, segment_row, *layer_weights)
            current, pullback = jax.vjp(apply_layer, current, *layer_params)
            pullbacks.append(pullback)
            outputs.append(current)
        grad_rows = grad_seq.reshape(LEN, D).astype(jnp.float32)
        input_grads = [None] * N_SECTION
        layer_grads = [None] * N_SECTION
        for layer_index in reversed(range(N_SECTION)):
            pieces = pullbacks[layer_index](grad_rows)
            grad_rows = low(pieces[0])
            input_grads[layer_index] = grad_rows
            layer_grads[layer_index] = pieces[1:]
        totals = tuple((total + jnp.stack([grads[member_index] for grads in layer_grads]) for member_index, total in enumerate(totals)))
        return (totals, (jnp.stack(outputs).astype(jnp.bfloat16), jnp.stack(input_grads).astype(jnp.bfloat16)))
    zero_grads = tuple((jnp.zeros(member.shape, jnp.float32) for member in params))
    totals, (block_rows, grad_rows) = lax.scan(one_sequence, zero_grads, (inputs, cotangent, segments))
    block_out = block_rows.reshape(SEQS, N_SECTION, MB, SPAN, D).transpose(1, 0, 2, 3, 4)
    input_grad = grad_rows.reshape(SEQS, N_SECTION, MB, SPAN, D).transpose(1, 0, 2, 3, 4)
    split_at = D + KV_HEADS * HEAD_DIM
    return (block_out, input_grad, totals[0], totals[1][:, :split_at], totals[1][:, split_at:], totals[2], totals[3], totals[4], totals[5], totals[6], totals[7])
```

```python
import functools

import jax
import jax.numpy as jnp
import numpy as np
from jax import lax
from jax.experimental import pallas as pl
from jax.experimental.pallas import tpu as pltpu
from jax.sharding import PartitionSpec as P

D = 896
HEADS = 14
KV = 128
HALF = 32
FF = 4864
QUARTER = FF // 4
QKV = 1152
ROWS = 128
SPAN = 1024
LEN = 2048
PAIRS = 7
EPSILON = 1e-06
THETA = 1000000.0
NEGATIVE = -1e30
SCALE = 0.125
VMEM_LIMIT = 56 * 1024 * 1024
MESH = pl.DeviceIdType.MESH
BF = jnp.bfloat16
F32 = jnp.float32
VMEM_SPEC = pl.BlockSpec(memory_space=pltpu.VMEM)
ANY_SPEC = pl.BlockSpec(memory_space=pl.ANY)


def nn(a, b):
    return lax.dot_general(a, b, (((1,), (0,)), ((), ())), preferred_element_type=F32)


def nt(a, b):
    return lax.dot_general(a, b, (((1,), (1,)), ((), ())), preferred_element_type=F32)


def tn(a, b):
    return lax.dot_general(a, b, (((0,), (0,)), ((), ())), preferred_element_type=F32)


def params(collective_id=None):
    if collective_id is None:
        return pltpu.CompilerParams(vmem_limit_bytes=VMEM_LIMIT)
    return pltpu.CompilerParams(
        vmem_limit_bytes=VMEM_LIMIT, collective_id=collective_id, has_side_effects=True
    )


def shaped(*shape, dtype=BF):
    return jax.ShapeDtypeStruct(shape, dtype)


def local_call(kernel, name, out_shape, scratch=()):
    return pl.pallas_call(
        kernel,
        out_shape=out_shape,
        scratch_shapes=list(scratch),
        compiler_params=params(),
        name=name,
    )


def signal(devices):
    barrier = pltpu.get_barrier_semaphore()
    for device in devices:
        pl.semaphore_signal(barrier, inc=1, device_id=device, device_id_type=MESH)


def greeted(count):
    pl.semaphore_wait(pltpu.get_barrier_semaphore(), count)


def grid_place():
    me = lax.axis_index("group")
    z = me // 4
    y = lax.rem(me, 4)

    def along_y(step):
        return {"group": z * 4 + lax.rem(y + step, 4)}

    def along_z(step):
        return {"group": lax.rem(z + step, 4) * 4 + y}

    return z, y, along_y, along_z


def neighbours(along_y, along_z):
    return [along_y(1), along_y(3), along_z(1), along_z(3)]


class Copies:
    def __init__(self, send, recv):
        self.send, self.recv, self.used = send, recv, 0

    def __call__(self, src, dst, device):
        index = self.used
        self.used += 1
        each = pltpu.make_async_remote_copy(
            src_ref=src,
            dst_ref=dst,
            send_sem=self.send.at[index],
            recv_sem=self.recv.at[index],
            device_id=device,
            device_id_type=MESH,
        )
        each.start()
        return each


def gather_phase(firsts, seconds, place, device_at, copies):
    def copy(block, slot, step):
        return copies(block(slot), block(slot), device_at(step))

    firsts_right = [copy(block, place, 1) for block in firsts]
    seconds_left = [copy(block, place, 3) for block in seconds]
    others = [copy(block, place, 3) for block in firsts] + [copy(block, place, 1) for block in seconds]

    def relay():
        relays = []
        for block, came in zip(firsts, firsts_right):
            came.wait_recv()
            relays.append(copy(block, lax.rem(place + 3, 4), 1))
        for block, came in zip(seconds, seconds_left):
            came.wait_recv()
            relays.append(copy(block, lax.rem(place + 1, 4), 3))

        def finish():
            for each in others + relays:
                each.wait_recv()
            for each in firsts_right + seconds_left + others + relays:
                each.wait_send()

        return finish

    return relay


def gather_both(first_a, second_a, first_b, second_b, copies):
    z, y, along_y, along_z = grid_place()
    relay_a = gather_phase([first_a[0]], [second_a[0]], y, along_y, copies)
    relay_b = gather_phase([first_b[0]], [second_b[0]], z, along_z, copies)
    yield
    finish_a = relay_a()
    finish_b = relay_b()
    yield
    finish_a()
    relay_a = gather_phase([first_a[1]], [second_a[1]], z, along_z, copies)
    finish_b()
    relay_b = gather_phase([first_b[1]], [second_b[1]], y, along_y, copies)
    yield
    finish_a = relay_a()
    finish_b = relay_b()
    yield
    finish_a()
    finish_b()


def run(steps):
    for _ in steps:
        pass


def y_then_z(ref, *tail):
    z = lax.axis_index("group") // 4
    return (lambda at: ref.at[(z, at, *tail)]), (lambda at: ref.at[(at, slice(None), *tail)])


def z_then_y(ref, *tail):
    y = lax.rem(lax.axis_index("group"), 4)
    return (lambda at: ref.at[(at, y, *tail)]), (lambda at: ref.at[(slice(None), at, *tail)])


def quarter_route():
    group, replica = lax.axis_index("group"), lax.axis_index("replica")
    target = {"group": 4 * lax.rem(group, 4) + replica, "replica": group // 4}
    source = {"group": 4 * replica + group // 4, "replica": lax.rem(group, 4)}
    stays = (target["group"] == group) & (target["replica"] == replica)
    return target, source, stays


def first_kernel(
    gate, up, down, qkv, out, x_ref, cos_ref, sin_ref, kseg_ref,
    gate_all, up_all, down_all, qkv_w, out_w, bias_ref, gain1_ref, gain2_ref, hidden_ref, normed2_ref,
    qkv_all, out_all, normed_ref, q_ref, kv_ref, context_ref, keys_ref, values_ref, bias0, bias1, send, recv, local
):
    z, y, along_y, along_z = grid_place()
    core = lax.rem(lax.axis_index("replica"), 2)
    mate = {"replica": lax.axis_index("replica") + 1 - 2 * core}
    target, source, stays = quarter_route()
    moves = jnp.logical_not(stays)
    signal(neighbours(along_y, along_z) + [mate])
    places = (qkv_all.at[core, z, y], out_all.at[core, z, y], gate_all.at[z, y], up_all.at[z, y])
    own = []
    for index, (src, dst) in enumerate(zip((qkv, out, gate, up), places)):
        own.append(pltpu.make_async_copy(src, dst, local.at[index]))
        own[-1].start()
    there = target["group"]
    moved = pltpu.make_async_remote_copy(
        src_ref=down,
        dst_ref=down_all.at[there // 4, lax.rem(there, 4)],
        send_sem=local.at[5],
        recv_sem=local.at[6],
        device_id=target,
        device_id_type=MESH,
    )
    stayed = pltpu.make_async_copy(down, down_all.at[z, y], local.at[4])

    @pl.when(moves)
    def _():
        signal([source])
        greeted(6)
        moved.start()

    @pl.when(stays)
    def _():
        greeted(5)
        stayed.start()

    copies = Copies(send, recv)
    own[0].wait()
    own[1].wait()
    top, bottom = (slice(0, 16), slice(None)), (slice(16, 32), slice(None))
    dense = gather_both(
        y_then_z(qkv_all.at[core], *top),
        y_then_z(qkv_all.at[core], *bottom),
        z_then_y(out_all.at[core], *top),
        z_then_y(out_all.at[core], *bottom),
        copies,
    )
    next(dense)
    next(dense)
    next(dense)
    own[2].wait()
    own[3].wait()

    @pl.when(moves)
    def _():
        moved.wait()

    @pl.when(stays)
    def _():
        stayed.wait()

    left, right = (slice(None), slice(0, 512)), (slice(None), slice(512, D))
    wide = gather_both(
        y_then_z(gate_all), y_then_z(down_all, *left), z_then_y(up_all), z_then_y(down_all, *right), copies
    )
    next(wide)
    next(dense)
    next(wide)
    run(dense)
    halves = [copies(ref.at[core], ref.at[core], mate) for ref in (qkv_all, out_all)]
    next(wide)
    for each in halves:
        each.wait()
    for at in range(16):
        rows, cut = 56 * at, 56 * at + 32
        qkv_w[rows:cut] = qkv_all[0, at // 4, at % 4]
        qkv_w[cut : rows + 56] = qkv_all[1, at // 4, at % 4, :24]
        out_w[rows:cut] = out_all[0, at // 4, at % 4]
        out_w[cut : rows + 56] = out_all[1, at // 4, at % 4, :24]
    small = [qkv_all[1, at // 4, at % 4, 24:32].astype(F32)[:1] for at in range(16)]
    bias_ref[...] = jnp.concatenate([each[:, :72] for each in small], axis=1)
    gain1_ref[...] = jnp.concatenate([each[:, 72:128] for each in small], axis=1)
    gain2_ref[...] = jnp.concatenate([each[:, 128:184] for each in small], axis=1)
    front_work(x_ref, qkv_w, bias_ref, gain1_ref, cos_ref, sin_ref, normed_ref, q_ref, kv_ref, copies, lambda: None)
    next(wide)
    attention_work(
        x_ref, q_ref, kv_ref, kseg_ref, out_w, gain2_ref, context_ref, hidden_ref, normed2_ref,
        keys_ref, values_ref, bias0, bias1
    )
    run(wide)


def first(gate, up, down, qkv, out, x, cosine, sine, kseg):
    return pl.pallas_call(
        first_kernel,
        out_shape=(
            shaped(4, 4, *gate.shape),
            shaped(4, 4, *up.shape),
            shaped(4, 4, *down.shape),
            shaped(D, QKV),
            shaped(D, D),
            shaped(1, QKV, dtype=F32),
            shaped(1, D, dtype=F32),
            shaped(1, D, dtype=F32),
            shaped(ROWS, D, dtype=F32),
            shaped(ROWS, D),
        ),
        in_specs=[ANY_SPEC] * 5 + [VMEM_SPEC] * 4,
        out_specs=[ANY_SPEC] * 3 + [VMEM_SPEC] * 7,
        scratch_shapes=[
            pltpu.VMEM((2, 4, 4, *qkv.shape), BF),
            pltpu.VMEM((2, 4, 4, *out.shape), BF),
            pltpu.VMEM((ROWS, D), BF),
            pltpu.VMEM((ROWS, D), BF),
            pltpu.VMEM((2, 4, 4, 64, 2 * KV), BF),
            pltpu.VMEM((ROWS, D), BF),
        ]
        + ATTENTION_SCRATCH
        + [
            pltpu.SemaphoreType.DMA((74,)),
            pltpu.SemaphoreType.DMA((74,)),
            pltpu.SemaphoreType.DMA((7,)),
        ],
        compiler_params=params(0),
        name="first",
    )(gate, up, down, qkv, out, x, cosine, sine, kseg)


def scatter_phase(firsts, seconds, place, device_at, copies):
    right, left, far = (lax.rem(place + step, 4) for step in (1, 3, 2))

    def load(ref):
        return ref[...].astype(F32)

    first_far = [copies(block(far), bufs[0], device_at(1)) for block, bufs, put in firsts]
    second_far = [copies(block(far), bufs[0], device_at(3)) for block, bufs, put in seconds]
    first_near = [copies(block(left), bufs[2], device_at(3)) for block, bufs, put in firsts]
    second_near = [copies(block(right), bufs[1], device_at(1)) for block, bufs, put in seconds]

    def pass_on():
        first_sum, second_sum = [], []
        for came, (block, bufs, put) in zip(first_far, firsts):
            came.wait_recv()
            bufs[3][...] = (load(block(right)) + load(bufs[0])).astype(BF)
            first_sum.append(copies(bufs[3], bufs[1], device_at(1)))
        for came, (block, bufs, put) in zip(second_far, seconds):
            came.wait_recv()
            bufs[3][...] = (load(block(left)) + load(bufs[0])).astype(BF)
            second_sum.append(copies(bufs[3], bufs[2], device_at(3)))

        def finish():
            near, far_sum = first_near + second_near, first_sum + second_sum
            for one, two, (block, bufs, put) in zip(near, far_sum, firsts + seconds):
                one.wait_recv()
                two.wait_recv()
                put(load(block(place)) + load(bufs[1]) + load(bufs[2]))
            for each in first_far + second_far + near + far_sum:
                each.wait_send()

        return finish

    return pass_on


def scatter_both(first_a, second_a, first_b, second_b, copies):
    z, y, along_y, along_z = grid_place()

    def wide(parts):
        out = []
        for block, bufs, kept, _, _ in parts:
            def put(value, kept=kept):
                kept[...] = value.astype(BF)

            out.append((block, bufs, put))
        return out

    def slim(parts):
        return [((lambda at, kept=kept: kept.at[at]), bufs, put) for _, _, kept, bufs, put in parts]

    pass_a = scatter_phase(wide(first_a), wide(second_a), y, along_y, copies)
    pass_b = scatter_phase(wide(first_b), wide(second_b), z, along_z, copies)
    yield
    finish_a = pass_a()
    finish_b = pass_b()
    finish_a()
    pass_a = scatter_phase(slim(first_a), slim(second_a), z, along_z, copies)
    finish_b()
    pass_b = scatter_phase(slim(first_b), slim(second_b), y, along_y, copies)
    finish_a = pass_a()
    finish_b = pass_b()
    finish_a()
    finish_b()


def scatter_scratch(*shapes):
    scratch = []
    for shape in shapes:
        scratch += [pltpu.VMEM((4, *shape), BF)] * 5 + [pltpu.VMEM(shape, BF)] * 4
    return scratch


def scatter_part(scratch, index, block, put):
    mine = scratch[9 * index : 9 * index + 9]
    return block, mine[:4], mine[4], mine[5:], put


def stored_in(ref, *at):
    def put(value):
        ref[at if at else ...] = value.astype(ref.dtype)

    return put


DOWN_STARTS = (0, 80, 160, 224)
DOWN_ROWS = 80


def mlp_terms(rows_ref, dgate_ref, dup_ref, product_ref, dout_ref, gate_terms, up_terms, down_terms):
    def flat(ref):
        return ref[...].reshape(4 * ROWS, ref.shape[-1])

    rows = flat(rows_ref)
    for terms, grads in ((gate_terms, dgate_ref), (up_terms, dup_ref)):
        whole = tn(rows, flat(grads))
        for at in range(16):
            terms[at // 4, at % 4] = whole[56 * at : 56 * at + 56].astype(BF)
    whole = tn(flat(product_ref), flat(dout_ref)).astype(BF)
    for at in range(16):
        start = 304 * (at // 4) + DOWN_STARTS[at % 4]
        down_terms[at // 4, at % 4] = whole[start : start + DOWN_ROWS]


def mlp_sums(gate_terms, up_terms, down_terms, gate_out, up_out, down_out, scratch, copies):
    left, right = slice(0, 512), slice(512, D)
    return scatter_both(
        [scatter_part(scratch, 0, lambda at: gate_terms.at[:, at], stored_in(gate_out))],
        [
            scatter_part(
                scratch,
                2,
                lambda at: down_terms.at[:, at, :, left],
                stored_in(down_out, slice(None), left),
            )
        ],
        [scatter_part(scratch, 1, lambda at: up_terms.at[at], stored_in(up_out))],
        [
            scatter_part(
                scratch,
                3,
                lambda at: down_terms.at[at, :, :, right],
                stored_in(down_out, slice(None), right),
            )
        ],
        copies,
    )


MLP_SUMS_SHAPES = ((56, QUARTER), (56, QUARTER), (DOWN_ROWS, 512), (DOWN_ROWS, D - 512))


def qkv_scatter_kernel(
    normed_ref, dprojected_ref, small_ref, context_ref, dlow_ref, qkv_out, out_out, *rest
):
    qkv_terms, out_terms, qkv_landed, out_landed, qkv_half, out_half = rest[:6]
    scratch, (send, recv) = rest[6:-2], rest[-2:]
    z, y, along_y, along_z = grid_place()
    core = lax.rem(lax.axis_index("replica"), 2)
    mate = {"replica": lax.axis_index("replica") + 1 - 2 * core}
    signal(neighbours(along_y, along_z) + [mate])
    whole = tn(normed_ref[...], dprojected_ref[...])
    for at in range(16):
        rows = jnp.concatenate([whole[56 * at : 56 * at + 56], small_ref[at]], axis=0)
        qkv_terms[at // 4, at % 4] = rows.astype(BF)
    whole = tn(context_ref[...], dlow_ref[...])
    for at in range(16):
        rows = jnp.concatenate([whole[56 * at : 56 * at + 56], jnp.zeros((8, D), F32)], axis=0)
        out_terms[at // 4, at % 4] = rows.astype(BF)
    greeted(5)
    copies = Copies(send, recv)
    mine = pl.ds(pl.multiple_of(32 * core, 32), 32)
    theirs = pl.ds(pl.multiple_of(32 - 32 * core, 32), 32)
    pairs = ((qkv_terms, qkv_landed, qkv_half), (out_terms, out_landed, out_half))
    sent = [copies(terms.at[:, :, theirs], landed, mate) for terms, landed, half in pairs]
    for each, (terms, landed, half) in zip(sent, pairs):
        each.wait_recv()
        half[...] = (terms[:, :, mine].astype(F32) + landed[...].astype(F32)).astype(BF)
    top, bottom = pl.ds(0, 16), pl.ds(16, 16)
    steps = scatter_both(
        [scatter_part(scratch, 0, lambda at: qkv_half.at[:, at, top], stored_in(qkv_out, slice(0, 16)))],
        [scatter_part(scratch, 1, lambda at: qkv_half.at[:, at, bottom], stored_in(qkv_out, slice(16, 32)))],
        [scatter_part(scratch, 2, lambda at: out_half.at[at, :, top], stored_in(out_out, slice(0, 16)))],
        [scatter_part(scratch, 3, lambda at: out_half.at[at, :, bottom], stored_in(out_out, slice(16, 32)))],
        copies,
    )
    run(steps)
    for each in sent:
        each.wait_send()


def qkv_scatter(normed, dprojected, small, context, dlow):
    return pl.pallas_call(
        qkv_scatter_kernel,
        out_shape=(shaped(32, QKV, dtype=F32), shaped(32, D, dtype=F32)),
        scratch_shapes=[
            pltpu.VMEM((4, 4, 64, QKV), BF),
            pltpu.VMEM((4, 4, 64, D), BF),
            pltpu.VMEM((4, 4, 32, QKV), BF),
            pltpu.VMEM((4, 4, 32, D), BF),
            pltpu.VMEM((4, 4, 32, QKV), BF),
            pltpu.VMEM((4, 4, 32, D), BF),
        ]
        + scatter_scratch((16, QKV), (16, QKV), (16, D), (16, D))
        + [pltpu.SemaphoreType.DMA((32,)), pltpu.SemaphoreType.DMA((32,))],
        compiler_params=params(2),
        name="qkv_scatter",
    )(normed, dprojected, small, context, dlow)


def replica_partners():
    me = lax.axis_index("replica")
    return me, me + 1 - 2 * lax.rem(me, 2), lax.rem(me + 2, 4), 3 - me


def exchange(own_ref, all_ref, part, far_part, near_sum, part_in, far_in, near_in, copies, work):
    me, mate, next_, far = replica_partners()
    halves = (slice(0, 64), slice(64, 128))
    to_mate, to_next = {"replica": mate}, {"replica": next_}
    greeted(2)
    across = [copies(own_ref.at[half], all_ref.at[me, half], to_next) for half in halves]
    beside = copies(own_ref, all_ref.at[me], to_mate)
    all_ref[me] = own_ref[...]
    total = work([(me, slice(0, ROWS))])
    beside.wait_recv()
    part[...] = work([(mate, slice(0, ROWS))]).astype(BF)
    sent = [copies(part, part_in, to_mate)]
    forwards, sums = [], []
    for index, half in enumerate(halves):
        across[index].wait_recv()
        forwards.append(copies(all_ref.at[next_, half], all_ref.at[next_, half], to_mate))
        forwards[-1].wait_recv()
        terms = work([(next_, half), (far, half)])
        far_part[index] = terms[64:].astype(BF)
        passed = copies(far_part.at[index], far_in.at[index], to_mate)
        passed.wait_recv()
        near_sum[index] = (terms[:64] + far_in[index].astype(F32)).astype(BF)
        sums.append(copies(near_sum.at[index], near_in.at[index], to_next))
        sent.append(passed)
    sent[0].wait_recv()
    total = total + part_in[...].astype(F32)
    for each in sums:
        each.wait_recv()
    total = total + near_in[...].reshape(ROWS, D).astype(F32)
    for each in across + [beside] + forwards + sent + sums:
        each.wait_send()
    return total


EXCHANGE_SCRATCH = [
    pltpu.VMEM((D, QUARTER), BF),
    pltpu.VMEM((D, QUARTER), BF),
    pltpu.VMEM((QUARTER, D), BF),
    pltpu.VMEM((ROWS, D), BF),
    pltpu.VMEM((2, 64, D), BF),
    pltpu.VMEM((2, 64, D), BF),
    pltpu.VMEM((ROWS, D), BF),
    pltpu.VMEM((2, 64, D), BF),
    pltpu.VMEM((2, 64, D), BF),
    pltpu.SemaphoreType.DMA((10,)),
    pltpu.SemaphoreType.DMA((10,)),
    pltpu.SemaphoreType.DMA((18,)),
]


def mlp_start(hbm, vmem, local):
    me, mate, next_, far = replica_partners()
    signal([{"replica": mate}, {"replica": next_}])
    loads = [pltpu.make_async_copy(src, dst, local.at[i]) for i, (src, dst) in enumerate(zip(hbm[:2], vmem[:2]))]
    for at in range(16):
        skip = 80 * (at % 4) - DOWN_STARTS[at % 4]
        rows = pl.ds(304 * (at // 4) + 80 * (at % 4), DOWN_ROWS - skip)
        piece = hbm[2].at[at // 4, at % 4, pl.ds(skip, DOWN_ROWS - skip)]
        loads.append(pltpu.make_async_copy(piece, vmem[2].at[rows], local.at[2 + at]))
    for each in loads:
        each.start()
    return loads


def split_rows(value, parts):
    start = 0
    for source, rows in parts:
        count = rows.stop - rows.start
        yield source, rows, value[start : start + count]
        start += count


def mlp_forward_kernel(
    normed_ref, hidden_ref, gate_hbm, up_hbm, down_hbm, out_ref, all_ref, gate_ref, up_ref,
    gate_w, up_w, down_w, part, far_part, near_sum, part_in, far_in, near_in, send, recv, local
):
    loads = mlp_start((gate_hbm, up_hbm, down_hbm), (gate_w, up_w, down_w), local)
    waiting = list(loads)

    def work(parts):
        while waiting:
            waiting.pop().wait()
        rows = jnp.concatenate([all_ref[source, rows] for source, rows in parts], axis=0)
        gate = nn(rows, gate_w[...])
        up = nn(rows, up_w[...])
        for source, at, value in split_rows(gate, parts):
            gate_ref[source, at] = value.astype(BF)
        for source, at, value in split_rows(up, parts):
            up_ref[source, at] = value.astype(BF)
        product = (gate * jax.nn.sigmoid(gate) * up).astype(BF)
        return nn(product, down_w[...])

    total = exchange(
        normed_ref, all_ref, part, far_part, near_sum, part_in, far_in, near_in, Copies(send, recv), work
    )
    out_ref[...] = (hidden_ref[...] + total).astype(BF)


def mlp_forward(normed2, hidden, gate_w, up_w, down_w):
    return pl.pallas_call(
        mlp_forward_kernel,
        out_shape=(
            shaped(ROWS, D),
            shaped(4, ROWS, D),
            shaped(4, ROWS, QUARTER),
            shaped(4, ROWS, QUARTER),
        ),
        in_specs=[VMEM_SPEC] * 2 + [ANY_SPEC] * 3,
        scratch_shapes=EXCHANGE_SCRATCH,
        compiler_params=params(3),
        name="mlp_forward",
    )(normed2, hidden, gate_w, up_w, down_w)


def mlp_backward_kernel(
    dout_ref, gate_ref, up_ref, gate_hbm, up_hbm, down_hbm,
    dnormed_ref, all_ref, dgate_ref, dup_ref, product_ref,
    gate_w, up_w, down_w, part, far_part, near_sum, part_in, far_in, near_in, send, recv, local
):
    loads = mlp_start((gate_hbm, up_hbm, down_hbm), (gate_w, up_w, down_w), local)
    waiting = list(loads)

    def work(parts):
        while waiting:
            waiting.pop().wait()

        def stacked(ref):
            return jnp.concatenate([ref[source, rows] for source, rows in parts], axis=0)

        dproduct = nt(stacked(all_ref), down_w[...])
        gate = stacked(gate_ref).astype(F32)
        up = stacked(up_ref).astype(F32)
        s = jax.nn.sigmoid(gate)
        silu = gate * s
        product = (silu * up).astype(BF)
        dgate = (dproduct * up * (s * (1.0 + gate * (1.0 - s)))).astype(BF)
        dup = (dproduct * silu).astype(BF)
        for to, whole in ((product_ref, product), (dgate_ref, dgate), (dup_ref, dup)):
            for source, at, value in split_rows(whole, parts):
                to[source, at] = value
        return nt(dgate, gate_w[...]) + nt(dup, up_w[...])

    dnormed_ref[...] = exchange(
        dout_ref, all_ref, part, far_part, near_sum, part_in, far_in, near_in, Copies(send, recv), work
    )


def mlp_backward(dout, gate, up, gate_w, up_w, down_w):
    return pl.pallas_call(
        mlp_backward_kernel,
        out_shape=(
            shaped(ROWS, D, dtype=F32),
            shaped(4, ROWS, D),
            shaped(4, ROWS, QUARTER),
            shaped(4, ROWS, QUARTER),
            shaped(4, ROWS, QUARTER),
        ),
        in_specs=[VMEM_SPEC] * 3 + [ANY_SPEC] * 3,
        scratch_shapes=EXCHANGE_SCRATCH,
        compiler_params=params(4),
        name="mlp_backward",
    )(dout, gate, up, gate_w, up_w, down_w)


def replica_sum_kernel(
    gate, up, down, qkv, out, gate_all, up_all, down_all, qkv_all, out_all,
    qkv_low, out_low, qkv_in, out_in, send, recv, local
):
    me, mate, next_, far = replica_partners()
    to_mate, to_next = {"replica": mate}, {"replica": next_}
    core = lax.rem(me, 2)
    target, source, stays = quarter_route()
    signal([to_mate, to_next])

    @pl.when(jnp.logical_not(stays))
    def _():
        signal([target])
        greeted(3)

    @pl.when(stays)
    def _():
        greeted(2)

    copies = Copies(send, recv)
    qkv_low[...] = qkv[...].astype(BF)
    out_low[...] = out[...].astype(BF)
    across = [copies(qkv_low, qkv_in, to_next), copies(out_low, out_in, to_next)]
    across += [copies(ref, all_ref.at[me], to_next) for ref, all_ref in ((gate, gate_all), (up, up_all))]
    beside = [copies(ref, all_ref.at[me], to_mate) for ref, all_ref in ((gate, gate_all), (up, up_all))]
    own = []
    for index, (ref, all_ref) in enumerate(((gate, gate_all), (up, up_all))):
        own.append(pltpu.make_async_copy(ref, all_ref.at[me], local.at[index]))
        own[-1].start()

    @pl.when(jnp.logical_not(stays))
    def _():
        each = pltpu.make_async_remote_copy(
            src_ref=down,
            dst_ref=down_all.at[source["replica"]],
            send_sem=local.at[3],
            recv_sem=local.at[4],
            device_id=source,
            device_id_type=MESH,
        )
        each.start()
        each.wait()

    @pl.when(stays)
    def _():
        stored = pltpu.make_async_copy(down, down_all.at[me], local.at[2])
        stored.start()
        stored.wait()

    across.append(copies(down_all.at[me], down_all.at[me], to_next))
    beside.append(copies(down_all.at[me], down_all.at[me], to_mate))
    across[0].wait_recv()
    qkv_all[core] = qkv[...] + qkv_in[...].astype(F32)
    across[1].wait_recv()
    out_all[core] = out[...] + out_in[...].astype(F32)
    beside += [copies(ref.at[core], ref.at[core], to_mate) for ref in (qkv_all, out_all)]
    for came, all_ref in zip(across[2:], (gate_all, up_all, down_all)):
        came.wait_recv()
        beside.append(copies(all_ref.at[next_], all_ref.at[next_], to_mate))
    for each in beside:
        each.wait_recv()
    for each in own:
        each.wait()
    for each in across + beside:
        each.wait_send()


def replica_sum(gate, up, down, qkv, out):
    return pl.pallas_call(
        replica_sum_kernel,
        out_shape=(
            shaped(4, *gate.shape),
            shaped(4, *up.shape),
            shaped(4, *down.shape),
            shaped(2, *qkv.shape, dtype=F32),
            shaped(2, *out.shape, dtype=F32),
        ),
        scratch_shapes=[
            pltpu.VMEM(qkv.shape, BF),
            pltpu.VMEM(out.shape, BF),
            pltpu.VMEM(qkv.shape, BF),
            pltpu.VMEM(out.shape, BF),
            pltpu.SemaphoreType.DMA((13,)),
            pltpu.SemaphoreType.DMA((13,)),
            pltpu.SemaphoreType.DMA((5,)),
        ],
        compiler_params=params(5),
        name="replica_sum",
    )(gate, up, down, qkv, out)


def outputs_kernel(gate, up, down, qkv, out, gate_out, up_out, down_out, qkv_out, small_out, out_out):
    for r in range(4):
        lanes = slice(QUARTER * r, QUARTER * r + QUARTER)
        gate_out[:, lanes] = gate[r].astype(F32)
        up_out[:, lanes] = up[r].astype(F32)
        skip = 80 * r - DOWN_STARTS[r]
        down_out[80 * r : DOWN_STARTS[r] + DOWN_ROWS] = down[r, skip:].astype(F32)
    qkv_out[:32] = qkv[0]
    qkv_out[32:] = qkv[1, :24]
    small_out[...] = qkv[1, 24:, :256]
    out_out[:32] = out[0]
    out_out[32:] = out[1, :24]


def outputs(gate, up, down, qkv, out):
    return local_call(
        outputs_kernel,
        "outputs",
        (
            shaped(56, FF, dtype=F32),
            shaped(56, FF, dtype=F32),
            shaped(FF // 16, D, dtype=F32),
            shaped(56, QKV, dtype=F32),
            shaped(8, 256, dtype=F32),
            shaped(56, D, dtype=F32),
        ),
    )(gate, up, down, qkv, out)


def turn(values, cosine, sine, sign):
    width = values.shape[1]
    up = pltpu.roll(values, width - HALF, 1)
    down = pltpu.roll(values, HALF, 1)
    lane = lax.broadcasted_iota(jnp.int32, values.shape, 1)
    swapped = jnp.where(lax.rem(lane, 2 * HALF) < HALF, up, down)
    repeat = width // KV
    cosine = jnp.concatenate([cosine] * repeat, axis=1)
    sine = jnp.concatenate([sine] * repeat, axis=1)
    return values * cosine + sign * (swapped * sine)


def front_work(x_ref, w_ref, b_ref, g_ref, cos_ref, sin_ref, normed_ref, q_ref, kv_ref, copies, ready):
    z, y, along_y, along_z = grid_place()
    x = x_ref[...].astype(F32)
    inverse = lax.rsqrt(jnp.mean(x * x, axis=-1, keepdims=True) + EPSILON)
    normed = (x * inverse * g_ref[...]).astype(BF)
    normed_ref[...] = normed
    projected = nn(normed, w_ref[:, D:]) + b_ref[:, D:]
    turned = turn(projected[:, :KV], cos_ref[...], sin_ref[...], 1.0)
    kv = jnp.concatenate([turned, projected[:, KV:]], axis=1).astype(BF)
    kv_ref[0, z, y] = kv[:64]
    kv_ref[1, z, y] = kv[64:]
    ready()
    top, bottom = (slice(0, 32), slice(None)), (slice(32, 64), slice(None))
    steps = gather_both(
        y_then_z(kv_ref.at[0], *top),
        y_then_z(kv_ref.at[0], *bottom),
        z_then_y(kv_ref.at[1], *top),
        z_then_y(kv_ref.at[1], *bottom),
        copies,
    )
    next(steps)
    projected = nn(normed, w_ref[:, :D]) + b_ref[:, :D]
    q_ref[...] = turn(projected, cos_ref[...], sin_ref[...], 1.0).astype(BF)
    run(steps)


def front_kernel(x_ref, w_ref, b_ref, g_ref, cos_ref, sin_ref, normed_ref, q_ref, kv_ref, send, recv):
    z, y, along_y, along_z = grid_place()
    signal(neighbours(along_y, along_z))
    front_work(
        x_ref, w_ref, b_ref, g_ref, cos_ref, sin_ref, normed_ref, q_ref, kv_ref,
        Copies(send, recv), lambda: greeted(4)
    )


def front(x, w_qkv, b_qkv, g_attn, cosine, sine):
    return pl.pallas_call(
        front_kernel,
        out_shape=(shaped(ROWS, D), shaped(ROWS, D), shaped(2, 4, 4, 64, 2 * KV)),
        scratch_shapes=[pltpu.SemaphoreType.DMA((24,)), pltpu.SemaphoreType.DMA((24,))],
        compiler_params=params(6),
        name="front",
    )(x, w_qkv, b_qkv, g_attn, cosine, sine)


def low_lanes(rows):
    return lax.broadcasted_iota(jnp.int32, (rows, KV), 1) < KV // 2


def spread(kv_ref, start, to_ref):
    mixed = kv_ref[:, :, :, :, start : start + KV].reshape(LEN, KV)
    other = pltpu.roll(mixed.astype(F32), KV // 2, 1).astype(BF)
    low = low_lanes(LEN)
    to_ref[0] = jnp.where(low, mixed, other)
    to_ref[1] = mixed
    to_ref[2] = jnp.where(low, other, mixed)


def fill_bias(kseg_ref, bias_refs):
    first_row = 64 * lax.axis_index("group")
    for block, bias_ref in enumerate(bias_refs):
        keys = SPAN * (block + 1)
        kpos = lax.broadcasted_iota(jnp.int32, (64, keys), 1)
        qpos = SPAN * block + first_row + lax.broadcasted_iota(jnp.int32, (64, keys), 0)
        kseg = jnp.broadcast_to(kseg_ref[:, :keys], (64, keys)).astype(F32)
        qseg = jnp.sum(jnp.where(kpos == qpos, kseg, 0.0), axis=1, keepdims=True)
        bias_ref[...] = jnp.where((kpos <= qpos) & (kseg == qseg), 0.0, NEGATIVE)


def two_heads(pair):
    low = low_lanes(64)
    zero = jnp.zeros_like(pair)
    return jnp.concatenate([jnp.where(low, pair, zero), jnp.where(low, zero, pair)], axis=0)


def one_pair(stacked):
    return jnp.where(low_lanes(64), stacked[:64], stacked[64:])


def softmax(queries, keys, bias_ref):
    count = keys.shape[0]
    scores = nt(queries, keys).reshape(2, 64, count) + bias_ref[...][None]
    highest = jnp.max(scores, axis=-1, keepdims=True)
    exponent = jnp.exp(scores - highest)
    total = jnp.sum(exponent, axis=-1, keepdims=True)
    return (exponent * (1.0 / total)).reshape(2 * 64, count)


def variant_of(pair):
    return jnp.where(pair < 3, 0, jnp.where(pair == 3, 1, 2))


def attention_work(
    x_ref, q_ref, kv_ref, kseg_ref, w_ref, g_ref, context_ref, hidden_ref, normed_ref,
    keys_ref, values_ref, bias0, bias1
):
    spread(kv_ref, 0, keys_ref)
    spread(kv_ref, KV, values_ref)
    fill_bias(kseg_ref, (bias0, bias1))

    def one(pair, carry):
        variant = variant_of(pair)
        lanes = pl.ds(pl.multiple_of(pair * KV, KV), KV)
        for block, bias_ref in enumerate((bias0, bias1)):
            rows = slice(64 * block, 64 * block + 64)
            keys = pl.ds(0, SPAN * (block + 1))
            queries = two_heads(q_ref[rows, lanes] * SCALE).astype(BF)
            weights = softmax(queries, keys_ref[variant, keys], bias_ref).astype(BF)
            context = nn(weights, values_ref[variant, keys])
            context_ref[rows, lanes] = one_pair(context).astype(BF)
        return carry

    lax.fori_loop(0, PAIRS, one, 0)
    hidden = x_ref[...].astype(F32) + nn(context_ref[...], w_ref[...])
    hidden_ref[...] = hidden
    inverse = lax.rsqrt(jnp.mean(hidden * hidden, axis=-1, keepdims=True) + EPSILON)
    normed_ref[...] = (hidden * inverse * g_ref[...]).astype(BF)


ATTENTION_SCRATCH = [
    pltpu.VMEM((3, LEN, KV), BF),
    pltpu.VMEM((3, LEN, KV), BF),
    pltpu.VMEM((64, SPAN), F32),
    pltpu.VMEM((64, LEN), F32),
]


def attention(x, q, kv, kseg, w_out, g_mlp):
    return local_call(
        attention_work,
        "attention",
        (shaped(ROWS, D), shaped(ROWS, D, dtype=F32), shaped(ROWS, D)),
        ATTENTION_SCRATCH,
    )(x, q, kv, kseg, w_out, g_mlp)


def norm_backward(values, gain, grads):
    inverse = lax.rsqrt(jnp.mean(values * values, axis=-1, keepdims=True) + EPSILON)
    scaled = grads * gain
    dvalues = inverse * scaled - values * (
        inverse * inverse * inverse * jnp.mean(scaled * values, axis=-1, keepdims=True)
    )
    return dvalues, jnp.sum(grads * values * inverse, axis=0, keepdims=True)


def attention_backward_work(
    dout_ref, dnormed_ref, hidden_ref, g_ref, w_ref, q_ref, kv_ref, kseg_ref,
    dhidden_ref, dlow_ref, dq_ref, dkv_ref, dgain_ref,
    keys_ref, values_ref, bias0, bias1, dcontext_ref, dkeys, dvalues
):
    dnorm, dgain = norm_backward(hidden_ref[...], g_ref[...], dnormed_ref[...])
    dgain_ref[...] = dgain
    dhidden = dout_ref[...].astype(F32) + dnorm
    dhidden_ref[...] = dhidden
    dlow = dhidden.astype(BF)
    dlow_ref[...] = dlow
    dcontext_ref[...] = nt(dlow, w_ref[...]).astype(BF)
    spread(kv_ref, 0, keys_ref)
    spread(kv_ref, KV, values_ref)
    fill_bias(kseg_ref, (bias0, bias1))
    dkeys[...] = jnp.zeros_like(dkeys)
    dvalues[...] = jnp.zeros_like(dvalues)

    def one(pair, carry):
        variant = variant_of(pair)
        lanes = pl.ds(pl.multiple_of(pair * KV, KV), KV)
        for block, bias_ref in enumerate((bias0, bias1)):
            rows = slice(64 * block, 64 * block + 64)
            keys = pl.ds(0, SPAN * (block + 1))
            queries = two_heads(q_ref[rows, lanes] * SCALE).astype(BF)
            dcontext = two_heads(dcontext_ref[rows, lanes])
            key_rows = keys_ref[variant, keys]
            weights = softmax(queries, key_rows, bias_ref)
            dweights = nt(dcontext, values_ref[variant, keys])
            inner = jnp.sum(weights * dweights, axis=-1, keepdims=True)
            dscores = (weights * (dweights - inner)).astype(BF)
            dq_ref[rows, lanes] = one_pair(nn(dscores, key_rows)) * SCALE
            dkeys[variant, keys] += tn(dscores, queries)
            dvalues[variant, keys] += tn(weights.astype(BF), dcontext)
        return carry

    lax.fori_loop(0, PAIRS, one, 0)
    low = low_lanes(LEN)
    for start, total in ((0, dkeys), (KV, dvalues)):
        head0 = total[0] + pltpu.roll(total[0], KV // 2, 1)
        head1 = total[2] + pltpu.roll(total[2], KV // 2, 1)
        whole = (jnp.where(low, head0, head1) + total[1]).astype(BF)
        dkv_ref[:, :, :, :, start : start + KV] = whole.reshape(2, 4, 4, 64, KV)


ATTENTION_BACKWARD_OUT = (
    shaped(ROWS, D, dtype=F32),
    shaped(ROWS, D),
    shaped(ROWS, D, dtype=F32),
    shaped(2, 4, 4, 64, 2 * KV),
    shaped(1, D, dtype=F32),
)
ATTENTION_BACKWARD_SCRATCH = ATTENTION_SCRATCH + [
    pltpu.VMEM((ROWS, D), BF),
    pltpu.VMEM((3, LEN, KV), F32),
    pltpu.VMEM((3, LEN, KV), F32),
]


def attention_backward(*operands):
    return local_call(
        attention_backward_work, "attention_backward", ATTENTION_BACKWARD_OUT, ATTENTION_BACKWARD_SCRATCH
    )(*operands)


def last_kernel(*refs):
    ins, terms_in, outs, sums_out = refs[:8], refs[8:13], refs[13:18], refs[18:21]
    scratch, terms, bufs, (send, recv) = refs[21:28], refs[28:31], refs[31:-2], refs[-2:]
    z, y, along_y, along_z = grid_place()
    signal(neighbours(along_y, along_z))
    mlp_terms(*terms_in, *terms)
    greeted(4)
    steps = mlp_sums(*terms, *sums_out, bufs, Copies(send, recv))
    next(steps)
    attention_backward_work(*ins, *outs, *scratch)
    run(steps)


def last(*operands):
    return pl.pallas_call(
        last_kernel,
        out_shape=ATTENTION_BACKWARD_OUT
        + (shaped(56, QUARTER), shaped(56, QUARTER), shaped(DOWN_ROWS, D)),
        scratch_shapes=ATTENTION_BACKWARD_SCRATCH
        + [
            pltpu.VMEM((4, 4, 56, QUARTER), BF),
            pltpu.VMEM((4, 4, 56, QUARTER), BF),
            pltpu.VMEM((4, 4, DOWN_ROWS, D), BF),
        ]
        + scatter_scratch(*MLP_SUMS_SHAPES)
        + [pltpu.SemaphoreType.DMA((24,)), pltpu.SemaphoreType.DMA((24,))],
        compiler_params=params(1),
        name="last",
    )(*operands)


def rear_kernel(
    dkv_ref, dq_ref, cos_ref, sin_ref, w_ref, x_ref, g_ref, dhidden_ref,
    dprojected_ref, dinput_ref, dgain_ref, dbias_ref, *rest
):
    total, scratch, (send, recv) = rest[0], rest[1:-2], rest[-2:]
    z, y, along_y, along_z = grid_place()
    signal(neighbours(along_y, along_z))
    greeted(4)
    top, bottom = slice(0, 32), slice(32, 64)
    steps = scatter_both(
        [scatter_part(scratch, 0, lambda at: dkv_ref.at[0, :, at, top], stored_in(total, slice(0, 32)))],
        [scatter_part(scratch, 1, lambda at: dkv_ref.at[0, :, at, bottom], stored_in(total, slice(32, 64)))],
        [scatter_part(scratch, 2, lambda at: dkv_ref.at[1, at, :, top], stored_in(total, slice(64, 96)))],
        [scatter_part(scratch, 3, lambda at: dkv_ref.at[1, at, :, bottom], stored_in(total, slice(96, 128)))],
        Copies(send, recv),
    )
    next(steps)
    dquery = turn(dq_ref[...], cos_ref[...], sin_ref[...], -1.0).astype(BF)
    dprojected_ref[:, :D] = dquery
    dbias_ref[:, :D] = jnp.sum(dquery.astype(F32), axis=0, keepdims=True)
    dnormed = nt(dquery, w_ref[:, :D])
    run(steps)
    turned = turn(total[:, :KV], cos_ref[...], sin_ref[...], -1.0)
    dkv = jnp.concatenate([turned, total[:, KV:]], axis=1).astype(BF)
    dprojected_ref[:, D:] = dkv
    dbias_ref[:, D:] = jnp.sum(dkv.astype(F32), axis=0, keepdims=True)
    dnormed = dnormed + nt(dkv, w_ref[:, D:])
    dnorm, dgain = norm_backward(x_ref[...].astype(F32), g_ref[...], dnormed)
    dgain_ref[...] = dgain
    dinput_ref[...] = (dhidden_ref[...] + dnorm).astype(BF)


def rear(dkv, dq, cosine, sine, w_qkv, x, g_attn, dhidden):
    return pl.pallas_call(
        rear_kernel,
        out_shape=(shaped(ROWS, QKV), shaped(ROWS, D), shaped(1, D, dtype=F32), shaped(1, QKV, dtype=F32)),
        scratch_shapes=[pltpu.VMEM((ROWS, 2 * KV), F32)]
        + scatter_scratch(*[(32, 2 * KV)] * 4)
        + [pltpu.SemaphoreType.DMA((24,)), pltpu.SemaphoreType.DMA((24,))],
        compiler_params=params(7),
        name="rear",
    )(dkv, dq, cosine, sine, w_qkv, x, g_attn, dhidden)


def rotary(group):
    lane = np.arange(KV)
    frequency = jnp.asarray(THETA ** (-(lane % HALF) * 2.0 / (2 * HALF)), F32)
    sign = jnp.asarray(np.where(lane % (2 * HALF) < HALF, -1.0, 1.0), F32)
    row = lax.broadcasted_iota(jnp.int32, (ROWS, KV), 0)
    positions = group * 64 + lax.rem(row, 64) + SPAN * (row // 64)
    angles = positions.astype(F32) * frequency[None, :]
    return jnp.cos(angles), jnp.sin(angles) * sign[None, :]


def body(inputs, cotangent, segments, w_qkv, b_qkv, w_out, w_gate, w_up, w_down, g_attn, g_mlp):
    section = lax.axis_index("section")
    group = lax.axis_index("group")
    replica = lax.axis_index("replica")
    core = lax.rem(replica, 2)

    down_piece = lax.dynamic_slice(w_down[0], (jnp.minimum(80 * replica, 224), 0), (DOWN_ROWS, D))
    gate_piece = lax.dynamic_slice(w_gate[0], (0, replica * QUARTER), (D // 16, QUARTER))
    up_piece = lax.dynamic_slice(w_up[0], (0, replica * QUARTER), (D // 16, QUARTER))
    small = jnp.concatenate([b_qkv[0], g_attn[0], g_mlp[0]])
    small = jnp.pad(small[None], ((0, 7), (0, QKV - small.shape[0])))
    qkv_piece = lax.dynamic_slice(jnp.concatenate([w_qkv[0], small], axis=0), (32 * core, 0), (32, QKV))
    out_piece = lax.dynamic_slice(jnp.pad(w_out[0], ((0, 8), (0, 0))), (32 * core, 0), (32, D))

    cosine, sine = rotary(group)
    kseg = segments
    x_in = inputs[0].reshape(ROWS, D)
    cotangent_in = cotangent[0].reshape(ROWS, D)
    gate_w, up_w, down_w, qkv_w, out_w, bias, gain1, gain2, hidden, normed2 = first(
        gate_piece, up_piece, down_piece, qkv_piece, out_piece, x_in, cosine, sine, kseg
    )
    gate_w = gate_w.reshape(D, QUARTER)
    up_w = up_w.reshape(D, QUARTER)

    def forward(x):
        normed, q, kv = front(x, qkv_w, bias, gain1, cosine, sine)
        context, hidden, normed2 = attention(x, q, kv, kseg, out_w, gain2)
        output, normed2_all, gate, up = mlp_forward(normed2, hidden, gate_w, up_w, down_w)
        return output, (x, normed, q, kv, context, hidden, normed2_all, gate, up)

    def backward(dout, kept, finishing):
        x, normed, q, kv, context, hidden, normed2_all, gate, up = kept
        dnormed2, dout_all, dgate, dup, product = mlp_backward(dout, gate, up, gate_w, up_w, down_w)
        operands = (dout, dnormed2, hidden, gain2, out_w, q, kv, kseg)
        if finishing:
            dhidden, dlow, dq, dkv, dgain2, *grads = last(
                *operands, normed2_all, dgate, dup, product, dout_all
            )
        else:
            dhidden, dlow, dq, dkv, dgain2 = attention_backward(*operands)
            grads = ()
        dprojected, dinput, dgain1, dbias = rear(dkv, dq, cosine, sine, qkv_w, x, gain1, dhidden)
        return dinput, (grads, dlow, dprojected, dgain1, dgain2, dbias)

    relayed, *_ = mlp_forward(normed2, hidden, gate_w, up_w, down_w)
    relayed = lax.ppermute(relayed, "section", [(0, 1)])
    output, kept = forward(jnp.where(section == 0, x_in, relayed))
    returned, _ = backward(cotangent_in, kept, False)
    returned = lax.ppermute(returned, "section", [(1, 0)])
    dinput, terms = backward(jnp.where(section == 1, cotangent_in, returned), kept, True)

    x, normed, q, kv, context, hidden, normed2_all, gate, up = kept
    (grad_gate, grad_up, grad_down), dlow, dprojected, dgain1, dgain2, dbias = terms

    small = jnp.concatenate(
        [
            dbias[:, : D + KV].reshape(16, 64),
            dbias[:, D + KV :].reshape(16, 8),
            dgain1.reshape(16, 56),
            dgain2.reshape(16, 56),
        ],
        axis=1,
    )
    small = jnp.pad(small[:, None], ((0, 0), (0, 7), (0, QKV - small.shape[1])))
    grad_qkv, grad_out = qkv_scatter(normed, dprojected, small, context, dlow)
    parts = replica_sum(grad_gate, grad_up, grad_down, grad_qkv, grad_out)
    grad_gate, grad_up, grad_down, grad_qkv, small, grad_out = outputs(*parts)
    return (
        output.reshape(1, 1, 2, 64, D),
        dinput.reshape(1, 1, 2, 64, D),
        grad_qkv[None],
        small[:1, :64],
        small[:1, 64:72],
        grad_out[None],
        grad_gate[None],
        grad_up[None],
        grad_down[None],
        small[:1, 72:128],
        small[:1, 128:184],
    )


def solution(mesh):
    in_specs = (
        P("replica", None, "group", None),
        P("replica", None, "group", None),
        P("replica", None),
        P("section", "group", None),
        P("section", "group"),
        P("section", "group", None),
        P("section", "group", None),
        P("section", "group", None),
        P("section", "group", None),
        P("section", "group"),
        P("section", "group"),
    )
    out_specs = (
        P("section", "replica", None, "group", None),
        P("section", "replica", None, "group", None),
        P("section", "group", None),
        P("section", "group"),
        P("section", "group"),
        P("section", "group", None),
        P("section", "group", None),
        P("section", "group", None),
        P("section", "group", None),
        P("section", "group"),
        P("section", "group"),
    )
    return jax.shard_map(body, mesh=mesh, in_specs=in_specs, out_specs=out_specs, check_vma=False)
```

```python
import functools

import jax
import jax.numpy as jnp
import numpy as np
from jax import lax
from jax.experimental import pallas as pl
from jax.experimental.pallas import tpu as pltpu
from jax.sharding import PartitionSpec as P

D = 896
HEADS = 14
KV = 128
HALF = 32
FF = 4864
QUARTER = FF // 4
QKV = 1152
ROWS = 128
SPAN = 1024
LEN = 2048
PAIRS = 7
EPSILON = 1e-06
THETA = 1000000.0
NEGATIVE = -1e30
SCALE = 0.125
VMEM_LIMIT = 60 * 1024 * 1024
MESH = pl.DeviceIdType.MESH
BF = jnp.bfloat16
F32 = jnp.float32
VMEM_SPEC = pl.BlockSpec(memory_space=pltpu.VMEM)
ANY_SPEC = pl.BlockSpec(memory_space=pl.ANY)


def nn(a, b):
    return lax.dot_general(a, b, (((1,), (0,)), ((), ())), preferred_element_type=F32)


def nt(a, b):
    return lax.dot_general(a, b, (((1,), (1,)), ((), ())), preferred_element_type=F32)


def tn(a, b):
    return lax.dot_general(a, b, (((0,), (0,)), ((), ())), preferred_element_type=F32)


def params(collective_id=None):
    if collective_id is None:
        return pltpu.CompilerParams(vmem_limit_bytes=VMEM_LIMIT)
    return pltpu.CompilerParams(
        vmem_limit_bytes=VMEM_LIMIT, collective_id=collective_id, has_side_effects=True
    )


def shaped(*shape, dtype=BF):
    return jax.ShapeDtypeStruct(shape, dtype)


def local_call(kernel, name, out_shape, scratch=()):
    return pl.pallas_call(
        kernel,
        out_shape=out_shape,
        scratch_shapes=list(scratch),
        compiler_params=params(),
        name=name,
    )


def signal(devices):
    barrier = pltpu.get_barrier_semaphore()
    for device in devices:
        pl.semaphore_signal(barrier, inc=1, device_id=device, device_id_type=MESH)


def greeted(count):
    pl.semaphore_wait(pltpu.get_barrier_semaphore(), count)


def grid_place():
    me = lax.axis_index("group")
    z = me // 4
    y = lax.rem(me, 4)

    def along_y(step):
        return {"group": z * 4 + lax.rem(y + step, 4)}

    def along_z(step):
        return {"group": lax.rem(z + step, 4) * 4 + y}

    return z, y, along_y, along_z


def neighbours(along_y, along_z):
    return [along_y(1), along_y(3), along_z(1), along_z(3)]


class Copies:
    def __init__(self, send, recv):
        self.send, self.recv, self.used = send, recv, 0

    def __call__(self, src, dst, device):
        index = self.used
        self.used += 1
        each = pltpu.make_async_remote_copy(
            src_ref=src,
            dst_ref=dst,
            send_sem=self.send.at[index],
            recv_sem=self.recv.at[index],
            device_id=device,
            device_id_type=MESH,
        )
        each.start()
        return each


def gather_phase(firsts, seconds, place, device_at, copies):
    def copy(block, slot, step):
        return copies(block(slot), block(slot), device_at(step))

    firsts_right = [copy(block, place, 1) for block in firsts]
    seconds_left = [copy(block, place, 3) for block in seconds]
    others = [copy(block, place, 3) for block in firsts] + [copy(block, place, 1) for block in seconds]

    def relay():
        relays = []
        for block, came in zip(firsts, firsts_right):
            came.wait_recv()
            relays.append(copy(block, lax.rem(place + 3, 4), 1))
        for block, came in zip(seconds, seconds_left):
            came.wait_recv()
            relays.append(copy(block, lax.rem(place + 1, 4), 3))

        def finish():
            for each in others + relays:
                each.wait_recv()
            for each in firsts_right + seconds_left + others + relays:
                each.wait_send()

        return finish

    return relay


def gather_both(first_a, second_a, first_b, second_b, copies):
    z, y, along_y, along_z = grid_place()
    relay_a = gather_phase([first_a[0]], [second_a[0]], y, along_y, copies)
    relay_b = gather_phase([first_b[0]], [second_b[0]], z, along_z, copies)
    yield
    finish_a = relay_a()
    finish_b = relay_b()
    yield
    finish_a()
    relay_a = gather_phase([first_a[1]], [second_a[1]], z, along_z, copies)
    finish_b()
    relay_b = gather_phase([first_b[1]], [second_b[1]], y, along_y, copies)
    yield
    finish_a = relay_a()
    finish_b = relay_b()
    yield
    finish_a()
    finish_b()


def run(steps):
    for _ in steps:
        pass


def y_then_z(ref, *tail):
    z = lax.axis_index("group") // 4
    return (lambda at: ref.at[(z, at, *tail)]), (lambda at: ref.at[(at, slice(None), *tail)])


def z_then_y(ref, *tail):
    y = lax.rem(lax.axis_index("group"), 4)
    return (lambda at: ref.at[(at, y, *tail)]), (lambda at: ref.at[(slice(None), at, *tail)])


def quarter_route():
    group, replica = lax.axis_index("group"), lax.axis_index("replica")
    target = {"group": 4 * lax.rem(group, 4) + replica, "replica": group // 4}
    source = {"group": 4 * replica + group // 4, "replica": lax.rem(group, 4)}
    stays = (target["group"] == group) & (target["replica"] == replica)
    return target, source, stays


def first_kernel(
    gate, up, down, qkv, out, x_ref, cos_ref, sin_ref, kseg_ref,
    gate_all, up_all, down_all, qkv_w, out_w, bias_ref, gain1_ref, gain2_ref, hidden_ref, normed2_ref,
    qkv_all, out_all, normed_ref, q_ref, kv_ref, context_ref, keys_ref, values_ref, bias0, bias1, send, recv, local
):
    z, y, along_y, along_z = grid_place()
    core = lax.rem(lax.axis_index("replica"), 2)
    mate = {"replica": lax.axis_index("replica") + 1 - 2 * core}
    target, source, stays = quarter_route()
    moves = jnp.logical_not(stays)
    signal(neighbours(along_y, along_z) + [mate])
    places = (qkv_all.at[core, z, y], out_all.at[core, z, y], gate_all.at[z, y], up_all.at[z, y])
    own = []
    for index, (src, dst) in enumerate(zip((qkv, out, gate, up), places)):
        own.append(pltpu.make_async_copy(src, dst, local.at[index]))
        own[-1].start()
    there = target["group"]
    moved = pltpu.make_async_remote_copy(
        src_ref=down,
        dst_ref=down_all.at[there // 4, lax.rem(there, 4)],
        send_sem=local.at[5],
        recv_sem=local.at[6],
        device_id=target,
        device_id_type=MESH,
    )
    stayed = pltpu.make_async_copy(down, down_all.at[z, y], local.at[4])

    @pl.when(moves)
    def _():
        signal([source])
        greeted(6)
        moved.start()

    @pl.when(stays)
    def _():
        greeted(5)
        stayed.start()

    copies = Copies(send, recv)
    own[0].wait()
    own[1].wait()
    top, bottom = (slice(0, 16), slice(None)), (slice(16, 32), slice(None))
    dense = gather_both(
        y_then_z(qkv_all.at[core], *top),
        y_then_z(qkv_all.at[core], *bottom),
        z_then_y(out_all.at[core], *top),
        z_then_y(out_all.at[core], *bottom),
        copies,
    )
    next(dense)
    next(dense)
    next(dense)
    own[2].wait()
    own[3].wait()

    @pl.when(moves)
    def _():
        moved.wait()

    @pl.when(stays)
    def _():
        stayed.wait()

    left, right = (slice(None), slice(0, 512)), (slice(None), slice(512, D))
    wide = gather_both(
        y_then_z(gate_all), y_then_z(down_all, *left), z_then_y(up_all), z_then_y(down_all, *right), copies
    )
    next(wide)
    next(dense)
    next(wide)
    run(dense)
    halves = [copies(ref.at[core], ref.at[core], mate) for ref in (qkv_all, out_all)]
    next(wide)
    for each in halves:
        each.wait()
    for at in range(16):
        rows, cut = 56 * at, 56 * at + 32
        qkv_w[rows:cut] = qkv_all[0, at // 4, at % 4]
        qkv_w[cut : rows + 56] = qkv_all[1, at // 4, at % 4, :24]
        out_w[rows:cut] = out_all[0, at // 4, at % 4]
        out_w[cut : rows + 56] = out_all[1, at // 4, at % 4, :24]
    small = [qkv_all[1, at // 4, at % 4, 24:32].astype(F32)[:1] for at in range(16)]
    bias_ref[...] = jnp.concatenate([each[:, :72] for each in small], axis=1)
    gain1_ref[...] = jnp.concatenate([each[:, 72:128] for each in small], axis=1)
    gain2_ref[...] = jnp.concatenate([each[:, 128:184] for each in small], axis=1)
    front_work(x_ref, qkv_w, bias_ref, gain1_ref, cos_ref, sin_ref, normed_ref, q_ref, kv_ref, copies, lambda: None)
    next(wide)
    attention_work(
        x_ref, q_ref, kv_ref, kseg_ref, out_w, gain2_ref, context_ref, hidden_ref, normed2_ref,
        keys_ref, values_ref, bias0, bias1
    )
    run(wide)


def first(gate, up, down, qkv, out, x, cosine, sine, kseg):
    return pl.pallas_call(
        first_kernel,
        out_shape=(
            shaped(4, 4, *gate.shape),
            shaped(4, 4, *up.shape),
            shaped(4, 4, *down.shape),
            shaped(D, QKV),
            shaped(D, D),
            shaped(1, QKV, dtype=F32),
            shaped(1, D, dtype=F32),
            shaped(1, D, dtype=F32),
            shaped(ROWS, D, dtype=F32),
            shaped(ROWS, D),
        ),
        in_specs=[ANY_SPEC] * 5 + [VMEM_SPEC] * 4,
        out_specs=[ANY_SPEC] * 3 + [VMEM_SPEC] * 7,
        scratch_shapes=[
            pltpu.VMEM((2, 4, 4, *qkv.shape), BF),
            pltpu.VMEM((2, 4, 4, *out.shape), BF),
            pltpu.VMEM((ROWS, D), BF),
            pltpu.VMEM((ROWS, D), BF),
            pltpu.VMEM((2, 4, 4, 64, 2 * KV), BF),
            pltpu.VMEM((ROWS, D), BF),
        ]
        + ATTENTION_SCRATCH
        + [
            pltpu.SemaphoreType.DMA((74,)),
            pltpu.SemaphoreType.DMA((74,)),
            pltpu.SemaphoreType.DMA((7,)),
        ],
        compiler_params=params(0),
        name="first",
    )(gate, up, down, qkv, out, x, cosine, sine, kseg)


def scatter_phase(firsts, seconds, place, device_at, copies):
    right, left, far = (lax.rem(place + step, 4) for step in (1, 3, 2))

    def load(ref):
        return ref[...].astype(F32)

    first_far = [copies(block(far), bufs[0], device_at(1)) for block, bufs, put in firsts]
    second_far = [copies(block(far), bufs[0], device_at(3)) for block, bufs, put in seconds]
    first_near = [copies(block(left), bufs[2], device_at(3)) for block, bufs, put in firsts]
    second_near = [copies(block(right), bufs[1], device_at(1)) for block, bufs, put in seconds]

    def pass_on():
        first_sum, second_sum = [], []
        for came, (block, bufs, put) in zip(first_far, firsts):
            came.wait_recv()
            bufs[0][...] = (load(block(right)) + load(bufs[0])).astype(BF)
            first_sum.append(copies(bufs[0], bufs[1], device_at(1)))
        for came, (block, bufs, put) in zip(second_far, seconds):
            came.wait_recv()
            bufs[0][...] = (load(block(left)) + load(bufs[0])).astype(BF)
            second_sum.append(copies(bufs[0], bufs[2], device_at(3)))

        def finish():
            near, far_sum = first_near + second_near, first_sum + second_sum
            for one, two, (block, bufs, put) in zip(near, far_sum, firsts + seconds):
                one.wait_recv()
                two.wait_recv()
                put(load(block(place)) + load(bufs[1]) + load(bufs[2]))
            for each in first_far + second_far + near + far_sum:
                each.wait_send()

        return finish

    return pass_on


def scatter_both(first_a, second_a, first_b, second_b, copies):
    z, y, along_y, along_z = grid_place()

    def wide(part):
        block, bufs, _, _ = part
        return [(block, bufs, stored_in(bufs[1]))]

    def slim(part):
        _, kept, bufs, put = part
        return [((lambda at: kept[1].at[at]), bufs, put)]

    pass_a = scatter_phase(wide(first_a), wide(second_a), y, along_y, copies)
    pass_b = scatter_phase(wide(first_b), wide(second_b), z, along_z, copies)
    yield
    finish_a = pass_a()
    finish_b = pass_b()
    yield
    finish_a()
    pass_a = scatter_phase(slim(first_a), slim(second_a), z, along_z, copies)
    finish_b()
    pass_b = scatter_phase(slim(first_b), slim(second_b), y, along_y, copies)
    yield
    finish_a = pass_a()
    finish_b = pass_b()
    yield
    finish_a()
    finish_b()


def scatter_scratch(*shapes):
    scratch = []
    for shape in shapes:
        scratch += [pltpu.VMEM((4, *shape), BF)] * 3 + [pltpu.VMEM(shape, BF)] * 3
    return scratch


def scatter_part(scratch, index, block, put):
    mine = scratch[6 * index : 6 * index + 6]
    return block, mine[:3], mine[3:], put


def stored_in(ref, *at):
    def put(value):
        ref[at if at else ...] = value.astype(ref.dtype)

    return put


DOWN_STARTS = (0, 80, 160, 224)
DOWN_ROWS = 80


def mlp_terms(rows_ref, dgate_ref, dup_ref, product_ref, dout_ref, gate_terms, up_terms, down_terms):
    def flat(ref):
        return ref[...].reshape(4 * ROWS, ref.shape[-1])

    rows = flat(rows_ref)
    for terms, grads in ((gate_terms, dgate_ref), (up_terms, dup_ref)):
        whole = tn(rows, flat(grads))
        for at in range(16):
            terms[at // 4, at % 4] = whole[56 * at : 56 * at + 56].astype(BF)
    whole = tn(flat(product_ref), flat(dout_ref)).astype(BF)
    for at in range(16):
        start = 304 * (at // 4) + DOWN_STARTS[at % 4]
        down_terms[at // 4, at % 4] = whole[start : start + DOWN_ROWS]


def mlp_sums(gate_terms, up_terms, down_terms, gate_out, up_out, down_out, scratch, copies):
    left, right = slice(0, 512), slice(512, D)
    return scatter_both(
        scatter_part(scratch, 0, lambda at: gate_terms.at[:, at], stored_in(gate_out)),
        scatter_part(
            scratch, 2, lambda at: down_terms.at[:, at, :, left], stored_in(down_out, slice(None), left)
        ),
        scatter_part(scratch, 1, lambda at: up_terms.at[at], stored_in(up_out)),
        scatter_part(
            scratch, 3, lambda at: down_terms.at[at, :, :, right], stored_in(down_out, slice(None), right)
        ),
        copies,
    )


MLP_SUMS_SHAPES = ((56, QUARTER), (56, QUARTER), (DOWN_ROWS, 512), (DOWN_ROWS, D - 512))


def qkv_sums(qkv_half, out_half, qkv_sum, out_sum, scratch, copies):
    top, bottom = slice(0, 16), slice(16, 32)
    return scatter_both(
        scatter_part(scratch, 0, lambda at: qkv_half.at[:, at, top], stored_in(qkv_sum, top)),
        scatter_part(scratch, 1, lambda at: qkv_half.at[:, at, bottom], stored_in(qkv_sum, bottom)),
        scatter_part(scratch, 2, lambda at: out_half.at[at, :, top], stored_in(out_sum, top)),
        scatter_part(scratch, 3, lambda at: out_half.at[at, :, bottom], stored_in(out_sum, bottom)),
        copies,
    )


def kv_sums(dkv_ref, total, scratch, copies):
    top, bottom = slice(0, 32), slice(32, 64)
    return scatter_both(
        scatter_part(scratch, 0, lambda at: dkv_ref.at[0, :, at, top], stored_in(total, slice(0, 32))),
        scatter_part(scratch, 1, lambda at: dkv_ref.at[0, :, at, bottom], stored_in(total, slice(32, 64))),
        scatter_part(scratch, 2, lambda at: dkv_ref.at[1, at, :, top], stored_in(total, slice(64, 96))),
        scatter_part(scratch, 3, lambda at: dkv_ref.at[1, at, :, bottom], stored_in(total, slice(96, 128))),
        copies,
    )


def replica_partners():
    me = lax.axis_index("replica")
    return me, me + 1 - 2 * lax.rem(me, 2), lax.rem(me + 2, 4), 3 - me


def exchange(own_ref, all_ref, part, far_part, near_sum, part_in, far_in, near_in, copies, work):
    me, mate, next_, far = replica_partners()
    halves = (slice(0, 64), slice(64, 128))
    to_mate, to_next = {"replica": mate}, {"replica": next_}
    greeted(2)
    across = [copies(own_ref.at[half], all_ref.at[me, half], to_next) for half in halves]
    beside = copies(own_ref, all_ref.at[me], to_mate)
    all_ref[me] = own_ref[...]
    total = work([(me, slice(0, ROWS))])
    beside.wait_recv()
    part[...] = work([(mate, slice(0, ROWS))]).astype(BF)
    sent = [copies(part, part_in, to_mate)]
    forwards, sums = [], []
    for index, half in enumerate(halves):
        across[index].wait_recv()
        forwards.append(copies(all_ref.at[next_, half], all_ref.at[next_, half], to_mate))
        forwards[-1].wait_recv()
        terms = work([(next_, half), (far, half)])
        far_part[index] = terms[64:].astype(BF)
        passed = copies(far_part.at[index], far_in.at[index], to_mate)
        passed.wait_recv()
        near_sum[index] = (terms[:64] + far_in[index].astype(F32)).astype(BF)
        sums.append(copies(near_sum.at[index], near_in.at[index], to_next))
        sent.append(passed)
    sent[0].wait_recv()
    total = total + part_in[...].astype(F32)
    for each in sums:
        each.wait_recv()
    total = total + near_in[...].reshape(ROWS, D).astype(F32)
    for each in across + [beside] + forwards + sent + sums:
        each.wait_send()
    return total


EXCHANGE_SCRATCH = [
    pltpu.VMEM((D, QUARTER), BF),
    pltpu.VMEM((D, QUARTER), BF),
    pltpu.VMEM((QUARTER, D), BF),
    pltpu.VMEM((ROWS, D), BF),
    pltpu.VMEM((2, 64, D), BF),
    pltpu.VMEM((2, 64, D), BF),
    pltpu.VMEM((ROWS, D), BF),
    pltpu.VMEM((2, 64, D), BF),
    pltpu.VMEM((2, 64, D), BF),
    pltpu.SemaphoreType.DMA((10,)),
    pltpu.SemaphoreType.DMA((10,)),
    pltpu.SemaphoreType.DMA((18,)),
]


def mlp_start(hbm, vmem, local):
    me, mate, next_, far = replica_partners()
    signal([{"replica": mate}, {"replica": next_}])
    loads = [pltpu.make_async_copy(src, dst, local.at[i]) for i, (src, dst) in enumerate(zip(hbm[:2], vmem[:2]))]
    for at in range(16):
        skip = 80 * (at % 4) - DOWN_STARTS[at % 4]
        rows = pl.ds(304 * (at // 4) + 80 * (at % 4), DOWN_ROWS - skip)
        piece = hbm[2].at[at // 4, at % 4, pl.ds(skip, DOWN_ROWS - skip)]
        loads.append(pltpu.make_async_copy(piece, vmem[2].at[rows], local.at[2 + at]))
    for each in loads:
        each.start()
    return loads


def split_rows(value, parts):
    start = 0
    for source, rows in parts:
        count = rows.stop - rows.start
        yield source, rows, value[start : start + count]
        start += count


def mlp_forward_kernel(
    normed_ref, hidden_ref, gate_hbm, up_hbm, down_hbm, out_ref, all_ref, gate_ref, up_ref,
    gate_w, up_w, down_w, part, far_part, near_sum, part_in, far_in, near_in, send, recv, local
):
    loads = mlp_start((gate_hbm, up_hbm, down_hbm), (gate_w, up_w, down_w), local)
    waiting = list(loads)

    def work(parts):
        while waiting:
            waiting.pop().wait()
        rows = jnp.concatenate([all_ref[source, rows] for source, rows in parts], axis=0)
        gate = nn(rows, gate_w[...])
        up = nn(rows, up_w[...])
        for source, at, value in split_rows(gate, parts):
            gate_ref[source, at] = value.astype(BF)
        for source, at, value in split_rows(up, parts):
            up_ref[source, at] = value.astype(BF)
        product = (gate * jax.nn.sigmoid(gate) * up).astype(BF)
        return nn(product, down_w[...])

    total = exchange(
        normed_ref, all_ref, part, far_part, near_sum, part_in, far_in, near_in, Copies(send, recv), work
    )
    out_ref[...] = (hidden_ref[...] + total).astype(BF)


def mlp_forward(normed2, hidden, gate_w, up_w, down_w):
    return pl.pallas_call(
        mlp_forward_kernel,
        out_shape=(
            shaped(ROWS, D),
            shaped(4, ROWS, D),
            shaped(4, ROWS, QUARTER),
            shaped(4, ROWS, QUARTER),
        ),
        in_specs=[VMEM_SPEC] * 2 + [ANY_SPEC] * 3,
        scratch_shapes=EXCHANGE_SCRATCH,
        compiler_params=params(3),
        name="mlp_forward",
    )(normed2, hidden, gate_w, up_w, down_w)


def mlp_backward_kernel(
    dout_ref, gate_ref, up_ref, gate_hbm, up_hbm, down_hbm,
    dnormed_ref, all_ref, dgate_ref, dup_ref, product_ref,
    gate_w, up_w, down_w, part, far_part, near_sum, part_in, far_in, near_in, send, recv, local
):
    loads = mlp_start((gate_hbm, up_hbm, down_hbm), (gate_w, up_w, down_w), local)
    waiting = list(loads)

    def work(parts):
        while waiting:
            waiting.pop().wait()

        def stacked(ref):
            return jnp.concatenate([ref[source, rows] for source, rows in parts], axis=0)

        dproduct = nt(stacked(all_ref), down_w[...])
        gate = stacked(gate_ref).astype(F32)
        up = stacked(up_ref).astype(F32)
        s = jax.nn.sigmoid(gate)
        silu = gate * s
        product = (silu * up).astype(BF)
        dgate = (dproduct * up * (s * (1.0 + gate * (1.0 - s)))).astype(BF)
        dup = (dproduct * silu).astype(BF)
        for to, whole in ((product_ref, product), (dgate_ref, dgate), (dup_ref, dup)):
            for source, at, value in split_rows(whole, parts):
                to[source, at] = value
        return nt(dgate, gate_w[...]) + nt(dup, up_w[...])

    dnormed_ref[...] = exchange(
        dout_ref, all_ref, part, far_part, near_sum, part_in, far_in, near_in, Copies(send, recv), work
    )


def mlp_backward(dout, gate, up, gate_w, up_w, down_w):
    return pl.pallas_call(
        mlp_backward_kernel,
        out_shape=(
            shaped(ROWS, D, dtype=F32),
            shaped(4, ROWS, D),
            shaped(4, ROWS, QUARTER),
            shaped(4, ROWS, QUARTER),
            shaped(4, ROWS, QUARTER),
        ),
        in_specs=[VMEM_SPEC] * 3 + [ANY_SPEC] * 3,
        scratch_shapes=EXCHANGE_SCRATCH,
        compiler_params=params(4),
        name="mlp_backward",
    )(dout, gate, up, gate_w, up_w, down_w)


def outputs_kernel(
    gate, up, down, qkv, out, gate_out, up_out, down_out, qkv_out, out_out, bias_out, value_out, gain1_out, gain2_out
):
    for r in range(4):
        lanes = slice(QUARTER * r, QUARTER * r + QUARTER)
        gate_out[:, lanes] = gate[r].astype(F32)
        up_out[:, lanes] = up[r].astype(F32)
        skip = 80 * r - DOWN_STARTS[r]
        down_out[80 * r : DOWN_STARTS[r] + DOWN_ROWS] = down[r, skip:].astype(F32)
    qkv_out[:32] = qkv[0]
    qkv_out[32:] = qkv[1, :24]
    out_out[:32] = out[0]
    out_out[32:] = out[1, :24]
    small = qkv[1, 24:][:1]
    bias_out[...] = small[:, :64]
    value_out[...] = small[:, 64:72]
    gain1_out[...] = small[:, 72:128]
    gain2_out[...] = small[:, 128:184]


def outputs(gate, up, down, qkv, out):
    return local_call(
        outputs_kernel,
        "outputs",
        (
            shaped(56, FF, dtype=F32),
            shaped(56, FF, dtype=F32),
            shaped(FF // 16, D, dtype=F32),
            shaped(56, QKV, dtype=F32),
            shaped(56, D, dtype=F32),
            shaped(1, 64, dtype=F32),
            shaped(1, 8, dtype=F32),
            shaped(1, 56, dtype=F32),
            shaped(1, 56, dtype=F32),
        ),
    )(gate, up, down, qkv, out)


def turn(values, cosine, sine, sign):
    width = values.shape[1]
    up = pltpu.roll(values, width - HALF, 1)
    down = pltpu.roll(values, HALF, 1)
    lane = lax.broadcasted_iota(jnp.int32, values.shape, 1)
    swapped = jnp.where(lax.rem(lane, 2 * HALF) < HALF, up, down)
    repeat = width // KV
    cosine = jnp.concatenate([cosine] * repeat, axis=1)
    sine = jnp.concatenate([sine] * repeat, axis=1)
    return values * cosine + sign * (swapped * sine)


def front_work(x_ref, w_ref, b_ref, g_ref, cos_ref, sin_ref, normed_ref, q_ref, kv_ref, copies, ready):
    z, y, along_y, along_z = grid_place()
    x = x_ref[...].astype(F32)
    inverse = lax.rsqrt(jnp.mean(x * x, axis=-1, keepdims=True) + EPSILON)
    normed = (x * inverse * g_ref[...]).astype(BF)
    normed_ref[...] = normed
    projected = nn(normed, w_ref[:, D:]) + b_ref[:, D:]
    turned = turn(projected[:, :KV], cos_ref[...], sin_ref[...], 1.0)
    kv = jnp.concatenate([turned, projected[:, KV:]], axis=1).astype(BF)
    kv_ref[0, z, y] = kv[:64]
    kv_ref[1, z, y] = kv[64:]
    ready()
    top, bottom = (slice(0, 32), slice(None)), (slice(32, 64), slice(None))
    steps = gather_both(
        y_then_z(kv_ref.at[0], *top),
        y_then_z(kv_ref.at[0], *bottom),
        z_then_y(kv_ref.at[1], *top),
        z_then_y(kv_ref.at[1], *bottom),
        copies,
    )
    next(steps)
    projected = nn(normed, w_ref[:, :D]) + b_ref[:, :D]
    q_ref[...] = turn(projected, cos_ref[...], sin_ref[...], 1.0).astype(BF)
    run(steps)


def front_kernel(x_ref, w_ref, b_ref, g_ref, cos_ref, sin_ref, normed_ref, q_ref, kv_ref, send, recv):
    z, y, along_y, along_z = grid_place()
    signal(neighbours(along_y, along_z))
    front_work(
        x_ref, w_ref, b_ref, g_ref, cos_ref, sin_ref, normed_ref, q_ref, kv_ref,
        Copies(send, recv), lambda: greeted(4)
    )


def front(x, w_qkv, b_qkv, g_attn, cosine, sine):
    return pl.pallas_call(
        front_kernel,
        out_shape=(shaped(ROWS, D), shaped(ROWS, D), shaped(2, 4, 4, 64, 2 * KV)),
        scratch_shapes=[pltpu.SemaphoreType.DMA((24,)), pltpu.SemaphoreType.DMA((24,))],
        compiler_params=params(6),
        name="front",
    )(x, w_qkv, b_qkv, g_attn, cosine, sine)


def low_lanes(rows):
    return lax.broadcasted_iota(jnp.int32, (rows, KV), 1) < KV // 2


def spread(kv_ref, start, to_ref):
    mixed = kv_ref[:, :, :, :, start : start + KV].reshape(LEN, KV)
    other = pltpu.roll(mixed.astype(F32), KV // 2, 1).astype(BF)
    low = low_lanes(LEN)
    to_ref[0] = jnp.where(low, mixed, other)
    to_ref[1] = mixed
    to_ref[2] = jnp.where(low, other, mixed)


def fill_bias(kseg_ref, bias_refs):
    first_row = 64 * lax.axis_index("group")
    for block, bias_ref in enumerate(bias_refs):
        keys = SPAN * (block + 1)
        kpos = lax.broadcasted_iota(jnp.int32, (64, keys), 1)
        qpos = SPAN * block + first_row + lax.broadcasted_iota(jnp.int32, (64, keys), 0)
        kseg = jnp.broadcast_to(kseg_ref[:, :keys], (64, keys)).astype(F32)
        qseg = jnp.sum(jnp.where(kpos == qpos, kseg, 0.0), axis=1, keepdims=True)
        bias_ref[...] = jnp.where((kpos <= qpos) & (kseg == qseg), 0.0, NEGATIVE)


def two_heads(pair):
    low = low_lanes(64)
    zero = jnp.zeros_like(pair)
    return jnp.concatenate([jnp.where(low, pair, zero), jnp.where(low, zero, pair)], axis=0)


def one_pair(stacked):
    return jnp.where(low_lanes(64), stacked[:64], stacked[64:])


def softmax(queries, keys, bias_ref):
    count = keys.shape[0]
    scores = nt(queries, keys).reshape(2, 64, count) + bias_ref[...][None]
    highest = jnp.max(scores, axis=-1, keepdims=True)
    exponent = jnp.exp(scores - highest)
    total = jnp.sum(exponent, axis=-1, keepdims=True)
    return (exponent * (1.0 / total)).reshape(2 * 64, count)


def variant_of(pair):
    return jnp.where(pair < 3, 0, jnp.where(pair == 3, 1, 2))


def attention_work(
    x_ref, q_ref, kv_ref, kseg_ref, w_ref, g_ref, context_ref, hidden_ref, normed_ref,
    keys_ref, values_ref, bias0, bias1
):
    spread(kv_ref, 0, keys_ref)
    spread(kv_ref, KV, values_ref)
    fill_bias(kseg_ref, (bias0, bias1))

    def one(pair, carry):
        variant = variant_of(pair)
        lanes = pl.ds(pl.multiple_of(pair * KV, KV), KV)
        for block, bias_ref in enumerate((bias0, bias1)):
            rows = slice(64 * block, 64 * block + 64)
            keys = pl.ds(0, SPAN * (block + 1))
            queries = two_heads(q_ref[rows, lanes] * SCALE).astype(BF)
            weights = softmax(queries, keys_ref[variant, keys], bias_ref).astype(BF)
            context = nn(weights, values_ref[variant, keys])
            context_ref[rows, lanes] = one_pair(context).astype(BF)
        return carry

    lax.fori_loop(0, PAIRS, one, 0)
    hidden = x_ref[...].astype(F32) + nn(context_ref[...], w_ref[...])
    hidden_ref[...] = hidden
    inverse = lax.rsqrt(jnp.mean(hidden * hidden, axis=-1, keepdims=True) + EPSILON)
    normed_ref[...] = (hidden * inverse * g_ref[...]).astype(BF)


ATTENTION_SCRATCH = [
    pltpu.VMEM((3, LEN, KV), BF),
    pltpu.VMEM((3, LEN, KV), BF),
    pltpu.VMEM((64, SPAN), F32),
    pltpu.VMEM((64, LEN), F32),
]


def attention(x, q, kv, kseg, w_out, g_mlp):
    return local_call(
        attention_work,
        "attention",
        (shaped(ROWS, D), shaped(ROWS, D, dtype=F32), shaped(ROWS, D)),
        ATTENTION_SCRATCH,
    )(x, q, kv, kseg, w_out, g_mlp)


def norm_backward(values, gain, grads):
    inverse = lax.rsqrt(jnp.mean(values * values, axis=-1, keepdims=True) + EPSILON)
    scaled = grads * gain
    dvalues = inverse * scaled - values * (
        inverse * inverse * inverse * jnp.mean(scaled * values, axis=-1, keepdims=True)
    )
    return dvalues, jnp.sum(grads * values * inverse, axis=0, keepdims=True)


def attention_backward_work(
    dout_ref, dnormed_ref, hidden_ref, g_ref, w_ref, q_ref, kv_ref, kseg_ref,
    dhidden_ref, dlow_ref, dq_ref, dkv_ref, dgain_ref,
    keys_ref, values_ref, bias0, bias1, dcontext_ref, dkeys, dvalues
):
    dnorm, dgain = norm_backward(hidden_ref[...], g_ref[...], dnormed_ref[...])
    dgain_ref[...] = dgain
    dhidden = dout_ref[...].astype(F32) + dnorm
    dhidden_ref[...] = dhidden
    dlow = dhidden.astype(BF)
    dlow_ref[...] = dlow
    dcontext_ref[...] = nt(dlow, w_ref[...]).astype(BF)
    spread(kv_ref, 0, keys_ref)
    spread(kv_ref, KV, values_ref)
    fill_bias(kseg_ref, (bias0, bias1))
    dkeys[...] = jnp.zeros_like(dkeys)
    dvalues[...] = jnp.zeros_like(dvalues)

    def one(pair, carry):
        variant = variant_of(pair)
        lanes = pl.ds(pl.multiple_of(pair * KV, KV), KV)
        for block, bias_ref in enumerate((bias0, bias1)):
            rows = slice(64 * block, 64 * block + 64)
            keys = pl.ds(0, SPAN * (block + 1))
            queries = two_heads(q_ref[rows, lanes] * SCALE).astype(BF)
            dcontext = two_heads(dcontext_ref[rows, lanes])
            key_rows = keys_ref[variant, keys]
            weights = softmax(queries, key_rows, bias_ref)
            dweights = nt(dcontext, values_ref[variant, keys])
            inner = jnp.sum(weights * dweights, axis=-1, keepdims=True)
            dscores = (weights * (dweights - inner)).astype(BF)
            dq_ref[rows, lanes] = one_pair(nn(dscores, key_rows)) * SCALE
            dkeys[variant, keys] += tn(dscores, queries)
            dvalues[variant, keys] += tn(weights.astype(BF), dcontext)
        return carry

    lax.fori_loop(0, PAIRS, one, 0)
    low = low_lanes(LEN)
    for start, total in ((0, dkeys), (KV, dvalues)):
        head0 = total[0] + pltpu.roll(total[0], KV // 2, 1)
        head1 = total[2] + pltpu.roll(total[2], KV // 2, 1)
        whole = (jnp.where(low, head0, head1) + total[1]).astype(BF)
        dkv_ref[:, :, :, :, start : start + KV] = whole.reshape(2, 4, 4, 64, KV)


ATTENTION_BACKWARD_OUT = (
    shaped(ROWS, D, dtype=F32),
    shaped(ROWS, D),
    shaped(ROWS, D, dtype=F32),
    shaped(2, 4, 4, 64, 2 * KV),
    shaped(1, D, dtype=F32),
)
ATTENTION_BACKWARD_SCRATCH = ATTENTION_SCRATCH + [
    pltpu.VMEM((ROWS, D), BF),
    pltpu.VMEM((3, LEN, KV), F32),
    pltpu.VMEM((3, LEN, KV), F32),
]


def attention_backward(*operands):
    return local_call(
        attention_backward_work, "attention_backward", ATTENTION_BACKWARD_OUT, ATTENTION_BACKWARD_SCRATCH
    )(*operands)


def rear_query(dq_ref, cos_ref, sin_ref, w_ref, dprojected_ref, dbias_ref):
    dquery = turn(dq_ref[...], cos_ref[...], sin_ref[...], -1.0).astype(BF)
    dprojected_ref[:, :D] = dquery
    dbias_ref[:, :D] = jnp.sum(dquery.astype(F32), axis=0, keepdims=True)
    return nt(dquery, w_ref[:, :D])


def rear_rest(
    dnormed, total, cos_ref, sin_ref, w_ref, x_ref, g_ref, dhidden_ref, dprojected_ref, dinput_ref, dgain_ref, dbias_ref
):
    turned = turn(total[:, :KV], cos_ref[...], sin_ref[...], -1.0)
    dkv = jnp.concatenate([turned, total[:, KV:]], axis=1).astype(BF)
    dprojected_ref[:, D:] = dkv
    dbias_ref[:, D:] = jnp.sum(dkv.astype(F32), axis=0, keepdims=True)
    dnormed = dnormed + nt(dkv, w_ref[:, D:])
    dnorm, dgain = norm_backward(x_ref[...].astype(F32), g_ref[...], dnormed)
    dgain_ref[...] = dgain
    dinput_ref[...] = (dhidden_ref[...] + dnorm).astype(BF)


REAR_SCRATCH = [
    pltpu.VMEM((ROWS, QKV), BF),
    pltpu.VMEM((1, D), F32),
    pltpu.VMEM((1, QKV), F32),
    pltpu.VMEM((ROWS, 2 * KV), F32),
] + scatter_scratch(*[(32, 2 * KV)] * 4)


def rear_kernel(
    dkv_ref, dq_ref, cos_ref, sin_ref, w_ref, x_ref, g_ref, dhidden_ref, dinput_ref,
    dprojected_ref, dgain_ref, dbias_ref, total, *rest
):
    scratch, (send, recv) = rest[:-2], rest[-2:]
    z, y, along_y, along_z = grid_place()
    signal(neighbours(along_y, along_z))
    greeted(4)
    steps = kv_sums(dkv_ref, total, scratch, Copies(send, recv))
    next(steps)
    dnormed = rear_query(dq_ref, cos_ref, sin_ref, w_ref, dprojected_ref, dbias_ref)
    run(steps)
    rear_rest(
        dnormed, total, cos_ref, sin_ref, w_ref, x_ref, g_ref, dhidden_ref,
        dprojected_ref, dinput_ref, dgain_ref, dbias_ref
    )


def rear(dkv, dq, cosine, sine, w_qkv, x, g_attn, dhidden):
    return pl.pallas_call(
        rear_kernel,
        out_shape=shaped(ROWS, D),
        scratch_shapes=REAR_SCRATCH + [pltpu.SemaphoreType.DMA((24,)), pltpu.SemaphoreType.DMA((24,))],
        compiler_params=params(7),
        name="rear",
    )(dkv, dq, cosine, sine, w_qkv, x, g_attn, dhidden)


TAIL_SCRATCH = [
    pltpu.VMEM((4, 4, 56, QUARTER), BF),
    pltpu.VMEM((4, 4, 56, QUARTER), BF),
    pltpu.VMEM((4, 4, DOWN_ROWS, D), BF),
    pltpu.VMEM((56, QUARTER), BF),
    pltpu.VMEM((56, QUARTER), BF),
    pltpu.VMEM((DOWN_ROWS, D), BF),
    pltpu.VMEM((4, 4, 64, QKV), BF),
    pltpu.VMEM((4, 4, 64, D), BF),
    pltpu.VMEM((4, 4, 32, QKV), BF),
    pltpu.VMEM((4, 4, 32, D), BF),
    pltpu.VMEM((32, QKV), F32),
    pltpu.VMEM((32, D), F32),
    pltpu.VMEM((32, QKV), BF),
    pltpu.VMEM((32, D), BF),
    pltpu.VMEM((32, QKV), BF),
    pltpu.VMEM((32, D), BF),
]
TAIL_COPIES = 24 * 3 + 2 + 13


def tail_kernel(*refs):
    refs = list(refs)

    def take(count):
        taken = refs[:count]
        del refs[:count]
        return taken

    attention_in = take(8)
    mlp_in = take(5)
    cos_ref, sin_ref, qkv_w, x_ref, gain1_ref, normed_ref, context_ref = take(7)
    dinput_ref, gate_all, up_all, down_all, qkv_all, out_all = take(6)
    attention_out = take(5)
    dhidden_ref, dlow_ref, dq_ref, dkv_ref, dgain2_ref = attention_out
    attention_scratch = take(len(ATTENTION_BACKWARD_SCRATCH))
    dprojected_ref, dgain1_ref, dbias_ref, total = take(4)
    kv_bufs = take(24)
    mlp_term_refs, mlp_sum_refs = take(3), take(3)
    qkv_terms, out_terms, qkv_half, out_half, qkv_sum, out_sum, qkv_low, out_low, qkv_in, out_in = take(10)
    mlp_bufs, qkv_bufs = take(24), take(24)
    send, recv, local = take(3)

    z, y, along_y, along_z = grid_place()
    me, mate, next_, far = replica_partners()
    core = lax.rem(me, 2)
    to_mate, to_next = {"replica": mate}, {"replica": next_}
    target, source, stays = quarter_route()
    moves = jnp.logical_not(stays)
    signal(neighbours(along_y, along_z) + [to_mate, to_next])
    mlp_terms(*mlp_in, *mlp_term_refs)

    @pl.when(moves)
    def _():
        signal([target])
        greeted(7)

    @pl.when(stays)
    def _():
        greeted(6)

    copies = Copies(send, recv)
    mlp = mlp_sums(*mlp_term_refs, *mlp_sum_refs, mlp_bufs, copies)
    next(mlp)
    attention_backward_work(*attention_in, *attention_out, *attention_scratch)
    kv = kv_sums(dkv_ref, total, kv_bufs, copies)
    next(kv)
    next(mlp)

    mine = pl.ds(pl.multiple_of(32 * core, 32), 32)
    theirs = pl.ds(pl.multiple_of(32 - 32 * core, 32), 32)

    def add_mate(sent, terms, half):
        sent.wait_recv()
        half[...] = (terms[:, :, mine].astype(F32) + half[...].astype(F32)).astype(BF)

    dnormed = rear_query(dq_ref, cos_ref, sin_ref, qkv_w, dprojected_ref, dbias_ref)
    next(kv)
    whole = tn(context_ref[...], dlow_ref[...])
    for at in range(16):
        rows = jnp.concatenate([whole[56 * at : 56 * at + 56], jnp.zeros((8, D), F32)], axis=0)
        out_terms[at // 4, at % 4] = rows.astype(BF)
    out_sent = copies(out_terms.at[:, :, theirs], out_half, to_mate)
    next(kv)
    add_mate(out_sent, out_terms, out_half)
    run(kv)
    rear_rest(
        dnormed, total, cos_ref, sin_ref, qkv_w, x_ref, gain1_ref, dhidden_ref,
        dprojected_ref, dinput_ref, dgain1_ref, dbias_ref
    )
    whole = tn(normed_ref[...], dprojected_ref[...])
    dbias, dgain1, dgain2 = dbias_ref[...], dgain1_ref[...], dgain2_ref[...]
    for at in range(16):
        small = jnp.concatenate(
            [
                dbias[:, 64 * at : 64 * at + 64],
                dbias[:, D + KV + 8 * at : D + KV + 8 * at + 8],
                dgain1[:, 56 * at : 56 * at + 56],
                dgain2[:, 56 * at : 56 * at + 56],
                jnp.zeros((1, QKV - 184), F32),
            ],
            axis=1,
        )
        rows = jnp.concatenate([whole[56 * at : 56 * at + 56], jnp.broadcast_to(small, (8, QKV))], axis=0)
        qkv_terms[at // 4, at % 4] = rows.astype(BF)
    qkv_sent = copies(qkv_terms.at[:, :, theirs], qkv_half, to_mate)
    next(mlp)
    add_mate(qkv_sent, qkv_terms, qkv_half)
    dense = qkv_sums(qkv_half, out_half, qkv_sum, out_sum, qkv_bufs, copies)
    next(dense)
    next(mlp)
    next(dense)
    run(mlp)

    gate, up, down = mlp_sum_refs
    moved = pltpu.make_async_remote_copy(
        src_ref=down,
        dst_ref=down_all.at[source["replica"]],
        send_sem=local.at[0],
        recv_sem=local.at[1],
        device_id=source,
        device_id_type=MESH,
    )
    stayed = pltpu.make_async_copy(down, down_all.at[me], local.at[2])

    @pl.when(moves)
    def _():
        moved.start()

    @pl.when(stays)
    def _():
        stayed.start()

    pairs = ((gate, gate_all), (up, up_all))
    across = [copies(ref, all_ref.at[me], to_next) for ref, all_ref in pairs]
    beside = [copies(ref, all_ref.at[me], to_mate) for ref, all_ref in pairs]
    for ref, all_ref in pairs:
        all_ref[me] = ref[...]
    next(dense)

    @pl.when(moves)
    def _():
        moved.wait()

    @pl.when(stays)
    def _():
        stayed.wait()

    across.append(copies(down_all.at[me], down_all.at[me], to_next))
    beside.append(copies(down_all.at[me], down_all.at[me], to_mate))
    next(dense)
    run(dense)
    qkv_low[...] = qkv_sum[...].astype(BF)
    out_low[...] = out_sum[...].astype(BF)
    sums = [copies(qkv_low, qkv_in, to_next), copies(out_low, out_in, to_next)]
    for came, all_ref in zip(across, (gate_all, up_all, down_all)):
        came.wait_recv()
        beside.append(copies(all_ref.at[next_], all_ref.at[next_], to_mate))
    sums[0].wait_recv()
    qkv_all[core] = qkv_sum[...] + qkv_in[...].astype(F32)
    sums[1].wait_recv()
    out_all[core] = out_sum[...] + out_in[...].astype(F32)
    beside += [copies(ref.at[core], ref.at[core], to_mate) for ref in (qkv_all, out_all)]
    for each in beside:
        each.wait_recv()
    for each in [out_sent, qkv_sent] + across + beside + sums:
        each.wait_send()


def tail(*operands):
    return pl.pallas_call(
        tail_kernel,
        out_shape=(
            shaped(ROWS, D),
            shaped(4, 56, QUARTER),
            shaped(4, 56, QUARTER),
            shaped(4, DOWN_ROWS, D),
            shaped(2, 32, QKV, dtype=F32),
            shaped(2, 32, D, dtype=F32),
        ),
        scratch_shapes=[pltpu.VMEM(each.shape, each.dtype) for each in ATTENTION_BACKWARD_OUT]
        + ATTENTION_BACKWARD_SCRATCH
        + REAR_SCRATCH
        + TAIL_SCRATCH
        + scatter_scratch(*MLP_SUMS_SHAPES)
        + scatter_scratch((16, QKV), (16, QKV), (16, D), (16, D))
        + [
            pltpu.SemaphoreType.DMA((TAIL_COPIES,)),
            pltpu.SemaphoreType.DMA((TAIL_COPIES,)),
            pltpu.SemaphoreType.DMA((3,)),
        ],
        compiler_params=params(1),
        name="tail",
    )(*operands)


def rotary(group):
    lane = np.arange(KV)
    frequency = jnp.asarray(THETA ** (-(lane % HALF) * 2.0 / (2 * HALF)), F32)
    sign = jnp.asarray(np.where(lane % (2 * HALF) < HALF, -1.0, 1.0), F32)
    row = lax.broadcasted_iota(jnp.int32, (ROWS, KV), 0)
    positions = group * 64 + lax.rem(row, 64) + SPAN * (row // 64)
    angles = positions.astype(F32) * frequency[None, :]
    return jnp.cos(angles), jnp.sin(angles) * sign[None, :]


def body(inputs, cotangent, segments, w_qkv, b_qkv, w_out, w_gate, w_up, w_down, g_attn, g_mlp):
    section = lax.axis_index("section")
    group = lax.axis_index("group")
    replica = lax.axis_index("replica")
    core = lax.rem(replica, 2)

    down_piece = lax.dynamic_slice(w_down[0], (jnp.minimum(80 * replica, 224), 0), (DOWN_ROWS, D))
    gate_piece = lax.dynamic_slice(w_gate[0], (0, replica * QUARTER), (D // 16, QUARTER))
    up_piece = lax.dynamic_slice(w_up[0], (0, replica * QUARTER), (D // 16, QUARTER))
    small = jnp.concatenate([b_qkv[0], g_attn[0], g_mlp[0]])
    small = jnp.pad(small[None], ((0, 7), (0, QKV - small.shape[0])))
    qkv_piece = lax.dynamic_slice(jnp.concatenate([w_qkv[0], small], axis=0), (32 * core, 0), (32, QKV))
    out_piece = lax.dynamic_slice(jnp.pad(w_out[0], ((0, 8), (0, 0))), (32 * core, 0), (32, D))

    cosine, sine = rotary(group)
    kseg = segments
    x_in = inputs[0].reshape(ROWS, D)
    cotangent_in = cotangent[0].reshape(ROWS, D)
    gate_w, up_w, down_w, qkv_w, out_w, bias, gain1, gain2, hidden, normed2 = first(
        gate_piece, up_piece, down_piece, qkv_piece, out_piece, x_in, cosine, sine, kseg
    )
    gate_w = gate_w.reshape(D, QUARTER)
    up_w = up_w.reshape(D, QUARTER)

    def forward(x):
        normed, q, kv = front(x, qkv_w, bias, gain1, cosine, sine)
        context, hidden, normed2 = attention(x, q, kv, kseg, out_w, gain2)
        output, normed2_all, gate, up = mlp_forward(normed2, hidden, gate_w, up_w, down_w)
        return output, (x, normed, q, kv, context, hidden, normed2_all, gate, up)

    def backward_start(dout):
        dnormed2, *grads = mlp_backward(dout, gate, up, gate_w, up_w, down_w)
        dout_all, dgate, dup, product = grads
        return (dout, dnormed2, hidden, gain2, out_w, q, kv, kseg), (normed2_all, dgate, dup, product, dout_all)

    relayed, *_ = mlp_forward(normed2, hidden, gate_w, up_w, down_w)
    relayed = lax.ppermute(relayed, "section", [(0, 1)])
    output, kept = forward(jnp.where(section == 0, x_in, relayed))
    x, normed, q, kv, context, hidden, normed2_all, gate, up = kept
    operands, _ = backward_start(cotangent_in)
    dhidden, _, dq, dkv, _ = attention_backward(*operands)
    returned = rear(dkv, dq, cosine, sine, qkv_w, x, gain1, dhidden)
    returned = lax.ppermute(returned, "section", [(1, 0)])
    operands, mlp_operands = backward_start(jnp.where(section == 1, cotangent_in, returned))
    dinput, *parts = tail(*operands, *mlp_operands, cosine, sine, qkv_w, x, gain1, normed, context)
    grad_gate, grad_up, grad_down, grad_qkv, grad_out, bias, value_bias, gain1, gain2 = outputs(*parts)
    return (
        output.reshape(1, 1, 2, 64, D),
        dinput.reshape(1, 1, 2, 64, D),
        grad_qkv[None],
        bias,
        value_bias,
        grad_out[None],
        grad_gate[None],
        grad_up[None],
        grad_down[None],
        gain1,
        gain2,
    )


def solution(mesh):
    in_specs = (
        P("replica", None, "group", None),
        P("replica", None, "group", None),
        P("replica", None),
        P("section", "group", None),
        P("section", "group"),
        P("section", "group", None),
        P("section", "group", None),
        P("section", "group", None),
        P("section", "group", None),
        P("section", "group"),
        P("section", "group"),
    )
    out_specs = (
        P("section", "replica", None, "group", None),
        P("section", "replica", None, "group", None),
        P("section", "group", None),
        P("section", "group"),
        P("section", "group"),
        P("section", "group", None),
        P("section", "group", None),
        P("section", "group", None),
        P("section", "group", None),
        P("section", "group"),
        P("section", "group"),
    )
    return jax.shard_map(body, mesh=mesh, in_specs=in_specs, out_specs=out_specs, check_vma=False)
```

```python
import functools

import jax
import jax.numpy as jnp
import numpy as np
from jax import lax
from jax.experimental import pallas as pl
from jax.experimental.pallas import tpu as pltpu
from jax.sharding import PartitionSpec as P

D = 896
HEADS = 14
KV = 128
HALF = 32
FF = 4864
QUARTER = FF // 4
QKV = 1152
ROWS = 128
SPAN = 1024
LEN = 2048
PAIRS = 7
EPSILON = 1e-06
THETA = 1000000.0
NEGATIVE = -1e30
SCALE = 0.125
VMEM_LIMIT = 60 * 1024 * 1024
MESH = pl.DeviceIdType.MESH
BF = jnp.bfloat16
F32 = jnp.float32
VMEM_SPEC = pl.BlockSpec(memory_space=pltpu.VMEM)
ANY_SPEC = pl.BlockSpec(memory_space=pl.ANY)


def nn(a, b):
    return lax.dot_general(a, b, (((1,), (0,)), ((), ())), preferred_element_type=F32)


def nt(a, b):
    return lax.dot_general(a, b, (((1,), (1,)), ((), ())), preferred_element_type=F32)


def tn(a, b):
    return lax.dot_general(a, b, (((0,), (0,)), ((), ())), preferred_element_type=F32)


def params(collective_id=None):
    if collective_id is None:
        return pltpu.CompilerParams(vmem_limit_bytes=VMEM_LIMIT)
    return pltpu.CompilerParams(
        vmem_limit_bytes=VMEM_LIMIT, collective_id=collective_id, has_side_effects=True
    )


def shaped(*shape, dtype=BF):
    return jax.ShapeDtypeStruct(shape, dtype)


def local_call(kernel, name, out_shape, scratch=()):
    return pl.pallas_call(
        kernel,
        out_shape=out_shape,
        scratch_shapes=list(scratch),
        compiler_params=params(),
        name=name,
    )


def signal(devices):
    barrier = pltpu.get_barrier_semaphore()
    for device in devices:
        pl.semaphore_signal(barrier, inc=1, device_id=device, device_id_type=MESH)


def greeted(count):
    pl.semaphore_wait(pltpu.get_barrier_semaphore(), count)


def grid_place():
    me = lax.axis_index("group")
    z = me // 4
    y = lax.rem(me, 4)

    def along_y(step):
        return {"group": z * 4 + lax.rem(y + step, 4)}

    def along_z(step):
        return {"group": lax.rem(z + step, 4) * 4 + y}

    return z, y, along_y, along_z


def neighbours(along_y, along_z):
    return [along_y(1), along_y(3), along_z(1), along_z(3)]


class Copies:
    def __init__(self, send, recv):
        self.send, self.recv, self.used = send, recv, 0

    def __call__(self, src, dst, device, start=True):
        index = self.used
        self.used += 1
        each = pltpu.make_async_remote_copy(
            src_ref=src,
            dst_ref=dst,
            send_sem=self.send.at[index],
            recv_sem=self.recv.at[index],
            device_id=device,
            device_id_type=MESH,
        )
        if start:
            each.start()
        return each


def gather_phase(firsts, seconds, place, device_at, copies):
    def copy(block, slot, step):
        return copies(block(slot), block(slot), device_at(step), False)

    firsts_right = [copy(block, place, 1) for block in firsts]
    seconds_left = [copy(block, place, 3) for block in seconds]
    others = [copy(block, place, 3) for block in firsts] + [copy(block, place, 1) for block in seconds]
    relays = [copy(block, lax.rem(place + 3, 4), 1) for block in firsts]
    relays += [copy(block, lax.rem(place + 1, 4), 3) for block in seconds]

    def start():
        for each in firsts_right + seconds_left + others:
            each.start()

    def relay():
        for came, each in zip(firsts_right + seconds_left, relays):
            came.wait_recv()
            each.start()

    def finish():
        for each in others + relays:
            each.wait_recv()
        for each in firsts_right + seconds_left + others + relays:
            each.wait_send()

    return start, relay, finish


def gather_both(first_a, second_a, first_b, second_b, copies):
    z, y, along_y, along_z = grid_place()
    start_a, relay_a, finish_a = gather_phase([first_a[0]], [second_a[0]], y, along_y, copies)
    start_b, relay_b, finish_b = gather_phase([first_b[0]], [second_b[0]], z, along_z, copies)
    then_a, last_a, end_a = gather_phase([first_a[1]], [second_a[1]], z, along_z, copies)
    then_b, last_b, end_b = gather_phase([first_b[1]], [second_b[1]], y, along_y, copies)
    start_a()
    start_b()
    yield
    relay_a()
    relay_b()
    yield
    finish_a()
    then_a()
    finish_b()
    then_b()
    yield
    last_a()
    last_b()
    yield
    end_a()
    end_b()


def gather_split(first_a, second_a, first_b, second_b, copies):
    z, y, along_y, along_z = grid_place()
    slim = [
        gather_phase([first_a[0]], [second_a[0]], y, along_y, copies),
        gather_phase([first_b[0]], [second_b[0]], z, along_z, copies),
    ]

    def wide(half):
        def part(function):
            return [lambda at: function(at, half)]

        return [
            gather_phase(part(first_a[1]), part(second_a[1]), z, along_z, copies),
            gather_phase(part(first_b[1]), part(second_b[1]), y, along_y, copies),
        ]

    halves = [wide(slice(0, 2)), wide(slice(2, 4))]
    for start, _, _ in slim:
        start()
    yield
    for _, relay, _ in slim:
        relay()
    yield
    for _, _, finish in slim:
        finish()
    for phases in halves:
        for start, _, _ in phases:
            start()
        yield
        for _, relay, _ in phases:
            relay()
        yield
    for phases in halves:
        for _, _, finish in phases:
            finish()


def run(steps):
    for _ in steps:
        pass


def y_then_z(ref, *tail):
    z = lax.axis_index("group") // 4
    return (lambda at: ref.at[(z, at, *tail)]), (lambda at, part=slice(None): ref.at[(at, part, *tail)])


def z_then_y(ref, *tail):
    y = lax.rem(lax.axis_index("group"), 4)
    return (lambda at: ref.at[(at, y, *tail)]), (lambda at, part=slice(None): ref.at[(part, at, *tail)])


def quarter_route():
    group, replica = lax.axis_index("group"), lax.axis_index("replica")
    target = {"group": 4 * lax.rem(group, 4) + replica, "replica": group // 4}
    source = {"group": 4 * replica + group // 4, "replica": lax.rem(group, 4)}
    stays = (target["group"] == group) & (target["replica"] == replica)
    return target, source, stays


def first_kernel(
    gate, up, down, qkv, out, x_ref, cos_ref, sin_ref, kseg_ref,
    gate_all, up_all, down_all, qkv_w, out_w, bias_ref, gain1_ref, gain2_ref, hidden_ref, normed2_ref,
    qkv_all, out_all, normed_ref, q_ref, kv_ref, context_ref, keys_ref, values_ref, bias0, bias1, send, recv, local
):
    z, y, along_y, along_z = grid_place()
    core = lax.rem(lax.axis_index("replica"), 2)
    mate = {"replica": lax.axis_index("replica") + 1 - 2 * core}
    target, source, stays = quarter_route()
    moves = jnp.logical_not(stays)
    signal(neighbours(along_y, along_z) + [mate])
    places = (qkv_all.at[core, z, y], out_all.at[core, z, y], gate_all.at[z, y], up_all.at[z, y])
    own = []
    for index, (src, dst) in enumerate(zip((qkv, out, gate, up), places)):
        own.append(pltpu.make_async_copy(src, dst, local.at[index]))
        own[-1].start()
    there = target["group"]
    moved = pltpu.make_async_remote_copy(
        src_ref=down,
        dst_ref=down_all.at[there // 4, lax.rem(there, 4)],
        send_sem=local.at[5],
        recv_sem=local.at[6],
        device_id=target,
        device_id_type=MESH,
    )
    stayed = pltpu.make_async_copy(down, down_all.at[z, y], local.at[4])

    @pl.when(moves)
    def _():
        signal([source])
        greeted(6)
        moved.start()

    @pl.when(stays)
    def _():
        greeted(5)
        stayed.start()

    copies = Copies(send, recv)
    own[0].wait()
    own[1].wait()
    top, bottom = (slice(0, 16), slice(None)), (slice(16, 32), slice(None))
    dense = gather_both(
        y_then_z(qkv_all.at[core], *top),
        y_then_z(qkv_all.at[core], *bottom),
        z_then_y(out_all.at[core], *top),
        z_then_y(out_all.at[core], *bottom),
        copies,
    )
    next(dense)
    next(dense)
    next(dense)
    own[2].wait()
    own[3].wait()

    @pl.when(moves)
    def _():
        moved.wait()

    @pl.when(stays)
    def _():
        stayed.wait()

    left, right = (slice(None), slice(0, 512)), (slice(None), slice(512, D))
    wide = gather_split(
        y_then_z(gate_all), y_then_z(down_all, *left), z_then_y(up_all), z_then_y(down_all, *right), copies
    )
    next(wide)
    next(dense)
    next(wide)
    run(dense)
    halves = [copies(ref.at[core], ref.at[core], mate) for ref in (qkv_all, out_all)]
    next(wide)
    for each in halves:
        each.wait()
    for at in range(16):
        rows, cut = 56 * at, 56 * at + 32
        qkv_w[rows:cut] = qkv_all[0, at // 4, at % 4]
        qkv_w[cut : rows + 56] = qkv_all[1, at // 4, at % 4, :24]
        out_w[rows:cut] = out_all[0, at // 4, at % 4]
        out_w[cut : rows + 56] = out_all[1, at // 4, at % 4, :24]
    small = [qkv_all[1, at // 4, at % 4, 24:32].astype(F32)[:1] for at in range(16)]
    bias_ref[...] = jnp.concatenate([each[:, :72] for each in small], axis=1)
    gain1_ref[...] = jnp.concatenate([each[:, 72:128] for each in small], axis=1)
    gain2_ref[...] = jnp.concatenate([each[:, 128:184] for each in small], axis=1)
    kv = front_work(x_ref, qkv_w, bias_ref, gain1_ref, cos_ref, sin_ref, normed_ref, q_ref, kv_ref, copies, None)
    next(kv)
    next(wide)
    next(kv)
    next(kv)
    next(wide)
    run(kv)
    attention_work(
        x_ref, q_ref, kv_ref, kseg_ref, out_w, gain2_ref, context_ref, hidden_ref, normed2_ref,
        keys_ref, values_ref, bias0, bias1, lambda: next(wide)
    )
    run(wide)


def first(gate, up, down, qkv, out, x, cosine, sine, kseg):
    return pl.pallas_call(
        first_kernel,
        out_shape=(
            shaped(4, 4, *gate.shape),
            shaped(4, 4, *up.shape),
            shaped(4, 4, *down.shape),
            shaped(D, QKV),
            shaped(D, D),
            shaped(1, QKV, dtype=F32),
            shaped(1, D, dtype=F32),
            shaped(1, D, dtype=F32),
            shaped(ROWS, D, dtype=F32),
            shaped(ROWS, D),
        ),
        in_specs=[ANY_SPEC] * 5 + [VMEM_SPEC] * 4,
        out_specs=[ANY_SPEC] * 3 + [VMEM_SPEC] * 7,
        scratch_shapes=[
            pltpu.VMEM((2, 4, 4, *qkv.shape), BF),
            pltpu.VMEM((2, 4, 4, *out.shape), BF),
            pltpu.VMEM((ROWS, D), BF),
            pltpu.VMEM((ROWS, D), BF),
            pltpu.VMEM((2, 4, 4, 64, 2 * KV), BF),
            pltpu.VMEM((ROWS, D), BF),
        ]
        + ATTENTION_SCRATCH
        + [
            pltpu.SemaphoreType.DMA((86,)),
            pltpu.SemaphoreType.DMA((86,)),
            pltpu.SemaphoreType.DMA((7,)),
        ],
        compiler_params=params(0),
        name="first",
    )(gate, up, down, qkv, out, x, cosine, sine, kseg)


def scatter_phase(firsts, seconds, place, device_at, copies):
    right, left, far = (lax.rem(place + step, 4) for step in (1, 3, 2))

    def load(ref):
        return ref[...].astype(F32)

    def copy(src, dst, step):
        return copies(src, dst, device_at(step), False)

    first_far = [copy(block(far), bufs[0], 1) for block, bufs, put in firsts]
    second_far = [copy(block(far), bufs[0], 3) for block, bufs, put in seconds]
    first_near = [copy(block(left), bufs[2], 3) for block, bufs, put in firsts]
    second_near = [copy(block(right), bufs[1], 1) for block, bufs, put in seconds]
    first_sum = [copy(bufs[0], bufs[1], 1) for block, bufs, put in firsts]
    second_sum = [copy(bufs[0], bufs[2], 3) for block, bufs, put in seconds]

    def start():
        for each in first_far + second_far + first_near + second_near:
            each.start()

    def pass_on():
        for came, each, (block, bufs, put) in zip(first_far, first_sum, firsts):
            came.wait_recv()
            bufs[0][...] = (load(block(right)) + load(bufs[0])).astype(BF)
            each.start()
        for came, each, (block, bufs, put) in zip(second_far, second_sum, seconds):
            came.wait_recv()
            bufs[0][...] = (load(block(left)) + load(bufs[0])).astype(BF)
            each.start()

    def finish():
        near, far_sum = first_near + second_near, first_sum + second_sum
        for one, two, (block, bufs, put) in zip(near, far_sum, firsts + seconds):
            one.wait_recv()
            two.wait_recv()
            put(load(block(place)) + load(bufs[1]) + load(bufs[2]))
        for each in first_far + second_far + near + far_sum:
            each.wait_send()

    return start, pass_on, finish


def scatter_both(first_a, second_a, first_b, second_b, copies):
    z, y, along_y, along_z = grid_place()

    def wide(part):
        block, bufs, _, _ = part
        return [(block, bufs, stored_in(bufs[1]))]

    def slim(part):
        _, kept, bufs, put = part
        return [((lambda at: kept[1].at[at]), bufs, put)]

    start_a, pass_a, finish_a = scatter_phase(wide(first_a), wide(second_a), y, along_y, copies)
    start_b, pass_b, finish_b = scatter_phase(wide(first_b), wide(second_b), z, along_z, copies)
    then_a, last_a, end_a = scatter_phase(slim(first_a), slim(second_a), z, along_z, copies)
    then_b, last_b, end_b = scatter_phase(slim(first_b), slim(second_b), y, along_y, copies)
    start_a()
    start_b()
    yield
    pass_a()
    pass_b()
    yield
    finish_a()
    then_a()
    finish_b()
    then_b()
    yield
    last_a()
    last_b()
    yield
    end_a()
    end_b()


def scatter_split(first_a, second_a, first_b, second_b, copies):
    z, y, along_y, along_z = grid_place()

    def slim(part):
        _, kept, bufs, put = part
        return [((lambda at: kept[1].at[at]), bufs, put)]

    def halved(half):
        def wide(part):
            block, bufs, _, _ = part
            views = [each.at[half] for each in bufs]
            return [(lambda at: block(at, half), views, stored_in(views[1]))]

        return [
            scatter_phase(wide(first_a), wide(second_a), y, along_y, copies),
            scatter_phase(wide(first_b), wide(second_b), z, along_z, copies),
        ]

    halves = [halved(pl.ds(0, 2)), halved(pl.ds(2, 2))]
    last_phases = [
        scatter_phase(slim(first_a), slim(second_a), z, along_z, copies),
        scatter_phase(slim(first_b), slim(second_b), y, along_y, copies),
    ]
    for start, _, _ in halves[0]:
        start()
    yield
    for _, pass_on, _ in halves[0]:
        pass_on()
    for start, _, _ in halves[1]:
        start()
    yield
    for _, pass_on, _ in halves[1]:
        pass_on()
    yield
    for phases in halves:
        for _, _, finish in phases:
            finish()
    for start, _, _ in last_phases:
        start()
    yield
    for _, pass_on, _ in last_phases:
        pass_on()
    yield
    for _, _, finish in last_phases:
        finish()


def scatter_scratch(*shapes):
    scratch = []
    for shape in shapes:
        scratch += [pltpu.VMEM((4, *shape), BF)] * 3 + [pltpu.VMEM(shape, BF)] * 3
    return scratch


def scatter_part(scratch, index, block, put):
    mine = scratch[6 * index : 6 * index + 6]
    return block, mine[:3], mine[3:], put


def stored_in(ref, *at):
    def put(value):
        ref[at if at else ...] = value.astype(ref.dtype)

    return put


DOWN_STARTS = (0, 80, 160, 224)
DOWN_ROWS = 80


def mlp_terms(rows_ref, dgate_ref, dup_ref, product_ref, dout_ref, gate_terms, up_terms, down_terms):
    def flat(ref):
        return ref[...].reshape(4 * ROWS, ref.shape[-1])

    rows = flat(rows_ref)
    for terms, grads in ((gate_terms, dgate_ref), (up_terms, dup_ref)):
        whole = tn(rows, flat(grads))
        for at in range(16):
            terms[at // 4, at % 4] = whole[56 * at : 56 * at + 56].astype(BF)
    whole = tn(flat(product_ref), flat(dout_ref)).astype(BF)
    for at in range(16):
        start = 304 * (at // 4) + DOWN_STARTS[at % 4]
        down_terms[at // 4, at % 4] = whole[start : start + DOWN_ROWS]


def mlp_sums(gate_terms, up_terms, down_terms, gate_out, up_out, down_out, scratch, copies):
    left, right = slice(0, 512), slice(512, D)
    return scatter_split(
        scatter_part(scratch, 0, lambda at, part: gate_terms.at[part, at], stored_in(gate_out)),
        scatter_part(
            scratch, 2, lambda at, part: down_terms.at[part, at, :, left], stored_in(down_out, slice(None), left)
        ),
        scatter_part(scratch, 1, lambda at, part: up_terms.at[at, part], stored_in(up_out)),
        scatter_part(
            scratch, 3, lambda at, part: down_terms.at[at, part, :, right], stored_in(down_out, slice(None), right)
        ),
        copies,
    )


MLP_SUMS_SHAPES = ((56, QUARTER), (56, QUARTER), (DOWN_ROWS, 512), (DOWN_ROWS, D - 512))


def qkv_sums(qkv_half, out_half, qkv_sum, out_sum, scratch, copies):
    top, bottom = slice(0, 16), slice(16, 32)
    return scatter_both(
        scatter_part(scratch, 0, lambda at: qkv_half.at[:, at, top], stored_in(qkv_sum, top)),
        scatter_part(scratch, 1, lambda at: qkv_half.at[:, at, bottom], stored_in(qkv_sum, bottom)),
        scatter_part(scratch, 2, lambda at: out_half.at[at, :, top], stored_in(out_sum, top)),
        scatter_part(scratch, 3, lambda at: out_half.at[at, :, bottom], stored_in(out_sum, bottom)),
        copies,
    )


def kv_sums(dkv_ref, total, scratch, copies):
    top, bottom = slice(0, 32), slice(32, 64)
    return scatter_both(
        scatter_part(scratch, 0, lambda at: dkv_ref.at[0, :, at, top], stored_in(total, slice(0, 32))),
        scatter_part(scratch, 1, lambda at: dkv_ref.at[0, :, at, bottom], stored_in(total, slice(32, 64))),
        scatter_part(scratch, 2, lambda at: dkv_ref.at[1, at, :, top], stored_in(total, slice(64, 96))),
        scatter_part(scratch, 3, lambda at: dkv_ref.at[1, at, :, bottom], stored_in(total, slice(96, 128))),
        copies,
    )


def replica_partners():
    me = lax.axis_index("replica")
    return me, me + 1 - 2 * lax.rem(me, 2), lax.rem(me + 2, 4), 3 - me


def exchange(
    own_ref, all_ref, total_ref, near_terms, part, far_part, near_sum, part_in, far_in, near_in, copies, loads, work
):
    me, mate, next_, far = replica_partners()
    halves = (slice(0, 64), slice(64, 128))
    to_mate, to_next = {"replica": mate}, {"replica": next_}
    greeted(2)
    across = [copies(own_ref.at[half], all_ref.at[me, half], to_next) for half in halves]
    beside = copies(own_ref, all_ref.at[me], to_mate)
    forwards = [copies(all_ref.at[next_, half], all_ref.at[next_, half], to_mate, False) for half in halves]
    passed = [copies(far_part.at[index], far_in.at[index], to_mate, False) for index in (0, 1)]
    sums = [copies(near_sum.at[index], near_in.at[index], to_next, False) for index in (0, 1)]
    sent = copies(part, part_in, to_mate, False)
    all_ref[me] = own_ref[...]
    for each in loads:
        each.wait()

    def send_sum(index):
        passed[index].wait_recv()
        near_sum[index] = (near_terms[index] + far_in[index].astype(F32)).astype(BF)
        sums[index].start()

    def step(at, carry):
        one = jnp.where(at == 0, me, jnp.where(at == 3, mate, next_))
        two = jnp.where(at == 0, me, jnp.where(at == 3, mate, far))
        first_rows = pl.ds(pl.multiple_of(jnp.where(at == 2, 64, 0), 64), 64)
        second_rows = pl.ds(pl.multiple_of(jnp.where(at == 1, 0, 64), 64), 64)

        @pl.when(at == 1)
        def _():
            across[0].wait_recv()
            forwards[0].start()
            forwards[0].wait_recv()

        @pl.when(at == 2)
        def _():
            across[1].wait_recv()
            forwards[1].start()
            send_sum(0)
            forwards[1].wait_recv()

        @pl.when(at == 3)
        def _():
            send_sum(1)
            beside.wait_recv()

        terms = work([(one, first_rows), (two, second_rows)])

        @pl.when(at == 0)
        def _():
            total_ref[...] = terms

        for index in (0, 1):

            @pl.when(at == 1 + index)
            def _(index=index):
                near_terms[index] = terms[:64]
                far_part[index] = terms[64:].astype(BF)
                passed[index].start()

        @pl.when(at == 3)
        def _():
            part[...] = terms.astype(BF)
            sent.start()

        return carry

    lax.fori_loop(0, 4, step, 0)
    sent.wait_recv()
    total = total_ref[...] + part_in[...].astype(F32)
    for each in sums:
        each.wait_recv()
    total = total + near_in[...].reshape(ROWS, D).astype(F32)
    for each in across + [beside, sent] + forwards + passed + sums:
        each.wait_send()
    return total


EXCHANGE_SCRATCH = [
    pltpu.VMEM((D, QUARTER), BF),
    pltpu.VMEM((D, QUARTER), BF),
    pltpu.VMEM((QUARTER, D), BF),
    pltpu.VMEM((ROWS, D), F32),
    pltpu.VMEM((2, 64, D), F32),
    pltpu.VMEM((ROWS, D), BF),
    pltpu.VMEM((2, 64, D), BF),
    pltpu.VMEM((2, 64, D), BF),
    pltpu.VMEM((ROWS, D), BF),
    pltpu.VMEM((2, 64, D), BF),
    pltpu.VMEM((2, 64, D), BF),
    pltpu.SemaphoreType.DMA((10,)),
    pltpu.SemaphoreType.DMA((10,)),
    pltpu.SemaphoreType.DMA((18,)),
]


def mlp_start(hbm, vmem, local):
    me, mate, next_, far = replica_partners()
    signal([{"replica": mate}, {"replica": next_}])
    loads = [pltpu.make_async_copy(src, dst, local.at[i]) for i, (src, dst) in enumerate(zip(hbm[:2], vmem[:2]))]
    for at in range(16):
        skip = 80 * (at % 4) - DOWN_STARTS[at % 4]
        rows = pl.ds(304 * (at // 4) + 80 * (at % 4), DOWN_ROWS - skip)
        piece = hbm[2].at[at // 4, at % 4, pl.ds(skip, DOWN_ROWS - skip)]
        loads.append(pltpu.make_async_copy(piece, vmem[2].at[rows], local.at[2 + at]))
    for each in loads:
        each.start()
    return loads


def split_rows(value, parts):
    for index, (source, rows) in enumerate(parts):
        yield source, rows, value[64 * index : 64 * index + 64]


def mlp_forward_kernel(
    normed_ref, hidden_ref, gate_hbm, up_hbm, down_hbm, out_ref, all_ref, gate_ref, up_ref,
    gate_w, up_w, down_w, total_ref, near_terms, part, far_part, near_sum, part_in, far_in, near_in, send, recv, local
):
    loads = mlp_start((gate_hbm, up_hbm, down_hbm), (gate_w, up_w, down_w), local)

    def work(parts):
        rows = jnp.concatenate([all_ref[source, rows] for source, rows in parts], axis=0)
        gate = nn(rows, gate_w[...])
        up = nn(rows, up_w[...])
        for source, at, value in split_rows(gate, parts):
            gate_ref[source, at] = value.astype(BF)
        for source, at, value in split_rows(up, parts):
            up_ref[source, at] = value.astype(BF)
        product = (gate * jax.nn.sigmoid(gate) * up).astype(BF)
        return nn(product, down_w[...])

    total = exchange(
        normed_ref, all_ref, total_ref, near_terms, part, far_part, near_sum, part_in, far_in, near_in,
        Copies(send, recv), loads, work
    )
    out_ref[...] = (hidden_ref[...] + total).astype(BF)


def mlp_forward(normed2, hidden, gate_w, up_w, down_w):
    return pl.pallas_call(
        mlp_forward_kernel,
        out_shape=(
            shaped(ROWS, D),
            shaped(4, ROWS, D),
            shaped(4, ROWS, QUARTER),
            shaped(4, ROWS, QUARTER),
        ),
        in_specs=[VMEM_SPEC] * 2 + [ANY_SPEC] * 3,
        scratch_shapes=EXCHANGE_SCRATCH,
        compiler_params=params(3),
        name="mlp_forward",
    )(normed2, hidden, gate_w, up_w, down_w)


def mlp_backward_kernel(
    dout_ref, gate_ref, up_ref, gate_hbm, up_hbm, down_hbm,
    dnormed_ref, all_ref, dgate_ref, dup_ref, product_ref,
    gate_w, up_w, down_w, total_ref, near_terms, part, far_part, near_sum, part_in, far_in, near_in, send, recv, local
):
    loads = mlp_start((gate_hbm, up_hbm, down_hbm), (gate_w, up_w, down_w), local)

    def work(parts):

        def stacked(ref):
            return jnp.concatenate([ref[source, rows] for source, rows in parts], axis=0)

        dproduct = nt(stacked(all_ref), down_w[...])
        gate = stacked(gate_ref).astype(F32)
        up = stacked(up_ref).astype(F32)
        s = jax.nn.sigmoid(gate)
        silu = gate * s
        product = (silu * up).astype(BF)
        dgate = (dproduct * up * (s * (1.0 + gate * (1.0 - s)))).astype(BF)
        dup = (dproduct * silu).astype(BF)
        for to, whole in ((product_ref, product), (dgate_ref, dgate), (dup_ref, dup)):
            for source, at, value in split_rows(whole, parts):
                to[source, at] = value
        return nt(dgate, gate_w[...]) + nt(dup, up_w[...])

    dnormed_ref[...] = exchange(
        dout_ref, all_ref, total_ref, near_terms, part, far_part, near_sum, part_in, far_in, near_in,
        Copies(send, recv), loads, work
    )


def mlp_backward(dout, gate, up, gate_w, up_w, down_w):
    return pl.pallas_call(
        mlp_backward_kernel,
        out_shape=(
            shaped(ROWS, D, dtype=F32),
            shaped(4, ROWS, D),
            shaped(4, ROWS, QUARTER),
            shaped(4, ROWS, QUARTER),
            shaped(4, ROWS, QUARTER),
        ),
        in_specs=[VMEM_SPEC] * 3 + [ANY_SPEC] * 3,
        scratch_shapes=EXCHANGE_SCRATCH,
        compiler_params=params(4),
        name="mlp_backward",
    )(dout, gate, up, gate_w, up_w, down_w)


def outputs_kernel(
    gate, up, down, qkv, out, gate_out, up_out, down_out, qkv_out, out_out, bias_out, value_out, gain1_out, gain2_out
):
    for r in range(4):
        lanes = slice(QUARTER * r, QUARTER * r + QUARTER)
        gate_out[:, lanes] = gate[r].astype(F32)
        up_out[:, lanes] = up[r].astype(F32)
        skip = 80 * r - DOWN_STARTS[r]
        down_out[80 * r : DOWN_STARTS[r] + DOWN_ROWS] = down[r, skip:].astype(F32)
    qkv_out[:32] = qkv[0]
    qkv_out[32:] = qkv[1, :24]
    out_out[:32] = out[0]
    out_out[32:] = out[1, :24]
    small = qkv[1, 24:][:1]
    bias_out[...] = small[:, :64]
    value_out[...] = small[:, 64:72]
    gain1_out[...] = small[:, 72:128]
    gain2_out[...] = small[:, 128:184]


def outputs(gate, up, down, qkv, out):
    return local_call(
        outputs_kernel,
        "outputs",
        (
            shaped(56, FF, dtype=F32),
            shaped(56, FF, dtype=F32),
            shaped(FF // 16, D, dtype=F32),
            shaped(56, QKV, dtype=F32),
            shaped(56, D, dtype=F32),
            shaped(1, 64, dtype=F32),
            shaped(1, 8, dtype=F32),
            shaped(1, 56, dtype=F32),
            shaped(1, 56, dtype=F32),
        ),
    )(gate, up, down, qkv, out)


def turn(values, cosine, sine, sign):
    width = values.shape[1]
    up = pltpu.roll(values, width - HALF, 1)
    down = pltpu.roll(values, HALF, 1)
    lane = lax.broadcasted_iota(jnp.int32, values.shape, 1)
    swapped = jnp.where(lax.rem(lane, 2 * HALF) < HALF, up, down)
    repeat = width // KV
    cosine = jnp.concatenate([cosine] * repeat, axis=1)
    sine = jnp.concatenate([sine] * repeat, axis=1)
    return values * cosine + sign * (swapped * sine)


def front_work(x_ref, w_ref, b_ref, g_ref, cos_ref, sin_ref, normed_ref, q_ref, kv_ref, copies, ready):
    z, y, along_y, along_z = grid_place()
    x = x_ref[...].astype(F32)
    inverse = lax.rsqrt(jnp.mean(x * x, axis=-1, keepdims=True) + EPSILON)
    normed = (x * inverse * g_ref[...]).astype(BF)
    normed_ref[...] = normed
    projected = nn(normed, w_ref[:, D:]) + b_ref[:, D:]
    turned = turn(projected[:, :KV], cos_ref[...], sin_ref[...], 1.0)
    kv = jnp.concatenate([turned, projected[:, KV:]], axis=1).astype(BF)
    kv_ref[0, z, y] = kv[:64]
    kv_ref[1, z, y] = kv[64:]
    if ready:
        ready()
    top, bottom = (slice(0, 32), slice(None)), (slice(32, 64), slice(None))
    steps = gather_both(
        y_then_z(kv_ref.at[0], *top),
        y_then_z(kv_ref.at[0], *bottom),
        z_then_y(kv_ref.at[1], *top),
        z_then_y(kv_ref.at[1], *bottom),
        copies,
    )
    next(steps)
    projected = nn(normed, w_ref[:, :D]) + b_ref[:, :D]
    q_ref[...] = turn(projected, cos_ref[...], sin_ref[...], 1.0).astype(BF)
    return steps


def front_kernel(x_ref, w_ref, b_ref, g_ref, cos_ref, sin_ref, normed_ref, q_ref, kv_ref, send, recv):
    z, y, along_y, along_z = grid_place()
    signal(neighbours(along_y, along_z))
    steps = front_work(
        x_ref, w_ref, b_ref, g_ref, cos_ref, sin_ref, normed_ref, q_ref, kv_ref,
        Copies(send, recv), lambda: greeted(4)
    )
    run(steps)


def front(x, w_qkv, b_qkv, g_attn, cosine, sine):
    return pl.pallas_call(
        front_kernel,
        out_shape=(shaped(ROWS, D), shaped(ROWS, D), shaped(2, 4, 4, 64, 2 * KV)),
        scratch_shapes=[pltpu.SemaphoreType.DMA((24,)), pltpu.SemaphoreType.DMA((24,))],
        compiler_params=params(6),
        name="front",
    )(x, w_qkv, b_qkv, g_attn, cosine, sine)


def low_lanes(rows):
    return lax.broadcasted_iota(jnp.int32, (rows, KV), 1) < KV // 2


def spread(kv_ref, start, to_ref):
    mixed = kv_ref[:, :, :, :, start : start + KV].reshape(LEN, KV)
    other = pltpu.roll(mixed.astype(F32), KV // 2, 1).astype(BF)
    low = low_lanes(LEN)
    to_ref[0] = jnp.where(low, mixed, other)
    to_ref[1] = mixed
    to_ref[2] = jnp.where(low, other, mixed)


def fill_bias(kseg_ref, bias_refs):
    first_row = 64 * lax.axis_index("group")
    for block, bias_ref in enumerate(bias_refs):
        keys = SPAN * (block + 1)
        kpos = lax.broadcasted_iota(jnp.int32, (64, keys), 1)
        qpos = SPAN * block + first_row + lax.broadcasted_iota(jnp.int32, (64, keys), 0)
        kseg = jnp.broadcast_to(kseg_ref[:, :keys], (64, keys)).astype(F32)
        qseg = jnp.sum(jnp.where(kpos == qpos, kseg, 0.0), axis=1, keepdims=True)
        bias_ref[...] = jnp.where((kpos <= qpos) & (kseg == qseg), 0.0, NEGATIVE)


def two_heads(pair):
    low = low_lanes(64)
    zero = jnp.zeros_like(pair)
    return jnp.concatenate([jnp.where(low, pair, zero), jnp.where(low, zero, pair)], axis=0)


def one_pair(stacked):
    return jnp.where(low_lanes(64), stacked[:64], stacked[64:])


def softmax(queries, keys, bias_ref):
    count = keys.shape[0]
    scores = nt(queries, keys).reshape(2, 64, count) + bias_ref[...][None]
    highest = jnp.max(scores, axis=-1, keepdims=True)
    exponent = jnp.exp(scores - highest)
    total = jnp.sum(exponent, axis=-1, keepdims=True)
    return (exponent * (1.0 / total)).reshape(2 * 64, count)


def variant_of(pair):
    return jnp.where(pair < 3, 0, jnp.where(pair == 3, 1, 2))


def attention_work(
    x_ref, q_ref, kv_ref, kseg_ref, w_ref, g_ref, context_ref, hidden_ref, normed_ref,
    keys_ref, values_ref, bias0, bias1, between=None
):
    spread(kv_ref, 0, keys_ref)
    spread(kv_ref, KV, values_ref)
    fill_bias(kseg_ref, (bias0, bias1))

    def one(pair, carry):
        if between:
            pl.when(pair == 4)(between)
        variant = variant_of(pair)
        lanes = pl.ds(pl.multiple_of(pair * KV, KV), KV)
        for block, bias_ref in enumerate((bias0, bias1)):
            rows = slice(64 * block, 64 * block + 64)
            keys = pl.ds(0, SPAN * (block + 1))
            queries = two_heads(q_ref[rows, lanes] * SCALE).astype(BF)
            weights = softmax(queries, keys_ref[variant, keys], bias_ref).astype(BF)
            context = nn(weights, values_ref[variant, keys])
            context_ref[rows, lanes] = one_pair(context).astype(BF)
        return carry

    lax.fori_loop(0, PAIRS, one, 0)
    hidden = x_ref[...].astype(F32) + nn(context_ref[...], w_ref[...])
    hidden_ref[...] = hidden
    inverse = lax.rsqrt(jnp.mean(hidden * hidden, axis=-1, keepdims=True) + EPSILON)
    normed_ref[...] = (hidden * inverse * g_ref[...]).astype(BF)


ATTENTION_SCRATCH = [
    pltpu.VMEM((3, LEN, KV), BF),
    pltpu.VMEM((3, LEN, KV), BF),
    pltpu.VMEM((64, SPAN), F32),
    pltpu.VMEM((64, LEN), F32),
]


def attention(x, q, kv, kseg, w_out, g_mlp):
    return local_call(
        attention_work,
        "attention",
        (shaped(ROWS, D), shaped(ROWS, D, dtype=F32), shaped(ROWS, D)),
        ATTENTION_SCRATCH,
    )(x, q, kv, kseg, w_out, g_mlp)


def norm_backward(values, gain, grads):
    inverse = lax.rsqrt(jnp.mean(values * values, axis=-1, keepdims=True) + EPSILON)
    scaled = grads * gain
    dvalues = inverse * scaled - values * (
        inverse * inverse * inverse * jnp.mean(scaled * values, axis=-1, keepdims=True)
    )
    return dvalues, jnp.sum(grads * values * inverse, axis=0, keepdims=True)


def attention_backward_work(
    dout_ref, dnormed_ref, hidden_ref, g_ref, w_ref, q_ref, kv_ref, kseg_ref,
    dhidden_ref, dlow_ref, dq_ref, dkv_ref, dgain_ref,
    keys_ref, values_ref, bias0, bias1, dcontext_ref, dkeys, dvalues, between=None
):
    dnorm, dgain = norm_backward(hidden_ref[...], g_ref[...], dnormed_ref[...])
    dgain_ref[...] = dgain
    dhidden = dout_ref[...].astype(F32) + dnorm
    dhidden_ref[...] = dhidden
    dlow = dhidden.astype(BF)
    dlow_ref[...] = dlow
    dcontext_ref[...] = nt(dlow, w_ref[...]).astype(BF)
    spread(kv_ref, 0, keys_ref)
    spread(kv_ref, KV, values_ref)
    fill_bias(kseg_ref, (bias0, bias1))
    dkeys[...] = jnp.zeros_like(dkeys)
    dvalues[...] = jnp.zeros_like(dvalues)

    def one(pair, carry):
        if between:
            pl.when(pair == 4)(between)
        variant = variant_of(pair)
        lanes = pl.ds(pl.multiple_of(pair * KV, KV), KV)
        for block, bias_ref in enumerate((bias0, bias1)):
            rows = slice(64 * block, 64 * block + 64)
            keys = pl.ds(0, SPAN * (block + 1))
            queries = two_heads(q_ref[rows, lanes] * SCALE).astype(BF)
            dcontext = two_heads(dcontext_ref[rows, lanes])
            key_rows = keys_ref[variant, keys]
            weights = softmax(queries, key_rows, bias_ref)
            dweights = nt(dcontext, values_ref[variant, keys])
            inner = jnp.sum(weights * dweights, axis=-1, keepdims=True)
            dscores = (weights * (dweights - inner)).astype(BF)
            dq_ref[rows, lanes] = one_pair(nn(dscores, key_rows)) * SCALE
            dkeys[variant, keys] += tn(dscores, queries)
            dvalues[variant, keys] += tn(weights.astype(BF), dcontext)
        return carry

    lax.fori_loop(0, PAIRS, one, 0)
    low = low_lanes(LEN)
    for start, total in ((0, dkeys), (KV, dvalues)):
        head0 = total[0] + pltpu.roll(total[0], KV // 2, 1)
        head1 = total[2] + pltpu.roll(total[2], KV // 2, 1)
        whole = (jnp.where(low, head0, head1) + total[1]).astype(BF)
        dkv_ref[:, :, :, :, start : start + KV] = whole.reshape(2, 4, 4, 64, KV)


ATTENTION_BACKWARD_OUT = (
    shaped(ROWS, D, dtype=F32),
    shaped(ROWS, D),
    shaped(ROWS, D, dtype=F32),
    shaped(2, 4, 4, 64, 2 * KV),
    shaped(1, D, dtype=F32),
)
ATTENTION_BACKWARD_SCRATCH = ATTENTION_SCRATCH + [
    pltpu.VMEM((ROWS, D), BF),
    pltpu.VMEM((3, LEN, KV), F32),
    pltpu.VMEM((3, LEN, KV), F32),
]


def attention_backward(*operands):
    return local_call(
        attention_backward_work, "attention_backward", ATTENTION_BACKWARD_OUT, ATTENTION_BACKWARD_SCRATCH
    )(*operands)


def rear_query(dq_ref, cos_ref, sin_ref, w_ref, dprojected_ref, dbias_ref):
    dquery = turn(dq_ref[...], cos_ref[...], sin_ref[...], -1.0).astype(BF)
    dprojected_ref[:, :D] = dquery
    dbias_ref[:, :D] = jnp.sum(dquery.astype(F32), axis=0, keepdims=True)
    return nt(dquery, w_ref[:, :D])


def rear_rest(
    dnormed, total, cos_ref, sin_ref, w_ref, x_ref, g_ref, dhidden_ref, dprojected_ref, dinput_ref, dgain_ref, dbias_ref
):
    turned = turn(total[:, :KV], cos_ref[...], sin_ref[...], -1.0)
    dkv = jnp.concatenate([turned, total[:, KV:]], axis=1).astype(BF)
    dprojected_ref[:, D:] = dkv
    dbias_ref[:, D:] = jnp.sum(dkv.astype(F32), axis=0, keepdims=True)
    dnormed = dnormed + nt(dkv, w_ref[:, D:])
    dnorm, dgain = norm_backward(x_ref[...].astype(F32), g_ref[...], dnormed)
    dgain_ref[...] = dgain
    dinput_ref[...] = (dhidden_ref[...] + dnorm).astype(BF)


REAR_SCRATCH = [
    pltpu.VMEM((ROWS, QKV), BF),
    pltpu.VMEM((1, D), F32),
    pltpu.VMEM((1, QKV), F32),
    pltpu.VMEM((ROWS, 2 * KV), F32),
] + scatter_scratch(*[(32, 2 * KV)] * 4)


def rear_kernel(
    dkv_ref, dq_ref, cos_ref, sin_ref, w_ref, x_ref, g_ref, dhidden_ref, dinput_ref,
    dprojected_ref, dgain_ref, dbias_ref, total, *rest
):
    scratch, (send, recv) = rest[:-2], rest[-2:]
    z, y, along_y, along_z = grid_place()
    signal(neighbours(along_y, along_z))
    greeted(4)
    steps = kv_sums(dkv_ref, total, scratch, Copies(send, recv))
    next(steps)
    dnormed = rear_query(dq_ref, cos_ref, sin_ref, w_ref, dprojected_ref, dbias_ref)
    run(steps)
    rear_rest(
        dnormed, total, cos_ref, sin_ref, w_ref, x_ref, g_ref, dhidden_ref,
        dprojected_ref, dinput_ref, dgain_ref, dbias_ref
    )


def rear(dkv, dq, cosine, sine, w_qkv, x, g_attn, dhidden):
    return pl.pallas_call(
        rear_kernel,
        out_shape=shaped(ROWS, D),
        scratch_shapes=REAR_SCRATCH + [pltpu.SemaphoreType.DMA((24,)), pltpu.SemaphoreType.DMA((24,))],
        compiler_params=params(7),
        name="rear",
    )(dkv, dq, cosine, sine, w_qkv, x, g_attn, dhidden)


TAIL_SCRATCH = [
    pltpu.VMEM((4, 4, 56, QUARTER), BF),
    pltpu.VMEM((4, 4, 56, QUARTER), BF),
    pltpu.VMEM((4, 4, DOWN_ROWS, D), BF),
    pltpu.VMEM((56, QUARTER), BF),
    pltpu.VMEM((56, QUARTER), BF),
    pltpu.VMEM((DOWN_ROWS, D), BF),
    pltpu.VMEM((4, 4, 64, QKV), BF),
    pltpu.VMEM((4, 4, 64, D), BF),
    pltpu.VMEM((4, 4, 32, QKV), BF),
    pltpu.VMEM((4, 4, 32, D), BF),
    pltpu.VMEM((32, QKV), F32),
    pltpu.VMEM((32, D), F32),
    pltpu.VMEM((32, QKV), BF),
    pltpu.VMEM((32, D), BF),
    pltpu.VMEM((32, QKV), BF),
    pltpu.VMEM((32, D), BF),
]
TAIL_COPIES = 24 + 36 + 24 + 2 + 13


def tail_kernel(*refs):
    refs = list(refs)

    def take(count):
        taken = refs[:count]
        del refs[:count]
        return taken

    attention_in = take(8)
    mlp_in = take(5)
    cos_ref, sin_ref, qkv_w, x_ref, gain1_ref, normed_ref, context_ref = take(7)
    dinput_ref, gate_all, up_all, down_all, qkv_all, out_all = take(6)
    attention_out = take(5)
    dhidden_ref, dlow_ref, dq_ref, dkv_ref, dgain2_ref = attention_out
    attention_scratch = take(len(ATTENTION_BACKWARD_SCRATCH))
    dprojected_ref, dgain1_ref, dbias_ref, total = take(4)
    kv_bufs = take(24)
    mlp_term_refs, mlp_sum_refs = take(3), take(3)
    qkv_terms, out_terms, qkv_half, out_half, qkv_sum, out_sum, qkv_low, out_low, qkv_in, out_in = take(10)
    mlp_bufs, qkv_bufs = take(24), take(24)
    send, recv, local = take(3)

    z, y, along_y, along_z = grid_place()
    me, mate, next_, far = replica_partners()
    core = lax.rem(me, 2)
    to_mate, to_next = {"replica": mate}, {"replica": next_}
    target, source, stays = quarter_route()
    moves = jnp.logical_not(stays)
    signal(neighbours(along_y, along_z) + [to_mate, to_next])
    mlp_terms(*mlp_in, *mlp_term_refs)

    @pl.when(moves)
    def _():
        signal([target])
        greeted(7)

    @pl.when(stays)
    def _():
        greeted(6)

    copies = Copies(send, recv)
    mlp = mlp_sums(*mlp_term_refs, *mlp_sum_refs, mlp_bufs, copies)
    next(mlp)
    attention_backward_work(*attention_in, *attention_out, *attention_scratch, lambda: next(mlp))
    kv = kv_sums(dkv_ref, total, kv_bufs, copies)
    next(kv)
    next(mlp)

    mine = pl.ds(pl.multiple_of(32 * core, 32), 32)
    theirs = pl.ds(pl.multiple_of(32 - 32 * core, 32), 32)

    def add_mate(sent, terms, half):
        sent.wait_recv()
        half[...] = (terms[:, :, mine].astype(F32) + half[...].astype(F32)).astype(BF)

    dnormed = rear_query(dq_ref, cos_ref, sin_ref, qkv_w, dprojected_ref, dbias_ref)
    next(kv)
    whole = tn(context_ref[...], dlow_ref[...])
    for at in range(16):
        rows = jnp.concatenate([whole[56 * at : 56 * at + 56], jnp.zeros((8, D), F32)], axis=0)
        out_terms[at // 4, at % 4] = rows.astype(BF)
    out_sent = copies(out_terms.at[:, :, theirs], out_half, to_mate)
    next(kv)
    add_mate(out_sent, out_terms, out_half)
    run(kv)
    rear_rest(
        dnormed, total, cos_ref, sin_ref, qkv_w, x_ref, gain1_ref, dhidden_ref,
        dprojected_ref, dinput_ref, dgain1_ref, dbias_ref
    )
    whole = tn(normed_ref[...], dprojected_ref[...])
    dbias, dgain1, dgain2 = dbias_ref[...], dgain1_ref[...], dgain2_ref[...]
    for at in range(16):
        small = jnp.concatenate(
            [
                dbias[:, 64 * at : 64 * at + 64],
                dbias[:, D + KV + 8 * at : D + KV + 8 * at + 8],
                dgain1[:, 56 * at : 56 * at + 56],
                dgain2[:, 56 * at : 56 * at + 56],
                jnp.zeros((1, QKV - 184), F32),
            ],
            axis=1,
        )
        rows = jnp.concatenate([whole[56 * at : 56 * at + 56], jnp.broadcast_to(small, (8, QKV))], axis=0)
        qkv_terms[at // 4, at % 4] = rows.astype(BF)
    qkv_sent = copies(qkv_terms.at[:, :, theirs], qkv_half, to_mate)
    next(mlp)
    add_mate(qkv_sent, qkv_terms, qkv_half)
    dense = qkv_sums(qkv_half, out_half, qkv_sum, out_sum, qkv_bufs, copies)
    next(dense)
    next(mlp)
    next(dense)
    run(mlp)

    gate, up, down = mlp_sum_refs
    moved = pltpu.make_async_remote_copy(
        src_ref=down,
        dst_ref=down_all.at[source["replica"]],
        send_sem=local.at[0],
        recv_sem=local.at[1],
        device_id=source,
        device_id_type=MESH,
    )
    stayed = pltpu.make_async_copy(down, down_all.at[me], local.at[2])

    @pl.when(moves)
    def _():
        moved.start()

    @pl.when(stays)
    def _():
        stayed.start()

    pairs = ((gate, gate_all), (up, up_all))
    across = [copies(ref, all_ref.at[me], to_next) for ref, all_ref in pairs]
    beside = [copies(ref, all_ref.at[me], to_mate) for ref, all_ref in pairs]
    for ref, all_ref in pairs:
        all_ref[me] = ref[...]
    next(dense)

    @pl.when(moves)
    def _():
        moved.wait()

    @pl.when(stays)
    def _():
        stayed.wait()

    across.append(copies(down_all.at[me], down_all.at[me], to_next))
    beside.append(copies(down_all.at[me], down_all.at[me], to_mate))
    next(dense)
    run(dense)
    qkv_low[...] = qkv_sum[...].astype(BF)
    out_low[...] = out_sum[...].astype(BF)
    sums = [copies(qkv_low, qkv_in, to_next), copies(out_low, out_in, to_next)]
    for came, all_ref in zip(across, (gate_all, up_all, down_all)):
        came.wait_recv()
        beside.append(copies(all_ref.at[next_], all_ref.at[next_], to_mate))
    sums[0].wait_recv()
    qkv_all[core] = qkv_sum[...] + qkv_in[...].astype(F32)
    sums[1].wait_recv()
    out_all[core] = out_sum[...] + out_in[...].astype(F32)
    beside += [copies(ref.at[core], ref.at[core], to_mate) for ref in (qkv_all, out_all)]
    for each in beside:
        each.wait_recv()
    for each in [out_sent, qkv_sent] + across + beside + sums:
        each.wait_send()


def tail(*operands):
    return pl.pallas_call(
        tail_kernel,
        out_shape=(
            shaped(ROWS, D),
            shaped(4, 56, QUARTER),
            shaped(4, 56, QUARTER),
            shaped(4, DOWN_ROWS, D),
            shaped(2, 32, QKV, dtype=F32),
            shaped(2, 32, D, dtype=F32),
        ),
        scratch_shapes=[pltpu.VMEM(each.shape, each.dtype) for each in ATTENTION_BACKWARD_OUT]
        + ATTENTION_BACKWARD_SCRATCH
        + REAR_SCRATCH
        + TAIL_SCRATCH
        + scatter_scratch(*MLP_SUMS_SHAPES)
        + scatter_scratch((16, QKV), (16, QKV), (16, D), (16, D))
        + [
            pltpu.SemaphoreType.DMA((TAIL_COPIES,)),
            pltpu.SemaphoreType.DMA((TAIL_COPIES,)),
            pltpu.SemaphoreType.DMA((3,)),
        ],
        compiler_params=params(1),
        name="tail",
    )(*operands)


def rotary(group):
    lane = np.arange(KV)
    frequency = jnp.asarray(THETA ** (-(lane % HALF) * 2.0 / (2 * HALF)), F32)
    sign = jnp.asarray(np.where(lane % (2 * HALF) < HALF, -1.0, 1.0), F32)
    row = lax.broadcasted_iota(jnp.int32, (ROWS, KV), 0)
    positions = group * 64 + lax.rem(row, 64) + SPAN * (row // 64)
    angles = positions.astype(F32) * frequency[None, :]
    return jnp.cos(angles), jnp.sin(angles) * sign[None, :]


def body(inputs, cotangent, segments, w_qkv, b_qkv, w_out, w_gate, w_up, w_down, g_attn, g_mlp):
    section = lax.axis_index("section")
    group = lax.axis_index("group")
    replica = lax.axis_index("replica")
    core = lax.rem(replica, 2)

    down_piece = lax.dynamic_slice(w_down[0], (jnp.minimum(80 * replica, 224), 0), (DOWN_ROWS, D))
    gate_piece = lax.dynamic_slice(w_gate[0], (0, replica * QUARTER), (D // 16, QUARTER))
    up_piece = lax.dynamic_slice(w_up[0], (0, replica * QUARTER), (D // 16, QUARTER))
    small = jnp.concatenate([b_qkv[0], g_attn[0], g_mlp[0]])
    small = jnp.pad(small[None], ((0, 7), (0, QKV - small.shape[0])))
    qkv_piece = lax.dynamic_slice(jnp.concatenate([w_qkv[0], small], axis=0), (32 * core, 0), (32, QKV))
    out_piece = lax.dynamic_slice(jnp.pad(w_out[0], ((0, 8), (0, 0))), (32 * core, 0), (32, D))

    cosine, sine = rotary(group)
    kseg = segments
    x_in = inputs[0].reshape(ROWS, D)
    cotangent_in = cotangent[0].reshape(ROWS, D)
    gate_w, up_w, down_w, qkv_w, out_w, bias, gain1, gain2, hidden, normed2 = first(
        gate_piece, up_piece, down_piece, qkv_piece, out_piece, x_in, cosine, sine, kseg
    )
    gate_w = gate_w.reshape(D, QUARTER)
    up_w = up_w.reshape(D, QUARTER)

    def forward(x):
        normed, q, kv = front(x, qkv_w, bias, gain1, cosine, sine)
        context, hidden, normed2 = attention(x, q, kv, kseg, out_w, gain2)
        output, normed2_all, gate, up = mlp_forward(normed2, hidden, gate_w, up_w, down_w)
        return output, (x, normed, q, kv, context, hidden, normed2_all, gate, up)

    def backward_start(dout):
        dnormed2, *grads = mlp_backward(dout, gate, up, gate_w, up_w, down_w)
        dout_all, dgate, dup, product = grads
        return (dout, dnormed2, hidden, gain2, out_w, q, kv, kseg), (normed2_all, dgate, dup, product, dout_all)

    relayed, *_ = mlp_forward(normed2, hidden, gate_w, up_w, down_w)
    relayed = lax.ppermute(relayed, "section", [(0, 1)])
    output, kept = forward(jnp.where(section == 0, x_in, relayed))
    x, normed, q, kv, context, hidden, normed2_all, gate, up = kept
    operands, _ = backward_start(cotangent_in)
    dhidden, _, dq, dkv, _ = attention_backward(*operands)
    returned = rear(dkv, dq, cosine, sine, qkv_w, x, gain1, dhidden)
    returned = lax.ppermute(returned, "section", [(1, 0)])
    operands, mlp_operands = backward_start(jnp.where(section == 1, cotangent_in, returned))
    dinput, *parts = tail(*operands, *mlp_operands, cosine, sine, qkv_w, x, gain1, normed, context)
    grad_gate, grad_up, grad_down, grad_qkv, grad_out, bias, value_bias, gain1, gain2 = outputs(*parts)
    return (
        output.reshape(1, 1, 2, 64, D),
        dinput.reshape(1, 1, 2, 64, D),
        grad_qkv[None],
        bias,
        value_bias,
        grad_out[None],
        grad_gate[None],
        grad_up[None],
        grad_down[None],
        gain1,
        gain2,
    )


def solution(mesh):
    in_specs = (
        P("replica", None, "group", None),
        P("replica", None, "group", None),
        P("replica", None),
        P("section", "group", None),
        P("section", "group"),
        P("section", "group", None),
        P("section", "group", None),
        P("section", "group", None),
        P("section", "group", None),
        P("section", "group"),
        P("section", "group"),
    )
    out_specs = (
        P("section", "replica", None, "group", None),
        P("section", "replica", None, "group", None),
        P("section", "group", None),
        P("section", "group"),
        P("section", "group"),
        P("section", "group", None),
        P("section", "group", None),
        P("section", "group", None),
        P("section", "group", None),
        P("section", "group"),
        P("section", "group"),
    )
    return jax.shard_map(body, mesh=mesh, in_specs=in_specs, out_specs=out_specs, check_vma=False)
```

```python
import functools

import jax
import jax.numpy as jnp
import numpy as np
from jax import lax
from jax.experimental import pallas as pl
from jax.experimental.pallas import tpu as pltpu
from jax.sharding import PartitionSpec as P

D = 896
HEADS = 14
KV = 128
HALF = 32
FF = 4864
QUARTER = FF // 4
QKV = 1152
ROWS = 128
SPAN = 1024
LEN = 2048
PAIRS = 7
EPSILON = 1e-06
THETA = 1000000.0
NEGATIVE = -1e30
SCALE = 0.125
VMEM_LIMIT = 60 * 1024 * 1024
MESH = pl.DeviceIdType.MESH
BF = jnp.bfloat16
F32 = jnp.float32
VMEM_SPEC = pl.BlockSpec(memory_space=pltpu.VMEM)
ANY_SPEC = pl.BlockSpec(memory_space=pl.ANY)


def nn(a, b):
    return lax.dot_general(a, b, (((1,), (0,)), ((), ())), preferred_element_type=F32)


def nt(a, b):
    return lax.dot_general(a, b, (((1,), (1,)), ((), ())), preferred_element_type=F32)


def tn(a, b):
    return lax.dot_general(a, b, (((0,), (0,)), ((), ())), preferred_element_type=F32)


def params(collective_id=None):
    if collective_id is None:
        return pltpu.CompilerParams(vmem_limit_bytes=VMEM_LIMIT)
    return pltpu.CompilerParams(
        vmem_limit_bytes=VMEM_LIMIT, collective_id=collective_id, has_side_effects=True
    )


def shaped(*shape, dtype=BF):
    return jax.ShapeDtypeStruct(shape, dtype)


def local_call(kernel, name, out_shape, scratch=()):
    return pl.pallas_call(
        kernel,
        out_shape=out_shape,
        scratch_shapes=list(scratch),
        compiler_params=params(),
        name=name,
    )


def signal(devices):
    barrier = pltpu.get_barrier_semaphore()
    for device in devices:
        pl.semaphore_signal(barrier, inc=1, device_id=device, device_id_type=MESH)


def greeted(count):
    pl.semaphore_wait(pltpu.get_barrier_semaphore(), count)


def grid_place():
    me = lax.axis_index("group")
    z = me // 4
    y = lax.rem(me, 4)

    def along_y(step):
        return {"group": z * 4 + lax.rem(y + step, 4)}

    def along_z(step):
        return {"group": lax.rem(z + step, 4) * 4 + y}

    return z, y, along_y, along_z


def neighbours(along_y, along_z):
    return [along(step) for along in (along_y, along_z) for step in (1, 3, 2)]


class Copies:
    def __init__(self, send, recv):
        self.send, self.recv, self.used = send, recv, 0

    def __call__(self, src, dst, device, start=True):
        index = self.used
        self.used += 1
        each = pltpu.make_async_remote_copy(
            src_ref=src,
            dst_ref=dst,
            send_sem=self.send.at[index],
            recv_sem=self.recv.at[index],
            device_id=device,
            device_id_type=MESH,
        )
        if start:
            each.start()
        return each


def gather_phase(firsts, seconds, place, device_at, copies):
    def copy(block, slot, step):
        return copies(block(slot), block(slot), device_at(step), False)

    firsts_right = [copy(block, place, 1) for block in firsts]
    seconds_left = [copy(block, place, 3) for block in seconds]
    others = [copy(block, place, 3) for block in firsts] + [copy(block, place, 1) for block in seconds]
    relays = [copy(block, lax.rem(place + 3, 4), 1) for block in firsts]
    relays += [copy(block, lax.rem(place + 1, 4), 3) for block in seconds]

    def start():
        for each in firsts_right + seconds_left + others:
            each.start()

    def relay():
        for came, each in zip(firsts_right + seconds_left, relays):
            came.wait_recv()
            each.start()

    def finish():
        for each in others + relays:
            each.wait_recv()
        for each in firsts_right + seconds_left + others + relays:
            each.wait_send()

    return start, relay, finish


def gather_direct(firsts, seconds, place, device_at, copies):
    sent = []
    for block in firsts + seconds:
        sent += [copies(block(place), block(place), device_at(step), False) for step in (1, 3, 2)]

    def start():
        for each in sent:
            each.start()

    def finish():
        for each in sent:
            each.wait_recv()
        for each in sent:
            each.wait_send()

    return start, lambda: None, finish


def gather_both(first_a, second_a, first_b, second_b, copies, phase=gather_phase):
    z, y, along_y, along_z = grid_place()
    start_a, relay_a, finish_a = phase([first_a[0]], [second_a[0]], y, along_y, copies)
    start_b, relay_b, finish_b = phase([first_b[0]], [second_b[0]], z, along_z, copies)
    then_a, last_a, end_a = phase([first_a[1]], [second_a[1]], z, along_z, copies)
    then_b, last_b, end_b = phase([first_b[1]], [second_b[1]], y, along_y, copies)
    start_a()
    start_b()
    yield
    relay_a()
    relay_b()
    yield
    finish_a()
    then_a()
    finish_b()
    then_b()
    yield
    last_a()
    last_b()
    yield
    end_a()
    end_b()


def gather_split(first_a, second_a, first_b, second_b, copies):
    z, y, along_y, along_z = grid_place()
    slim = [
        gather_phase([first_a[0]], [second_a[0]], y, along_y, copies),
        gather_phase([first_b[0]], [second_b[0]], z, along_z, copies),
    ]

    def wide(half):
        def part(function):
            return [lambda at: function(at, half)]

        return [
            gather_phase(part(first_a[1]), part(second_a[1]), z, along_z, copies),
            gather_phase(part(first_b[1]), part(second_b[1]), y, along_y, copies),
        ]

    halves = [wide(slice(0, 2)), wide(slice(2, 4))]
    for start, _, _ in slim:
        start()
    yield
    for _, relay, _ in slim:
        relay()
    yield
    for _, _, finish in slim:
        finish()
    for phases in halves:
        for start, _, _ in phases:
            start()
        yield
        for _, relay, _ in phases:
            relay()
        yield
    for phases in halves:
        for _, _, finish in phases:
            finish()


def run(steps):
    for _ in steps:
        pass


def y_then_z(ref, *tail):
    z = lax.axis_index("group") // 4
    return (lambda at: ref.at[(z, at, *tail)]), (lambda at, part=slice(None): ref.at[(at, part, *tail)])


def z_then_y(ref, *tail):
    y = lax.rem(lax.axis_index("group"), 4)
    return (lambda at: ref.at[(at, y, *tail)]), (lambda at, part=slice(None): ref.at[(part, at, *tail)])


def quarter_route():
    group, replica = lax.axis_index("group"), lax.axis_index("replica")
    target = {"group": 4 * lax.rem(group, 4) + replica, "replica": group // 4}
    source = {"group": 4 * replica + group // 4, "replica": lax.rem(group, 4)}
    stays = (target["group"] == group) & (target["replica"] == replica)
    return target, source, stays


def first_kernel(
    gate, up, down, qkv, out, x_ref, cos_ref, sin_ref, kseg_ref,
    gate_all, up_all, down_all, qkv_w, out_w, bias_ref, gain1_ref, gain2_ref, hidden_ref, normed2_ref,
    qkv_all, out_all, normed_ref, q_ref, kv_ref, context_ref, keys_ref, values_ref, bias0, bias1, send, recv, local
):
    z, y, along_y, along_z = grid_place()
    core = lax.rem(lax.axis_index("replica"), 2)
    mate = {"replica": lax.axis_index("replica") + 1 - 2 * core}
    target, source, stays = quarter_route()
    moves = jnp.logical_not(stays)
    signal(neighbours(along_y, along_z) + [mate])
    places = (qkv_all.at[core, z, y], out_all.at[core, z, y], gate_all.at[z, y], up_all.at[z, y])
    own = []
    for index, (src, dst) in enumerate(zip((qkv, out, gate, up), places)):
        own.append(pltpu.make_async_copy(src, dst, local.at[index]))
        own[-1].start()
    there = target["group"]
    moved = pltpu.make_async_remote_copy(
        src_ref=down,
        dst_ref=down_all.at[there // 4, lax.rem(there, 4)],
        send_sem=local.at[5],
        recv_sem=local.at[6],
        device_id=target,
        device_id_type=MESH,
    )
    stayed = pltpu.make_async_copy(down, down_all.at[z, y], local.at[4])

    @pl.when(moves)
    def _():
        signal([source])
        greeted(8)
        moved.start()

    @pl.when(stays)
    def _():
        greeted(7)
        stayed.start()

    copies = Copies(send, recv)
    own[0].wait()
    own[1].wait()
    top, bottom = (slice(0, 16), slice(None)), (slice(16, 32), slice(None))
    dense = gather_both(
        y_then_z(qkv_all.at[core], *top),
        y_then_z(qkv_all.at[core], *bottom),
        z_then_y(out_all.at[core], *top),
        z_then_y(out_all.at[core], *bottom),
        copies,
    )
    next(dense)
    next(dense)
    next(dense)
    own[2].wait()
    own[3].wait()

    @pl.when(moves)
    def _():
        moved.wait()

    @pl.when(stays)
    def _():
        stayed.wait()

    left, right = (slice(None), slice(0, 512)), (slice(None), slice(512, D))
    wide = gather_split(
        y_then_z(gate_all), y_then_z(down_all, *left), z_then_y(up_all), z_then_y(down_all, *right), copies
    )
    next(wide)
    next(dense)
    next(wide)
    run(dense)
    halves = [copies(ref.at[core], ref.at[core], mate) for ref in (qkv_all, out_all)]
    next(wide)
    for each in halves:
        each.wait()
    for at in range(16):
        rows, cut = 56 * at, 56 * at + 32
        qkv_w[rows:cut] = qkv_all[0, at // 4, at % 4]
        qkv_w[cut : rows + 56] = qkv_all[1, at // 4, at % 4, :24]
        out_w[rows:cut] = out_all[0, at // 4, at % 4]
        out_w[cut : rows + 56] = out_all[1, at // 4, at % 4, :24]
    small = [qkv_all[1, at // 4, at % 4, 24:32].astype(F32)[:1] for at in range(16)]
    bias_ref[...] = jnp.concatenate([each[:, :72] for each in small], axis=1)
    gain1_ref[...] = jnp.concatenate([each[:, 72:128] for each in small], axis=1)
    gain2_ref[...] = jnp.concatenate([each[:, 128:184] for each in small], axis=1)
    kv = front_work(x_ref, qkv_w, bias_ref, gain1_ref, cos_ref, sin_ref, normed_ref, q_ref, kv_ref, copies, None)
    next(kv)
    next(wide)
    next(kv)
    next(kv)
    next(wide)
    run(kv)
    attention_work(
        x_ref, q_ref, kv_ref, kseg_ref, out_w, gain2_ref, context_ref, hidden_ref, normed2_ref,
        keys_ref, values_ref, bias0, bias1, lambda: next(wide)
    )
    run(wide)


def first(gate, up, down, qkv, out, x, cosine, sine, kseg):
    return pl.pallas_call(
        first_kernel,
        out_shape=(
            shaped(4, 4, *gate.shape),
            shaped(4, 4, *up.shape),
            shaped(4, 4, *down.shape),
            shaped(D, QKV),
            shaped(D, D),
            shaped(1, QKV, dtype=F32),
            shaped(1, D, dtype=F32),
            shaped(1, D, dtype=F32),
            shaped(ROWS, D, dtype=F32),
            shaped(ROWS, D),
        ),
        in_specs=[ANY_SPEC] * 5 + [VMEM_SPEC] * 4,
        out_specs=[ANY_SPEC] * 3 + [VMEM_SPEC] * 7,
        scratch_shapes=[
            pltpu.VMEM((2, 4, 4, *qkv.shape), BF),
            pltpu.VMEM((2, 4, 4, *out.shape), BF),
            pltpu.VMEM((ROWS, D), BF),
            pltpu.VMEM((ROWS, D), BF),
            pltpu.VMEM((2, 4, 4, 64, 2 * KV), BF),
            pltpu.VMEM((ROWS, D), BF),
        ]
        + ATTENTION_SCRATCH
        + [
            pltpu.SemaphoreType.DMA((86,)),
            pltpu.SemaphoreType.DMA((86,)),
            pltpu.SemaphoreType.DMA((7,)),
        ],
        compiler_params=params(0),
        name="first",
    )(gate, up, down, qkv, out, x, cosine, sine, kseg)


def scatter_phase(firsts, seconds, place, device_at, copies):
    right, left, far = (lax.rem(place + step, 4) for step in (1, 3, 2))

    def load(ref):
        return ref[...].astype(F32)

    def copy(src, dst, step):
        return copies(src, dst, device_at(step), False)

    first_far = [copy(block(far), bufs[0], 1) for block, bufs, put in firsts]
    second_far = [copy(block(far), bufs[0], 3) for block, bufs, put in seconds]
    first_near = [copy(block(left), bufs[2], 3) for block, bufs, put in firsts]
    second_near = [copy(block(right), bufs[1], 1) for block, bufs, put in seconds]
    first_sum = [copy(bufs[0], bufs[1], 1) for block, bufs, put in firsts]
    second_sum = [copy(bufs[0], bufs[2], 3) for block, bufs, put in seconds]

    def start():
        for each in first_far + second_far + first_near + second_near:
            each.start()

    def pass_on():
        for came, each, (block, bufs, put) in zip(first_far, first_sum, firsts):
            came.wait_recv()
            bufs[0][...] = (load(block(right)) + load(bufs[0])).astype(BF)
            each.start()
        for came, each, (block, bufs, put) in zip(second_far, second_sum, seconds):
            came.wait_recv()
            bufs[0][...] = (load(block(left)) + load(bufs[0])).astype(BF)
            each.start()

    def finish():
        near, far_sum = first_near + second_near, first_sum + second_sum
        for one, two, (block, bufs, put) in zip(near, far_sum, firsts + seconds):
            one.wait_recv()
            two.wait_recv()
            put(load(block(place)) + load(bufs[1]) + load(bufs[2]))
        for each in first_far + second_far + near + far_sum:
            each.wait_send()

    return start, pass_on, finish


def scatter_direct(firsts, seconds, place, device_at, copies):
    parts = firsts + seconds
    sent = []
    for block, bufs, put in parts:
        sent.append(
            [
                copies(block(lax.rem(place + step, 4)), bufs[index], device_at(step), False)
                for index, step in enumerate((1, 3, 2))
            ]
        )

    def start():
        for each in sum(sent, []):
            each.start()

    def finish():
        for came, (block, bufs, put) in zip(sent, parts):
            total = block(place)[...].astype(F32)
            for each, landed in zip(came, bufs):
                each.wait_recv()
                total = total + landed[...].astype(F32)
            for each in came:
                each.wait_send()
            put(total)

    return start, lambda: None, finish


def scatter_both(first_a, second_a, first_b, second_b, copies, phase=scatter_phase):
    z, y, along_y, along_z = grid_place()

    def wide(part):
        block, bufs, _, _ = part
        return [(block, bufs, stored_in(bufs[1]))]

    def slim(part):
        _, kept, bufs, put = part
        return [((lambda at: kept[1].at[at]), bufs, put)]

    start_a, pass_a, finish_a = phase(wide(first_a), wide(second_a), y, along_y, copies)
    start_b, pass_b, finish_b = phase(wide(first_b), wide(second_b), z, along_z, copies)
    then_a, last_a, end_a = phase(slim(first_a), slim(second_a), z, along_z, copies)
    then_b, last_b, end_b = phase(slim(first_b), slim(second_b), y, along_y, copies)
    start_a()
    start_b()
    yield
    pass_a()
    pass_b()
    yield
    finish_a()
    then_a()
    finish_b()
    then_b()
    yield
    last_a()
    last_b()
    yield
    end_a()
    end_b()


def scatter_split(first_a, second_a, first_b, second_b, copies):
    z, y, along_y, along_z = grid_place()

    def slim(part):
        _, kept, bufs, put = part
        return [((lambda at: kept[1].at[at]), bufs, put)]

    def halved(half):
        def wide(part):
            block, bufs, _, _ = part
            views = [each.at[half] for each in bufs]
            return [(lambda at: block(at, half), views, stored_in(views[1]))]

        return [
            scatter_phase(wide(first_a), wide(second_a), y, along_y, copies),
            scatter_phase(wide(first_b), wide(second_b), z, along_z, copies),
        ]

    halves = [halved(pl.ds(0, 2)), halved(pl.ds(2, 2))]
    last_phases = [
        scatter_phase(slim(first_a), slim(second_a), z, along_z, copies),
        scatter_phase(slim(first_b), slim(second_b), y, along_y, copies),
    ]
    for start, _, _ in halves[0]:
        start()
    yield
    for _, pass_on, _ in halves[0]:
        pass_on()
    for start, _, _ in halves[1]:
        start()
    yield
    for _, pass_on, _ in halves[1]:
        pass_on()
    yield
    for phases in halves:
        for _, _, finish in phases:
            finish()
    for start, _, _ in last_phases:
        start()
    yield
    for _, pass_on, _ in last_phases:
        pass_on()
    yield
    for _, _, finish in last_phases:
        finish()


def scatter_scratch(*shapes):
    scratch = []
    for shape in shapes:
        scratch += [pltpu.VMEM((4, *shape), BF)] * 3 + [pltpu.VMEM(shape, BF)] * 3
    return scratch


def scatter_part(scratch, index, block, put):
    mine = scratch[6 * index : 6 * index + 6]
    return block, mine[:3], mine[3:], put


def stored_in(ref, *at):
    def put(value):
        ref[at if at else ...] = value.astype(ref.dtype)

    return put


DOWN_STARTS = (0, 80, 160, 224)
DOWN_ROWS = 80


def mlp_terms(rows_ref, dgate_ref, dup_ref, product_ref, dout_ref, gate_terms, up_terms, down_terms):
    def flat(ref):
        return ref[...].reshape(4 * ROWS, ref.shape[-1])

    rows = flat(rows_ref)
    for terms, grads in ((gate_terms, dgate_ref), (up_terms, dup_ref)):
        whole = tn(rows, flat(grads))
        for at in range(16):
            terms[at // 4, at % 4] = whole[56 * at : 56 * at + 56].astype(BF)
    whole = tn(flat(product_ref), flat(dout_ref)).astype(BF)
    for at in range(16):
        start = 304 * (at // 4) + DOWN_STARTS[at % 4]
        down_terms[at // 4, at % 4] = whole[start : start + DOWN_ROWS]


def mlp_sums(gate_terms, up_terms, down_terms, gate_out, up_out, down_out, scratch, copies):
    left, right = slice(0, 512), slice(512, D)
    return scatter_split(
        scatter_part(scratch, 0, lambda at, part: gate_terms.at[part, at], stored_in(gate_out)),
        scatter_part(
            scratch, 2, lambda at, part: down_terms.at[part, at, :, left], stored_in(down_out, slice(None), left)
        ),
        scatter_part(scratch, 1, lambda at, part: up_terms.at[at, part], stored_in(up_out)),
        scatter_part(
            scratch, 3, lambda at, part: down_terms.at[at, part, :, right], stored_in(down_out, slice(None), right)
        ),
        copies,
    )


MLP_SUMS_SHAPES = ((56, QUARTER), (56, QUARTER), (DOWN_ROWS, 512), (DOWN_ROWS, D - 512))


def qkv_sums(qkv_half, out_half, qkv_sum, out_sum, scratch, copies):
    top, bottom = slice(0, 16), slice(16, 32)
    return scatter_both(
        scatter_part(scratch, 0, lambda at: qkv_half.at[:, at, top], stored_in(qkv_sum, top)),
        scatter_part(scratch, 1, lambda at: qkv_half.at[:, at, bottom], stored_in(qkv_sum, bottom)),
        scatter_part(scratch, 2, lambda at: out_half.at[at, :, top], stored_in(out_sum, top)),
        scatter_part(scratch, 3, lambda at: out_half.at[at, :, bottom], stored_in(out_sum, bottom)),
        copies,
    )


def kv_sums(dkv_ref, total, scratch, copies):
    top, bottom = slice(0, 32), slice(32, 64)
    return scatter_both(
        scatter_part(scratch, 0, lambda at: dkv_ref.at[0, :, at, top], stored_in(total, slice(0, 32))),
        scatter_part(scratch, 1, lambda at: dkv_ref.at[0, :, at, bottom], stored_in(total, slice(32, 64))),
        scatter_part(scratch, 2, lambda at: dkv_ref.at[1, at, :, top], stored_in(total, slice(64, 96))),
        scatter_part(scratch, 3, lambda at: dkv_ref.at[1, at, :, bottom], stored_in(total, slice(96, 128))),
        copies,
        scatter_direct,
    )


def replica_partners():
    me = lax.axis_index("replica")
    return me, me + 1 - 2 * lax.rem(me, 2), lax.rem(me + 2, 4), 3 - me


def other_section():
    return {"section": 1 - lax.axis_index("section")}


def exchange(
    own_ref, all_ref, total_ref, near_terms, part, far_part, near_sum, part_in, far_in, near_in, copies, loads, work, greetings=2
):
    me, mate, next_, far = replica_partners()
    halves = (slice(0, 64), slice(64, 128))
    to_mate, to_next = {"replica": mate}, {"replica": next_}
    greeted(greetings)
    across = [copies(own_ref.at[half], all_ref.at[me, half], to_next) for half in halves]
    beside = copies(own_ref, all_ref.at[me], to_mate)
    forwards = [copies(all_ref.at[next_, half], all_ref.at[next_, half], to_mate, False) for half in halves]
    passed = [copies(far_part.at[index], far_in.at[index], to_mate, False) for index in (0, 1)]
    sums = [copies(near_sum.at[index], near_in.at[index], to_next, False) for index in (0, 1)]
    sent = copies(part, part_in, to_mate, False)
    all_ref[me] = own_ref[...]
    for each in loads:
        each.wait()

    def send_sum(index):
        passed[index].wait_recv()
        near_sum[index] = (near_terms[index] + far_in[index].astype(F32)).astype(BF)
        sums[index].start()

    def step(at, carry):
        one = jnp.where(at == 0, me, jnp.where(at == 3, mate, next_))
        two = jnp.where(at == 0, me, jnp.where(at == 3, mate, far))
        first_rows = pl.ds(pl.multiple_of(jnp.where(at == 2, 64, 0), 64), 64)
        second_rows = pl.ds(pl.multiple_of(jnp.where(at == 1, 0, 64), 64), 64)

        @pl.when(at == 1)
        def _():
            across[0].wait_recv()
            forwards[0].start()
            forwards[0].wait_recv()

        @pl.when(at == 2)
        def _():
            across[1].wait_recv()
            forwards[1].start()
            send_sum(0)
            forwards[1].wait_recv()

        @pl.when(at == 3)
        def _():
            send_sum(1)
            beside.wait_recv()

        terms = work([(one, first_rows), (two, second_rows)])

        @pl.when(at == 0)
        def _():
            total_ref[...] = terms

        for index in (0, 1):

            @pl.when(at == 1 + index)
            def _(index=index):
                near_terms[index] = terms[:64]
                far_part[index] = terms[64:].astype(BF)
                passed[index].start()

        @pl.when(at == 3)
        def _():
            part[...] = terms.astype(BF)
            sent.start()

        return carry

    lax.fori_loop(0, 4, step, 0)
    sent.wait_recv()
    total = total_ref[...] + part_in[...].astype(F32)
    for each in sums:
        each.wait_recv()
    total = total + near_in[...].reshape(ROWS, D).astype(F32)
    for each in across + [beside, sent] + forwards + passed + sums:
        each.wait_send()
    return total


EXCHANGE_SCRATCH = [
    pltpu.VMEM((D, QUARTER), BF),
    pltpu.VMEM((D, QUARTER), BF),
    pltpu.VMEM((QUARTER, D), BF),
    pltpu.VMEM((ROWS, D), F32),
    pltpu.VMEM((2, 64, D), F32),
    pltpu.VMEM((ROWS, D), BF),
    pltpu.VMEM((2, 64, D), BF),
    pltpu.VMEM((2, 64, D), BF),
    pltpu.VMEM((ROWS, D), BF),
    pltpu.VMEM((2, 64, D), BF),
    pltpu.VMEM((2, 64, D), BF),
    pltpu.SemaphoreType.DMA((11,)),
    pltpu.SemaphoreType.DMA((11,)),
    pltpu.SemaphoreType.DMA((18,)),
]


def mlp_start(hbm, vmem, local):
    me, mate, next_, far = replica_partners()
    signal([{"replica": mate}, {"replica": next_}])
    loads = [pltpu.make_async_copy(src, dst, local.at[i]) for i, (src, dst) in enumerate(zip(hbm[:2], vmem[:2]))]
    for at in range(16):
        skip = 80 * (at % 4) - DOWN_STARTS[at % 4]
        rows = pl.ds(304 * (at // 4) + 80 * (at % 4), DOWN_ROWS - skip)
        piece = hbm[2].at[at // 4, at % 4, pl.ds(skip, DOWN_ROWS - skip)]
        loads.append(pltpu.make_async_copy(piece, vmem[2].at[rows], local.at[2 + at]))
    for each in loads:
        each.start()
    return loads


def split_rows(value, parts):
    for index, (source, rows) in enumerate(parts):
        yield source, rows, value[64 * index : 64 * index + 64]


def mlp_forward_kernel(
    normed_ref, hidden_ref, gate_hbm, up_hbm, down_hbm, out_ref, all_ref, gate_ref, up_ref,
    gate_w, up_w, down_w, total_ref, near_terms, part, far_part, near_sum, part_in, far_in, near_in, send, recv, local
):
    loads = mlp_start((gate_hbm, up_hbm, down_hbm), (gate_w, up_w, down_w), local)

    def work(parts):
        rows = jnp.concatenate([all_ref[source, rows] for source, rows in parts], axis=0)
        gate = nn(rows, gate_w[...])
        up = nn(rows, up_w[...])
        for source, at, value in split_rows(gate, parts):
            gate_ref[source, at] = value.astype(BF)
        for source, at, value in split_rows(up, parts):
            up_ref[source, at] = value.astype(BF)
        product = (gate * jax.nn.sigmoid(gate) * up).astype(BF)
        return nn(product, down_w[...])

    total = exchange(
        normed_ref, all_ref, total_ref, near_terms, part, far_part, near_sum, part_in, far_in, near_in,
        Copies(send, recv), loads, work
    )
    out_ref[...] = (hidden_ref[...] + total).astype(BF)


def mlp_relay_kernel(
    normed_ref, hidden_ref, x_ref, gate_hbm, up_hbm, down_hbm, next_ref, all_ref, out_ref, relayed_ref,
    gate_w, up_w, down_w, total_ref, near_terms, part, far_part, near_sum, part_in, far_in, near_in, send, recv, local
):
    signal([other_section()])
    loads = mlp_start((gate_hbm, up_hbm, down_hbm), (gate_w, up_w, down_w), local)

    def work(parts):
        rows = jnp.concatenate([all_ref[source, rows] for source, rows in parts], axis=0)
        gate = nn(rows, gate_w[...])
        up = nn(rows, up_w[...])
        product = (gate * jax.nn.sigmoid(gate) * up).astype(BF)
        return nn(product, down_w[...])

    copies = Copies(send, recv)
    total = exchange(
        normed_ref, all_ref, total_ref, near_terms, part, far_part, near_sum, part_in, far_in, near_in,
        copies, loads, work, 3
    )
    out_ref[...] = (hidden_ref[...] + total).astype(BF)
    relay = copies(out_ref, relayed_ref, other_section())
    relay.wait()
    first_section = jnp.broadcast_to(lax.axis_index("section") == 0, (ROWS, D))
    next_ref[...] = jnp.where(first_section, x_ref[...], relayed_ref[...])


def mlp_relay(normed2, hidden, x, gate_w, up_w, down_w):
    return pl.pallas_call(
        mlp_relay_kernel,
        out_shape=shaped(ROWS, D),
        in_specs=[VMEM_SPEC] * 3 + [ANY_SPEC] * 3,
        scratch_shapes=[pltpu.VMEM((4, ROWS, D), BF), pltpu.VMEM((ROWS, D), BF), pltpu.VMEM((ROWS, D), BF)]
        + EXCHANGE_SCRATCH,
        compiler_params=params(2),
        name="mlp_relay",
    )(normed2, hidden, x, gate_w, up_w, down_w)


def mlp_forward(normed2, hidden, gate_w, up_w, down_w):
    return pl.pallas_call(
        mlp_forward_kernel,
        out_shape=(
            shaped(ROWS, D),
            shaped(4, ROWS, D),
            shaped(4, ROWS, QUARTER),
            shaped(4, ROWS, QUARTER),
        ),
        in_specs=[VMEM_SPEC] * 2 + [ANY_SPEC] * 3,
        scratch_shapes=EXCHANGE_SCRATCH,
        compiler_params=params(3),
        name="mlp_forward",
    )(normed2, hidden, gate_w, up_w, down_w)


def mlp_backward_kernel(
    dout_ref, gate_ref, up_ref, gate_hbm, up_hbm, down_hbm,
    dnormed_ref, all_ref, dgate_ref, dup_ref, product_ref,
    gate_w, up_w, down_w, total_ref, near_terms, part, far_part, near_sum, part_in, far_in, near_in, send, recv, local
):
    loads = mlp_start((gate_hbm, up_hbm, down_hbm), (gate_w, up_w, down_w), local)

    def work(parts):

        def stacked(ref):
            return jnp.concatenate([ref[source, rows] for source, rows in parts], axis=0)

        dproduct = nt(stacked(all_ref), down_w[...])
        gate = stacked(gate_ref).astype(F32)
        up = stacked(up_ref).astype(F32)
        s = jax.nn.sigmoid(gate)
        silu = gate * s
        product = (silu * up).astype(BF)
        dgate = (dproduct * up * (s * (1.0 + gate * (1.0 - s)))).astype(BF)
        dup = (dproduct * silu).astype(BF)
        for to, whole in ((product_ref, product), (dgate_ref, dgate), (dup_ref, dup)):
            for source, at, value in split_rows(whole, parts):
                to[source, at] = value
        return nt(dgate, gate_w[...]) + nt(dup, up_w[...])

    dnormed_ref[...] = exchange(
        dout_ref, all_ref, total_ref, near_terms, part, far_part, near_sum, part_in, far_in, near_in,
        Copies(send, recv), loads, work
    )


def mlp_backward(dout, gate, up, gate_w, up_w, down_w):
    return pl.pallas_call(
        mlp_backward_kernel,
        out_shape=(
            shaped(ROWS, D, dtype=F32),
            shaped(4, ROWS, D),
            shaped(4, ROWS, QUARTER),
            shaped(4, ROWS, QUARTER),
            shaped(4, ROWS, QUARTER),
        ),
        in_specs=[VMEM_SPEC] * 3 + [ANY_SPEC] * 3,
        scratch_shapes=EXCHANGE_SCRATCH,
        compiler_params=params(4),
        name="mlp_backward",
    )(dout, gate, up, gate_w, up_w, down_w)


def outputs_kernel(
    gate, up, down, qkv, out, gate_out, up_out, down_out, qkv_out, out_out, bias_out, value_out, gain1_out, gain2_out
):
    for r in range(4):
        lanes = slice(QUARTER * r, QUARTER * r + QUARTER)
        gate_out[:, lanes] = gate[r].astype(F32)
        up_out[:, lanes] = up[r].astype(F32)
        skip = 80 * r - DOWN_STARTS[r]
        down_out[80 * r : DOWN_STARTS[r] + DOWN_ROWS] = down[r, skip:].astype(F32)
    qkv_out[:32] = qkv[0]
    qkv_out[32:] = qkv[1, :24]
    out_out[:32] = out[0]
    out_out[32:] = out[1, :24]
    small = qkv[1, 24:][:1]
    bias_out[...] = small[:, :64]
    value_out[...] = small[:, 64:72]
    gain1_out[...] = small[:, 72:128]
    gain2_out[...] = small[:, 128:184]


def outputs(gate, up, down, qkv, out):
    return local_call(
        outputs_kernel,
        "outputs",
        (
            shaped(56, FF, dtype=F32),
            shaped(56, FF, dtype=F32),
            shaped(FF // 16, D, dtype=F32),
            shaped(56, QKV, dtype=F32),
            shaped(56, D, dtype=F32),
            shaped(1, 64, dtype=F32),
            shaped(1, 8, dtype=F32),
            shaped(1, 56, dtype=F32),
            shaped(1, 56, dtype=F32),
        ),
    )(gate, up, down, qkv, out)


def turn(values, cosine, sine, sign):
    width = values.shape[1]
    up = pltpu.roll(values, width - HALF, 1)
    down = pltpu.roll(values, HALF, 1)
    lane = lax.broadcasted_iota(jnp.int32, values.shape, 1)
    swapped = jnp.where(lax.rem(lane, 2 * HALF) < HALF, up, down)
    repeat = width // KV
    cosine = jnp.concatenate([cosine] * repeat, axis=1)
    sine = jnp.concatenate([sine] * repeat, axis=1)
    return values * cosine + sign * (swapped * sine)


def front_work(x_ref, w_ref, b_ref, g_ref, cos_ref, sin_ref, normed_ref, q_ref, kv_ref, copies, ready):
    z, y, along_y, along_z = grid_place()
    x = x_ref[...].astype(F32)
    inverse = lax.rsqrt(jnp.mean(x * x, axis=-1, keepdims=True) + EPSILON)
    normed = (x * inverse * g_ref[...]).astype(BF)
    normed_ref[...] = normed
    projected = nn(normed, w_ref[:, D:]) + b_ref[:, D:]
    turned = turn(projected[:, :KV], cos_ref[...], sin_ref[...], 1.0)
    kv = jnp.concatenate([turned, projected[:, KV:]], axis=1).astype(BF)
    kv_ref[0, z, y] = kv[:64]
    kv_ref[1, z, y] = kv[64:]
    if ready:
        ready()
    top, bottom = (slice(0, 32), slice(None)), (slice(32, 64), slice(None))
    steps = gather_both(
        y_then_z(kv_ref.at[0], *top),
        y_then_z(kv_ref.at[0], *bottom),
        z_then_y(kv_ref.at[1], *top),
        z_then_y(kv_ref.at[1], *bottom),
        copies,
        gather_direct,
    )
    next(steps)
    projected = nn(normed, w_ref[:, :D]) + b_ref[:, :D]
    q_ref[...] = turn(projected, cos_ref[...], sin_ref[...], 1.0).astype(BF)
    return steps


def front_kernel(x_ref, w_ref, b_ref, g_ref, cos_ref, sin_ref, normed_ref, q_ref, kv_ref, send, recv):
    z, y, along_y, along_z = grid_place()
    signal(neighbours(along_y, along_z))
    steps = front_work(
        x_ref, w_ref, b_ref, g_ref, cos_ref, sin_ref, normed_ref, q_ref, kv_ref,
        Copies(send, recv), lambda: greeted(6)
    )
    run(steps)


def front(x, w_qkv, b_qkv, g_attn, cosine, sine):
    return pl.pallas_call(
        front_kernel,
        out_shape=(shaped(ROWS, D), shaped(ROWS, D), shaped(2, 4, 4, 64, 2 * KV)),
        scratch_shapes=[pltpu.SemaphoreType.DMA((24,)), pltpu.SemaphoreType.DMA((24,))],
        compiler_params=params(6),
        name="front",
    )(x, w_qkv, b_qkv, g_attn, cosine, sine)


def low_lanes(rows):
    return lax.broadcasted_iota(jnp.int32, (rows, KV), 1) < KV // 2


def spread(kv_ref, start, to_ref):
    mixed = kv_ref[:, :, :, :, start : start + KV].reshape(LEN, KV)
    other = pltpu.roll(mixed.astype(F32), KV // 2, 1).astype(BF)
    low = low_lanes(LEN)
    to_ref[0] = jnp.where(low, mixed, other)
    to_ref[1] = mixed
    to_ref[2] = jnp.where(low, other, mixed)


def fill_bias(kseg_ref, bias_refs):
    first_row = 64 * lax.axis_index("group")
    for block, bias_ref in enumerate(bias_refs):
        keys = SPAN * (block + 1)
        kpos = lax.broadcasted_iota(jnp.int32, (64, keys), 1)
        qpos = SPAN * block + first_row + lax.broadcasted_iota(jnp.int32, (64, keys), 0)
        kseg = jnp.broadcast_to(kseg_ref[:, :keys], (64, keys)).astype(F32)
        qseg = jnp.sum(jnp.where(kpos == qpos, kseg, 0.0), axis=1, keepdims=True)
        bias_ref[...] = jnp.where((kpos <= qpos) & (kseg == qseg), 0.0, NEGATIVE)


def two_heads(pair):
    low = low_lanes(64)
    zero = jnp.zeros_like(pair)
    return jnp.concatenate([jnp.where(low, pair, zero), jnp.where(low, zero, pair)], axis=0)


def one_pair(stacked):
    return jnp.where(low_lanes(64), stacked[:64], stacked[64:])


def softmax(queries, keys, bias_ref):
    count = keys.shape[0]
    scores = nt(queries, keys).reshape(2, 64, count) + bias_ref[...][None]
    highest = jnp.max(scores, axis=-1, keepdims=True)
    exponent = jnp.exp(scores - highest)
    total = jnp.sum(exponent, axis=-1, keepdims=True)
    return (exponent * (1.0 / total)).reshape(2 * 64, count)


def variant_of(pair):
    return jnp.where(pair < 3, 0, jnp.where(pair == 3, 1, 2))


def attention_work(
    x_ref, q_ref, kv_ref, kseg_ref, w_ref, g_ref, context_ref, hidden_ref, normed_ref,
    keys_ref, values_ref, bias0, bias1, between=None
):
    spread(kv_ref, 0, keys_ref)
    spread(kv_ref, KV, values_ref)
    fill_bias(kseg_ref, (bias0, bias1))

    def one(pair, carry):
        if between:
            pl.when(pair == 4)(between)
        variant = variant_of(pair)
        lanes = pl.ds(pl.multiple_of(pair * KV, KV), KV)
        for block, bias_ref in enumerate((bias0, bias1)):
            rows = slice(64 * block, 64 * block + 64)
            keys = pl.ds(0, SPAN * (block + 1))
            queries = two_heads(q_ref[rows, lanes] * SCALE).astype(BF)
            weights = softmax(queries, keys_ref[variant, keys], bias_ref).astype(BF)
            context = nn(weights, values_ref[variant, keys])
            context_ref[rows, lanes] = one_pair(context).astype(BF)
        return carry

    lax.fori_loop(0, PAIRS, one, 0)
    hidden = x_ref[...].astype(F32) + nn(context_ref[...], w_ref[...])
    hidden_ref[...] = hidden
    inverse = lax.rsqrt(jnp.mean(hidden * hidden, axis=-1, keepdims=True) + EPSILON)
    normed_ref[...] = (hidden * inverse * g_ref[...]).astype(BF)


ATTENTION_SCRATCH = [
    pltpu.VMEM((3, LEN, KV), BF),
    pltpu.VMEM((3, LEN, KV), BF),
    pltpu.VMEM((64, SPAN), F32),
    pltpu.VMEM((64, LEN), F32),
]


def attention(x, q, kv, kseg, w_out, g_mlp):
    return local_call(
        attention_work,
        "attention",
        (shaped(ROWS, D), shaped(ROWS, D, dtype=F32), shaped(ROWS, D)),
        ATTENTION_SCRATCH,
    )(x, q, kv, kseg, w_out, g_mlp)


def norm_backward(values, gain, grads):
    inverse = lax.rsqrt(jnp.mean(values * values, axis=-1, keepdims=True) + EPSILON)
    scaled = grads * gain
    dvalues = inverse * scaled - values * (
        inverse * inverse * inverse * jnp.mean(scaled * values, axis=-1, keepdims=True)
    )
    return dvalues, jnp.sum(grads * values * inverse, axis=0, keepdims=True)


def attention_backward_work(
    dout_ref, dnormed_ref, hidden_ref, g_ref, w_ref, q_ref, kv_ref, kseg_ref,
    dhidden_ref, dlow_ref, dq_ref, dkv_ref, dgain_ref,
    keys_ref, values_ref, bias0, bias1, dcontext_ref, dkeys, dvalues, between=None
):
    dnorm, dgain = norm_backward(hidden_ref[...], g_ref[...], dnormed_ref[...])
    dgain_ref[...] = dgain
    dhidden = dout_ref[...].astype(F32) + dnorm
    dhidden_ref[...] = dhidden
    dlow = dhidden.astype(BF)
    dlow_ref[...] = dlow
    dcontext_ref[...] = nt(dlow, w_ref[...]).astype(BF)
    spread(kv_ref, 0, keys_ref)
    spread(kv_ref, KV, values_ref)
    fill_bias(kseg_ref, (bias0, bias1))
    dkeys[...] = jnp.zeros_like(dkeys)
    dvalues[...] = jnp.zeros_like(dvalues)

    def one(pair, carry):
        if between:
            pl.when(pair == 4)(between)
        variant = variant_of(pair)
        lanes = pl.ds(pl.multiple_of(pair * KV, KV), KV)
        for block, bias_ref in enumerate((bias0, bias1)):
            rows = slice(64 * block, 64 * block + 64)
            keys = pl.ds(0, SPAN * (block + 1))
            queries = two_heads(q_ref[rows, lanes] * SCALE).astype(BF)
            dcontext = two_heads(dcontext_ref[rows, lanes])
            key_rows = keys_ref[variant, keys]
            weights = softmax(queries, key_rows, bias_ref)
            dweights = nt(dcontext, values_ref[variant, keys])
            inner = jnp.sum(weights * dweights, axis=-1, keepdims=True)
            dscores = (weights * (dweights - inner)).astype(BF)
            dq_ref[rows, lanes] = one_pair(nn(dscores, key_rows)) * SCALE
            dkeys[variant, keys] += tn(dscores, queries)
            dvalues[variant, keys] += tn(weights.astype(BF), dcontext)
        return carry

    lax.fori_loop(0, PAIRS, one, 0)
    low = low_lanes(LEN)
    for start, total in ((0, dkeys), (KV, dvalues)):
        head0 = total[0] + pltpu.roll(total[0], KV // 2, 1)
        head1 = total[2] + pltpu.roll(total[2], KV // 2, 1)
        whole = (jnp.where(low, head0, head1) + total[1]).astype(BF)
        dkv_ref[:, :, :, :, start : start + KV] = whole.reshape(2, 4, 4, 64, KV)


ATTENTION_BACKWARD_OUT = (
    shaped(ROWS, D, dtype=F32),
    shaped(ROWS, D),
    shaped(ROWS, D, dtype=F32),
    shaped(2, 4, 4, 64, 2 * KV),
    shaped(1, D, dtype=F32),
)
ATTENTION_BACKWARD_SCRATCH = ATTENTION_SCRATCH + [
    pltpu.VMEM((ROWS, D), BF),
    pltpu.VMEM((3, LEN, KV), F32),
    pltpu.VMEM((3, LEN, KV), F32),
]


def attention_backward(*operands):
    return local_call(
        attention_backward_work, "attention_backward", ATTENTION_BACKWARD_OUT, ATTENTION_BACKWARD_SCRATCH
    )(*operands)


def rear_query(dq_ref, cos_ref, sin_ref, w_ref, dprojected_ref, dbias_ref):
    dquery = turn(dq_ref[...], cos_ref[...], sin_ref[...], -1.0).astype(BF)
    dprojected_ref[:, :D] = dquery
    dbias_ref[:, :D] = jnp.sum(dquery.astype(F32), axis=0, keepdims=True)
    return nt(dquery, w_ref[:, :D])


def rear_rest(
    dnormed, total, cos_ref, sin_ref, w_ref, x_ref, g_ref, dhidden_ref, dprojected_ref, dinput_ref, dgain_ref, dbias_ref
):
    turned = turn(total[:, :KV], cos_ref[...], sin_ref[...], -1.0)
    dkv = jnp.concatenate([turned, total[:, KV:]], axis=1).astype(BF)
    dprojected_ref[:, D:] = dkv
    dbias_ref[:, D:] = jnp.sum(dkv.astype(F32), axis=0, keepdims=True)
    dnormed = dnormed + nt(dkv, w_ref[:, D:])
    dnorm, dgain = norm_backward(x_ref[...].astype(F32), g_ref[...], dnormed)
    dgain_ref[...] = dgain
    dinput_ref[...] = (dhidden_ref[...] + dnorm).astype(BF)


REAR_SCRATCH = [
    pltpu.VMEM((ROWS, QKV), BF),
    pltpu.VMEM((1, D), F32),
    pltpu.VMEM((1, QKV), F32),
    pltpu.VMEM((ROWS, 2 * KV), F32),
] + scatter_scratch(*[(32, 2 * KV)] * 4)


def rear_kernel(
    dkv_ref, dq_ref, cos_ref, sin_ref, w_ref, x_ref, g_ref, dhidden_ref, cotangent_ref, next_ref,
    dinput_ref, returned_ref, dprojected_ref, dgain_ref, dbias_ref, total, *rest
):
    scratch, (send, recv) = rest[:-2], rest[-2:]
    z, y, along_y, along_z = grid_place()
    signal(neighbours(along_y, along_z) + [other_section()])
    greeted(7)
    copies = Copies(send, recv)
    steps = kv_sums(dkv_ref, total, scratch, copies)
    next(steps)
    dnormed = rear_query(dq_ref, cos_ref, sin_ref, w_ref, dprojected_ref, dbias_ref)
    run(steps)
    rear_rest(
        dnormed, total, cos_ref, sin_ref, w_ref, x_ref, g_ref, dhidden_ref,
        dprojected_ref, dinput_ref, dgain_ref, dbias_ref
    )
    relay = copies(dinput_ref, returned_ref, other_section())
    relay.wait()
    last_section = jnp.broadcast_to(lax.axis_index("section") == 1, (ROWS, D))
    next_ref[...] = jnp.where(last_section, cotangent_ref[...], returned_ref[...])


def rear(*operands):
    return pl.pallas_call(
        rear_kernel,
        out_shape=shaped(ROWS, D),
        scratch_shapes=[pltpu.VMEM((ROWS, D), BF), pltpu.VMEM((ROWS, D), BF)]
        + REAR_SCRATCH
        + [pltpu.SemaphoreType.DMA((25,)), pltpu.SemaphoreType.DMA((25,))],
        compiler_params=params(7),
        name="rear",
    )(*operands)


TAIL_SCRATCH = [
    pltpu.VMEM((4, 4, 56, QUARTER), BF),
    pltpu.VMEM((4, 4, 56, QUARTER), BF),
    pltpu.VMEM((4, 4, DOWN_ROWS, D), BF),
    pltpu.VMEM((56, QUARTER), BF),
    pltpu.VMEM((56, QUARTER), BF),
    pltpu.VMEM((DOWN_ROWS, D), BF),
    pltpu.VMEM((4, 4, 64, QKV), BF),
    pltpu.VMEM((4, 4, 64, D), BF),
    pltpu.VMEM((4, 4, 32, QKV), BF),
    pltpu.VMEM((4, 4, 32, D), BF),
    pltpu.VMEM((32, QKV), F32),
    pltpu.VMEM((32, D), F32),
    pltpu.VMEM((32, QKV), BF),
    pltpu.VMEM((32, D), BF),
    pltpu.VMEM((32, QKV), BF),
    pltpu.VMEM((32, D), BF),
]
TAIL_COPIES = 24 + 36 + 24 + 2 + 13


def tail_kernel(*refs):
    refs = list(refs)

    def take(count):
        taken = refs[:count]
        del refs[:count]
        return taken

    attention_in = take(8)
    mlp_in = take(5)
    cos_ref, sin_ref, qkv_w, x_ref, gain1_ref, normed_ref, context_ref = take(7)
    dinput_ref, gate_all, up_all, down_all, qkv_all, out_all = take(6)
    attention_out = take(5)
    dhidden_ref, dlow_ref, dq_ref, dkv_ref, dgain2_ref = attention_out
    attention_scratch = take(len(ATTENTION_BACKWARD_SCRATCH))
    dprojected_ref, dgain1_ref, dbias_ref, total = take(4)
    kv_bufs = take(24)
    mlp_term_refs, mlp_sum_refs = take(3), take(3)
    qkv_terms, out_terms, qkv_half, out_half, qkv_sum, out_sum, qkv_low, out_low, qkv_in, out_in = take(10)
    mlp_bufs, qkv_bufs = take(24), take(24)
    send, recv, local = take(3)

    z, y, along_y, along_z = grid_place()
    me, mate, next_, far = replica_partners()
    core = lax.rem(me, 2)
    to_mate, to_next = {"replica": mate}, {"replica": next_}
    target, source, stays = quarter_route()
    moves = jnp.logical_not(stays)
    signal(neighbours(along_y, along_z) + [to_mate, to_next])
    mlp_terms(*mlp_in, *mlp_term_refs)

    @pl.when(moves)
    def _():
        signal([target])
        greeted(9)

    @pl.when(stays)
    def _():
        greeted(8)

    copies = Copies(send, recv)
    mlp = mlp_sums(*mlp_term_refs, *mlp_sum_refs, mlp_bufs, copies)
    next(mlp)
    attention_backward_work(*attention_in, *attention_out, *attention_scratch, lambda: next(mlp))
    kv = kv_sums(dkv_ref, total, kv_bufs, copies)
    next(kv)
    next(mlp)

    mine = pl.ds(pl.multiple_of(32 * core, 32), 32)
    theirs = pl.ds(pl.multiple_of(32 - 32 * core, 32), 32)

    def add_mate(sent, terms, half):
        sent.wait_recv()
        half[...] = (terms[:, :, mine].astype(F32) + half[...].astype(F32)).astype(BF)

    dnormed = rear_query(dq_ref, cos_ref, sin_ref, qkv_w, dprojected_ref, dbias_ref)
    next(kv)
    whole = tn(context_ref[...], dlow_ref[...])
    for at in range(16):
        rows = jnp.concatenate([whole[56 * at : 56 * at + 56], jnp.zeros((8, D), F32)], axis=0)
        out_terms[at // 4, at % 4] = rows.astype(BF)
    out_sent = copies(out_terms.at[:, :, theirs], out_half, to_mate)
    next(kv)
    add_mate(out_sent, out_terms, out_half)
    run(kv)
    rear_rest(
        dnormed, total, cos_ref, sin_ref, qkv_w, x_ref, gain1_ref, dhidden_ref,
        dprojected_ref, dinput_ref, dgain1_ref, dbias_ref
    )
    whole = tn(normed_ref[...], dprojected_ref[...])
    dbias, dgain1, dgain2 = dbias_ref[...], dgain1_ref[...], dgain2_ref[...]
    for at in range(16):
        small = jnp.concatenate(
            [
                dbias[:, 64 * at : 64 * at + 64],
                dbias[:, D + KV + 8 * at : D + KV + 8 * at + 8],
                dgain1[:, 56 * at : 56 * at + 56],
                dgain2[:, 56 * at : 56 * at + 56],
                jnp.zeros((1, QKV - 184), F32),
            ],
            axis=1,
        )
        rows = jnp.concatenate([whole[56 * at : 56 * at + 56], jnp.broadcast_to(small, (8, QKV))], axis=0)
        qkv_terms[at // 4, at % 4] = rows.astype(BF)
    qkv_sent = copies(qkv_terms.at[:, :, theirs], qkv_half, to_mate)
    next(mlp)
    add_mate(qkv_sent, qkv_terms, qkv_half)
    dense = qkv_sums(qkv_half, out_half, qkv_sum, out_sum, qkv_bufs, copies)
    next(dense)
    next(mlp)
    next(dense)
    run(mlp)

    gate, up, down = mlp_sum_refs
    moved = pltpu.make_async_remote_copy(
        src_ref=down,
        dst_ref=down_all.at[source["replica"]],
        send_sem=local.at[0],
        recv_sem=local.at[1],
        device_id=source,
        device_id_type=MESH,
    )
    stayed = pltpu.make_async_copy(down, down_all.at[me], local.at[2])

    @pl.when(moves)
    def _():
        moved.start()

    @pl.when(stays)
    def _():
        stayed.start()

    pairs = ((gate, gate_all), (up, up_all))
    across = [copies(ref, all_ref.at[me], to_next) for ref, all_ref in pairs]
    beside = [copies(ref, all_ref.at[me], to_mate) for ref, all_ref in pairs]
    for ref, all_ref in pairs:
        all_ref[me] = ref[...]
    next(dense)

    @pl.when(moves)
    def _():
        moved.wait()

    @pl.when(stays)
    def _():
        stayed.wait()

    across.append(copies(down_all.at[me], down_all.at[me], to_next))
    beside.append(copies(down_all.at[me], down_all.at[me], to_mate))
    next(dense)
    run(dense)
    qkv_low[...] = qkv_sum[...].astype(BF)
    out_low[...] = out_sum[...].astype(BF)
    sums = [copies(qkv_low, qkv_in, to_next), copies(out_low, out_in, to_next)]
    for came, all_ref in zip(across, (gate_all, up_all, down_all)):
        came.wait_recv()
        beside.append(copies(all_ref.at[next_], all_ref.at[next_], to_mate))
    sums[0].wait_recv()
    qkv_all[core] = qkv_sum[...] + qkv_in[...].astype(F32)
    sums[1].wait_recv()
    out_all[core] = out_sum[...] + out_in[...].astype(F32)
    beside += [copies(ref.at[core], ref.at[core], to_mate) for ref in (qkv_all, out_all)]
    for each in beside:
        each.wait_recv()
    for each in [out_sent, qkv_sent] + across + beside + sums:
        each.wait_send()


def tail(*operands):
    return pl.pallas_call(
        tail_kernel,
        out_shape=(
            shaped(ROWS, D),
            shaped(4, 56, QUARTER),
            shaped(4, 56, QUARTER),
            shaped(4, DOWN_ROWS, D),
            shaped(2, 32, QKV, dtype=F32),
            shaped(2, 32, D, dtype=F32),
        ),
        scratch_shapes=[pltpu.VMEM(each.shape, each.dtype) for each in ATTENTION_BACKWARD_OUT]
        + ATTENTION_BACKWARD_SCRATCH
        + REAR_SCRATCH
        + TAIL_SCRATCH
        + scatter_scratch(*MLP_SUMS_SHAPES)
        + scatter_scratch((16, QKV), (16, QKV), (16, D), (16, D))
        + [
            pltpu.SemaphoreType.DMA((TAIL_COPIES,)),
            pltpu.SemaphoreType.DMA((TAIL_COPIES,)),
            pltpu.SemaphoreType.DMA((3,)),
        ],
        compiler_params=params(1),
        name="tail",
    )(*operands)


def rotary(group):
    lane = np.arange(KV)
    frequency = jnp.asarray(THETA ** (-(lane % HALF) * 2.0 / (2 * HALF)), F32)
    sign = jnp.asarray(np.where(lane % (2 * HALF) < HALF, -1.0, 1.0), F32)
    row = lax.broadcasted_iota(jnp.int32, (ROWS, KV), 0)
    positions = group * 64 + lax.rem(row, 64) + SPAN * (row // 64)
    angles = positions.astype(F32) * frequency[None, :]
    return jnp.cos(angles), jnp.sin(angles) * sign[None, :]


def body(inputs, cotangent, segments, w_qkv, b_qkv, w_out, w_gate, w_up, w_down, g_attn, g_mlp):
    group = lax.axis_index("group")
    replica = lax.axis_index("replica")
    core = lax.rem(replica, 2)

    down_piece = lax.dynamic_slice(w_down[0], (jnp.minimum(80 * replica, 224), 0), (DOWN_ROWS, D))
    gate_piece = lax.dynamic_slice(w_gate[0], (0, replica * QUARTER), (D // 16, QUARTER))
    up_piece = lax.dynamic_slice(w_up[0], (0, replica * QUARTER), (D // 16, QUARTER))
    small = jnp.concatenate([b_qkv[0], g_attn[0], g_mlp[0]])
    small = jnp.pad(small[None], ((0, 7), (0, QKV - small.shape[0])))
    qkv_piece = lax.dynamic_slice(jnp.concatenate([w_qkv[0], small], axis=0), (32 * core, 0), (32, QKV))
    out_piece = lax.dynamic_slice(jnp.pad(w_out[0], ((0, 8), (0, 0))), (32 * core, 0), (32, D))

    cosine, sine = rotary(group)
    kseg = segments
    x_in = inputs[0].reshape(ROWS, D)
    cotangent_in = cotangent[0].reshape(ROWS, D)
    gate_w, up_w, down_w, qkv_w, out_w, bias, gain1, gain2, hidden, normed2 = first(
        gate_piece, up_piece, down_piece, qkv_piece, out_piece, x_in, cosine, sine, kseg
    )
    gate_w = gate_w.reshape(D, QUARTER)
    up_w = up_w.reshape(D, QUARTER)

    def forward(x):
        normed, q, kv = front(x, qkv_w, bias, gain1, cosine, sine)
        context, hidden, normed2 = attention(x, q, kv, kseg, out_w, gain2)
        output, normed2_all, gate, up = mlp_forward(normed2, hidden, gate_w, up_w, down_w)
        return output, (x, normed, q, kv, context, hidden, normed2_all, gate, up)

    def backward_start(dout):
        dnormed2, *grads = mlp_backward(dout, gate, up, gate_w, up_w, down_w)
        dout_all, dgate, dup, product = grads
        return (dout, dnormed2, hidden, gain2, out_w, q, kv, kseg), (normed2_all, dgate, dup, product, dout_all)

    output, kept = forward(mlp_relay(normed2, hidden, x_in, gate_w, up_w, down_w))
    x, normed, q, kv, context, hidden, normed2_all, gate, up = kept
    operands, _ = backward_start(cotangent_in)
    dhidden, _, dq, dkv, _ = attention_backward(*operands)
    dout = rear(dkv, dq, cosine, sine, qkv_w, x, gain1, dhidden, cotangent_in)
    operands, mlp_operands = backward_start(dout)
    dinput, *parts = tail(*operands, *mlp_operands, cosine, sine, qkv_w, x, gain1, normed, context)
    grad_gate, grad_up, grad_down, grad_qkv, grad_out, bias, value_bias, gain1, gain2 = outputs(*parts)
    return (
        output.reshape(1, 1, 2, 64, D),
        dinput.reshape(1, 1, 2, 64, D),
        grad_qkv[None],
        bias,
        value_bias,
        grad_out[None],
        grad_gate[None],
        grad_up[None],
        grad_down[None],
        gain1,
        gain2,
    )


def solution(mesh):
    in_specs = (
        P("replica", None, "group", None),
        P("replica", None, "group", None),
        P("replica", None),
        P("section", "group", None),
        P("section", "group"),
        P("section", "group", None),
        P("section", "group", None),
        P("section", "group", None),
        P("section", "group", None),
        P("section", "group"),
        P("section", "group"),
    )
    out_specs = (
        P("section", "replica", None, "group", None),
        P("section", "replica", None, "group", None),
        P("section", "group", None),
        P("section", "group"),
        P("section", "group"),
        P("section", "group", None),
        P("section", "group", None),
        P("section", "group", None),
        P("section", "group", None),
        P("section", "group"),
        P("section", "group"),
    )
    return jax.shard_map(body, mesh=mesh, in_specs=in_specs, out_specs=out_specs, check_vma=False)
```

```python
import functools

import jax
import jax.numpy as jnp
import numpy as np
from jax import lax
from jax.experimental import pallas as pl
from jax.experimental.pallas import tpu as pltpu
from jax.sharding import PartitionSpec as P

D = 896
HEADS = 14
KV = 128
HALF = 32
FF = 4864
QUARTER = FF // 4
QKV = 1152
ROWS = 128
SPAN = 1024
LEN = 2048
PAIRS = 7
EPSILON = 1e-06
THETA = 1000000.0
NEGATIVE = -1e30
SCALE = 0.125
VMEM_LIMIT = 60 * 1024 * 1024
MESH = pl.DeviceIdType.MESH
BF = jnp.bfloat16
F32 = jnp.float32
VMEM_SPEC = pl.BlockSpec(memory_space=pltpu.VMEM)
ANY_SPEC = pl.BlockSpec(memory_space=pl.ANY)


def nn(a, b):
    return lax.dot_general(a, b, (((1,), (0,)), ((), ())), preferred_element_type=F32)


def nt(a, b):
    return lax.dot_general(a, b, (((1,), (1,)), ((), ())), preferred_element_type=F32)


def tn(a, b):
    return lax.dot_general(a, b, (((0,), (0,)), ((), ())), preferred_element_type=F32)


def params(collective_id=None):
    if collective_id is None:
        return pltpu.CompilerParams(vmem_limit_bytes=VMEM_LIMIT)
    return pltpu.CompilerParams(
        vmem_limit_bytes=VMEM_LIMIT, collective_id=collective_id, has_side_effects=True
    )


def shaped(*shape, dtype=BF):
    return jax.ShapeDtypeStruct(shape, dtype)


def local_call(kernel, name, out_shape, scratch=()):
    return pl.pallas_call(
        kernel,
        out_shape=out_shape,
        scratch_shapes=list(scratch),
        compiler_params=params(),
        name=name,
    )


def signal(devices):
    barrier = pltpu.get_barrier_semaphore()
    for device in devices:
        pl.semaphore_signal(barrier, inc=1, device_id=device, device_id_type=MESH)


def greeted(count):
    pl.semaphore_wait(pltpu.get_barrier_semaphore(), count)


def grid_place():
    me = lax.axis_index("group")
    z = me // 4
    y = lax.rem(me, 4)

    def along_y(step):
        return {"group": z * 4 + lax.rem(y + step, 4)}

    def along_z(step):
        return {"group": lax.rem(z + step, 4) * 4 + y}

    return z, y, along_y, along_z


def neighbours(along_y, along_z):
    return [along(step) for along in (along_y, along_z) for step in (1, 3, 2)]


class Copies:
    def __init__(self, send, recv):
        self.send, self.recv, self.used = send, recv, 0

    def __call__(self, src, dst, device, start=True):
        index = self.used
        self.used += 1
        each = pltpu.make_async_remote_copy(
            src_ref=src,
            dst_ref=dst,
            send_sem=self.send.at[index],
            recv_sem=self.recv.at[index],
            device_id=device,
            device_id_type=MESH,
        )
        if start:
            each.start()
        return each


def gather_phase(firsts, seconds, place, device_at, copies):
    def copy(block, slot, step):
        return copies(block(slot), block(slot), device_at(step), False)

    firsts_right = [copy(block, place, 1) for block in firsts]
    seconds_left = [copy(block, place, 3) for block in seconds]
    others = [copy(block, place, 3) for block in firsts] + [copy(block, place, 1) for block in seconds]
    relays = [copy(block, lax.rem(place + 3, 4), 1) for block in firsts]
    relays += [copy(block, lax.rem(place + 1, 4), 3) for block in seconds]

    def start():
        for each in firsts_right + seconds_left + others:
            each.start()

    def relay():
        for came, each in zip(firsts_right + seconds_left, relays):
            came.wait_recv()
            each.start()

    def finish():
        for each in others + relays:
            each.wait_recv()
        for each in firsts_right + seconds_left + others + relays:
            each.wait_send()

    return start, relay, finish


def gather_direct(firsts, seconds, place, device_at, copies):
    sent = []
    for block in firsts + seconds:
        sent += [copies(block(place), block(place), device_at(step), False) for step in (1, 3, 2)]

    def start():
        for each in sent:
            each.start()

    def finish():
        for each in sent:
            each.wait_recv()
        for each in sent:
            each.wait_send()

    return start, lambda: None, finish


def gather_both(first_a, second_a, first_b, second_b, copies, phase=gather_phase, then=gather_phase):
    z, y, along_y, along_z = grid_place()
    start_a, relay_a, finish_a = phase([first_a[0]], [second_a[0]], y, along_y, copies)
    start_b, relay_b, finish_b = phase([first_b[0]], [second_b[0]], z, along_z, copies)
    then_a, last_a, end_a = then([first_a[1]], [second_a[1]], z, along_z, copies)
    then_b, last_b, end_b = then([first_b[1]], [second_b[1]], y, along_y, copies)
    start_a()
    start_b()
    yield
    relay_a()
    relay_b()
    yield
    finish_a()
    then_a()
    finish_b()
    then_b()
    yield
    last_a()
    last_b()
    yield
    end_a()
    end_b()


def gather_split(first_a, second_a, first_b, second_b, copies):
    z, y, along_y, along_z = grid_place()
    slim = [
        gather_phase([first_a[0]], [second_a[0]], y, along_y, copies),
        gather_phase([first_b[0]], [second_b[0]], z, along_z, copies),
    ]

    def wide(half):
        def part(function):
            return [lambda at: function(at, half)]

        return [
            gather_phase(part(first_a[1]), part(second_a[1]), z, along_z, copies),
            gather_phase(part(first_b[1]), part(second_b[1]), y, along_y, copies),
        ]

    halves = [wide(slice(0, 2)), wide(slice(2, 4))]
    for start, _, _ in slim:
        start()
    yield
    for _, relay, _ in slim:
        relay()
    yield
    for _, _, finish in slim:
        finish()
    for phases in halves:
        for start, _, _ in phases:
            start()
        yield
        for _, relay, _ in phases:
            relay()
        yield
    for phases in halves:
        for _, _, finish in phases:
            finish()


def run(steps):
    for _ in steps:
        pass


def y_then_z(ref, *tail):
    z = lax.axis_index("group") // 4
    return (lambda at: ref.at[(z, at, *tail)]), (lambda at, part=slice(None): ref.at[(at, part, *tail)])


def z_then_y(ref, *tail):
    y = lax.rem(lax.axis_index("group"), 4)
    return (lambda at: ref.at[(at, y, *tail)]), (lambda at, part=slice(None): ref.at[(part, at, *tail)])


def quarter_route():
    group, replica = lax.axis_index("group"), lax.axis_index("replica")
    target = {"group": 4 * lax.rem(group, 4) + replica, "replica": group // 4}
    source = {"group": 4 * replica + group // 4, "replica": lax.rem(group, 4)}
    stays = (target["group"] == group) & (target["replica"] == replica)
    return target, source, stays


def first_kernel(
    gate, up, down, qkv, out, x_ref, cos_ref, sin_ref, kseg_ref,
    gate_all, up_all, down_all, qkv_w, out_w, bias_ref, gain1_ref, gain2_ref, hidden_ref, normed2_ref,
    qkv_all, out_all, normed_ref, q_ref, kv_ref, context_ref, keys_ref, values_ref, bias0, bias1, send, recv, local
):
    z, y, along_y, along_z = grid_place()
    core = lax.rem(lax.axis_index("replica"), 2)
    mate = {"replica": lax.axis_index("replica") + 1 - 2 * core}
    target, source, stays = quarter_route()
    moves = jnp.logical_not(stays)
    signal(neighbours(along_y, along_z) + [mate])
    places = (qkv_all.at[core, z, y], out_all.at[core, z, y], gate_all.at[z, y], up_all.at[z, y])
    own = []
    for index, (src, dst) in enumerate(zip((qkv, out, gate, up), places)):
        own.append(pltpu.make_async_copy(src, dst, local.at[index]))
        own[-1].start()
    there = target["group"]
    moved = pltpu.make_async_remote_copy(
        src_ref=down,
        dst_ref=down_all.at[there // 4, lax.rem(there, 4)],
        send_sem=local.at[5],
        recv_sem=local.at[6],
        device_id=target,
        device_id_type=MESH,
    )
    stayed = pltpu.make_async_copy(down, down_all.at[z, y], local.at[4])

    @pl.when(moves)
    def _():
        signal([source])
        greeted(8)
        moved.start()

    @pl.when(stays)
    def _():
        greeted(7)
        stayed.start()

    copies = Copies(send, recv)
    own[0].wait()
    own[1].wait()
    top, bottom = (slice(0, 16), slice(None)), (slice(16, 32), slice(None))
    dense = gather_both(
        y_then_z(qkv_all.at[core], *top),
        y_then_z(qkv_all.at[core], *bottom),
        z_then_y(out_all.at[core], *top),
        z_then_y(out_all.at[core], *bottom),
        copies,
        gather_direct,
    )
    next(dense)
    next(dense)
    next(dense)
    own[2].wait()
    own[3].wait()

    @pl.when(moves)
    def _():
        moved.wait()

    @pl.when(stays)
    def _():
        stayed.wait()

    left, right = (slice(None), slice(0, 512)), (slice(None), slice(512, D))
    wide = gather_split(
        y_then_z(gate_all), y_then_z(down_all, *left), z_then_y(up_all), z_then_y(down_all, *right), copies
    )
    next(wide)
    next(dense)
    next(wide)
    run(dense)
    halves = [copies(ref.at[core], ref.at[core], mate) for ref in (qkv_all, out_all)]
    next(wide)
    for each in halves:
        each.wait()
    for at in range(16):
        rows, cut = 56 * at, 56 * at + 32
        qkv_w[rows:cut] = qkv_all[0, at // 4, at % 4]
        qkv_w[cut : rows + 56] = qkv_all[1, at // 4, at % 4, :24]
        out_w[rows:cut] = out_all[0, at // 4, at % 4]
        out_w[cut : rows + 56] = out_all[1, at // 4, at % 4, :24]
    small = [qkv_all[1, at // 4, at % 4, 24:32].astype(F32)[:1] for at in range(16)]
    bias_ref[...] = jnp.concatenate([each[:, :72] for each in small], axis=1)
    gain1_ref[...] = jnp.concatenate([each[:, 72:128] for each in small], axis=1)
    gain2_ref[...] = jnp.concatenate([each[:, 128:184] for each in small], axis=1)
    kv = front_work(x_ref, qkv_w, bias_ref, gain1_ref, cos_ref, sin_ref, normed_ref, q_ref, kv_ref, copies, None)
    next(kv)
    next(wide)
    next(kv)
    next(kv)
    next(wide)
    run(kv)
    attention_work(
        x_ref, q_ref, kv_ref, kseg_ref, out_w, gain2_ref, context_ref, hidden_ref, normed2_ref,
        keys_ref, values_ref, bias0, bias1, (4, lambda: next(wide))
    )
    run(wide)


def first(gate, up, down, qkv, out, x, cosine, sine, kseg):
    return pl.pallas_call(
        first_kernel,
        out_shape=(
            shaped(4, 4, *gate.shape),
            shaped(4, 4, *up.shape),
            shaped(4, 4, *down.shape),
            shaped(D, QKV),
            shaped(D, D),
            shaped(1, QKV, dtype=F32),
            shaped(1, D, dtype=F32),
            shaped(1, D, dtype=F32),
            shaped(ROWS, D, dtype=F32),
            shaped(ROWS, D),
        ),
        in_specs=[ANY_SPEC] * 5 + [VMEM_SPEC] * 4,
        out_specs=[ANY_SPEC] * 3 + [VMEM_SPEC] * 7,
        scratch_shapes=[
            pltpu.VMEM((2, 4, 4, *qkv.shape), BF),
            pltpu.VMEM((2, 4, 4, *out.shape), BF),
            pltpu.VMEM((ROWS, D), BF),
            pltpu.VMEM((ROWS, D), BF),
            pltpu.VMEM((2, 4, 4, 64, 2 * KV), BF),
            pltpu.VMEM((ROWS, D), BF),
        ]
        + ATTENTION_SCRATCH
        + [
            pltpu.SemaphoreType.DMA((86,)),
            pltpu.SemaphoreType.DMA((86,)),
            pltpu.SemaphoreType.DMA((7,)),
        ],
        compiler_params=params(0),
        name="first",
    )(gate, up, down, qkv, out, x, cosine, sine, kseg)


def scatter_phase(firsts, seconds, place, device_at, copies):
    right, left, far = (lax.rem(place + step, 4) for step in (1, 3, 2))

    def load(ref):
        return ref[...].astype(F32)

    def copy(src, dst, step):
        return copies(src, dst, device_at(step), False)

    first_far = [copy(block(far), bufs[0], 1) for block, bufs, put in firsts]
    second_far = [copy(block(far), bufs[0], 3) for block, bufs, put in seconds]
    first_near = [copy(block(left), bufs[2], 3) for block, bufs, put in firsts]
    second_near = [copy(block(right), bufs[1], 1) for block, bufs, put in seconds]
    first_sum = [copy(bufs[0], bufs[1], 1) for block, bufs, put in firsts]
    second_sum = [copy(bufs[0], bufs[2], 3) for block, bufs, put in seconds]

    def start(which=(0, 1)):
        for index in which:
            for each in ((first_far + first_near), (second_far + second_near))[index]:
                each.start()

    def pass_on():
        for came, each, (block, bufs, put) in zip(first_far, first_sum, firsts):
            came.wait_recv()
            bufs[0][...] = (load(block(right)) + load(bufs[0])).astype(BF)
            each.start()
        for came, each, (block, bufs, put) in zip(second_far, second_sum, seconds):
            came.wait_recv()
            bufs[0][...] = (load(block(left)) + load(bufs[0])).astype(BF)
            each.start()

    def finish():
        near, far_sum = first_near + second_near, first_sum + second_sum
        for one, two, (block, bufs, put) in zip(near, far_sum, firsts + seconds):
            one.wait_recv()
            two.wait_recv()
            put(load(block(place)) + load(bufs[1]) + load(bufs[2]))
        for each in first_far + second_far + near + far_sum:
            each.wait_send()

    return start, pass_on, finish


def scatter_direct(firsts, seconds, place, device_at, copies):
    parts = firsts + seconds
    sent = []
    for block, bufs, put in parts:
        sent.append(
            [
                copies(block(lax.rem(place + step, 4)), bufs[index], device_at(step), False)
                for index, step in enumerate((1, 3, 2))
            ]
        )

    def start():
        for each in sum(sent, []):
            each.start()

    def finish():
        for came, (block, bufs, put) in zip(sent, parts):
            total = block(place)[...].astype(F32)
            for each, landed in zip(came, bufs):
                each.wait_recv()
                total = total + landed[...].astype(F32)
            for each in came:
                each.wait_send()
            put(total)

    return start, lambda: None, finish


def scatter_both(first_a, second_a, first_b, second_b, copies, phase=scatter_phase):
    z, y, along_y, along_z = grid_place()

    def wide(part):
        block, bufs, _, _ = part
        return [(block, bufs, stored_in(bufs[1]))]

    def slim(part):
        _, kept, bufs, put = part
        return [((lambda at: kept[1].at[at]), bufs, put)]

    start_a, pass_a, finish_a = phase(wide(first_a), wide(second_a), y, along_y, copies)
    start_b, pass_b, finish_b = phase(wide(first_b), wide(second_b), z, along_z, copies)
    then_a, last_a, end_a = phase(slim(first_a), slim(second_a), z, along_z, copies)
    then_b, last_b, end_b = phase(slim(first_b), slim(second_b), y, along_y, copies)
    start_a()
    start_b()
    yield
    pass_a()
    pass_b()
    yield
    finish_a()
    then_a()
    finish_b()
    then_b()
    yield
    last_a()
    last_b()
    yield
    end_a()
    end_b()


def scatter_split(first_a, second_a, first_b, second_b, copies):
    z, y, along_y, along_z = grid_place()

    def slim(part):
        _, kept, bufs, put = part
        return [((lambda at: kept[1].at[at]), bufs, put)]

    def halved(half):
        def wide(part):
            block, bufs, _, _ = part
            views = [each.at[half] for each in bufs]
            return [(lambda at: block(at, half), views, stored_in(views[1]))]

        return [
            scatter_phase(wide(first_a), wide(second_a), y, along_y, copies),
            scatter_phase(wide(first_b), wide(second_b), z, along_z, copies),
        ]

    halves = [halved(pl.ds(0, 2)), halved(pl.ds(2, 2))]
    last_phases = [
        scatter_phase(slim(first_a), slim(second_a), z, along_z, copies),
        scatter_phase(slim(first_b), slim(second_b), y, along_y, copies),
    ]
    for start, _, _ in halves[0]:
        start([0])
        yield
    for start, _, _ in halves[0]:
        start([1])
    yield
    for _, pass_on, _ in halves[0]:
        pass_on()
    for start, _, _ in halves[1]:
        start()
    yield
    for _, pass_on, _ in halves[1]:
        pass_on()
    yield
    for phases in halves:
        for _, _, finish in phases:
            finish()
    for start, _, _ in last_phases:
        start()
    yield
    for _, pass_on, _ in last_phases:
        pass_on()
    yield
    for _, _, finish in last_phases:
        finish()


def scatter_scratch(*shapes):
    scratch = []
    for shape in shapes:
        scratch += [pltpu.VMEM((4, *shape), BF)] * 3 + [pltpu.VMEM(shape, BF)] * 3
    return scratch


def scatter_part(scratch, index, block, put):
    mine = scratch[6 * index : 6 * index + 6]
    return block, mine[:3], mine[3:], put


def stored_in(ref, *at):
    def put(value):
        ref[at if at else ...] = value.astype(ref.dtype)

    return put


DOWN_STARTS = (0, 80, 160, 224)
DOWN_ROWS = 80


def flat(ref):
    return ref[...].reshape(4 * ROWS, ref.shape[-1])


def wide_terms(rows_ref, grads_ref, terms):
    whole = tn(flat(rows_ref), flat(grads_ref))
    for at in range(16):
        terms[at // 4, at % 4] = whole[56 * at : 56 * at + 56].astype(BF)


def down_rows_terms(product_ref, dout_ref, terms):
    whole = tn(flat(product_ref), flat(dout_ref)).astype(BF)
    for at in range(16):
        start = 304 * (at // 4) + DOWN_STARTS[at % 4]
        terms[at // 4, at % 4] = whole[start : start + DOWN_ROWS]


def mlp_sums(gate_terms, up_terms, down_terms, gate_out, up_out, down_out, scratch, copies):
    left, right = slice(0, 512), slice(512, D)
    return scatter_split(
        scatter_part(scratch, 0, lambda at, part: gate_terms.at[part, at], stored_in(gate_out)),
        scatter_part(
            scratch, 2, lambda at, part: down_terms.at[part, at, :, left], stored_in(down_out, slice(None), left)
        ),
        scatter_part(scratch, 1, lambda at, part: up_terms.at[at, part], stored_in(up_out)),
        scatter_part(
            scratch, 3, lambda at, part: down_terms.at[at, part, :, right], stored_in(down_out, slice(None), right)
        ),
        copies,
    )


MLP_SUMS_SHAPES = ((56, QUARTER), (56, QUARTER), (DOWN_ROWS, 512), (DOWN_ROWS, D - 512))


def half_sums(half, to, cut, scratch, copies):
    top, bottom = slice(0, 16), slice(16, 32)
    left, right = slice(0, cut), slice(cut, to.shape[1])
    return scatter_both(
        scatter_part(scratch, 0, lambda at: half.at[:, at, top, left], stored_in(to, top, left)),
        scatter_part(scratch, 1, lambda at: half.at[:, at, bottom, left], stored_in(to, bottom, left)),
        scatter_part(scratch, 2, lambda at: half.at[at, :, top, right], stored_in(to, top, right)),
        scatter_part(scratch, 3, lambda at: half.at[at, :, bottom, right], stored_in(to, bottom, right)),
        copies,
        scatter_direct,
    )


def kv_sums(dkv_ref, total, scratch, copies):
    top, bottom = slice(0, 32), slice(32, 64)
    return scatter_both(
        scatter_part(scratch, 0, lambda at: dkv_ref.at[0, :, at, top], stored_in(total, slice(0, 32))),
        scatter_part(scratch, 1, lambda at: dkv_ref.at[0, :, at, bottom], stored_in(total, slice(32, 64))),
        scatter_part(scratch, 2, lambda at: dkv_ref.at[1, at, :, top], stored_in(total, slice(64, 96))),
        scatter_part(scratch, 3, lambda at: dkv_ref.at[1, at, :, bottom], stored_in(total, slice(96, 128))),
        copies,
        scatter_direct,
    )


def replica_partners():
    me = lax.axis_index("replica")
    return me, me + 1 - 2 * lax.rem(me, 2), lax.rem(me + 2, 4), 3 - me


def other_section():
    return {"section": 1 - lax.axis_index("section")}


def exchange(
    own_ref, all_ref, total_ref, near_terms, part, far_part, near_sum, part_in, far_in, near_in, copies, loads, work, greetings=2
):
    me, mate, next_, far = replica_partners()
    halves = (slice(0, 64), slice(64, 128))
    to_mate, to_next = {"replica": mate}, {"replica": next_}
    greeted(greetings)
    across = [copies(own_ref.at[half], all_ref.at[me, half], to_next) for half in halves]
    beside = copies(own_ref, all_ref.at[me], to_mate)
    forwards = [copies(all_ref.at[next_, half], all_ref.at[next_, half], to_mate, False) for half in halves]
    passed = [copies(far_part.at[index], far_in.at[index], to_mate, False) for index in (0, 1)]
    sums = [copies(near_sum.at[index], near_in.at[index], to_next, False) for index in (0, 1)]
    sent = copies(part, part_in, to_mate, False)
    all_ref[me] = own_ref[...]
    for each in loads:
        each.wait()

    def send_sum(index):
        passed[index].wait_recv()
        near_sum[index] = (near_terms[index] + far_in[index].astype(F32)).astype(BF)
        sums[index].start()

    def step(at, carry):
        one = jnp.where(at == 0, me, jnp.where(at == 3, mate, next_))
        two = jnp.where(at == 0, me, jnp.where(at == 3, mate, far))
        first_rows = pl.ds(pl.multiple_of(jnp.where(at == 2, 64, 0), 64), 64)
        second_rows = pl.ds(pl.multiple_of(jnp.where(at == 1, 0, 64), 64), 64)

        @pl.when(at == 1)
        def _():
            across[0].wait_recv()
            forwards[0].start()
            forwards[0].wait_recv()

        @pl.when(at == 2)
        def _():
            across[1].wait_recv()
            forwards[1].start()
            send_sum(0)
            forwards[1].wait_recv()

        @pl.when(at == 3)
        def _():
            send_sum(1)
            beside.wait_recv()

        terms = work([(one, first_rows), (two, second_rows)])

        @pl.when(at == 0)
        def _():
            total_ref[...] = terms

        for index in (0, 1):

            @pl.when(at == 1 + index)
            def _(index=index):
                near_terms[index] = terms[:64]
                far_part[index] = terms[64:].astype(BF)
                passed[index].start()

        @pl.when(at == 3)
        def _():
            part[...] = terms.astype(BF)
            sent.start()

        return carry

    lax.fori_loop(0, 4, step, 0)
    sent.wait_recv()
    total = total_ref[...] + part_in[...].astype(F32)
    for each in sums:
        each.wait_recv()
    total = total + near_in[...].reshape(ROWS, D).astype(F32)
    for each in across + [beside, sent] + forwards + passed + sums:
        each.wait_send()
    return total


EXCHANGE_SCRATCH = [
    pltpu.VMEM((D, QUARTER), BF),
    pltpu.VMEM((D, QUARTER), BF),
    pltpu.VMEM((QUARTER, D), BF),
    pltpu.VMEM((ROWS, D), F32),
    pltpu.VMEM((2, 64, D), F32),
    pltpu.VMEM((ROWS, D), BF),
    pltpu.VMEM((2, 64, D), BF),
    pltpu.VMEM((2, 64, D), BF),
    pltpu.VMEM((ROWS, D), BF),
    pltpu.VMEM((2, 64, D), BF),
    pltpu.VMEM((2, 64, D), BF),
    pltpu.SemaphoreType.DMA((11,)),
    pltpu.SemaphoreType.DMA((11,)),
    pltpu.SemaphoreType.DMA((18,)),
]


def mlp_start(hbm, vmem, local):
    me, mate, next_, far = replica_partners()
    signal([{"replica": mate}, {"replica": next_}])
    loads = [pltpu.make_async_copy(src, dst, local.at[i]) for i, (src, dst) in enumerate(zip(hbm[:2], vmem[:2]))]
    for at in range(16):
        skip = 80 * (at % 4) - DOWN_STARTS[at % 4]
        rows = pl.ds(304 * (at // 4) + 80 * (at % 4), DOWN_ROWS - skip)
        piece = hbm[2].at[at // 4, at % 4, pl.ds(skip, DOWN_ROWS - skip)]
        loads.append(pltpu.make_async_copy(piece, vmem[2].at[rows], local.at[2 + at]))
    for each in loads:
        each.start()
    return loads


def split_rows(value, parts):
    for index, (source, rows) in enumerate(parts):
        yield source, rows, value[64 * index : 64 * index + 64]


def mlp_forward_kernel(
    normed_ref, hidden_ref, gate_hbm, up_hbm, down_hbm, out_ref, all_ref, gate_ref, up_ref,
    gate_w, up_w, down_w, total_ref, near_terms, part, far_part, near_sum, part_in, far_in, near_in, send, recv, local
):
    loads = mlp_start((gate_hbm, up_hbm, down_hbm), (gate_w, up_w, down_w), local)

    def work(parts):
        rows = jnp.concatenate([all_ref[source, rows] for source, rows in parts], axis=0)
        gate = nn(rows, gate_w[...])
        up = nn(rows, up_w[...])
        for source, at, value in split_rows(gate, parts):
            gate_ref[source, at] = value.astype(BF)
        for source, at, value in split_rows(up, parts):
            up_ref[source, at] = value.astype(BF)
        product = (gate * jax.nn.sigmoid(gate) * up).astype(BF)
        return nn(product, down_w[...])

    total = exchange(
        normed_ref, all_ref, total_ref, near_terms, part, far_part, near_sum, part_in, far_in, near_in,
        Copies(send, recv), loads, work
    )
    out_ref[...] = (hidden_ref[...] + total).astype(BF)


def mlp_relay_kernel(
    normed_ref, hidden_ref, x_ref, gate_hbm, up_hbm, down_hbm, next_ref, all_ref, out_ref, relayed_ref,
    gate_w, up_w, down_w, total_ref, near_terms, part, far_part, near_sum, part_in, far_in, near_in, send, recv, local
):
    signal([other_section()])
    loads = mlp_start((gate_hbm, up_hbm, down_hbm), (gate_w, up_w, down_w), local)

    def work(parts):
        rows = jnp.concatenate([all_ref[source, rows] for source, rows in parts], axis=0)
        gate = nn(rows, gate_w[...])
        up = nn(rows, up_w[...])
        product = (gate * jax.nn.sigmoid(gate) * up).astype(BF)
        return nn(product, down_w[...])

    copies = Copies(send, recv)
    total = exchange(
        normed_ref, all_ref, total_ref, near_terms, part, far_part, near_sum, part_in, far_in, near_in,
        copies, loads, work, 3
    )
    out_ref[...] = (hidden_ref[...] + total).astype(BF)
    relay = copies(out_ref, relayed_ref, other_section(), False)

    @pl.when(lax.axis_index("section") == 0)
    def _():
        relay.start()
        next_ref[...] = x_ref[...]
        relay.wait_send()

    @pl.when(lax.axis_index("section") == 1)
    def _():
        relay.wait_recv()
        next_ref[...] = relayed_ref[...]


def mlp_relay(normed2, hidden, x, gate_w, up_w, down_w):
    return pl.pallas_call(
        mlp_relay_kernel,
        out_shape=shaped(ROWS, D),
        in_specs=[VMEM_SPEC] * 3 + [ANY_SPEC] * 3,
        scratch_shapes=[pltpu.VMEM((4, ROWS, D), BF), pltpu.VMEM((ROWS, D), BF), pltpu.VMEM((ROWS, D), BF)]
        + EXCHANGE_SCRATCH,
        compiler_params=params(2),
        name="mlp_relay",
    )(normed2, hidden, x, gate_w, up_w, down_w)


def mlp_forward(normed2, hidden, gate_w, up_w, down_w):
    return pl.pallas_call(
        mlp_forward_kernel,
        out_shape=(
            shaped(ROWS, D),
            shaped(4, ROWS, D),
            shaped(4, ROWS, QUARTER),
            shaped(4, ROWS, QUARTER),
        ),
        in_specs=[VMEM_SPEC] * 2 + [ANY_SPEC] * 3,
        scratch_shapes=EXCHANGE_SCRATCH,
        compiler_params=params(3),
        name="mlp_forward",
    )(normed2, hidden, gate_w, up_w, down_w)


def mlp_backward_kernel(
    dout_ref, gate_ref, up_ref, gate_hbm, up_hbm, down_hbm,
    dnormed_ref, all_ref, dgate_ref, dup_ref, product_ref,
    gate_w, up_w, down_w, total_ref, near_terms, part, far_part, near_sum, part_in, far_in, near_in, send, recv, local
):
    loads = mlp_start((gate_hbm, up_hbm, down_hbm), (gate_w, up_w, down_w), local)

    def work(parts):

        def stacked(ref):
            return jnp.concatenate([ref[source, rows] for source, rows in parts], axis=0)

        dproduct = nt(stacked(all_ref), down_w[...])
        gate = stacked(gate_ref).astype(F32)
        up = stacked(up_ref).astype(F32)
        s = jax.nn.sigmoid(gate)
        silu = gate * s
        product = (silu * up).astype(BF)
        dgate = (dproduct * up * (s * (1.0 + gate * (1.0 - s)))).astype(BF)
        dup = (dproduct * silu).astype(BF)
        for to, whole in ((product_ref, product), (dgate_ref, dgate), (dup_ref, dup)):
            for source, at, value in split_rows(whole, parts):
                to[source, at] = value
        return nt(dgate, gate_w[...]) + nt(dup, up_w[...])

    dnormed_ref[...] = exchange(
        dout_ref, all_ref, total_ref, near_terms, part, far_part, near_sum, part_in, far_in, near_in,
        Copies(send, recv), loads, work
    )


def mlp_backward(dout, gate, up, gate_w, up_w, down_w):
    return pl.pallas_call(
        mlp_backward_kernel,
        out_shape=(
            shaped(ROWS, D, dtype=F32),
            shaped(4, ROWS, D),
            shaped(4, ROWS, QUARTER),
            shaped(4, ROWS, QUARTER),
            shaped(4, ROWS, QUARTER),
        ),
        in_specs=[VMEM_SPEC] * 3 + [ANY_SPEC] * 3,
        scratch_shapes=EXCHANGE_SCRATCH,
        compiler_params=params(4),
        name="mlp_backward",
    )(dout, gate, up, gate_w, up_w, down_w)


def outputs_kernel(
    gate, up, down, qkv, out, gate_out, up_out, down_out, qkv_out, out_out, bias_out, value_out, gain1_out, gain2_out
):
    for r in range(4):
        lanes = slice(QUARTER * r, QUARTER * r + QUARTER)
        gate_out[:, lanes] = gate[r].astype(F32)
        up_out[:, lanes] = up[r].astype(F32)
        skip = 80 * r - DOWN_STARTS[r]
        down_out[80 * r : DOWN_STARTS[r] + DOWN_ROWS] = down[r, skip:].astype(F32)
    qkv_out[:32] = qkv[0]
    qkv_out[32:] = qkv[1, :24]
    out_out[:32] = out[0]
    out_out[32:] = out[1, :24]
    small = qkv[1, 24:][:1]
    bias_out[...] = small[:, :64]
    value_out[...] = small[:, 64:72]
    gain1_out[...] = small[:, 72:128]
    gain2_out[...] = small[:, 128:184]


def outputs(gate, up, down, qkv, out):
    return local_call(
        outputs_kernel,
        "outputs",
        (
            shaped(56, FF, dtype=F32),
            shaped(56, FF, dtype=F32),
            shaped(FF // 16, D, dtype=F32),
            shaped(56, QKV, dtype=F32),
            shaped(56, D, dtype=F32),
            shaped(1, 64, dtype=F32),
            shaped(1, 8, dtype=F32),
            shaped(1, 56, dtype=F32),
            shaped(1, 56, dtype=F32),
        ),
    )(gate, up, down, qkv, out)


def turn(values, cosine, sine, sign):
    width = values.shape[1]
    up = pltpu.roll(values, width - HALF, 1)
    down = pltpu.roll(values, HALF, 1)
    lane = lax.broadcasted_iota(jnp.int32, values.shape, 1)
    swapped = jnp.where(lax.rem(lane, 2 * HALF) < HALF, up, down)
    repeat = width // KV
    cosine = jnp.concatenate([cosine] * repeat, axis=1)
    sine = jnp.concatenate([sine] * repeat, axis=1)
    return values * cosine + sign * (swapped * sine)


def front_work(x_ref, w_ref, b_ref, g_ref, cos_ref, sin_ref, normed_ref, q_ref, kv_ref, copies, ready):
    z, y, along_y, along_z = grid_place()
    x = x_ref[...].astype(F32)
    inverse = lax.rsqrt(jnp.mean(x * x, axis=-1, keepdims=True) + EPSILON)
    normed = (x * inverse * g_ref[...]).astype(BF)
    normed_ref[...] = normed
    projected = nn(normed, w_ref[:, D:]) + b_ref[:, D:]
    turned = turn(projected[:, :KV], cos_ref[...], sin_ref[...], 1.0)
    kv = jnp.concatenate([turned, projected[:, KV:]], axis=1).astype(BF)
    kv_ref[0, z, y] = kv[:64]
    kv_ref[1, z, y] = kv[64:]
    if ready:
        ready()
    top, bottom = (slice(0, 32), slice(None)), (slice(32, 64), slice(None))
    steps = gather_both(
        y_then_z(kv_ref.at[0], *top),
        y_then_z(kv_ref.at[0], *bottom),
        z_then_y(kv_ref.at[1], *top),
        z_then_y(kv_ref.at[1], *bottom),
        copies,
        gather_direct,
        gather_direct,
    )
    next(steps)
    projected = nn(normed, w_ref[:, :D]) + b_ref[:, :D]
    q_ref[...] = turn(projected, cos_ref[...], sin_ref[...], 1.0).astype(BF)
    return steps


def front_kernel(x_ref, w_ref, b_ref, g_ref, cos_ref, sin_ref, normed_ref, q_ref, kv_ref, send, recv):
    z, y, along_y, along_z = grid_place()
    signal(neighbours(along_y, along_z))
    steps = front_work(
        x_ref, w_ref, b_ref, g_ref, cos_ref, sin_ref, normed_ref, q_ref, kv_ref,
        Copies(send, recv), lambda: greeted(6)
    )
    run(steps)


def front(x, w_qkv, b_qkv, g_attn, cosine, sine):
    return pl.pallas_call(
        front_kernel,
        out_shape=(shaped(ROWS, D), shaped(ROWS, D), shaped(2, 4, 4, 64, 2 * KV)),
        scratch_shapes=[pltpu.SemaphoreType.DMA((24,)), pltpu.SemaphoreType.DMA((24,))],
        compiler_params=params(6),
        name="front",
    )(x, w_qkv, b_qkv, g_attn, cosine, sine)


def low_lanes(rows):
    return lax.broadcasted_iota(jnp.int32, (rows, KV), 1) < KV // 2


def spread(kv_ref, start, to_ref):
    mixed = kv_ref[:, :, :, :, start : start + KV].reshape(LEN, KV)
    other = pltpu.roll(mixed.astype(F32), KV // 2, 1).astype(BF)
    low = low_lanes(LEN)
    to_ref[0] = jnp.where(low, mixed, other)
    to_ref[1] = mixed
    to_ref[2] = jnp.where(low, other, mixed)


def fill_bias(kseg_ref, bias_refs):
    first_row = 64 * lax.axis_index("group")
    for block, bias_ref in enumerate(bias_refs):
        keys = SPAN * (block + 1)
        kpos = lax.broadcasted_iota(jnp.int32, (64, keys), 1)
        qpos = SPAN * block + first_row + lax.broadcasted_iota(jnp.int32, (64, keys), 0)
        kseg = jnp.broadcast_to(kseg_ref[:, :keys], (64, keys)).astype(F32)
        qseg = jnp.sum(jnp.where(kpos == qpos, kseg, 0.0), axis=1, keepdims=True)
        bias_ref[...] = jnp.where((kpos <= qpos) & (kseg == qseg), 0.0, NEGATIVE)


def two_heads(pair):
    low = low_lanes(64)
    zero = jnp.zeros_like(pair)
    return jnp.concatenate([jnp.where(low, pair, zero), jnp.where(low, zero, pair)], axis=0)


def one_pair(stacked):
    return jnp.where(low_lanes(64), stacked[:64], stacked[64:])


def softmax(queries, keys, bias_ref):
    count = keys.shape[0]
    scores = nt(queries, keys).reshape(2, 64, count) + bias_ref[...][None]
    highest = jnp.max(scores, axis=-1, keepdims=True)
    exponent = jnp.exp(scores - highest)
    total = jnp.sum(exponent, axis=-1, keepdims=True)
    return (exponent * (1.0 / total)).reshape(2 * 64, count)


def variant_of(pair):
    return jnp.where(pair < 3, 0, jnp.where(pair == 3, 1, 2))


def attention_work(
    x_ref, q_ref, kv_ref, kseg_ref, w_ref, g_ref, context_ref, hidden_ref, normed_ref,
    keys_ref, values_ref, bias0, bias1, between=None
):
    spread(kv_ref, 0, keys_ref)
    spread(kv_ref, KV, values_ref)
    fill_bias(kseg_ref, (bias0, bias1))

    def one(pair, carry):
        if between:
            pl.when(pair == between[0])(between[1])
        variant = variant_of(pair)
        lanes = pl.ds(pl.multiple_of(pair * KV, KV), KV)
        for block, bias_ref in enumerate((bias0, bias1)):
            rows = slice(64 * block, 64 * block + 64)
            keys = pl.ds(0, SPAN * (block + 1))
            queries = two_heads(q_ref[rows, lanes] * SCALE).astype(BF)
            weights = softmax(queries, keys_ref[variant, keys], bias_ref).astype(BF)
            context = nn(weights, values_ref[variant, keys])
            context_ref[rows, lanes] = one_pair(context).astype(BF)
        return carry

    lax.fori_loop(0, PAIRS, one, 0)
    hidden = x_ref[...].astype(F32) + nn(context_ref[...], w_ref[...])
    hidden_ref[...] = hidden
    inverse = lax.rsqrt(jnp.mean(hidden * hidden, axis=-1, keepdims=True) + EPSILON)
    normed_ref[...] = (hidden * inverse * g_ref[...]).astype(BF)


ATTENTION_SCRATCH = [
    pltpu.VMEM((3, LEN, KV), BF),
    pltpu.VMEM((3, LEN, KV), BF),
    pltpu.VMEM((64, SPAN), F32),
    pltpu.VMEM((64, LEN), F32),
]


def attention(x, q, kv, kseg, w_out, g_mlp):
    return local_call(
        attention_work,
        "attention",
        (shaped(ROWS, D), shaped(ROWS, D, dtype=F32), shaped(ROWS, D)),
        ATTENTION_SCRATCH,
    )(x, q, kv, kseg, w_out, g_mlp)


def norm_backward(values, gain, grads):
    inverse = lax.rsqrt(jnp.mean(values * values, axis=-1, keepdims=True) + EPSILON)
    scaled = grads * gain
    dvalues = inverse * scaled - values * (
        inverse * inverse * inverse * jnp.mean(scaled * values, axis=-1, keepdims=True)
    )
    return dvalues, jnp.sum(grads * values * inverse, axis=0, keepdims=True)


def attention_backward_work(
    dout_ref, dnormed_ref, hidden_ref, g_ref, w_ref, q_ref, kv_ref, kseg_ref,
    dhidden_ref, dlow_ref, dq_ref, dkv_ref, dgain_ref,
    keys_ref, values_ref, bias0, bias1, dcontext_ref, dkeys, dvalues, between=None
):
    dnorm, dgain = norm_backward(hidden_ref[...], g_ref[...], dnormed_ref[...])
    dgain_ref[...] = dgain
    dhidden = dout_ref[...].astype(F32) + dnorm
    dhidden_ref[...] = dhidden
    dlow = dhidden.astype(BF)
    dlow_ref[...] = dlow
    dcontext_ref[...] = nt(dlow, w_ref[...]).astype(BF)
    spread(kv_ref, 0, keys_ref)
    spread(kv_ref, KV, values_ref)
    fill_bias(kseg_ref, (bias0, bias1))
    dkeys[...] = jnp.zeros_like(dkeys)
    dvalues[...] = jnp.zeros_like(dvalues)

    def one(pair, carry):
        if between:
            pl.when(pair == between[0])(between[1])
        variant = variant_of(pair)
        lanes = pl.ds(pl.multiple_of(pair * KV, KV), KV)
        for block, bias_ref in enumerate((bias0, bias1)):
            rows = slice(64 * block, 64 * block + 64)
            keys = pl.ds(0, SPAN * (block + 1))
            queries = two_heads(q_ref[rows, lanes] * SCALE).astype(BF)
            dcontext = two_heads(dcontext_ref[rows, lanes])
            key_rows = keys_ref[variant, keys]
            weights = softmax(queries, key_rows, bias_ref)
            dweights = nt(dcontext, values_ref[variant, keys])
            inner = jnp.sum(weights * dweights, axis=-1, keepdims=True)
            dscores = (weights * (dweights - inner)).astype(BF)
            dq_ref[rows, lanes] = one_pair(nn(dscores, key_rows)) * SCALE
            dkeys[variant, keys] += tn(dscores, queries)
            dvalues[variant, keys] += tn(weights.astype(BF), dcontext)
        return carry

    lax.fori_loop(0, PAIRS, one, 0)
    low = low_lanes(LEN)
    for start, total in ((0, dkeys), (KV, dvalues)):
        head0 = total[0] + pltpu.roll(total[0], KV // 2, 1)
        head1 = total[2] + pltpu.roll(total[2], KV // 2, 1)
        whole = (jnp.where(low, head0, head1) + total[1]).astype(BF)
        dkv_ref[:, :, :, :, start : start + KV] = whole.reshape(2, 4, 4, 64, KV)


ATTENTION_BACKWARD_OUT = (
    shaped(ROWS, D, dtype=F32),
    shaped(ROWS, D),
    shaped(ROWS, D, dtype=F32),
    shaped(2, 4, 4, 64, 2 * KV),
    shaped(1, D, dtype=F32),
)
ATTENTION_BACKWARD_SCRATCH = ATTENTION_SCRATCH + [
    pltpu.VMEM((ROWS, D), BF),
    pltpu.VMEM((3, LEN, KV), F32),
    pltpu.VMEM((3, LEN, KV), F32),
]


def attention_backward(*operands):
    return local_call(
        attention_backward_work, "attention_backward", ATTENTION_BACKWARD_OUT, ATTENTION_BACKWARD_SCRATCH
    )(*operands)


def rear_query(dq_ref, cos_ref, sin_ref, w_ref, dprojected_ref, dbias_ref):
    dquery = turn(dq_ref[...], cos_ref[...], sin_ref[...], -1.0).astype(BF)
    dprojected_ref[:, :D] = dquery
    dbias_ref[:, :D] = jnp.sum(dquery.astype(F32), axis=0, keepdims=True)
    return nt(dquery, w_ref[:, :D])


def rear_rest(
    dnormed, total, cos_ref, sin_ref, w_ref, x_ref, g_ref, dhidden_ref, dprojected_ref, dinput_ref, dgain_ref, dbias_ref
):
    turned = turn(total[:, :KV], cos_ref[...], sin_ref[...], -1.0)
    dkv = jnp.concatenate([turned, total[:, KV:]], axis=1).astype(BF)
    dprojected_ref[:, D:] = dkv
    dbias_ref[:, D:] = jnp.sum(dkv.astype(F32), axis=0, keepdims=True)
    dnormed = dnormed + nt(dkv, w_ref[:, D:])
    dnorm, dgain = norm_backward(x_ref[...].astype(F32), g_ref[...], dnormed)
    dgain_ref[...] = dgain
    dinput_ref[...] = (dhidden_ref[...] + dnorm).astype(BF)


REAR_SCRATCH = [
    pltpu.VMEM((ROWS, QKV), BF),
    pltpu.VMEM((1, D), F32),
    pltpu.VMEM((1, QKV), F32),
    pltpu.VMEM((ROWS, 2 * KV), F32),
] + scatter_scratch(*[(32, 2 * KV)] * 4)


def rear_kernel(
    dkv_ref, dq_ref, cos_ref, sin_ref, w_ref, x_ref, g_ref, dhidden_ref, cotangent_ref, next_ref,
    dinput_ref, returned_ref, dprojected_ref, dgain_ref, dbias_ref, total, *rest
):
    scratch, (send, recv) = rest[:-2], rest[-2:]
    z, y, along_y, along_z = grid_place()
    signal(neighbours(along_y, along_z) + [other_section()])
    greeted(7)
    copies = Copies(send, recv)
    steps = kv_sums(dkv_ref, total, scratch, copies)
    next(steps)
    dnormed = rear_query(dq_ref, cos_ref, sin_ref, w_ref, dprojected_ref, dbias_ref)
    run(steps)
    rear_rest(
        dnormed, total, cos_ref, sin_ref, w_ref, x_ref, g_ref, dhidden_ref,
        dprojected_ref, dinput_ref, dgain_ref, dbias_ref
    )
    relay = copies(dinput_ref, returned_ref, other_section(), False)

    @pl.when(lax.axis_index("section") == 1)
    def _():
        relay.start()
        next_ref[...] = cotangent_ref[...]
        relay.wait_send()

    @pl.when(lax.axis_index("section") == 0)
    def _():
        relay.wait_recv()
        next_ref[...] = returned_ref[...]


def rear(*operands):
    return pl.pallas_call(
        rear_kernel,
        out_shape=shaped(ROWS, D),
        scratch_shapes=[pltpu.VMEM((ROWS, D), BF), pltpu.VMEM((ROWS, D), BF)]
        + REAR_SCRATCH
        + [pltpu.SemaphoreType.DMA((25,)), pltpu.SemaphoreType.DMA((25,))],
        compiler_params=params(7),
        name="rear",
    )(*operands)


TAIL_SCRATCH = [
    pltpu.VMEM((4, 4, 56, QUARTER), BF),
    pltpu.VMEM((4, 4, 56, QUARTER), BF),
    pltpu.VMEM((4, 4, DOWN_ROWS, D), BF),
    pltpu.VMEM((56, QUARTER), BF),
    pltpu.VMEM((56, QUARTER), BF),
    pltpu.VMEM((DOWN_ROWS, D), BF),
    pltpu.VMEM((4, 4, 64, QKV), BF),
    pltpu.VMEM((4, 4, 64, D), BF),
    pltpu.VMEM((4, 4, 32, QKV), BF),
    pltpu.VMEM((4, 4, 32, D), BF),
    pltpu.VMEM((32, QKV), F32),
    pltpu.VMEM((32, D), F32),
    pltpu.VMEM((32, QKV), BF),
    pltpu.VMEM((32, D), BF),
    pltpu.VMEM((32, QKV), BF),
    pltpu.VMEM((32, D), BF),
]
LATE = (0, 1, 2, 4, 5, 6, 13, 14, 15, 16, 18, 19)
TAIL_COPIES = 24 + 36 + 48 + 2 + 13


def tail_kernel(*refs):
    refs = list(refs)

    def take(count):
        taken = refs[:count]
        del refs[:count]
        return taken

    operands = take(20)
    dinput_ref, gate_all, up_all, down_all, qkv_all, out_all = take(6)
    attention_out = take(5)
    dhidden_ref, dlow_ref, dq_ref, dkv_ref, dgain2_ref = attention_out
    attention_scratch = take(len(ATTENTION_BACKWARD_SCRATCH))
    dprojected_ref, dgain1_ref, dbias_ref, total = take(4)
    kv_bufs = take(24)
    mlp_term_refs, mlp_sum_refs = take(3), take(3)
    qkv_terms, out_terms, qkv_half, out_half, qkv_sum, out_sum, qkv_low, out_low, qkv_in, out_in = take(10)
    mlp_bufs, qkv_bufs, out_bufs = take(24), take(24), take(24)
    send, recv, local, load_sems = take(4)
    loads = []
    for index, (at, vmem) in enumerate(zip(LATE, take(len(LATE)))):
        loads.append(pltpu.make_async_copy(operands[at], vmem, load_sems.at[index]))
        loads[-1].start()
        operands[at] = vmem
    attention_in, mlp_in = operands[:8], operands[8:13]
    cos_ref, sin_ref, qkv_w, x_ref, gain1_ref, normed_ref, context_ref = operands[13:]

    z, y, along_y, along_z = grid_place()
    me, mate, next_, far = replica_partners()
    core = lax.rem(me, 2)
    to_mate, to_next = {"replica": mate}, {"replica": next_}
    target, source, stays = quarter_route()
    moves = jnp.logical_not(stays)
    signal(neighbours(along_y, along_z) + [to_mate, to_next])
    rows_all, dgate, dup, product, dout_all = mlp_in
    wide_terms(rows_all, dgate, mlp_term_refs[0])

    @pl.when(moves)
    def _():
        signal([target])
        greeted(9)

    @pl.when(stays)
    def _():
        greeted(8)

    copies = Copies(send, recv)
    mlp = mlp_sums(*mlp_term_refs, *mlp_sum_refs, mlp_bufs, copies)
    next(mlp)
    wide_terms(rows_all, dup, mlp_term_refs[1])
    next(mlp)
    down_rows_terms(product, dout_all, mlp_term_refs[2])
    next(mlp)
    for each in loads:
        each.wait()
    attention_backward_work(*attention_in, *attention_out, *attention_scratch, (3, lambda: next(mlp)))
    kv = kv_sums(dkv_ref, total, kv_bufs, copies)
    next(kv)
    next(mlp)

    mine = pl.ds(pl.multiple_of(32 * core, 32), 32)
    theirs = pl.ds(pl.multiple_of(32 - 32 * core, 32), 32)

    def add_mate(sent, terms, half):
        sent.wait_recv()
        half[...] = (terms[:, :, mine].astype(F32) + half[...].astype(F32)).astype(BF)

    dnormed = rear_query(dq_ref, cos_ref, sin_ref, qkv_w, dprojected_ref, dbias_ref)
    next(kv)
    whole = tn(context_ref[...], dlow_ref[...])
    for at in range(16):
        rows = jnp.concatenate([whole[56 * at : 56 * at + 56], jnp.zeros((8, D), F32)], axis=0)
        out_terms[at // 4, at % 4] = rows.astype(BF)
    out_sent = copies(out_terms.at[:, :, theirs], out_half, to_mate)
    next(kv)
    add_mate(out_sent, out_terms, out_half)
    outs = half_sums(out_half, out_sum, 512, out_bufs, copies)
    next(outs)
    run(kv)
    rear_rest(
        dnormed, total, cos_ref, sin_ref, qkv_w, x_ref, gain1_ref, dhidden_ref,
        dprojected_ref, dinput_ref, dgain1_ref, dbias_ref
    )
    whole = tn(normed_ref[...], dprojected_ref[...])
    dbias, dgain1, dgain2 = dbias_ref[...], dgain1_ref[...], dgain2_ref[...]
    for at in range(16):
        small = jnp.concatenate(
            [
                dbias[:, 64 * at : 64 * at + 64],
                dbias[:, D + KV + 8 * at : D + KV + 8 * at + 8],
                dgain1[:, 56 * at : 56 * at + 56],
                dgain2[:, 56 * at : 56 * at + 56],
                jnp.zeros((1, QKV - 184), F32),
            ],
            axis=1,
        )
        rows = jnp.concatenate([whole[56 * at : 56 * at + 56], jnp.broadcast_to(small, (8, QKV))], axis=0)
        qkv_terms[at // 4, at % 4] = rows.astype(BF)
    qkv_sent = copies(qkv_terms.at[:, :, theirs], qkv_half, to_mate)
    next(outs)
    next(outs)
    next(mlp)
    add_mate(qkv_sent, qkv_terms, qkv_half)
    dense = half_sums(qkv_half, qkv_sum, 640, qkv_bufs, copies)
    next(dense)
    next(mlp)
    run(outs)
    run(mlp)

    gate, up, down = mlp_sum_refs
    moved = pltpu.make_async_remote_copy(
        src_ref=down,
        dst_ref=down_all.at[source["replica"]],
        send_sem=local.at[0],
        recv_sem=local.at[1],
        device_id=source,
        device_id_type=MESH,
    )
    stayed = pltpu.make_async_copy(down, down_all.at[me], local.at[2])

    @pl.when(moves)
    def _():
        moved.start()

    @pl.when(stays)
    def _():
        stayed.start()

    pairs = ((gate, gate_all), (up, up_all))
    across = [copies(ref, all_ref.at[me], to_next) for ref, all_ref in pairs]
    beside = [copies(ref, all_ref.at[me], to_mate) for ref, all_ref in pairs]
    for ref, all_ref in pairs:
        all_ref[me] = ref[...]
    next(dense)
    next(dense)

    @pl.when(moves)
    def _():
        moved.wait()

    @pl.when(stays)
    def _():
        stayed.wait()

    across.append(copies(down_all.at[me], down_all.at[me], to_next))
    beside.append(copies(down_all.at[me], down_all.at[me], to_mate))
    run(dense)
    qkv_low[...] = qkv_sum[...].astype(BF)
    out_low[...] = out_sum[...].astype(BF)
    sums = [copies(qkv_low, qkv_in, to_next), copies(out_low, out_in, to_next)]
    for came, all_ref in zip(across, (gate_all, up_all, down_all)):
        came.wait_recv()
        beside.append(copies(all_ref.at[next_], all_ref.at[next_], to_mate))
    sums[0].wait_recv()
    qkv_all[core] = qkv_sum[...] + qkv_in[...].astype(F32)
    sums[1].wait_recv()
    out_all[core] = out_sum[...] + out_in[...].astype(F32)
    beside += [copies(ref.at[core], ref.at[core], to_mate) for ref in (qkv_all, out_all)]
    for each in beside:
        each.wait_recv()
    for each in [out_sent, qkv_sent] + across + beside + sums:
        each.wait_send()


def tail(*operands):
    return pl.pallas_call(
        tail_kernel,
        out_shape=(
            shaped(ROWS, D),
            shaped(4, 56, QUARTER),
            shaped(4, 56, QUARTER),
            shaped(4, DOWN_ROWS, D),
            shaped(2, 32, QKV, dtype=F32),
            shaped(2, 32, D, dtype=F32),
        ),
        scratch_shapes=[pltpu.VMEM(each.shape, each.dtype) for each in ATTENTION_BACKWARD_OUT]
        + ATTENTION_BACKWARD_SCRATCH
        + REAR_SCRATCH
        + TAIL_SCRATCH
        + scatter_scratch(*MLP_SUMS_SHAPES)
        + scatter_scratch((16, 640), (16, 640), (16, QKV - 640), (16, QKV - 640))
        + scatter_scratch((16, 512), (16, 512), (16, D - 512), (16, D - 512))
        + [
            pltpu.SemaphoreType.DMA((TAIL_COPIES,)),
            pltpu.SemaphoreType.DMA((TAIL_COPIES,)),
            pltpu.SemaphoreType.DMA((3,)),
            pltpu.SemaphoreType.DMA((len(LATE),)),
        ]
        + [pltpu.VMEM(operands[at].shape, operands[at].dtype) for at in LATE],
        in_specs=[ANY_SPEC if at in LATE else VMEM_SPEC for at in range(20)],
        compiler_params=params(1),
        name="tail",
    )(*operands)


def rotary(group):
    lane = np.arange(KV)
    frequency = jnp.asarray(THETA ** (-(lane % HALF) * 2.0 / (2 * HALF)), F32)
    sign = jnp.asarray(np.where(lane % (2 * HALF) < HALF, -1.0, 1.0), F32)
    row = lax.broadcasted_iota(jnp.int32, (ROWS, KV), 0)
    positions = group * 64 + lax.rem(row, 64) + SPAN * (row // 64)
    angles = positions.astype(F32) * frequency[None, :]
    return jnp.cos(angles), jnp.sin(angles) * sign[None, :]


def body(inputs, cotangent, segments, w_qkv, b_qkv, w_out, w_gate, w_up, w_down, g_attn, g_mlp):
    group = lax.axis_index("group")
    replica = lax.axis_index("replica")
    core = lax.rem(replica, 2)

    down_piece = lax.dynamic_slice(w_down[0], (jnp.minimum(80 * replica, 224), 0), (DOWN_ROWS, D))
    gate_piece = lax.dynamic_slice(w_gate[0], (0, replica * QUARTER), (D // 16, QUARTER))
    up_piece = lax.dynamic_slice(w_up[0], (0, replica * QUARTER), (D // 16, QUARTER))
    small = jnp.concatenate([b_qkv[0], g_attn[0], g_mlp[0]])
    small = jnp.pad(small[None], ((0, 7), (0, QKV - small.shape[0])))
    qkv_piece = lax.dynamic_slice(jnp.concatenate([w_qkv[0], small], axis=0), (32 * core, 0), (32, QKV))
    out_piece = lax.dynamic_slice(jnp.pad(w_out[0], ((0, 8), (0, 0))), (32 * core, 0), (32, D))

    cosine, sine = rotary(group)
    kseg = segments
    x_in = inputs[0].reshape(ROWS, D)
    cotangent_in = cotangent[0].reshape(ROWS, D)
    gate_w, up_w, down_w, qkv_w, out_w, bias, gain1, gain2, hidden, normed2 = first(
        gate_piece, up_piece, down_piece, qkv_piece, out_piece, x_in, cosine, sine, kseg
    )
    gate_w = gate_w.reshape(D, QUARTER)
    up_w = up_w.reshape(D, QUARTER)

    def forward(x):
        normed, q, kv = front(x, qkv_w, bias, gain1, cosine, sine)
        context, hidden, normed2 = attention(x, q, kv, kseg, out_w, gain2)
        output, normed2_all, gate, up = mlp_forward(normed2, hidden, gate_w, up_w, down_w)
        return output, (x, normed, q, kv, context, hidden, normed2_all, gate, up)

    def backward_start(dout):
        dnormed2, *grads = mlp_backward(dout, gate, up, gate_w, up_w, down_w)
        dout_all, dgate, dup, product = grads
        return (dout, dnormed2, hidden, gain2, out_w, q, kv, kseg), (normed2_all, dgate, dup, product, dout_all)

    output, kept = forward(mlp_relay(normed2, hidden, x_in, gate_w, up_w, down_w))
    x, normed, q, kv, context, hidden, normed2_all, gate, up = kept
    operands, _ = backward_start(cotangent_in)
    dhidden, _, dq, dkv, _ = attention_backward(*operands)
    dout = rear(dkv, dq, cosine, sine, qkv_w, x, gain1, dhidden, cotangent_in)
    operands, mlp_operands = backward_start(dout)
    dinput, *parts = tail(*operands, *mlp_operands, cosine, sine, qkv_w, x, gain1, normed, context)
    grad_gate, grad_up, grad_down, grad_qkv, grad_out, bias, value_bias, gain1, gain2 = outputs(*parts)
    return (
        output.reshape(1, 1, 2, 64, D),
        dinput.reshape(1, 1, 2, 64, D),
        grad_qkv[None],
        bias,
        value_bias,
        grad_out[None],
        grad_gate[None],
        grad_up[None],
        grad_down[None],
        gain1,
        gain2,
    )


def solution(mesh):
    in_specs = (
        P("replica", None, "group", None),
        P("replica", None, "group", None),
        P("replica", None),
        P("section", "group", None),
        P("section", "group"),
        P("section", "group", None),
        P("section", "group", None),
        P("section", "group", None),
        P("section", "group", None),
        P("section", "group"),
        P("section", "group"),
    )
    out_specs = (
        P("section", "replica", None, "group", None),
        P("section", "replica", None, "group", None),
        P("section", "group", None),
        P("section", "group"),
        P("section", "group"),
        P("section", "group", None),
        P("section", "group", None),
        P("section", "group", None),
        P("section", "group", None),
        P("section", "group"),
        P("section", "group"),
    )
    return jax.shard_map(body, mesh=mesh, in_specs=in_specs, out_specs=out_specs, check_vma=False)
```

```python
import functools

import jax
import jax.numpy as jnp
import numpy as np
from jax import lax
from jax.experimental import pallas as pl
from jax.experimental.pallas import tpu as pltpu
from jax.sharding import PartitionSpec as P

D = 896
HEADS = 14
KV = 128
HALF = 32
FF = 4864
QUARTER = FF // 4
QKV = 1152
ROWS = 128
SPAN = 1024
LEN = 2048
PAIRS = 7
EPSILON = 1e-06
THETA = 1000000.0
NEGATIVE = -1e30
SCALE = 0.125
VMEM_LIMIT = 60 * 1024 * 1024
MESH = pl.DeviceIdType.MESH
BF = jnp.bfloat16
F32 = jnp.float32
VMEM_SPEC = pl.BlockSpec(memory_space=pltpu.VMEM)
ANY_SPEC = pl.BlockSpec(memory_space=pl.ANY)


def nn(a, b):
    return lax.dot_general(a, b, (((1,), (0,)), ((), ())), preferred_element_type=F32)


def nt(a, b):
    return lax.dot_general(a, b, (((1,), (1,)), ((), ())), preferred_element_type=F32)


def tn(a, b):
    return lax.dot_general(a, b, (((0,), (0,)), ((), ())), preferred_element_type=F32)


def params(collective_id=None):
    if collective_id is None:
        return pltpu.CompilerParams(vmem_limit_bytes=VMEM_LIMIT)
    return pltpu.CompilerParams(
        vmem_limit_bytes=VMEM_LIMIT, collective_id=collective_id, has_side_effects=True
    )


def shaped(*shape, dtype=BF):
    return jax.ShapeDtypeStruct(shape, dtype)


def local_call(kernel, name, out_shape, scratch=()):
    return pl.pallas_call(
        kernel,
        out_shape=out_shape,
        scratch_shapes=list(scratch),
        compiler_params=params(),
        name=name,
    )


def signal(devices):
    barrier = pltpu.get_barrier_semaphore()
    for device in devices:
        pl.semaphore_signal(barrier, inc=1, device_id=device, device_id_type=MESH)


def greeted(count):
    pl.semaphore_wait(pltpu.get_barrier_semaphore(), count)


def grid_place():
    me = lax.axis_index("group")
    z = me // 4
    y = lax.rem(me, 4)

    def along_y(step):
        return {"group": z * 4 + lax.rem(y + step, 4)}

    def along_z(step):
        return {"group": lax.rem(z + step, 4) * 4 + y}

    return z, y, along_y, along_z


def neighbours(along_y, along_z):
    return [along(step) for along in (along_y, along_z) for step in (1, 3, 2)]


class Copies:
    def __init__(self, send, recv):
        self.send, self.recv, self.used = send, recv, 0

    def __call__(self, src, dst, device, start=True):
        index = self.used
        self.used += 1
        each = pltpu.make_async_remote_copy(
            src_ref=src,
            dst_ref=dst,
            send_sem=self.send.at[index],
            recv_sem=self.recv.at[index],
            device_id=device,
            device_id_type=MESH,
        )
        if start:
            each.start()
        return each


def gather_phase(firsts, seconds, place, device_at, copies):
    def copy(block, slot, step):
        return copies(block(slot), block(slot), device_at(step), False)

    firsts_right = [copy(block, place, 1) for block in firsts]
    seconds_left = [copy(block, place, 3) for block in seconds]
    others = [copy(block, place, 3) for block in firsts] + [copy(block, place, 1) for block in seconds]
    relays = [copy(block, lax.rem(place + 3, 4), 1) for block in firsts]
    relays += [copy(block, lax.rem(place + 1, 4), 3) for block in seconds]

    def start():
        for each in firsts_right + seconds_left + others:
            each.start()

    def relay():
        for came, each in zip(firsts_right + seconds_left, relays):
            came.wait_recv()
            each.start()

    def finish():
        for each in others + relays:
            each.wait_recv()
        for each in firsts_right + seconds_left + others + relays:
            each.wait_send()

    return start, relay, finish


def gather_direct(firsts, seconds, place, device_at, copies):
    sent = []
    for block in firsts + seconds:
        sent += [copies(block(place), block(place), device_at(step), False) for step in (1, 3, 2)]

    def start():
        for each in sent:
            each.start()

    def finish():
        for each in sent:
            each.wait_recv()
        for each in sent:
            each.wait_send()

    return start, lambda: None, finish


def gather_both(first_a, second_a, first_b, second_b, copies, phase=gather_phase, then=gather_phase):
    z, y, along_y, along_z = grid_place()
    start_a, relay_a, finish_a = phase([first_a[0]], [second_a[0]], y, along_y, copies)
    start_b, relay_b, finish_b = phase([first_b[0]], [second_b[0]], z, along_z, copies)
    then_a, last_a, end_a = then([first_a[1]], [second_a[1]], z, along_z, copies)
    then_b, last_b, end_b = then([first_b[1]], [second_b[1]], y, along_y, copies)
    start_a()
    start_b()
    yield
    relay_a()
    relay_b()
    yield
    finish_a()
    then_a()
    finish_b()
    then_b()
    yield
    last_a()
    last_b()
    yield
    end_a()
    end_b()


def gather_split(first_a, second_a, first_b, second_b, copies):
    z, y, along_y, along_z = grid_place()
    slim = [
        gather_phase([first_a[0]], [second_a[0]], y, along_y, copies),
        gather_phase([first_b[0]], [second_b[0]], z, along_z, copies),
    ]

    def wide(half):
        def part(function):
            return [lambda at: function(at, half)]

        return [
            gather_phase(part(first_a[1]), part(second_a[1]), z, along_z, copies),
            gather_phase(part(first_b[1]), part(second_b[1]), y, along_y, copies),
        ]

    halves = [wide(slice(0, 2)), wide(slice(2, 4))]
    for start, _, _ in slim:
        start()
    yield
    for _, relay, _ in slim:
        relay()
    yield
    for _, _, finish in slim:
        finish()
    for phases in halves:
        for start, _, _ in phases:
            start()
        yield
        for _, relay, _ in phases:
            relay()
        yield
    for phases in halves:
        for _, _, finish in phases:
            finish()


def run(steps):
    for _ in steps:
        pass


def y_then_z(ref, *tail):
    z = lax.axis_index("group") // 4
    return (lambda at: ref.at[(z, at, *tail)]), (lambda at, part=slice(None): ref.at[(at, part, *tail)])


def z_then_y(ref, *tail):
    y = lax.rem(lax.axis_index("group"), 4)
    return (lambda at: ref.at[(at, y, *tail)]), (lambda at, part=slice(None): ref.at[(part, at, *tail)])


def quarter_route():
    group, replica = lax.axis_index("group"), lax.axis_index("replica")
    target = {"group": 4 * lax.rem(group, 4) + replica, "replica": group // 4}
    source = {"group": 4 * replica + group // 4, "replica": lax.rem(group, 4)}
    stays = (target["group"] == group) & (target["replica"] == replica)
    return target, source, stays


def first_kernel(
    gate, up, down, qkv, out, x_ref, cos_ref, sin_ref, kseg_ref,
    gate_all, up_all, down_all, qkv_w, out_w, bias_ref, gain1_ref, gain2_ref, hidden_ref, normed2_ref,
    qkv_all, out_all, normed_ref, q_ref, kv_ref, context_ref, keys_ref, values_ref, bias0, bias1, send, recv, local
):
    z, y, along_y, along_z = grid_place()
    core = lax.rem(lax.axis_index("replica"), 2)
    mate = {"replica": lax.axis_index("replica") + 1 - 2 * core}
    target, source, stays = quarter_route()
    moves = jnp.logical_not(stays)
    signal(neighbours(along_y, along_z) + [mate])
    places = (qkv_all.at[core, z, y], out_all.at[core, z, y], gate_all.at[z, y], up_all.at[z, y])
    own = []
    for index, (src, dst) in enumerate(zip((qkv, out, gate, up), places)):
        own.append(pltpu.make_async_copy(src, dst, local.at[index]))
        own[-1].start()
    there = target["group"]
    moved = pltpu.make_async_remote_copy(
        src_ref=down,
        dst_ref=down_all.at[there // 4, lax.rem(there, 4)],
        send_sem=local.at[5],
        recv_sem=local.at[6],
        device_id=target,
        device_id_type=MESH,
    )
    stayed = pltpu.make_async_copy(down, down_all.at[z, y], local.at[4])

    @pl.when(moves)
    def _():
        signal([source])
        greeted(8)
        moved.start()

    @pl.when(stays)
    def _():
        greeted(7)
        stayed.start()

    copies = Copies(send, recv)
    own[0].wait()
    own[1].wait()
    top, bottom = (slice(0, 16), slice(None)), (slice(16, 32), slice(None))
    dense = gather_both(
        y_then_z(qkv_all.at[core], *top),
        y_then_z(qkv_all.at[core], *bottom),
        z_then_y(out_all.at[core], *top),
        z_then_y(out_all.at[core], *bottom),
        copies,
        gather_direct,
    )
    next(dense)
    next(dense)
    next(dense)
    own[2].wait()
    own[3].wait()

    @pl.when(moves)
    def _():
        moved.wait()

    @pl.when(stays)
    def _():
        stayed.wait()

    left, right = (slice(None), slice(0, 512)), (slice(None), slice(512, D))
    wide = gather_split(
        y_then_z(gate_all), y_then_z(down_all, *left), z_then_y(up_all), z_then_y(down_all, *right), copies
    )
    next(wide)
    next(dense)
    next(wide)
    run(dense)
    halves = [copies(ref.at[core], ref.at[core], mate) for ref in (qkv_all, out_all)]
    next(wide)
    for each in halves:
        each.wait()
    for at in range(16):
        rows, cut = 56 * at, 56 * at + 32
        qkv_w[rows:cut] = qkv_all[0, at // 4, at % 4]
        qkv_w[cut : rows + 56] = qkv_all[1, at // 4, at % 4, :24]
        out_w[rows:cut] = out_all[0, at // 4, at % 4]
        out_w[cut : rows + 56] = out_all[1, at // 4, at % 4, :24]
    small = [qkv_all[1, at // 4, at % 4, 24:32].astype(F32)[:1] for at in range(16)]
    bias_ref[...] = jnp.concatenate([each[:, :72] for each in small], axis=1)
    gain1_ref[...] = jnp.concatenate([each[:, 72:128] for each in small], axis=1)
    gain2_ref[...] = jnp.concatenate([each[:, 128:184] for each in small], axis=1)
    kv = front_work(x_ref, qkv_w, bias_ref, gain1_ref, cos_ref, sin_ref, normed_ref, q_ref, kv_ref, copies, None)
    next(kv)
    next(kv)
    next(wide)
    next(wide)
    run(kv)
    attention_work(
        x_ref, q_ref, kv_ref, kseg_ref, out_w, gain2_ref, context_ref, hidden_ref, normed2_ref,
        keys_ref, values_ref, bias0, bias1, (4, lambda: next(wide))
    )
    run(wide)


def first(gate, up, down, qkv, out, x, cosine, sine, kseg):
    return pl.pallas_call(
        first_kernel,
        out_shape=(
            shaped(4, 4, *gate.shape),
            shaped(4, 4, *up.shape),
            shaped(4, 4, *down.shape),
            shaped(D, QKV),
            shaped(D, D),
            shaped(1, QKV, dtype=F32),
            shaped(1, D, dtype=F32),
            shaped(1, D, dtype=F32),
            shaped(ROWS, D, dtype=F32),
            shaped(ROWS, D),
        ),
        in_specs=[ANY_SPEC] * 5 + [VMEM_SPEC] * 4,
        out_specs=[ANY_SPEC] * 3 + [VMEM_SPEC] * 7,
        scratch_shapes=[
            pltpu.VMEM((2, 4, 4, *qkv.shape), BF),
            pltpu.VMEM((2, 4, 4, *out.shape), BF),
            pltpu.VMEM((ROWS, D), BF),
            pltpu.VMEM((ROWS, D), BF),
            pltpu.VMEM((2, 4, 4, 64, 2 * KV), BF),
            pltpu.VMEM((ROWS, D), BF),
        ]
        + ATTENTION_SCRATCH
        + [
            pltpu.SemaphoreType.DMA((86,)),
            pltpu.SemaphoreType.DMA((86,)),
            pltpu.SemaphoreType.DMA((7,)),
        ],
        compiler_params=params(0),
        name="first",
    )(gate, up, down, qkv, out, x, cosine, sine, kseg)


def scatter_phase(firsts, seconds, place, device_at, copies):
    right, left, far = (lax.rem(place + step, 4) for step in (1, 3, 2))

    def load(ref):
        return ref[...].astype(F32)

    def copy(src, dst, step):
        return copies(src, dst, device_at(step), False)

    first_far = [copy(block(far), bufs[0], 1) for block, bufs, put in firsts]
    second_far = [copy(block(far), bufs[0], 3) for block, bufs, put in seconds]
    first_near = [copy(block(left), bufs[2], 3) for block, bufs, put in firsts]
    second_near = [copy(block(right), bufs[1], 1) for block, bufs, put in seconds]
    first_sum = [copy(bufs[0], bufs[1], 1) for block, bufs, put in firsts]
    second_sum = [copy(bufs[0], bufs[2], 3) for block, bufs, put in seconds]

    def start(which=(0, 1)):
        for index in which:
            for each in ((first_far + first_near), (second_far + second_near))[index]:
                each.start()

    def pass_on():
        for came, each, (block, bufs, put) in zip(first_far, first_sum, firsts):
            came.wait_recv()
            bufs[0][...] = (load(block(right)) + load(bufs[0])).astype(BF)
            each.start()
        for came, each, (block, bufs, put) in zip(second_far, second_sum, seconds):
            came.wait_recv()
            bufs[0][...] = (load(block(left)) + load(bufs[0])).astype(BF)
            each.start()

    def finish():
        near, far_sum = first_near + second_near, first_sum + second_sum
        for one, two, (block, bufs, put) in zip(near, far_sum, firsts + seconds):
            one.wait_recv()
            two.wait_recv()
            put(load(block(place)) + load(bufs[1]) + load(bufs[2]))
        for each in first_far + second_far + near + far_sum:
            each.wait_send()

    return start, pass_on, finish


def scatter_direct(firsts, seconds, place, device_at, copies):
    parts = firsts + seconds
    sent = []
    for block, bufs, put in parts:
        sent.append(
            [
                copies(block(lax.rem(place + step, 4)), bufs[index], device_at(step), False)
                for index, step in enumerate((1, 3, 2))
            ]
        )

    def start():
        for each in sum(sent, []):
            each.start()

    def finish():
        for came, (block, bufs, put) in zip(sent, parts):
            total = block(place)[...].astype(F32)
            for each, landed in zip(came, bufs):
                each.wait_recv()
                total = total + landed[...].astype(F32)
            for each in came:
                each.wait_send()
            put(total)

    return start, lambda: None, finish


def scatter_both(first_a, second_a, first_b, second_b, copies, phase=scatter_phase):
    z, y, along_y, along_z = grid_place()

    def wide(part):
        block, bufs, _, _ = part
        return [(block, bufs, stored_in(bufs[1]))]

    def slim(part):
        _, kept, bufs, put = part
        return [((lambda at: kept[1].at[at]), bufs, put)]

    start_a, pass_a, finish_a = phase(wide(first_a), wide(second_a), y, along_y, copies)
    start_b, pass_b, finish_b = phase(wide(first_b), wide(second_b), z, along_z, copies)
    then_a, last_a, end_a = phase(slim(first_a), slim(second_a), z, along_z, copies)
    then_b, last_b, end_b = phase(slim(first_b), slim(second_b), y, along_y, copies)
    start_a()
    start_b()
    yield
    pass_a()
    pass_b()
    yield
    finish_a()
    then_a()
    finish_b()
    then_b()
    yield
    last_a()
    last_b()
    yield
    end_a()
    end_b()


def scatter_split(first_a, second_a, first_b, second_b, copies):
    z, y, along_y, along_z = grid_place()

    def slim(part):
        _, kept, bufs, put = part
        return [((lambda at: kept[1].at[at]), bufs, put)]

    def halved(half):
        def wide(part):
            block, bufs, _, _ = part
            views = [each.at[half] for each in bufs]
            return [(lambda at: block(at, half), views, stored_in(views[1]))]

        return [
            scatter_phase(wide(first_a), wide(second_a), y, along_y, copies),
            scatter_phase(wide(first_b), wide(second_b), z, along_z, copies),
        ]

    halves = [halved(pl.ds(0, 2)), halved(pl.ds(2, 2))]
    last_phases = [
        scatter_phase(slim(first_a), slim(second_a), z, along_z, copies),
        scatter_phase(slim(first_b), slim(second_b), y, along_y, copies),
    ]
    for start, _, _ in halves[0]:
        start([0])
        yield
    for start, _, _ in halves[0]:
        start([1])
    yield
    for _, pass_on, _ in halves[0]:
        pass_on()
    for start, _, _ in halves[1]:
        start()
    yield
    for _, pass_on, _ in halves[1]:
        pass_on()
    yield
    for phases in halves:
        for _, _, finish in phases:
            finish()
    for start, _, _ in last_phases:
        start()
    yield
    for _, pass_on, _ in last_phases:
        pass_on()
    yield
    for _, _, finish in last_phases:
        finish()


def scatter_scratch(*shapes):
    scratch = []
    for shape in shapes:
        scratch += [pltpu.VMEM((4, *shape), BF)] * 3 + [pltpu.VMEM(shape, BF)] * 3
    return scratch


def scatter_part(scratch, index, block, put):
    mine = scratch[6 * index : 6 * index + 6]
    return block, mine[:3], mine[3:], put


def stored_in(ref, *at):
    def put(value):
        ref[at if at else ...] = value.astype(ref.dtype)

    return put


DOWN_STARTS = (0, 80, 160, 224)
DOWN_ROWS = 80


def flat(ref):
    return ref[...].reshape(4 * ROWS, ref.shape[-1])


def wide_terms(rows_ref, grads_ref, terms):
    whole = tn(flat(rows_ref), flat(grads_ref))
    for at in range(16):
        terms[at // 4, at % 4] = whole[56 * at : 56 * at + 56].astype(BF)


def down_rows_terms(product_ref, dout_ref, terms):
    whole = tn(flat(product_ref), flat(dout_ref)).astype(BF)
    for at in range(16):
        start = 304 * (at // 4) + DOWN_STARTS[at % 4]
        terms[at // 4, at % 4] = whole[start : start + DOWN_ROWS]


def mlp_sums(gate_terms, up_terms, down_terms, gate_out, up_out, down_out, scratch, copies):
    left, right = slice(0, 512), slice(512, D)
    return scatter_split(
        scatter_part(scratch, 0, lambda at, part: gate_terms.at[part, at], stored_in(gate_out)),
        scatter_part(
            scratch, 2, lambda at, part: down_terms.at[part, at, :, left], stored_in(down_out, slice(None), left)
        ),
        scatter_part(scratch, 1, lambda at, part: up_terms.at[at, part], stored_in(up_out)),
        scatter_part(
            scratch, 3, lambda at, part: down_terms.at[at, part, :, right], stored_in(down_out, slice(None), right)
        ),
        copies,
    )


MLP_SUMS_SHAPES = ((56, QUARTER), (56, QUARTER), (DOWN_ROWS, 512), (DOWN_ROWS, D - 512))


def half_sums(half, to, cut, scratch, copies):
    top, bottom = slice(0, 16), slice(16, 32)
    left, right = slice(0, cut), slice(cut, to.shape[1])
    return scatter_both(
        scatter_part(scratch, 0, lambda at: half.at[:, at, top, left], stored_in(to, top, left)),
        scatter_part(scratch, 1, lambda at: half.at[:, at, bottom, left], stored_in(to, bottom, left)),
        scatter_part(scratch, 2, lambda at: half.at[at, :, top, right], stored_in(to, top, right)),
        scatter_part(scratch, 3, lambda at: half.at[at, :, bottom, right], stored_in(to, bottom, right)),
        copies,
        scatter_direct,
    )


def kv_sums(dkv_ref, total, scratch, copies):
    top, bottom = slice(0, 32), slice(32, 64)
    return scatter_both(
        scatter_part(scratch, 0, lambda at: dkv_ref.at[0, :, at, top], stored_in(total, slice(0, 32))),
        scatter_part(scratch, 1, lambda at: dkv_ref.at[0, :, at, bottom], stored_in(total, slice(32, 64))),
        scatter_part(scratch, 2, lambda at: dkv_ref.at[1, at, :, top], stored_in(total, slice(64, 96))),
        scatter_part(scratch, 3, lambda at: dkv_ref.at[1, at, :, bottom], stored_in(total, slice(96, 128))),
        copies,
        scatter_direct,
    )


def replica_partners():
    me = lax.axis_index("replica")
    return me, me + 1 - 2 * lax.rem(me, 2), lax.rem(me + 2, 4), 3 - me


def other_section():
    return {"section": 1 - lax.axis_index("section")}


def exchange(
    own_ref, all_ref, total_ref, near_terms, part, far_part, near_sum, part_in, far_in, near_in, copies, loads, work, greetings=2
):
    me, mate, next_, far = replica_partners()
    halves = (slice(0, 64), slice(64, 128))
    to_mate, to_next = {"replica": mate}, {"replica": next_}
    greeted(greetings)
    across = [copies(own_ref.at[half], all_ref.at[me, half], to_next) for half in halves]
    beside = copies(own_ref, all_ref.at[me], to_mate)
    forwards = [copies(all_ref.at[next_, half], all_ref.at[next_, half], to_mate, False) for half in halves]
    passed = [copies(far_part.at[index], far_in.at[index], to_mate, False) for index in (0, 1)]
    sums = [copies(near_sum.at[index], near_in.at[index], to_next, False) for index in (0, 1)]
    sent = copies(part, part_in, to_mate, False)
    all_ref[me] = own_ref[...]
    for each in loads:
        each.wait()

    def send_sum(index):
        passed[index].wait_recv()
        near_sum[index] = (near_terms[index] + far_in[index].astype(F32)).astype(BF)
        sums[index].start()

    def step(at, carry):
        one = jnp.where(at == 0, me, jnp.where(at == 3, mate, next_))
        two = jnp.where(at == 0, me, jnp.where(at == 3, mate, far))
        first_rows = pl.ds(pl.multiple_of(jnp.where(at == 2, 64, 0), 64), 64)
        second_rows = pl.ds(pl.multiple_of(jnp.where(at == 1, 0, 64), 64), 64)

        @pl.when(at == 1)
        def _():
            across[0].wait_recv()
            forwards[0].start()
            forwards[0].wait_recv()

        @pl.when(at == 2)
        def _():
            across[1].wait_recv()
            forwards[1].start()
            send_sum(0)
            forwards[1].wait_recv()

        @pl.when(at == 3)
        def _():
            send_sum(1)
            beside.wait_recv()

        terms = work([(one, first_rows), (two, second_rows)])

        @pl.when(at == 0)
        def _():
            total_ref[...] = terms

        for index in (0, 1):

            @pl.when(at == 1 + index)
            def _(index=index):
                near_terms[index] = terms[:64]
                far_part[index] = terms[64:].astype(BF)
                passed[index].start()

        @pl.when(at == 3)
        def _():
            part[...] = terms.astype(BF)
            sent.start()

        return carry

    lax.fori_loop(0, 4, step, 0)
    sent.wait_recv()
    total = total_ref[...] + part_in[...].astype(F32)
    for each in sums:
        each.wait_recv()
    total = total + near_in[...].reshape(ROWS, D).astype(F32)
    for each in across + [beside, sent] + forwards + passed + sums:
        each.wait_send()
    return total


EXCHANGE_SCRATCH = [
    pltpu.VMEM((D, QUARTER), BF),
    pltpu.VMEM((D, QUARTER), BF),
    pltpu.VMEM((QUARTER, D), BF),
    pltpu.VMEM((ROWS, D), F32),
    pltpu.VMEM((2, 64, D), F32),
    pltpu.VMEM((ROWS, D), BF),
    pltpu.VMEM((2, 64, D), BF),
    pltpu.VMEM((2, 64, D), BF),
    pltpu.VMEM((ROWS, D), BF),
    pltpu.VMEM((2, 64, D), BF),
    pltpu.VMEM((2, 64, D), BF),
    pltpu.SemaphoreType.DMA((11,)),
    pltpu.SemaphoreType.DMA((11,)),
    pltpu.SemaphoreType.DMA((18,)),
]


def mlp_start(hbm, vmem, local):
    me, mate, next_, far = replica_partners()
    signal([{"replica": mate}, {"replica": next_}])
    loads = [pltpu.make_async_copy(src, dst, local.at[i]) for i, (src, dst) in enumerate(zip(hbm[:2], vmem[:2]))]
    for at in range(16):
        skip = 80 * (at % 4) - DOWN_STARTS[at % 4]
        rows = pl.ds(304 * (at // 4) + 80 * (at % 4), DOWN_ROWS - skip)
        piece = hbm[2].at[at // 4, at % 4, pl.ds(skip, DOWN_ROWS - skip)]
        loads.append(pltpu.make_async_copy(piece, vmem[2].at[rows], local.at[2 + at]))
    for each in loads:
        each.start()
    return loads


def split_rows(value, parts):
    for index, (source, rows) in enumerate(parts):
        yield source, rows, value[64 * index : 64 * index + 64]


def mlp_forward_kernel(
    normed_ref, hidden_ref, gate_hbm, up_hbm, down_hbm, out_ref, all_ref, gate_ref, up_ref,
    gate_w, up_w, down_w, total_ref, near_terms, part, far_part, near_sum, part_in, far_in, near_in, send, recv, local
):
    loads = mlp_start((gate_hbm, up_hbm, down_hbm), (gate_w, up_w, down_w), local)

    def work(parts):
        rows = jnp.concatenate([all_ref[source, rows] for source, rows in parts], axis=0)
        gate = nn(rows, gate_w[...])
        up = nn(rows, up_w[...])
        for source, at, value in split_rows(gate, parts):
            gate_ref[source, at] = value.astype(BF)
        for source, at, value in split_rows(up, parts):
            up_ref[source, at] = value.astype(BF)
        product = (gate * jax.nn.sigmoid(gate) * up).astype(BF)
        return nn(product, down_w[...])

    total = exchange(
        normed_ref, all_ref, total_ref, near_terms, part, far_part, near_sum, part_in, far_in, near_in,
        Copies(send, recv), loads, work
    )
    out_ref[...] = (hidden_ref[...] + total).astype(BF)


def mlp_relay_kernel(
    normed_ref, hidden_ref, x_ref, gate_hbm, up_hbm, down_hbm, next_ref, all_ref, out_ref, relayed_ref,
    gate_w, up_w, down_w, total_ref, near_terms, part, far_part, near_sum, part_in, far_in, near_in, send, recv, local
):
    signal([other_section()])
    loads = mlp_start((gate_hbm, up_hbm, down_hbm), (gate_w, up_w, down_w), local)

    def work(parts):
        rows = jnp.concatenate([all_ref[source, rows] for source, rows in parts], axis=0)
        gate = nn(rows, gate_w[...])
        up = nn(rows, up_w[...])
        product = (gate * jax.nn.sigmoid(gate) * up).astype(BF)
        return nn(product, down_w[...])

    copies = Copies(send, recv)
    total = exchange(
        normed_ref, all_ref, total_ref, near_terms, part, far_part, near_sum, part_in, far_in, near_in,
        copies, loads, work, 3
    )
    out_ref[...] = (hidden_ref[...] + total).astype(BF)
    relay = copies(out_ref, relayed_ref, other_section(), False)

    @pl.when(lax.axis_index("section") == 0)
    def _():
        relay.start()
        next_ref[...] = x_ref[...]
        relay.wait_send()

    @pl.when(lax.axis_index("section") == 1)
    def _():
        relay.wait_recv()
        next_ref[...] = relayed_ref[...]


def mlp_relay(normed2, hidden, x, gate_w, up_w, down_w):
    return pl.pallas_call(
        mlp_relay_kernel,
        out_shape=shaped(ROWS, D),
        in_specs=[VMEM_SPEC] * 3 + [ANY_SPEC] * 3,
        scratch_shapes=[pltpu.VMEM((4, ROWS, D), BF), pltpu.VMEM((ROWS, D), BF), pltpu.VMEM((ROWS, D), BF)]
        + EXCHANGE_SCRATCH,
        compiler_params=params(2),
        name="mlp_relay",
    )(normed2, hidden, x, gate_w, up_w, down_w)


def mlp_forward(normed2, hidden, gate_w, up_w, down_w):
    return pl.pallas_call(
        mlp_forward_kernel,
        out_shape=(
            shaped(ROWS, D),
            shaped(4, ROWS, D),
            shaped(4, ROWS, QUARTER),
            shaped(4, ROWS, QUARTER),
        ),
        in_specs=[VMEM_SPEC] * 2 + [ANY_SPEC] * 3,
        scratch_shapes=EXCHANGE_SCRATCH,
        compiler_params=params(3),
        name="mlp_forward",
    )(normed2, hidden, gate_w, up_w, down_w)


def mlp_backward_kernel(
    dout_ref, gate_ref, up_ref, gate_hbm, up_hbm, down_hbm,
    dnormed_ref, all_ref, dgate_ref, dup_ref, product_ref,
    gate_w, up_w, down_w, total_ref, near_terms, part, far_part, near_sum, part_in, far_in, near_in, send, recv, local
):
    loads = mlp_start((gate_hbm, up_hbm, down_hbm), (gate_w, up_w, down_w), local)

    def work(parts):

        def stacked(ref):
            return jnp.concatenate([ref[source, rows] for source, rows in parts], axis=0)

        dproduct = nt(stacked(all_ref), down_w[...])
        gate = stacked(gate_ref).astype(F32)
        up = stacked(up_ref).astype(F32)
        s = jax.nn.sigmoid(gate)
        silu = gate * s
        product = (silu * up).astype(BF)
        dgate = (dproduct * up * (s * (1.0 + gate * (1.0 - s)))).astype(BF)
        dup = (dproduct * silu).astype(BF)
        for to, whole in ((product_ref, product), (dgate_ref, dgate), (dup_ref, dup)):
            for source, at, value in split_rows(whole, parts):
                to[source, at] = value
        return nt(dgate, gate_w[...]) + nt(dup, up_w[...])

    dnormed_ref[...] = exchange(
        dout_ref, all_ref, total_ref, near_terms, part, far_part, near_sum, part_in, far_in, near_in,
        Copies(send, recv), loads, work
    )


def mlp_backward(dout, gate, up, gate_w, up_w, down_w):
    return pl.pallas_call(
        mlp_backward_kernel,
        out_shape=(
            shaped(ROWS, D, dtype=F32),
            shaped(4, ROWS, D),
            shaped(4, ROWS, QUARTER),
            shaped(4, ROWS, QUARTER),
            shaped(4, ROWS, QUARTER),
        ),
        in_specs=[VMEM_SPEC] * 3 + [ANY_SPEC] * 3,
        scratch_shapes=EXCHANGE_SCRATCH,
        compiler_params=params(4),
        name="mlp_backward",
    )(dout, gate, up, gate_w, up_w, down_w)


def outputs_kernel(
    gate, up, down, qkv, out, gate_out, up_out, down_out, qkv_out, out_out, bias_out, value_out, gain1_out, gain2_out
):
    for r in range(4):
        lanes = slice(QUARTER * r, QUARTER * r + QUARTER)
        gate_out[:, lanes] = gate[r].astype(F32)
        up_out[:, lanes] = up[r].astype(F32)
        skip = 80 * r - DOWN_STARTS[r]
        down_out[80 * r : DOWN_STARTS[r] + DOWN_ROWS] = down[r, skip:].astype(F32)
    qkv_out[:32] = qkv[0]
    qkv_out[32:] = qkv[1, :24]
    out_out[:32] = out[0]
    out_out[32:] = out[1, :24]
    small = qkv[1, 24:][:1]
    bias_out[...] = small[:, :64]
    value_out[...] = small[:, 64:72]
    gain1_out[...] = small[:, 72:128]
    gain2_out[...] = small[:, 128:184]


def outputs(gate, up, down, qkv, out):
    return local_call(
        outputs_kernel,
        "outputs",
        (
            shaped(56, FF, dtype=F32),
            shaped(56, FF, dtype=F32),
            shaped(FF // 16, D, dtype=F32),
            shaped(56, QKV, dtype=F32),
            shaped(56, D, dtype=F32),
            shaped(1, 64, dtype=F32),
            shaped(1, 8, dtype=F32),
            shaped(1, 56, dtype=F32),
            shaped(1, 56, dtype=F32),
        ),
    )(gate, up, down, qkv, out)


def turn(values, cosine, sine, sign):
    width = values.shape[1]
    up = pltpu.roll(values, width - HALF, 1)
    down = pltpu.roll(values, HALF, 1)
    lane = lax.broadcasted_iota(jnp.int32, values.shape, 1)
    swapped = jnp.where(lax.rem(lane, 2 * HALF) < HALF, up, down)
    repeat = width // KV
    cosine = jnp.concatenate([cosine] * repeat, axis=1)
    sine = jnp.concatenate([sine] * repeat, axis=1)
    return values * cosine + sign * (swapped * sine)


def front_work(x_ref, w_ref, b_ref, g_ref, cos_ref, sin_ref, normed_ref, q_ref, kv_ref, copies, ready):
    z, y, along_y, along_z = grid_place()
    x = x_ref[...].astype(F32)
    inverse = lax.rsqrt(jnp.mean(x * x, axis=-1, keepdims=True) + EPSILON)
    normed = (x * inverse * g_ref[...]).astype(BF)
    normed_ref[...] = normed
    projected = nn(normed, w_ref[:, D:]) + b_ref[:, D:]
    turned = turn(projected[:, :KV], cos_ref[...], sin_ref[...], 1.0)
    kv = jnp.concatenate([turned, projected[:, KV:]], axis=1).astype(BF)
    kv_ref[0, z, y] = kv[:64]
    kv_ref[1, z, y] = kv[64:]
    if ready:
        ready()
    top, bottom = (slice(0, 32), slice(None)), (slice(32, 64), slice(None))
    steps = gather_both(
        y_then_z(kv_ref.at[0], *top),
        y_then_z(kv_ref.at[0], *bottom),
        z_then_y(kv_ref.at[1], *top),
        z_then_y(kv_ref.at[1], *bottom),
        copies,
        gather_direct,
        gather_direct,
    )
    next(steps)
    projected = nn(normed, w_ref[:, :D]) + b_ref[:, :D]
    q_ref[...] = turn(projected, cos_ref[...], sin_ref[...], 1.0).astype(BF)
    return steps


def front_kernel(x_ref, w_ref, b_ref, g_ref, cos_ref, sin_ref, normed_ref, q_ref, kv_ref, send, recv):
    z, y, along_y, along_z = grid_place()
    signal(neighbours(along_y, along_z))
    steps = front_work(
        x_ref, w_ref, b_ref, g_ref, cos_ref, sin_ref, normed_ref, q_ref, kv_ref,
        Copies(send, recv), lambda: greeted(6)
    )
    run(steps)


def front(x, w_qkv, b_qkv, g_attn, cosine, sine):
    return pl.pallas_call(
        front_kernel,
        out_shape=(shaped(ROWS, D), shaped(ROWS, D), shaped(2, 4, 4, 64, 2 * KV)),
        scratch_shapes=[pltpu.SemaphoreType.DMA((24,)), pltpu.SemaphoreType.DMA((24,))],
        compiler_params=params(6),
        name="front",
    )(x, w_qkv, b_qkv, g_attn, cosine, sine)


def low_lanes(rows):
    return lax.broadcasted_iota(jnp.int32, (rows, KV), 1) < KV // 2


def spread(kv_ref, start, to_ref):
    mixed = kv_ref[:, :, :, :, start : start + KV].reshape(LEN, KV)
    other = pltpu.roll(mixed.astype(F32), KV // 2, 1).astype(BF)
    low = low_lanes(LEN)
    to_ref[0] = jnp.where(low, mixed, other)
    to_ref[1] = mixed
    to_ref[2] = jnp.where(low, other, mixed)


def fill_bias(kseg_ref, bias_refs):
    first_row = 64 * lax.axis_index("group")
    for block, bias_ref in enumerate(bias_refs):
        keys = SPAN * (block + 1)
        kpos = lax.broadcasted_iota(jnp.int32, (64, keys), 1)
        qpos = SPAN * block + first_row + lax.broadcasted_iota(jnp.int32, (64, keys), 0)
        kseg = jnp.broadcast_to(kseg_ref[:, :keys], (64, keys)).astype(F32)
        qseg = jnp.sum(jnp.where(kpos == qpos, kseg, 0.0), axis=1, keepdims=True)
        bias_ref[...] = jnp.where((kpos <= qpos) & (kseg == qseg), 0.0, NEGATIVE)


def two_heads(pair):
    low = low_lanes(64)
    zero = jnp.zeros_like(pair)
    return jnp.concatenate([jnp.where(low, pair, zero), jnp.where(low, zero, pair)], axis=0)


def one_pair(stacked):
    return jnp.where(low_lanes(64), stacked[:64], stacked[64:])


def softmax(queries, keys, bias_ref):
    count = keys.shape[0]
    scores = nt(queries, keys).reshape(2, 64, count) + bias_ref[...][None]
    highest = jnp.max(scores, axis=-1, keepdims=True)
    exponent = jnp.exp(scores - highest)
    total = jnp.sum(exponent, axis=-1, keepdims=True)
    return (exponent * (1.0 / total)).reshape(2 * 64, count)


def variant_of(pair):
    return jnp.where(pair < 3, 0, jnp.where(pair == 3, 1, 2))


def attention_work(
    x_ref, q_ref, kv_ref, kseg_ref, w_ref, g_ref, context_ref, hidden_ref, normed_ref,
    keys_ref, values_ref, bias0, bias1, between=None
):
    spread(kv_ref, 0, keys_ref)
    spread(kv_ref, KV, values_ref)
    fill_bias(kseg_ref, (bias0, bias1))

    def one(pair, carry):
        if between:
            pl.when(pair == between[0])(between[1])
        variant = variant_of(pair)
        lanes = pl.ds(pl.multiple_of(pair * KV, KV), KV)
        for block, bias_ref in enumerate((bias0, bias1)):
            rows = slice(64 * block, 64 * block + 64)
            keys = pl.ds(0, SPAN * (block + 1))
            queries = two_heads(q_ref[rows, lanes] * SCALE).astype(BF)
            weights = softmax(queries, keys_ref[variant, keys], bias_ref).astype(BF)
            context = nn(weights, values_ref[variant, keys])
            context_ref[rows, lanes] = one_pair(context).astype(BF)
        return carry

    lax.fori_loop(0, PAIRS, one, 0)
    hidden = x_ref[...].astype(F32) + nn(context_ref[...], w_ref[...])
    hidden_ref[...] = hidden
    inverse = lax.rsqrt(jnp.mean(hidden * hidden, axis=-1, keepdims=True) + EPSILON)
    normed_ref[...] = (hidden * inverse * g_ref[...]).astype(BF)


ATTENTION_SCRATCH = [
    pltpu.VMEM((3, LEN, KV), BF),
    pltpu.VMEM((3, LEN, KV), BF),
    pltpu.VMEM((64, SPAN), F32),
    pltpu.VMEM((64, LEN), F32),
]


def attention(x, q, kv, kseg, w_out, g_mlp):
    return local_call(
        attention_work,
        "attention",
        (shaped(ROWS, D), shaped(ROWS, D, dtype=F32), shaped(ROWS, D)),
        ATTENTION_SCRATCH,
    )(x, q, kv, kseg, w_out, g_mlp)


def norm_backward(values, gain, grads):
    inverse = lax.rsqrt(jnp.mean(values * values, axis=-1, keepdims=True) + EPSILON)
    scaled = grads * gain
    dvalues = inverse * scaled - values * (
        inverse * inverse * inverse * jnp.mean(scaled * values, axis=-1, keepdims=True)
    )
    return dvalues, jnp.sum(grads * values * inverse, axis=0, keepdims=True)


def attention_backward_work(
    dout_ref, dnormed_ref, hidden_ref, g_ref, w_ref, q_ref, kv_ref, kseg_ref,
    dhidden_ref, dlow_ref, dq_ref, dkv_ref, dgain_ref,
    keys_ref, values_ref, bias0, bias1, dcontext_ref, dkeys, dvalues, between=None
):
    dnorm, dgain = norm_backward(hidden_ref[...], g_ref[...], dnormed_ref[...])
    dgain_ref[...] = dgain
    dhidden = dout_ref[...].astype(F32) + dnorm
    dhidden_ref[...] = dhidden
    dlow = dhidden.astype(BF)
    dlow_ref[...] = dlow
    dcontext_ref[...] = nt(dlow, w_ref[...]).astype(BF)
    spread(kv_ref, 0, keys_ref)
    spread(kv_ref, KV, values_ref)
    fill_bias(kseg_ref, (bias0, bias1))
    dkeys[...] = jnp.zeros_like(dkeys)
    dvalues[...] = jnp.zeros_like(dvalues)

    def one(pair, carry):
        if between:
            pl.when(pair == between[0])(between[1])
        variant = variant_of(pair)
        lanes = pl.ds(pl.multiple_of(pair * KV, KV), KV)
        for block, bias_ref in enumerate((bias0, bias1)):
            rows = slice(64 * block, 64 * block + 64)
            keys = pl.ds(0, SPAN * (block + 1))
            queries = two_heads(q_ref[rows, lanes] * SCALE).astype(BF)
            dcontext = two_heads(dcontext_ref[rows, lanes])
            key_rows = keys_ref[variant, keys]
            weights = softmax(queries, key_rows, bias_ref)
            dweights = nt(dcontext, values_ref[variant, keys])
            inner = jnp.sum(weights * dweights, axis=-1, keepdims=True)
            dscores = (weights * (dweights - inner)).astype(BF)
            dq_ref[rows, lanes] = one_pair(nn(dscores, key_rows)) * SCALE
            dkeys[variant, keys] += tn(dscores, queries)
            dvalues[variant, keys] += tn(weights.astype(BF), dcontext)
        return carry

    lax.fori_loop(0, PAIRS, one, 0)
    low = low_lanes(LEN)
    for start, total in ((0, dkeys), (KV, dvalues)):
        head0 = total[0] + pltpu.roll(total[0], KV // 2, 1)
        head1 = total[2] + pltpu.roll(total[2], KV // 2, 1)
        whole = (jnp.where(low, head0, head1) + total[1]).astype(BF)
        dkv_ref[:, :, :, :, start : start + KV] = whole.reshape(2, 4, 4, 64, KV)


ATTENTION_BACKWARD_OUT = (
    shaped(ROWS, D, dtype=F32),
    shaped(ROWS, D),
    shaped(ROWS, D, dtype=F32),
    shaped(2, 4, 4, 64, 2 * KV),
    shaped(1, D, dtype=F32),
)
ATTENTION_BACKWARD_SCRATCH = ATTENTION_SCRATCH + [
    pltpu.VMEM((ROWS, D), BF),
    pltpu.VMEM((3, LEN, KV), F32),
    pltpu.VMEM((3, LEN, KV), F32),
]


def attention_backward(*operands):
    return local_call(
        attention_backward_work, "attention_backward", ATTENTION_BACKWARD_OUT, ATTENTION_BACKWARD_SCRATCH
    )(*operands)


def rear_query(dq_ref, cos_ref, sin_ref, w_ref, dprojected_ref, dbias_ref):
    dquery = turn(dq_ref[...], cos_ref[...], sin_ref[...], -1.0).astype(BF)
    dprojected_ref[:, :D] = dquery
    dbias_ref[:, :D] = jnp.sum(dquery.astype(F32), axis=0, keepdims=True)
    return nt(dquery, w_ref[:, :D])


def rear_rest(
    dnormed, total, cos_ref, sin_ref, w_ref, x_ref, g_ref, dhidden_ref, dprojected_ref, dinput_ref, dgain_ref, dbias_ref
):
    turned = turn(total[:, :KV], cos_ref[...], sin_ref[...], -1.0)
    dkv = jnp.concatenate([turned, total[:, KV:]], axis=1).astype(BF)
    dprojected_ref[:, D:] = dkv
    dbias_ref[:, D:] = jnp.sum(dkv.astype(F32), axis=0, keepdims=True)
    dnormed = dnormed + nt(dkv, w_ref[:, D:])
    dnorm, dgain = norm_backward(x_ref[...].astype(F32), g_ref[...], dnormed)
    dgain_ref[...] = dgain
    dinput_ref[...] = (dhidden_ref[...] + dnorm).astype(BF)


REAR_SCRATCH = [
    pltpu.VMEM((ROWS, QKV), BF),
    pltpu.VMEM((1, D), F32),
    pltpu.VMEM((1, QKV), F32),
    pltpu.VMEM((ROWS, 2 * KV), F32),
] + scatter_scratch(*[(32, 2 * KV)] * 4)


def rear_kernel(
    dkv_ref, dq_ref, cos_ref, sin_ref, w_ref, x_ref, g_ref, dhidden_ref, cotangent_ref, next_ref,
    dinput_ref, returned_ref, dprojected_ref, dgain_ref, dbias_ref, total, *rest
):
    scratch, (send, recv) = rest[:-2], rest[-2:]
    z, y, along_y, along_z = grid_place()
    signal(neighbours(along_y, along_z) + [other_section()])
    greeted(7)
    copies = Copies(send, recv)
    steps = kv_sums(dkv_ref, total, scratch, copies)
    next(steps)
    dnormed = rear_query(dq_ref, cos_ref, sin_ref, w_ref, dprojected_ref, dbias_ref)
    run(steps)
    rear_rest(
        dnormed, total, cos_ref, sin_ref, w_ref, x_ref, g_ref, dhidden_ref,
        dprojected_ref, dinput_ref, dgain_ref, dbias_ref
    )
    relay = copies(dinput_ref, returned_ref, other_section(), False)

    @pl.when(lax.axis_index("section") == 1)
    def _():
        relay.start()
        next_ref[...] = cotangent_ref[...]
        relay.wait_send()

    @pl.when(lax.axis_index("section") == 0)
    def _():
        relay.wait_recv()
        next_ref[...] = returned_ref[...]


def rear(*operands):
    return pl.pallas_call(
        rear_kernel,
        out_shape=shaped(ROWS, D),
        scratch_shapes=[pltpu.VMEM((ROWS, D), BF), pltpu.VMEM((ROWS, D), BF)]
        + REAR_SCRATCH
        + [pltpu.SemaphoreType.DMA((25,)), pltpu.SemaphoreType.DMA((25,))],
        compiler_params=params(7),
        name="rear",
    )(*operands)


TAIL_SCRATCH = [
    pltpu.VMEM((4, 4, 56, QUARTER), BF),
    pltpu.VMEM((4, 4, 56, QUARTER), BF),
    pltpu.VMEM((4, 4, DOWN_ROWS, D), BF),
    pltpu.VMEM((56, QUARTER), BF),
    pltpu.VMEM((56, QUARTER), BF),
    pltpu.VMEM((DOWN_ROWS, D), BF),
    pltpu.VMEM((4, 4, 64, QKV), BF),
    pltpu.VMEM((4, 4, 64, D), BF),
    pltpu.VMEM((4, 4, 32, QKV), BF),
    pltpu.VMEM((4, 4, 32, D), BF),
    pltpu.VMEM((32, QKV), F32),
    pltpu.VMEM((32, D), F32),
    pltpu.VMEM((32, QKV), BF),
    pltpu.VMEM((32, D), BF),
    pltpu.VMEM((32, QKV), BF),
    pltpu.VMEM((32, D), BF),
]
LATE = (0, 1, 2, 4, 5, 6, 13, 14, 15, 16, 18, 19)
TAIL_COPIES = 24 + 36 + 48 + 2 + 13


def tail_kernel(*refs):
    refs = list(refs)

    def take(count):
        taken = refs[:count]
        del refs[:count]
        return taken

    operands = take(20)
    dinput_ref, gate_all, up_all, down_all, qkv_all, out_all = take(6)
    attention_out = take(5)
    dhidden_ref, dlow_ref, dq_ref, dkv_ref, dgain2_ref = attention_out
    attention_scratch = take(len(ATTENTION_BACKWARD_SCRATCH))
    dprojected_ref, dgain1_ref, dbias_ref, total = take(4)
    kv_bufs = take(24)
    mlp_term_refs, mlp_sum_refs = take(3), take(3)
    qkv_terms, out_terms, qkv_half, out_half, qkv_sum, out_sum, qkv_low, out_low, qkv_in, out_in = take(10)
    mlp_bufs, qkv_bufs, out_bufs = take(24), take(24), take(24)
    send, recv, local, load_sems = take(4)
    loads = []
    for index, (at, vmem) in enumerate(zip(LATE, take(len(LATE)))):
        loads.append(pltpu.make_async_copy(operands[at], vmem, load_sems.at[index]))
        loads[-1].start()
        operands[at] = vmem
    attention_in, mlp_in = operands[:8], operands[8:13]
    cos_ref, sin_ref, qkv_w, x_ref, gain1_ref, normed_ref, context_ref = operands[13:]

    z, y, along_y, along_z = grid_place()
    me, mate, next_, far = replica_partners()
    core = lax.rem(me, 2)
    to_mate, to_next = {"replica": mate}, {"replica": next_}
    target, source, stays = quarter_route()
    moves = jnp.logical_not(stays)
    signal(neighbours(along_y, along_z) + [to_mate, to_next])
    rows_all, dgate, dup, product, dout_all = mlp_in
    wide_terms(rows_all, dgate, mlp_term_refs[0])

    @pl.when(moves)
    def _():
        signal([target])
        greeted(9)

    @pl.when(stays)
    def _():
        greeted(8)

    copies = Copies(send, recv)
    mlp = mlp_sums(*mlp_term_refs, *mlp_sum_refs, mlp_bufs, copies)
    next(mlp)
    wide_terms(rows_all, dup, mlp_term_refs[1])
    next(mlp)
    down_rows_terms(product, dout_all, mlp_term_refs[2])
    next(mlp)
    for each in loads:
        each.wait()
    attention_backward_work(*attention_in, *attention_out, *attention_scratch, (3, lambda: next(mlp)))
    kv = kv_sums(dkv_ref, total, kv_bufs, copies)
    next(kv)
    next(mlp)

    mine = pl.ds(pl.multiple_of(32 * core, 32), 32)
    theirs = pl.ds(pl.multiple_of(32 - 32 * core, 32), 32)

    def add_mate(sent, terms, half):
        sent.wait_recv()
        half[...] = (terms[:, :, mine].astype(F32) + half[...].astype(F32)).astype(BF)

    dnormed = rear_query(dq_ref, cos_ref, sin_ref, qkv_w, dprojected_ref, dbias_ref)
    next(kv)
    whole = tn(context_ref[...], dlow_ref[...])
    for at in range(16):
        rows = jnp.concatenate([whole[56 * at : 56 * at + 56], jnp.zeros((8, D), F32)], axis=0)
        out_terms[at // 4, at % 4] = rows.astype(BF)
    out_sent = copies(out_terms.at[:, :, theirs], out_half, to_mate)
    next(kv)
    add_mate(out_sent, out_terms, out_half)
    outs = half_sums(out_half, out_sum, 512, out_bufs, copies)
    next(outs)
    run(kv)
    next(mlp)
    rear_rest(
        dnormed, total, cos_ref, sin_ref, qkv_w, x_ref, gain1_ref, dhidden_ref,
        dprojected_ref, dinput_ref, dgain1_ref, dbias_ref
    )
    next(mlp)
    whole = tn(normed_ref[...], dprojected_ref[...])
    dbias, dgain1, dgain2 = dbias_ref[...], dgain1_ref[...], dgain2_ref[...]
    for at in range(16):
        small = jnp.concatenate(
            [
                dbias[:, 64 * at : 64 * at + 64],
                dbias[:, D + KV + 8 * at : D + KV + 8 * at + 8],
                dgain1[:, 56 * at : 56 * at + 56],
                dgain2[:, 56 * at : 56 * at + 56],
                jnp.zeros((1, QKV - 184), F32),
            ],
            axis=1,
        )
        rows = jnp.concatenate([whole[56 * at : 56 * at + 56], jnp.broadcast_to(small, (8, QKV))], axis=0)
        qkv_terms[at // 4, at % 4] = rows.astype(BF)
    qkv_sent = copies(qkv_terms.at[:, :, theirs], qkv_half, to_mate)
    next(outs)
    next(outs)
    run(mlp)

    gate, up, down = mlp_sum_refs
    moved = pltpu.make_async_remote_copy(
        src_ref=down,
        dst_ref=down_all.at[source["replica"]],
        send_sem=local.at[0],
        recv_sem=local.at[1],
        device_id=source,
        device_id_type=MESH,
    )
    stayed = pltpu.make_async_copy(down, down_all.at[me], local.at[2])

    @pl.when(moves)
    def _():
        moved.start()

    @pl.when(stays)
    def _():
        stayed.start()

    pairs = ((gate, gate_all), (up, up_all))
    across = [copies(ref, all_ref.at[me], to_next) for ref, all_ref in pairs]
    beside = [copies(ref, all_ref.at[me], to_mate) for ref, all_ref in pairs]
    add_mate(qkv_sent, qkv_terms, qkv_half)
    dense = half_sums(qkv_half, qkv_sum, 640, qkv_bufs, copies)
    next(dense)
    for ref, all_ref in pairs:
        all_ref[me] = ref[...]
    run(outs)
    out_low[...] = out_sum[...].astype(BF)
    out_sum_sent = copies(out_low, out_in, to_next)
    next(dense)
    next(dense)

    @pl.when(moves)
    def _():
        moved.wait()

    @pl.when(stays)
    def _():
        stayed.wait()

    across.append(copies(down_all.at[me], down_all.at[me], to_next))
    beside.append(copies(down_all.at[me], down_all.at[me], to_mate))
    run(dense)
    qkv_low[...] = qkv_sum[...].astype(BF)
    sums = [copies(qkv_low, qkv_in, to_next), out_sum_sent]
    for came, all_ref in zip(across, (gate_all, up_all, down_all)):
        came.wait_recv()
        beside.append(copies(all_ref.at[next_], all_ref.at[next_], to_mate))
    sums[0].wait_recv()
    qkv_all[core] = qkv_sum[...] + qkv_in[...].astype(F32)
    sums[1].wait_recv()
    out_all[core] = out_sum[...] + out_in[...].astype(F32)
    beside += [copies(ref.at[core], ref.at[core], to_mate) for ref in (qkv_all, out_all)]
    for each in beside:
        each.wait_recv()
    for each in [out_sent, qkv_sent] + across + beside + sums:
        each.wait_send()


def tail(*operands):
    return pl.pallas_call(
        tail_kernel,
        out_shape=(
            shaped(ROWS, D),
            shaped(4, 56, QUARTER),
            shaped(4, 56, QUARTER),
            shaped(4, DOWN_ROWS, D),
            shaped(2, 32, QKV, dtype=F32),
            shaped(2, 32, D, dtype=F32),
        ),
        scratch_shapes=[pltpu.VMEM(each.shape, each.dtype) for each in ATTENTION_BACKWARD_OUT]
        + ATTENTION_BACKWARD_SCRATCH
        + REAR_SCRATCH
        + TAIL_SCRATCH
        + scatter_scratch(*MLP_SUMS_SHAPES)
        + scatter_scratch((16, 640), (16, 640), (16, QKV - 640), (16, QKV - 640))
        + scatter_scratch((16, 512), (16, 512), (16, D - 512), (16, D - 512))
        + [
            pltpu.SemaphoreType.DMA((TAIL_COPIES,)),
            pltpu.SemaphoreType.DMA((TAIL_COPIES,)),
            pltpu.SemaphoreType.DMA((3,)),
            pltpu.SemaphoreType.DMA((len(LATE),)),
        ]
        + [pltpu.VMEM(operands[at].shape, operands[at].dtype) for at in LATE],
        in_specs=[ANY_SPEC if at in LATE else VMEM_SPEC for at in range(20)],
        compiler_params=params(1),
        name="tail",
    )(*operands)


def rotary(group):
    lane = np.arange(KV)
    frequency = jnp.asarray(THETA ** (-(lane % HALF) * 2.0 / (2 * HALF)), F32)
    sign = jnp.asarray(np.where(lane % (2 * HALF) < HALF, -1.0, 1.0), F32)
    row = lax.broadcasted_iota(jnp.int32, (ROWS, KV), 0)
    positions = group * 64 + lax.rem(row, 64) + SPAN * (row // 64)
    angles = positions.astype(F32) * frequency[None, :]
    return jnp.cos(angles), jnp.sin(angles) * sign[None, :]


def body(inputs, cotangent, segments, w_qkv, b_qkv, w_out, w_gate, w_up, w_down, g_attn, g_mlp):
    group = lax.axis_index("group")
    replica = lax.axis_index("replica")
    core = lax.rem(replica, 2)

    down_piece = lax.dynamic_slice(w_down[0], (jnp.minimum(80 * replica, 224), 0), (DOWN_ROWS, D))
    gate_piece = lax.dynamic_slice(w_gate[0], (0, replica * QUARTER), (D // 16, QUARTER))
    up_piece = lax.dynamic_slice(w_up[0], (0, replica * QUARTER), (D // 16, QUARTER))
    small = jnp.concatenate([b_qkv[0], g_attn[0], g_mlp[0]])
    small = jnp.pad(small[None], ((0, 7), (0, QKV - small.shape[0])))
    qkv_piece = lax.dynamic_slice(jnp.concatenate([w_qkv[0], small], axis=0), (32 * core, 0), (32, QKV))
    out_piece = lax.dynamic_slice(jnp.pad(w_out[0], ((0, 8), (0, 0))), (32 * core, 0), (32, D))

    cosine, sine = rotary(group)
    kseg = segments
    x_in = inputs[0].reshape(ROWS, D)
    cotangent_in = cotangent[0].reshape(ROWS, D)
    gate_w, up_w, down_w, qkv_w, out_w, bias, gain1, gain2, hidden, normed2 = first(
        gate_piece, up_piece, down_piece, qkv_piece, out_piece, x_in, cosine, sine, kseg
    )
    gate_w = gate_w.reshape(D, QUARTER)
    up_w = up_w.reshape(D, QUARTER)

    def forward(x):
        normed, q, kv = front(x, qkv_w, bias, gain1, cosine, sine)
        context, hidden, normed2 = attention(x, q, kv, kseg, out_w, gain2)
        output, normed2_all, gate, up = mlp_forward(normed2, hidden, gate_w, up_w, down_w)
        return output, (x, normed, q, kv, context, hidden, normed2_all, gate, up)

    def backward_start(dout):
        dnormed2, *grads = mlp_backward(dout, gate, up, gate_w, up_w, down_w)
        dout_all, dgate, dup, product = grads
        return (dout, dnormed2, hidden, gain2, out_w, q, kv, kseg), (normed2_all, dgate, dup, product, dout_all)

    output, kept = forward(mlp_relay(normed2, hidden, x_in, gate_w, up_w, down_w))
    x, normed, q, kv, context, hidden, normed2_all, gate, up = kept
    operands, _ = backward_start(cotangent_in)
    dhidden, _, dq, dkv, _ = attention_backward(*operands)
    dout = rear(dkv, dq, cosine, sine, qkv_w, x, gain1, dhidden, cotangent_in)
    operands, mlp_operands = backward_start(dout)
    dinput, *parts = tail(*operands, *mlp_operands, cosine, sine, qkv_w, x, gain1, normed, context)
    grad_gate, grad_up, grad_down, grad_qkv, grad_out, bias, value_bias, gain1, gain2 = outputs(*parts)
    return (
        output.reshape(1, 1, 2, 64, D),
        dinput.reshape(1, 1, 2, 64, D),
        grad_qkv[None],
        bias,
        value_bias,
        grad_out[None],
        grad_gate[None],
        grad_up[None],
        grad_down[None],
        gain1,
        gain2,
    )


def solution(mesh):
    in_specs = (
        P("replica", None, "group", None),
        P("replica", None, "group", None),
        P("replica", None),
        P("section", "group", None),
        P("section", "group"),
        P("section", "group", None),
        P("section", "group", None),
        P("section", "group", None),
        P("section", "group", None),
        P("section", "group"),
        P("section", "group"),
    )
    out_specs = (
        P("section", "replica", None, "group", None),
        P("section", "replica", None, "group", None),
        P("section", "group", None),
        P("section", "group"),
        P("section", "group"),
        P("section", "group", None),
        P("section", "group", None),
        P("section", "group", None),
        P("section", "group", None),
        P("section", "group"),
        P("section", "group"),
    )
    return jax.shard_map(body, mesh=mesh, in_specs=in_specs, out_specs=out_specs, check_vma=False)
```

```python
import functools

import jax
import jax.numpy as jnp
import numpy as np
from jax import lax
from jax.experimental import pallas as pl
from jax.experimental.pallas import tpu as pltpu
from jax.sharding import PartitionSpec as P

D = 896
HEADS = 14
KV = 128
HALF = 32
FF = 4864
QUARTER = FF // 4
QKV = 1152
ROWS = 128
SPAN = 1024
LEN = 2048
PAIRS = 7
EPSILON = 1e-06
THETA = 1000000.0
NEGATIVE = -1e30
SCALE = 0.125
MESH = pl.DeviceIdType.MESH
BF = jnp.bfloat16
F32 = jnp.float32
VMEM_SPEC = pl.BlockSpec(memory_space=pltpu.VMEM)
ANY_SPEC = pl.BlockSpec(memory_space=pl.ANY)


def nn(a, b):
    return lax.dot_general(a, b, (((1,), (0,)), ((), ())), preferred_element_type=F32)


def nt(a, b):
    return lax.dot_general(a, b, (((1,), (1,)), ((), ())), preferred_element_type=F32)


def tn(a, b):
    return lax.dot_general(a, b, (((0,), (0,)), ((), ())), preferred_element_type=F32)


def params(collective_id=None, megabytes=60):
    limit = megabytes * 1024 * 1024
    if collective_id is None:
        return pltpu.CompilerParams(vmem_limit_bytes=limit)
    return pltpu.CompilerParams(vmem_limit_bytes=limit, collective_id=collective_id, has_side_effects=True)


def shaped(*shape, dtype=BF):
    return jax.ShapeDtypeStruct(shape, dtype)


def local_call(kernel, name, out_shape, scratch=(), megabytes=30):
    return pl.pallas_call(
        kernel,
        out_shape=out_shape,
        scratch_shapes=list(scratch),
        compiler_params=params(None, megabytes),
        name=name,
    )


def signal(devices):
    barrier = pltpu.get_barrier_semaphore()
    for device in devices:
        pl.semaphore_signal(barrier, inc=1, device_id=device, device_id_type=MESH)


def greeted(count):
    pl.semaphore_wait(pltpu.get_barrier_semaphore(), count)


def grid_place():
    me = lax.axis_index("group")
    z = me // 4
    y = lax.rem(me, 4)

    def along_y(step):
        return {"group": z * 4 + lax.rem(y + step, 4)}

    def along_z(step):
        return {"group": lax.rem(z + step, 4) * 4 + y}

    return z, y, along_y, along_z


def neighbours(along_y, along_z):
    return [along(step) for along in (along_y, along_z) for step in (1, 3, 2)]


class Copies:
    def __init__(self, send, recv):
        self.send, self.recv, self.used = send, recv, 0

    def __call__(self, src, dst, device, start=True):
        index = self.used
        self.used += 1
        each = pltpu.make_async_remote_copy(
            src_ref=src,
            dst_ref=dst,
            send_sem=self.send.at[index],
            recv_sem=self.recv.at[index],
            device_id=device,
            device_id_type=MESH,
        )
        if start:
            each.start()
        return each


def gather_phase(firsts, seconds, place, device_at, copies):
    def copy(block, slot, step):
        return copies(block(slot), block(slot), device_at(step), False)

    firsts_right = [copy(block, place, 1) for block in firsts]
    seconds_left = [copy(block, place, 3) for block in seconds]
    others = [copy(block, place, 3) for block in firsts] + [copy(block, place, 1) for block in seconds]
    relays = [copy(block, lax.rem(place + 3, 4), 1) for block in firsts]
    relays += [copy(block, lax.rem(place + 1, 4), 3) for block in seconds]

    def start():
        for each in firsts_right + seconds_left + others:
            each.start()

    def relay():
        for came, each in zip(firsts_right + seconds_left, relays):
            came.wait_recv()
            each.start()

    def finish():
        for each in others + relays:
            each.wait_recv()
        for each in firsts_right + seconds_left + others + relays:
            each.wait_send()

    return start, relay, finish


def gather_direct(firsts, seconds, place, device_at, copies):
    sent = []
    for block in firsts + seconds:
        sent += [copies(block(place), block(place), device_at(step), False) for step in (1, 3, 2)]

    def start():
        for each in sent:
            each.start()

    def finish():
        for each in sent:
            each.wait_recv()
        for each in sent:
            each.wait_send()

    return start, lambda: None, finish


def gather_both(first_a, second_a, first_b, second_b, copies, phase=gather_phase, then=gather_phase):
    z, y, along_y, along_z = grid_place()
    start_a, relay_a, finish_a = phase([first_a[0]], [second_a[0]], y, along_y, copies)
    start_b, relay_b, finish_b = phase([first_b[0]], [second_b[0]], z, along_z, copies)
    then_a, last_a, end_a = then([first_a[1]], [second_a[1]], z, along_z, copies)
    then_b, last_b, end_b = then([first_b[1]], [second_b[1]], y, along_y, copies)
    start_a()
    start_b()
    yield
    relay_a()
    relay_b()
    yield
    finish_a()
    then_a()
    finish_b()
    then_b()
    yield
    last_a()
    last_b()
    yield
    end_a()
    end_b()


def gather_split(first_a, second_a, first_b, second_b, copies):
    z, y, along_y, along_z = grid_place()
    slim = [
        gather_phase([first_a[0]], [second_a[0]], y, along_y, copies),
        gather_phase([first_b[0]], [second_b[0]], z, along_z, copies),
    ]

    def wide(half):
        def part(function):
            return [lambda at: function(at, half)]

        return [
            gather_phase(part(first_a[1]), part(second_a[1]), z, along_z, copies),
            gather_phase(part(first_b[1]), part(second_b[1]), y, along_y, copies),
        ]

    halves = [wide(slice(0, 2)), wide(slice(2, 4))]
    for start, _, _ in slim:
        start()
    yield
    for _, relay, _ in slim:
        relay()
    yield
    for _, _, finish in slim:
        finish()
    for phases in halves:
        for start, _, _ in phases:
            start()
        yield
        for _, relay, _ in phases:
            relay()
        yield
    for phases in halves:
        for _, _, finish in phases:
            finish()


def run(steps):
    for _ in steps:
        pass


def y_then_z(ref, *tail):
    z = lax.axis_index("group") // 4
    return (lambda at: ref.at[(z, at, *tail)]), (lambda at, part=slice(None): ref.at[(at, part, *tail)])


def z_then_y(ref, *tail):
    y = lax.rem(lax.axis_index("group"), 4)
    return (lambda at: ref.at[(at, y, *tail)]), (lambda at, part=slice(None): ref.at[(part, at, *tail)])


def quarter_route():
    group, replica = lax.axis_index("group"), lax.axis_index("replica")
    target = {"group": 4 * lax.rem(group, 4) + replica, "replica": group // 4}
    source = {"group": 4 * replica + group // 4, "replica": lax.rem(group, 4)}
    stays = (target["group"] == group) & (target["replica"] == replica)
    return target, source, stays


def first_kernel(
    gate, up, down, qkv, out, x_ref, cos_ref, sin_ref, kseg_ref,
    gate_all, up_all, down_all, qkv_w, out_w, bias_ref, gain1_ref, gain2_ref, hidden_ref, normed2_ref,
    qkv_all, out_all, normed_ref, q_ref, kv_ref, context_ref, keys_ref, values_ref, bias0, bias1, send, recv, local
):
    z, y, along_y, along_z = grid_place()
    core = lax.rem(lax.axis_index("replica"), 2)
    mate = {"replica": lax.axis_index("replica") + 1 - 2 * core}
    target, source, stays = quarter_route()
    moves = jnp.logical_not(stays)
    signal(neighbours(along_y, along_z) + [mate])
    places = (qkv_all.at[core, z, y], out_all.at[core, z, y], gate_all.at[z, y], up_all.at[z, y])
    own = []
    for index, (src, dst) in enumerate(zip((qkv, out, gate, up), places)):
        own.append(pltpu.make_async_copy(src, dst, local.at[index]))
        own[-1].start()
    there = target["group"]
    moved = pltpu.make_async_remote_copy(
        src_ref=down,
        dst_ref=down_all.at[there // 4, lax.rem(there, 4)],
        send_sem=local.at[5],
        recv_sem=local.at[6],
        device_id=target,
        device_id_type=MESH,
    )
    stayed = pltpu.make_async_copy(down, down_all.at[z, y], local.at[4])

    @pl.when(moves)
    def _():
        signal([source])
        greeted(8)
        moved.start()

    @pl.when(stays)
    def _():
        greeted(7)
        stayed.start()

    copies = Copies(send, recv)
    own[0].wait()
    own[1].wait()
    top, bottom = (slice(0, 16), slice(None)), (slice(16, 32), slice(None))
    dense = gather_both(
        y_then_z(qkv_all.at[core], *top),
        y_then_z(qkv_all.at[core], *bottom),
        z_then_y(out_all.at[core], *top),
        z_then_y(out_all.at[core], *bottom),
        copies,
        gather_direct,
    )
    next(dense)
    next(dense)
    next(dense)
    own[2].wait()
    own[3].wait()

    @pl.when(moves)
    def _():
        moved.wait()

    @pl.when(stays)
    def _():
        stayed.wait()

    left, right = (slice(None), slice(0, 512)), (slice(None), slice(512, D))
    wide = gather_split(
        y_then_z(gate_all), y_then_z(down_all, *left), z_then_y(up_all), z_then_y(down_all, *right), copies
    )
    next(wide)
    next(dense)
    next(wide)
    run(dense)
    halves = [copies(ref.at[core], ref.at[core], mate) for ref in (qkv_all, out_all)]
    next(wide)
    for each in halves:
        each.wait()
    for at in range(16):
        rows, cut = 56 * at, 56 * at + 32
        qkv_w[rows:cut] = qkv_all[0, at // 4, at % 4]
        qkv_w[cut : rows + 56] = qkv_all[1, at // 4, at % 4, :24]
        out_w[rows:cut] = out_all[0, at // 4, at % 4]
        out_w[cut : rows + 56] = out_all[1, at // 4, at % 4, :24]
    small = [qkv_all[1, at // 4, at % 4, 24:32].astype(F32)[:1] for at in range(16)]
    bias_ref[...] = jnp.concatenate([each[:, :72] for each in small], axis=1)
    gain1_ref[...] = jnp.concatenate([each[:, 72:128] for each in small], axis=1)
    gain2_ref[...] = jnp.concatenate([each[:, 128:184] for each in small], axis=1)
    kv = front_work(x_ref, qkv_w, bias_ref, gain1_ref, cos_ref, sin_ref, normed_ref, q_ref, kv_ref, copies, None)
    next(kv)
    next(wide)
    next(kv)
    next(kv)
    next(wide)
    run(kv)
    attention_work(
        x_ref, q_ref, kv_ref, kseg_ref, out_w, gain2_ref, context_ref, hidden_ref, normed2_ref,
        keys_ref, values_ref, bias0, bias1, (4, lambda: next(wide))
    )
    run(wide)


def first(gate, up, down, qkv, out, x, cosine, sine, kseg):
    return pl.pallas_call(
        first_kernel,
        out_shape=(
            shaped(4, 4, *gate.shape),
            shaped(4, 4, *up.shape),
            shaped(4, 4, *down.shape),
            shaped(D, QKV),
            shaped(D, D),
            shaped(1, QKV, dtype=F32),
            shaped(1, D, dtype=F32),
            shaped(1, D, dtype=F32),
            shaped(ROWS, D, dtype=F32),
            shaped(ROWS, D),
        ),
        in_specs=[ANY_SPEC] * 5 + [VMEM_SPEC] * 4,
        out_specs=[ANY_SPEC] * 3 + [VMEM_SPEC] * 7,
        scratch_shapes=[
            pltpu.VMEM((2, 4, 4, *qkv.shape), BF),
            pltpu.VMEM((2, 4, 4, *out.shape), BF),
            pltpu.VMEM((ROWS, D), BF),
            pltpu.VMEM((ROWS, D), BF),
            pltpu.VMEM((2, 4, 4, 64, 2 * KV), BF),
            pltpu.VMEM((ROWS, D), BF),
        ]
        + ATTENTION_SCRATCH
        + [
            pltpu.SemaphoreType.DMA((86,)),
            pltpu.SemaphoreType.DMA((86,)),
            pltpu.SemaphoreType.DMA((7,)),
        ],
        compiler_params=params(0),
        name="first",
    )(gate, up, down, qkv, out, x, cosine, sine, kseg)


def scatter_phase(firsts, seconds, place, device_at, copies):
    right, left, far = (lax.rem(place + step, 4) for step in (1, 3, 2))

    def load(ref):
        return ref[...].astype(F32)

    def copy(src, dst, step):
        return copies(src, dst, device_at(step), False)

    first_far = [copy(block(far), bufs[0], 1) for block, bufs, put in firsts]
    second_far = [copy(block(far), bufs[0], 3) for block, bufs, put in seconds]
    first_near = [copy(block(left), bufs[2], 3) for block, bufs, put in firsts]
    second_near = [copy(block(right), bufs[1], 1) for block, bufs, put in seconds]
    first_sum = [copy(bufs[0], bufs[1], 1) for block, bufs, put in firsts]
    second_sum = [copy(bufs[0], bufs[2], 3) for block, bufs, put in seconds]

    def start(which=(0, 1)):
        for index in which:
            for each in ((first_far + first_near), (second_far + second_near))[index]:
                each.start()

    def pass_on():
        for came, each, (block, bufs, put) in zip(first_far, first_sum, firsts):
            came.wait_recv()
            bufs[0][...] = (load(block(right)) + load(bufs[0])).astype(BF)
            each.start()
        for came, each, (block, bufs, put) in zip(second_far, second_sum, seconds):
            came.wait_recv()
            bufs[0][...] = (load(block(left)) + load(bufs[0])).astype(BF)
            each.start()

    def finish():
        near, far_sum = first_near + second_near, first_sum + second_sum
        for one, two, (block, bufs, put) in zip(near, far_sum, firsts + seconds):
            one.wait_recv()
            two.wait_recv()
            put(load(block(place)) + load(bufs[1]) + load(bufs[2]))
        for each in first_far + second_far + near + far_sum:
            each.wait_send()

    return start, pass_on, finish


def scatter_direct(firsts, seconds, place, device_at, copies):
    parts = firsts + seconds
    sent = []
    for block, bufs, put in parts:
        sent.append(
            [
                copies(block(lax.rem(place + step, 4)), bufs[index], device_at(step), False)
                for index, step in enumerate((1, 3, 2))
            ]
        )

    def start():
        for each in sum(sent, []):
            each.start()

    def finish():
        for came, (block, bufs, put) in zip(sent, parts):
            total = block(place)[...].astype(F32)
            for each, landed in zip(came, bufs):
                each.wait_recv()
                total = total + landed[...].astype(F32)
            for each in came:
                each.wait_send()
            put(total)

    return start, lambda: None, finish


def scatter_both(first_a, second_a, first_b, second_b, copies, phase=scatter_phase):
    z, y, along_y, along_z = grid_place()

    def wide(part):
        block, bufs, _, _ = part
        return [(block, bufs, stored_in(bufs[1]))]

    def slim(part):
        _, kept, bufs, put = part
        return [((lambda at: kept[1].at[at]), bufs, put)]

    start_a, pass_a, finish_a = phase(wide(first_a), wide(second_a), y, along_y, copies)
    start_b, pass_b, finish_b = phase(wide(first_b), wide(second_b), z, along_z, copies)
    then_a, last_a, end_a = phase(slim(first_a), slim(second_a), z, along_z, copies)
    then_b, last_b, end_b = phase(slim(first_b), slim(second_b), y, along_y, copies)
    start_a()
    start_b()
    yield
    pass_a()
    pass_b()
    yield
    finish_a()
    then_a()
    finish_b()
    then_b()
    yield
    last_a()
    last_b()
    yield
    end_a()
    end_b()


def scatter_split(first_a, second_a, first_b, second_b, copies):
    z, y, along_y, along_z = grid_place()

    def slim(part):
        _, kept, bufs, put = part
        return [((lambda at: kept[1].at[at]), bufs, put)]

    def halved(half):
        def wide(part):
            block, bufs, _, _ = part
            views = [each.at[half] for each in bufs]
            return [(lambda at: block(at, half), views, stored_in(views[1]))]

        return [
            scatter_phase(wide(first_a), wide(second_a), y, along_y, copies),
            scatter_phase(wide(first_b), wide(second_b), z, along_z, copies),
        ]

    halves = [halved(pl.ds(0, 2)), halved(pl.ds(2, 2))]
    last_phases = [
        scatter_phase(slim(first_a), slim(second_a), z, along_z, copies),
        scatter_phase(slim(first_b), slim(second_b), y, along_y, copies),
    ]
    for start, _, _ in halves[0]:
        start([0])
        yield
    for start, _, _ in halves[0]:
        start([1])
    yield
    for _, pass_on, _ in halves[0]:
        pass_on()
    for start, _, _ in halves[1]:
        start()
    yield
    for _, pass_on, _ in halves[1]:
        pass_on()
    yield
    for phases in halves:
        for _, _, finish in phases:
            finish()
    for start, _, _ in last_phases:
        start()
    yield
    for _, pass_on, _ in last_phases:
        pass_on()
    yield
    for _, _, finish in last_phases:
        finish()


def scatter_scratch(*shapes):
    scratch = []
    for shape in shapes:
        scratch += [pltpu.VMEM((4, *shape), BF)] * 3 + [pltpu.VMEM(shape, BF)] * 3
    return scratch


def scatter_part(scratch, index, block, put):
    mine = scratch[6 * index : 6 * index + 6]
    return block, mine[:3], mine[3:], put


def stored_in(ref, *at):
    def put(value):
        ref[at if at else ...] = value.astype(ref.dtype)

    return put


DOWN_STARTS = (0, 80, 160, 224)
DOWN_ROWS = 80


def flat(ref):
    return ref[...].reshape(4 * ROWS, ref.shape[-1])


def wide_terms(rows_ref, grads_ref, terms):
    whole = tn(flat(rows_ref), flat(grads_ref))
    for at in range(16):
        terms[at // 4, at % 4] = whole[56 * at : 56 * at + 56].astype(BF)


def down_rows_terms(product_ref, dout_ref, terms):
    whole = tn(flat(product_ref), flat(dout_ref)).astype(BF)
    for at in range(16):
        start = 304 * (at // 4) + DOWN_STARTS[at % 4]
        terms[at // 4, at % 4] = whole[start : start + DOWN_ROWS]


def mlp_sums(gate_terms, up_terms, down_terms, gate_out, up_out, down_out, scratch, copies):
    left, right = slice(0, 512), slice(512, D)
    return scatter_split(
        scatter_part(scratch, 0, lambda at, part: gate_terms.at[part, at], stored_in(gate_out)),
        scatter_part(
            scratch, 2, lambda at, part: down_terms.at[part, at, :, left], stored_in(down_out, slice(None), left)
        ),
        scatter_part(scratch, 1, lambda at, part: up_terms.at[at, part], stored_in(up_out)),
        scatter_part(
            scratch, 3, lambda at, part: down_terms.at[at, part, :, right], stored_in(down_out, slice(None), right)
        ),
        copies,
    )


MLP_SUMS_SHAPES = ((56, QUARTER), (56, QUARTER), (DOWN_ROWS, 512), (DOWN_ROWS, D - 512))


def half_sums(half, to, cut, scratch, copies):
    top, bottom = slice(0, 16), slice(16, 32)
    left, right = slice(0, cut), slice(cut, to.shape[1])
    return scatter_both(
        scatter_part(scratch, 0, lambda at: half.at[:, at, top, left], stored_in(to, top, left)),
        scatter_part(scratch, 1, lambda at: half.at[:, at, bottom, left], stored_in(to, bottom, left)),
        scatter_part(scratch, 2, lambda at: half.at[at, :, top, right], stored_in(to, top, right)),
        scatter_part(scratch, 3, lambda at: half.at[at, :, bottom, right], stored_in(to, bottom, right)),
        copies,
        scatter_direct,
    )


def kv_sums(dkv_ref, total, scratch, copies):
    top, bottom = slice(0, 32), slice(32, 64)
    return scatter_both(
        scatter_part(scratch, 0, lambda at: dkv_ref.at[0, :, at, top], stored_in(total, slice(0, 32))),
        scatter_part(scratch, 1, lambda at: dkv_ref.at[0, :, at, bottom], stored_in(total, slice(32, 64))),
        scatter_part(scratch, 2, lambda at: dkv_ref.at[1, at, :, top], stored_in(total, slice(64, 96))),
        scatter_part(scratch, 3, lambda at: dkv_ref.at[1, at, :, bottom], stored_in(total, slice(96, 128))),
        copies,
        scatter_direct,
    )


def replica_partners():
    me = lax.axis_index("replica")
    return me, me + 1 - 2 * lax.rem(me, 2), lax.rem(me + 2, 4), 3 - me


def other_section():
    return {"section": 1 - lax.axis_index("section")}


def exchange(
    own_ref, all_ref, total_ref, near_terms, part, far_part, near_sum, part_in, far_in, near_in, copies, loads, work, greetings=2
):
    me, mate, next_, far = replica_partners()
    halves = (slice(0, 64), slice(64, 128))
    to_mate, to_next = {"replica": mate}, {"replica": next_}
    greeted(greetings)
    across = [copies(own_ref.at[half], all_ref.at[me, half], to_next) for half in halves]
    beside = copies(own_ref, all_ref.at[me], to_mate)
    forwards = [copies(all_ref.at[next_, half], all_ref.at[next_, half], to_mate, False) for half in halves]
    passed = [copies(far_part.at[index], far_in.at[index], to_mate, False) for index in (0, 1)]
    sums = [copies(near_sum.at[index], near_in.at[index], to_next, False) for index in (0, 1)]
    sent = copies(part, part_in, to_mate, False)
    all_ref[me] = own_ref[...]
    for each in loads:
        each.wait()

    def send_sum(index):
        passed[index].wait_recv()
        near_sum[index] = (near_terms[index] + far_in[index].astype(F32)).astype(BF)
        sums[index].start()

    def step(at, carry):
        one = jnp.where(at == 0, me, jnp.where(at == 3, mate, next_))
        two = jnp.where(at == 0, me, jnp.where(at == 3, mate, far))
        first_rows = pl.ds(pl.multiple_of(jnp.where(at == 2, 64, 0), 64), 64)
        second_rows = pl.ds(pl.multiple_of(jnp.where(at == 1, 0, 64), 64), 64)

        @pl.when(at == 1)
        def _():
            across[0].wait_recv()
            forwards[0].start()
            forwards[0].wait_recv()

        @pl.when(at == 2)
        def _():
            across[1].wait_recv()
            forwards[1].start()
            send_sum(0)
            forwards[1].wait_recv()

        @pl.when(at == 3)
        def _():
            send_sum(1)
            beside.wait_recv()

        terms = work([(one, first_rows), (two, second_rows)])

        @pl.when(at == 0)
        def _():
            total_ref[...] = terms

        for index in (0, 1):

            @pl.when(at == 1 + index)
            def _(index=index):
                near_terms[index] = terms[:64]
                far_part[index] = terms[64:].astype(BF)
                passed[index].start()

        @pl.when(at == 3)
        def _():
            part[...] = terms.astype(BF)
            sent.start()

        return carry

    lax.fori_loop(0, 4, step, 0)
    sent.wait_recv()
    total = total_ref[...] + part_in[...].astype(F32)
    for each in sums:
        each.wait_recv()
    total = total + near_in[...].reshape(ROWS, D).astype(F32)
    for each in across + [beside, sent] + forwards + passed + sums:
        each.wait_send()
    return total


EXCHANGE_SCRATCH = [
    pltpu.VMEM((D, QUARTER), BF),
    pltpu.VMEM((D, QUARTER), BF),
    pltpu.VMEM((QUARTER, D), BF),
    pltpu.VMEM((ROWS, D), F32),
    pltpu.VMEM((2, 64, D), F32),
    pltpu.VMEM((ROWS, D), BF),
    pltpu.VMEM((2, 64, D), BF),
    pltpu.VMEM((2, 64, D), BF),
    pltpu.VMEM((ROWS, D), BF),
    pltpu.VMEM((2, 64, D), BF),
    pltpu.VMEM((2, 64, D), BF),
    pltpu.SemaphoreType.DMA((11,)),
    pltpu.SemaphoreType.DMA((11,)),
    pltpu.SemaphoreType.DMA((18,)),
]


def mlp_start(hbm, vmem, local):
    me, mate, next_, far = replica_partners()
    signal([{"replica": mate}, {"replica": next_}])
    loads = [pltpu.make_async_copy(src, dst, local.at[i]) for i, (src, dst) in enumerate(zip(hbm[:2], vmem[:2]))]
    for at in range(16):
        skip = 80 * (at % 4) - DOWN_STARTS[at % 4]
        rows = pl.ds(304 * (at // 4) + 80 * (at % 4), DOWN_ROWS - skip)
        piece = hbm[2].at[at // 4, at % 4, pl.ds(skip, DOWN_ROWS - skip)]
        loads.append(pltpu.make_async_copy(piece, vmem[2].at[rows], local.at[2 + at]))
    for each in loads:
        each.start()
    return loads


def split_rows(value, parts):
    for index, (source, rows) in enumerate(parts):
        yield source, rows, value[64 * index : 64 * index + 64]


def mlp_forward_kernel(
    normed_ref, hidden_ref, gate_hbm, up_hbm, down_hbm, out_ref, all_ref, gate_ref, up_ref,
    gate_w, up_w, down_w, total_ref, near_terms, part, far_part, near_sum, part_in, far_in, near_in, send, recv, local
):
    loads = mlp_start((gate_hbm, up_hbm, down_hbm), (gate_w, up_w, down_w), local)

    def work(parts):
        rows = jnp.concatenate([all_ref[source, rows] for source, rows in parts], axis=0)
        gate = nn(rows, gate_w[...])
        up = nn(rows, up_w[...])
        for source, at, value in split_rows(gate, parts):
            gate_ref[source, at] = value.astype(BF)
        for source, at, value in split_rows(up, parts):
            up_ref[source, at] = value.astype(BF)
        product = (gate * jax.nn.sigmoid(gate) * up).astype(BF)
        return nn(product, down_w[...])

    total = exchange(
        normed_ref, all_ref, total_ref, near_terms, part, far_part, near_sum, part_in, far_in, near_in,
        Copies(send, recv), loads, work
    )
    out_ref[...] = (hidden_ref[...] + total).astype(BF)


def mlp_relay_kernel(
    normed_ref, hidden_ref, x_ref, gate_hbm, up_hbm, down_hbm, next_ref, all_ref, out_ref, relayed_ref,
    gate_w, up_w, down_w, total_ref, near_terms, part, far_part, near_sum, part_in, far_in, near_in, send, recv, local
):
    signal([other_section()])
    loads = mlp_start((gate_hbm, up_hbm, down_hbm), (gate_w, up_w, down_w), local)

    def work(parts):
        rows = jnp.concatenate([all_ref[source, rows] for source, rows in parts], axis=0)
        gate = nn(rows, gate_w[...])
        up = nn(rows, up_w[...])
        product = (gate * jax.nn.sigmoid(gate) * up).astype(BF)
        return nn(product, down_w[...])

    copies = Copies(send, recv)
    total = exchange(
        normed_ref, all_ref, total_ref, near_terms, part, far_part, near_sum, part_in, far_in, near_in,
        copies, loads, work, 3
    )
    out_ref[...] = (hidden_ref[...] + total).astype(BF)
    relay = copies(out_ref, relayed_ref, other_section(), False)

    @pl.when(lax.axis_index("section") == 0)
    def _():
        relay.start()
        next_ref[...] = x_ref[...]
        relay.wait_send()

    @pl.when(lax.axis_index("section") == 1)
    def _():
        relay.wait_recv()
        next_ref[...] = relayed_ref[...]


def mlp_relay(normed2, hidden, x, gate_w, up_w, down_w):
    return pl.pallas_call(
        mlp_relay_kernel,
        out_shape=shaped(ROWS, D),
        in_specs=[VMEM_SPEC] * 3 + [ANY_SPEC] * 3,
        scratch_shapes=[pltpu.VMEM((4, ROWS, D), BF), pltpu.VMEM((ROWS, D), BF), pltpu.VMEM((ROWS, D), BF)]
        + EXCHANGE_SCRATCH,
        compiler_params=params(2, 26),
        name="mlp_relay",
    )(normed2, hidden, x, gate_w, up_w, down_w)


def mlp_forward(normed2, hidden, gate_w, up_w, down_w):
    return pl.pallas_call(
        mlp_forward_kernel,
        out_shape=(
            shaped(ROWS, D),
            shaped(4, ROWS, D),
            shaped(4, ROWS, QUARTER),
            shaped(4, ROWS, QUARTER),
        ),
        in_specs=[VMEM_SPEC] * 2 + [ANY_SPEC] * 3,
        scratch_shapes=EXCHANGE_SCRATCH,
        compiler_params=params(3, 26),
        name="mlp_forward",
    )(normed2, hidden, gate_w, up_w, down_w)


def mlp_backward_kernel(
    dout_ref, gate_ref, up_ref, gate_hbm, up_hbm, down_hbm,
    dnormed_ref, all_ref, dgate_ref, dup_ref, product_ref,
    gate_w, up_w, down_w, total_ref, near_terms, part, far_part, near_sum, part_in, far_in, near_in, send, recv, local
):
    loads = mlp_start((gate_hbm, up_hbm, down_hbm), (gate_w, up_w, down_w), local)

    def work(parts):

        def stacked(ref):
            return jnp.concatenate([ref[source, rows] for source, rows in parts], axis=0)

        dproduct = nt(stacked(all_ref), down_w[...])
        gate = stacked(gate_ref).astype(F32)
        up = stacked(up_ref).astype(F32)
        s = jax.nn.sigmoid(gate)
        silu = gate * s
        product = (silu * up).astype(BF)
        dgate = (dproduct * up * (s * (1.0 + gate * (1.0 - s)))).astype(BF)
        dup = (dproduct * silu).astype(BF)
        for to, whole in ((product_ref, product), (dgate_ref, dgate), (dup_ref, dup)):
            for source, at, value in split_rows(whole, parts):
                to[source, at] = value
        return nt(dgate, gate_w[...]) + nt(dup, up_w[...])

    dnormed_ref[...] = exchange(
        dout_ref, all_ref, total_ref, near_terms, part, far_part, near_sum, part_in, far_in, near_in,
        Copies(send, recv), loads, work
    )


def mlp_backward(dout, gate, up, gate_w, up_w, down_w):
    return pl.pallas_call(
        mlp_backward_kernel,
        out_shape=(
            shaped(ROWS, D, dtype=F32),
            shaped(4, ROWS, D),
            shaped(4, ROWS, QUARTER),
            shaped(4, ROWS, QUARTER),
            shaped(4, ROWS, QUARTER),
        ),
        in_specs=[VMEM_SPEC] * 3 + [ANY_SPEC] * 3,
        scratch_shapes=EXCHANGE_SCRATCH,
        compiler_params=params(4, 30),
        name="mlp_backward",
    )(dout, gate, up, gate_w, up_w, down_w)


def outputs_kernel(
    gate, up, down, qkv, out, gate_out, up_out, down_out, qkv_out, out_out, bias_out, value_out, gain1_out, gain2_out
):
    for r in range(4):
        lanes = slice(QUARTER * r, QUARTER * r + QUARTER)
        gate_out[:, lanes] = gate[r].astype(F32)
        up_out[:, lanes] = up[r].astype(F32)
        skip = 80 * r - DOWN_STARTS[r]
        down_out[80 * r : DOWN_STARTS[r] + DOWN_ROWS] = down[r, skip:].astype(F32)
    qkv_out[:32] = qkv[0]
    qkv_out[32:] = qkv[1, :24]
    out_out[:32] = out[0]
    out_out[32:] = out[1, :24]
    small = qkv[1, 24:][:1]
    bias_out[...] = small[:, :64]
    value_out[...] = small[:, 64:72]
    gain1_out[...] = small[:, 72:128]
    gain2_out[...] = small[:, 128:184]


def outputs(gate, up, down, qkv, out):
    return local_call(
        outputs_kernel,
        "outputs",
        (
            shaped(56, FF, dtype=F32),
            shaped(56, FF, dtype=F32),
            shaped(FF // 16, D, dtype=F32),
            shaped(56, QKV, dtype=F32),
            shaped(56, D, dtype=F32),
            shaped(1, 64, dtype=F32),
            shaped(1, 8, dtype=F32),
            shaped(1, 56, dtype=F32),
            shaped(1, 56, dtype=F32),
        ),
    )(gate, up, down, qkv, out)


def turn(values, cosine, sine, sign):
    width = values.shape[1]
    up = pltpu.roll(values, width - HALF, 1)
    down = pltpu.roll(values, HALF, 1)
    lane = lax.broadcasted_iota(jnp.int32, values.shape, 1)
    swapped = jnp.where(lax.rem(lane, 2 * HALF) < HALF, up, down)
    repeat = width // KV
    cosine = jnp.concatenate([cosine] * repeat, axis=1)
    sine = jnp.concatenate([sine] * repeat, axis=1)
    return values * cosine + sign * (swapped * sine)


def front_work(x_ref, w_ref, b_ref, g_ref, cos_ref, sin_ref, normed_ref, q_ref, kv_ref, copies, ready):
    z, y, along_y, along_z = grid_place()
    x = x_ref[...].astype(F32)
    inverse = lax.rsqrt(jnp.mean(x * x, axis=-1, keepdims=True) + EPSILON)
    normed = (x * inverse * g_ref[...]).astype(BF)
    normed_ref[...] = normed
    projected = nn(normed, w_ref[:, D:]) + b_ref[:, D:]
    turned = turn(projected[:, :KV], cos_ref[...], sin_ref[...], 1.0)
    kv = jnp.concatenate([turned, projected[:, KV:]], axis=1).astype(BF)
    kv_ref[0, z, y] = kv[:64]
    kv_ref[1, z, y] = kv[64:]
    if ready:
        ready()
    top, bottom = (slice(0, 32), slice(None)), (slice(32, 64), slice(None))
    steps = gather_both(
        y_then_z(kv_ref.at[0], *top),
        y_then_z(kv_ref.at[0], *bottom),
        z_then_y(kv_ref.at[1], *top),
        z_then_y(kv_ref.at[1], *bottom),
        copies,
        gather_direct,
        gather_direct,
    )
    next(steps)
    projected = nn(normed, w_ref[:, :D]) + b_ref[:, :D]
    q_ref[...] = turn(projected, cos_ref[...], sin_ref[...], 1.0).astype(BF)
    return steps


def front_kernel(x_ref, w_ref, b_ref, g_ref, cos_ref, sin_ref, normed_ref, q_ref, kv_ref, send, recv):
    z, y, along_y, along_z = grid_place()
    signal(neighbours(along_y, along_z))
    steps = front_work(
        x_ref, w_ref, b_ref, g_ref, cos_ref, sin_ref, normed_ref, q_ref, kv_ref,
        Copies(send, recv), lambda: greeted(6)
    )
    run(steps)


def front(x, w_qkv, b_qkv, g_attn, cosine, sine):
    return pl.pallas_call(
        front_kernel,
        out_shape=(shaped(ROWS, D), shaped(ROWS, D), shaped(2, 4, 4, 64, 2 * KV)),
        scratch_shapes=[pltpu.SemaphoreType.DMA((24,)), pltpu.SemaphoreType.DMA((24,))],
        compiler_params=params(6, 14),
        name="front",
    )(x, w_qkv, b_qkv, g_attn, cosine, sine)


def low_lanes(rows):
    return lax.broadcasted_iota(jnp.int32, (rows, KV), 1) < KV // 2


def spread(kv_ref, start, to_ref):
    mixed = kv_ref[:, :, :, :, start : start + KV].reshape(LEN, KV)
    other = pltpu.roll(mixed.astype(F32), KV // 2, 1).astype(BF)
    low = low_lanes(LEN)
    to_ref[0] = jnp.where(low, mixed, other)
    to_ref[1] = mixed
    to_ref[2] = jnp.where(low, other, mixed)


def fill_bias(kseg_ref, bias_refs):
    first_row = 64 * lax.axis_index("group")
    for block, bias_ref in enumerate(bias_refs):
        keys = SPAN * (block + 1)
        kpos = lax.broadcasted_iota(jnp.int32, (64, keys), 1)
        qpos = SPAN * block + first_row + lax.broadcasted_iota(jnp.int32, (64, keys), 0)
        kseg = jnp.broadcast_to(kseg_ref[:, :keys], (64, keys)).astype(F32)
        qseg = jnp.sum(jnp.where(kpos == qpos, kseg, 0.0), axis=1, keepdims=True)
        bias_ref[...] = jnp.where((kpos <= qpos) & (kseg == qseg), 0.0, NEGATIVE)


def two_heads(pair):
    low = low_lanes(64)
    zero = jnp.zeros_like(pair)
    return jnp.concatenate([jnp.where(low, pair, zero), jnp.where(low, zero, pair)], axis=0)


def one_pair(stacked):
    return jnp.where(low_lanes(64), stacked[:64], stacked[64:])


def softmax(queries, keys, bias_ref):
    count = keys.shape[0]
    scores = nt(queries, keys).reshape(2, 64, count) + bias_ref[...][None]
    highest = jnp.max(scores, axis=-1, keepdims=True)
    exponent = jnp.exp(scores - highest)
    total = jnp.sum(exponent, axis=-1, keepdims=True)
    return (exponent * (1.0 / total)).reshape(2 * 64, count)


def variant_of(pair):
    return jnp.where(pair < 3, 0, jnp.where(pair == 3, 1, 2))


def attention_work(
    x_ref, q_ref, kv_ref, kseg_ref, w_ref, g_ref, context_ref, hidden_ref, normed_ref,
    keys_ref, values_ref, bias0, bias1, between=None
):
    spread(kv_ref, 0, keys_ref)
    spread(kv_ref, KV, values_ref)
    fill_bias(kseg_ref, (bias0, bias1))

    def one(pair, carry):
        if between:
            pl.when(pair == between[0])(between[1])
        variant = variant_of(pair)
        lanes = pl.ds(pl.multiple_of(pair * KV, KV), KV)
        for block, bias_ref in enumerate((bias0, bias1)):
            rows = slice(64 * block, 64 * block + 64)
            keys = pl.ds(0, SPAN * (block + 1))
            queries = two_heads(q_ref[rows, lanes] * SCALE).astype(BF)
            weights = softmax(queries, keys_ref[variant, keys], bias_ref).astype(BF)
            context = nn(weights, values_ref[variant, keys])
            context_ref[rows, lanes] = one_pair(context).astype(BF)
        return carry

    lax.fori_loop(0, PAIRS, one, 0)
    hidden = x_ref[...].astype(F32) + nn(context_ref[...], w_ref[...])
    hidden_ref[...] = hidden
    inverse = lax.rsqrt(jnp.mean(hidden * hidden, axis=-1, keepdims=True) + EPSILON)
    normed_ref[...] = (hidden * inverse * g_ref[...]).astype(BF)


ATTENTION_SCRATCH = [
    pltpu.VMEM((3, LEN, KV), BF),
    pltpu.VMEM((3, LEN, KV), BF),
    pltpu.VMEM((64, SPAN), F32),
    pltpu.VMEM((64, LEN), F32),
]


def attention(x, q, kv, kseg, w_out, g_mlp):
    return local_call(
        attention_work,
        "attention",
        (shaped(ROWS, D), shaped(ROWS, D, dtype=F32), shaped(ROWS, D)),
        ATTENTION_SCRATCH,
    )(x, q, kv, kseg, w_out, g_mlp)


def norm_backward(values, gain, grads):
    inverse = lax.rsqrt(jnp.mean(values * values, axis=-1, keepdims=True) + EPSILON)
    scaled = grads * gain
    dvalues = inverse * scaled - values * (
        inverse * inverse * inverse * jnp.mean(scaled * values, axis=-1, keepdims=True)
    )
    return dvalues, jnp.sum(grads * values * inverse, axis=0, keepdims=True)


def attention_backward_work(
    dout_ref, dnormed_ref, hidden_ref, g_ref, w_ref, q_ref, kv_ref, kseg_ref,
    dhidden_ref, dlow_ref, dq_ref, dkv_ref, dgain_ref,
    keys_ref, values_ref, bias0, bias1, dcontext_ref, dkeys, dvalues, between=None
):
    dnorm, dgain = norm_backward(hidden_ref[...], g_ref[...], dnormed_ref[...])
    dgain_ref[...] = dgain
    dhidden = dout_ref[...].astype(F32) + dnorm
    dhidden_ref[...] = dhidden
    dlow = dhidden.astype(BF)
    dlow_ref[...] = dlow
    dcontext_ref[...] = nt(dlow, w_ref[...]).astype(BF)
    spread(kv_ref, 0, keys_ref)
    spread(kv_ref, KV, values_ref)
    fill_bias(kseg_ref, (bias0, bias1))
    dkeys[...] = jnp.zeros_like(dkeys)
    dvalues[...] = jnp.zeros_like(dvalues)

    def one(pair, carry):
        if between:
            pl.when(pair == between[0])(between[1])
        variant = variant_of(pair)
        lanes = pl.ds(pl.multiple_of(pair * KV, KV), KV)
        for block, bias_ref in enumerate((bias0, bias1)):
            rows = slice(64 * block, 64 * block + 64)
            keys = pl.ds(0, SPAN * (block + 1))
            queries = two_heads(q_ref[rows, lanes] * SCALE).astype(BF)
            dcontext = two_heads(dcontext_ref[rows, lanes])
            key_rows = keys_ref[variant, keys]
            weights = softmax(queries, key_rows, bias_ref)
            dweights = nt(dcontext, values_ref[variant, keys])
            inner = jnp.sum(weights * dweights, axis=-1, keepdims=True)
            dscores = (weights * (dweights - inner)).astype(BF)
            dq_ref[rows, lanes] = one_pair(nn(dscores, key_rows)) * SCALE
            dkeys[variant, keys] += tn(dscores, queries)
            dvalues[variant, keys] += tn(weights.astype(BF), dcontext)
        return carry

    lax.fori_loop(0, PAIRS, one, 0)
    low = low_lanes(LEN)
    for start, total in ((0, dkeys), (KV, dvalues)):
        head0 = total[0] + pltpu.roll(total[0], KV // 2, 1)
        head1 = total[2] + pltpu.roll(total[2], KV // 2, 1)
        whole = (jnp.where(low, head0, head1) + total[1]).astype(BF)
        dkv_ref[:, :, :, :, start : start + KV] = whole.reshape(2, 4, 4, 64, KV)


ATTENTION_BACKWARD_OUT = (
    shaped(ROWS, D, dtype=F32),
    shaped(ROWS, D),
    shaped(ROWS, D, dtype=F32),
    shaped(2, 4, 4, 64, 2 * KV),
    shaped(1, D, dtype=F32),
)
ATTENTION_BACKWARD_SCRATCH = ATTENTION_SCRATCH + [
    pltpu.VMEM((ROWS, D), BF),
    pltpu.VMEM((3, LEN, KV), F32),
    pltpu.VMEM((3, LEN, KV), F32),
]


def attention_backward(*operands):
    return local_call(
        attention_backward_work, "attention_backward", ATTENTION_BACKWARD_OUT, ATTENTION_BACKWARD_SCRATCH
    )(*operands)


def rear_query(dq_ref, cos_ref, sin_ref, w_ref, dprojected_ref, dbias_ref):
    dquery = turn(dq_ref[...], cos_ref[...], sin_ref[...], -1.0).astype(BF)
    dprojected_ref[:, :D] = dquery
    dbias_ref[:, :D] = jnp.sum(dquery.astype(F32), axis=0, keepdims=True)
    return nt(dquery, w_ref[:, :D])


def rear_rest(
    dnormed, total, cos_ref, sin_ref, w_ref, x_ref, g_ref, dhidden_ref, dprojected_ref, dinput_ref, dgain_ref, dbias_ref
):
    turned = turn(total[:, :KV], cos_ref[...], sin_ref[...], -1.0)
    dkv = jnp.concatenate([turned, total[:, KV:]], axis=1).astype(BF)
    dprojected_ref[:, D:] = dkv
    dbias_ref[:, D:] = jnp.sum(dkv.astype(F32), axis=0, keepdims=True)
    dnormed = dnormed + nt(dkv, w_ref[:, D:])
    dnorm, dgain = norm_backward(x_ref[...].astype(F32), g_ref[...], dnormed)
    dgain_ref[...] = dgain
    dinput_ref[...] = (dhidden_ref[...] + dnorm).astype(BF)


REAR_SCRATCH = [
    pltpu.VMEM((ROWS, QKV), BF),
    pltpu.VMEM((1, D), F32),
    pltpu.VMEM((1, QKV), F32),
    pltpu.VMEM((ROWS, 2 * KV), F32),
] + scatter_scratch(*[(32, 2 * KV)] * 4)


def rear_kernel(
    dkv_ref, dq_ref, cos_ref, sin_ref, w_ref, x_ref, g_ref, dhidden_ref, cotangent_ref, next_ref,
    dinput_ref, returned_ref, dprojected_ref, dgain_ref, dbias_ref, total, *rest
):
    scratch, (send, recv) = rest[:-2], rest[-2:]
    z, y, along_y, along_z = grid_place()
    signal(neighbours(along_y, along_z) + [other_section()])
    greeted(7)
    copies = Copies(send, recv)
    steps = kv_sums(dkv_ref, total, scratch, copies)
    next(steps)
    dnormed = rear_query(dq_ref, cos_ref, sin_ref, w_ref, dprojected_ref, dbias_ref)
    run(steps)
    rear_rest(
        dnormed, total, cos_ref, sin_ref, w_ref, x_ref, g_ref, dhidden_ref,
        dprojected_ref, dinput_ref, dgain_ref, dbias_ref
    )
    relay = copies(dinput_ref, returned_ref, other_section(), False)

    @pl.when(lax.axis_index("section") == 1)
    def _():
        relay.start()
        next_ref[...] = cotangent_ref[...]
        relay.wait_send()

    @pl.when(lax.axis_index("section") == 0)
    def _():
        relay.wait_recv()
        next_ref[...] = returned_ref[...]


def rear(*operands):
    return pl.pallas_call(
        rear_kernel,
        out_shape=shaped(ROWS, D),
        scratch_shapes=[pltpu.VMEM((ROWS, D), BF), pltpu.VMEM((ROWS, D), BF)]
        + REAR_SCRATCH
        + [pltpu.SemaphoreType.DMA((25,)), pltpu.SemaphoreType.DMA((25,))],
        compiler_params=params(7, 16),
        name="rear",
    )(*operands)


TAIL_SCRATCH = [
    pltpu.VMEM((4, 4, 56, QUARTER), BF),
    pltpu.VMEM((4, 4, 56, QUARTER), BF),
    pltpu.VMEM((4, 4, DOWN_ROWS, D), BF),
    pltpu.VMEM((56, QUARTER), BF),
    pltpu.VMEM((56, QUARTER), BF),
    pltpu.VMEM((DOWN_ROWS, D), BF),
    pltpu.VMEM((4, 4, 64, QKV), BF),
    pltpu.VMEM((4, 4, 64, D), BF),
    pltpu.VMEM((4, 4, 32, QKV), BF),
    pltpu.VMEM((4, 4, 32, D), BF),
    pltpu.VMEM((32, QKV), F32),
    pltpu.VMEM((32, D), F32),
    pltpu.VMEM((32, QKV), BF),
    pltpu.VMEM((32, D), BF),
    pltpu.VMEM((32, QKV), BF),
    pltpu.VMEM((32, D), BF),
]
LATE = (0, 1, 2, 4, 5, 6, 13, 14, 15, 16, 18, 19)
TAIL_COPIES = 24 + 36 + 48 + 2 + 13


def tail_kernel(*refs):
    refs = list(refs)

    def take(count):
        taken = refs[:count]
        del refs[:count]
        return taken

    operands = take(20)
    dinput_ref, gate_all, up_all, down_all, qkv_all, out_all = take(6)
    attention_out = take(5)
    dhidden_ref, dlow_ref, dq_ref, dkv_ref, dgain2_ref = attention_out
    attention_scratch = take(len(ATTENTION_BACKWARD_SCRATCH))
    dprojected_ref, dgain1_ref, dbias_ref, total = take(4)
    kv_bufs = take(24)
    mlp_term_refs, mlp_sum_refs = take(3), take(3)
    qkv_terms, out_terms, qkv_half, out_half, qkv_sum, out_sum, qkv_low, out_low, qkv_in, out_in = take(10)
    mlp_bufs, qkv_bufs, out_bufs = take(24), take(24), take(24)
    send, recv, local, load_sems = take(4)
    loads = []
    for index, (at, vmem) in enumerate(zip(LATE, take(len(LATE)))):
        loads.append(pltpu.make_async_copy(operands[at], vmem, load_sems.at[index]))
        loads[-1].start()
        operands[at] = vmem
    attention_in, mlp_in = operands[:8], operands[8:13]
    cos_ref, sin_ref, qkv_w, x_ref, gain1_ref, normed_ref, context_ref = operands[13:]

    z, y, along_y, along_z = grid_place()
    me, mate, next_, far = replica_partners()
    core = lax.rem(me, 2)
    to_mate, to_next = {"replica": mate}, {"replica": next_}
    target, source, stays = quarter_route()
    moves = jnp.logical_not(stays)
    signal(neighbours(along_y, along_z) + [to_mate, to_next])
    rows_all, dgate, dup, product, dout_all = mlp_in
    wide_terms(rows_all, dgate, mlp_term_refs[0])

    @pl.when(moves)
    def _():
        signal([target])
        greeted(9)

    @pl.when(stays)
    def _():
        greeted(8)

    copies = Copies(send, recv)
    mlp = mlp_sums(*mlp_term_refs, *mlp_sum_refs, mlp_bufs, copies)
    next(mlp)
    wide_terms(rows_all, dup, mlp_term_refs[1])
    next(mlp)
    down_rows_terms(product, dout_all, mlp_term_refs[2])
    next(mlp)
    for each in loads:
        each.wait()
    attention_backward_work(*attention_in, *attention_out, *attention_scratch, (3, lambda: next(mlp)))
    kv = kv_sums(dkv_ref, total, kv_bufs, copies)
    next(kv)
    next(mlp)

    mine = pl.ds(pl.multiple_of(32 * core, 32), 32)
    theirs = pl.ds(pl.multiple_of(32 - 32 * core, 32), 32)

    def add_mate(sent, terms, half):
        sent.wait_recv()
        half[...] = (terms[:, :, mine].astype(F32) + half[...].astype(F32)).astype(BF)

    dnormed = rear_query(dq_ref, cos_ref, sin_ref, qkv_w, dprojected_ref, dbias_ref)
    next(kv)
    whole = tn(context_ref[...], dlow_ref[...])
    for at in range(16):
        rows = jnp.concatenate([whole[56 * at : 56 * at + 56], jnp.zeros((8, D), F32)], axis=0)
        out_terms[at // 4, at % 4] = rows.astype(BF)
    out_sent = copies(out_terms.at[:, :, theirs], out_half, to_mate)
    next(kv)
    add_mate(out_sent, out_terms, out_half)
    outs = half_sums(out_half, out_sum, 512, out_bufs, copies)
    next(outs)
    run(kv)
    rear_rest(
        dnormed, total, cos_ref, sin_ref, qkv_w, x_ref, gain1_ref, dhidden_ref,
        dprojected_ref, dinput_ref, dgain1_ref, dbias_ref
    )
    whole = tn(normed_ref[...], dprojected_ref[...])
    dbias, dgain1, dgain2 = dbias_ref[...], dgain1_ref[...], dgain2_ref[...]
    for at in range(16):
        small = jnp.concatenate(
            [
                dbias[:, 64 * at : 64 * at + 64],
                dbias[:, D + KV + 8 * at : D + KV + 8 * at + 8],
                dgain1[:, 56 * at : 56 * at + 56],
                dgain2[:, 56 * at : 56 * at + 56],
                jnp.zeros((1, QKV - 184), F32),
            ],
            axis=1,
        )
        rows = jnp.concatenate([whole[56 * at : 56 * at + 56], jnp.broadcast_to(small, (8, QKV))], axis=0)
        qkv_terms[at // 4, at % 4] = rows.astype(BF)
    qkv_sent = copies(qkv_terms.at[:, :, theirs], qkv_half, to_mate)
    next(outs)
    next(outs)
    next(mlp)
    add_mate(qkv_sent, qkv_terms, qkv_half)
    dense = half_sums(qkv_half, qkv_sum, 640, qkv_bufs, copies)
    next(dense)
    next(mlp)
    run(outs)
    run(mlp)

    gate, up, down = mlp_sum_refs
    moved = pltpu.make_async_remote_copy(
        src_ref=down,
        dst_ref=down_all.at[source["replica"]],
        send_sem=local.at[0],
        recv_sem=local.at[1],
        device_id=source,
        device_id_type=MESH,
    )
    stayed = pltpu.make_async_copy(down, down_all.at[me], local.at[2])

    @pl.when(moves)
    def _():
        moved.start()

    @pl.when(stays)
    def _():
        stayed.start()

    pairs = ((gate, gate_all), (up, up_all))
    across = [copies(ref, all_ref.at[me], to_next) for ref, all_ref in pairs]
    beside = [copies(ref, all_ref.at[me], to_mate) for ref, all_ref in pairs]
    for ref, all_ref in pairs:
        all_ref[me] = ref[...]
    next(dense)
    next(dense)

    @pl.when(moves)
    def _():
        moved.wait()

    @pl.when(stays)
    def _():
        stayed.wait()

    across.append(copies(down_all.at[me], down_all.at[me], to_next))
    beside.append(copies(down_all.at[me], down_all.at[me], to_mate))
    run(dense)
    qkv_low[...] = qkv_sum[...].astype(BF)
    out_low[...] = out_sum[...].astype(BF)
    sums = [copies(qkv_low, qkv_in, to_next), copies(out_low, out_in, to_next)]
    for came, all_ref in zip(across, (gate_all, up_all, down_all)):
        came.wait_recv()
        beside.append(copies(all_ref.at[next_], all_ref.at[next_], to_mate))
    sums[0].wait_recv()
    qkv_all[core] = qkv_sum[...] + qkv_in[...].astype(F32)
    sums[1].wait_recv()
    out_all[core] = out_sum[...] + out_in[...].astype(F32)
    beside += [copies(ref.at[core], ref.at[core], to_mate) for ref in (qkv_all, out_all)]
    for each in beside:
        each.wait_recv()
    for each in [out_sent, qkv_sent] + across + beside + sums:
        each.wait_send()


def tail(*operands):
    return pl.pallas_call(
        tail_kernel,
        out_shape=(
            shaped(ROWS, D),
            shaped(4, 56, QUARTER),
            shaped(4, 56, QUARTER),
            shaped(4, DOWN_ROWS, D),
            shaped(2, 32, QKV, dtype=F32),
            shaped(2, 32, D, dtype=F32),
        ),
        scratch_shapes=[pltpu.VMEM(each.shape, each.dtype) for each in ATTENTION_BACKWARD_OUT]
        + ATTENTION_BACKWARD_SCRATCH
        + REAR_SCRATCH
        + TAIL_SCRATCH
        + scatter_scratch(*MLP_SUMS_SHAPES)
        + scatter_scratch((16, 640), (16, 640), (16, QKV - 640), (16, QKV - 640))
        + scatter_scratch((16, 512), (16, 512), (16, D - 512), (16, D - 512))
        + [
            pltpu.SemaphoreType.DMA((TAIL_COPIES,)),
            pltpu.SemaphoreType.DMA((TAIL_COPIES,)),
            pltpu.SemaphoreType.DMA((3,)),
            pltpu.SemaphoreType.DMA((len(LATE),)),
        ]
        + [pltpu.VMEM(operands[at].shape, operands[at].dtype) for at in LATE],
        in_specs=[ANY_SPEC if at in LATE else VMEM_SPEC for at in range(20)],
        compiler_params=params(1),
        name="tail",
    )(*operands)


def rotary(group):
    lane = np.arange(KV)
    frequency = jnp.asarray(THETA ** (-(lane % HALF) * 2.0 / (2 * HALF)), F32)
    sign = jnp.asarray(np.where(lane % (2 * HALF) < HALF, -1.0, 1.0), F32)
    row = lax.broadcasted_iota(jnp.int32, (ROWS, KV), 0)
    positions = group * 64 + lax.rem(row, 64) + SPAN * (row // 64)
    angles = positions.astype(F32) * frequency[None, :]
    return jnp.cos(angles), jnp.sin(angles) * sign[None, :]


def body(inputs, cotangent, segments, w_qkv, b_qkv, w_out, w_gate, w_up, w_down, g_attn, g_mlp):
    group = lax.axis_index("group")
    replica = lax.axis_index("replica")
    core = lax.rem(replica, 2)

    down_piece = lax.dynamic_slice(w_down[0], (jnp.minimum(80 * replica, 224), 0), (DOWN_ROWS, D))
    gate_piece = lax.dynamic_slice(w_gate[0], (0, replica * QUARTER), (D // 16, QUARTER))
    up_piece = lax.dynamic_slice(w_up[0], (0, replica * QUARTER), (D // 16, QUARTER))
    small = jnp.concatenate([b_qkv[0], g_attn[0], g_mlp[0]])
    small = jnp.pad(small[None], ((0, 7), (0, QKV - small.shape[0])))
    qkv_piece = lax.dynamic_slice(jnp.concatenate([w_qkv[0], small], axis=0), (32 * core, 0), (32, QKV))
    out_piece = lax.dynamic_slice(jnp.pad(w_out[0], ((0, 8), (0, 0))), (32 * core, 0), (32, D))

    cosine, sine = rotary(group)
    kseg = segments
    x_in = inputs[0].reshape(ROWS, D)
    cotangent_in = cotangent[0].reshape(ROWS, D)
    gate_w, up_w, down_w, qkv_w, out_w, bias, gain1, gain2, hidden, normed2 = first(
        gate_piece, up_piece, down_piece, qkv_piece, out_piece, x_in, cosine, sine, kseg
    )
    gate_w = gate_w.reshape(D, QUARTER)
    up_w = up_w.reshape(D, QUARTER)

    def forward(x):
        normed, q, kv = front(x, qkv_w, bias, gain1, cosine, sine)
        context, hidden, normed2 = attention(x, q, kv, kseg, out_w, gain2)
        output, normed2_all, gate, up = mlp_forward(normed2, hidden, gate_w, up_w, down_w)
        return output, (x, normed, q, kv, context, hidden, normed2_all, gate, up)

    def backward_start(dout):
        dnormed2, *grads = mlp_backward(dout, gate, up, gate_w, up_w, down_w)
        dout_all, dgate, dup, product = grads
        return (dout, dnormed2, hidden, gain2, out_w, q, kv, kseg), (normed2_all, dgate, dup, product, dout_all)

    output, kept = forward(mlp_relay(normed2, hidden, x_in, gate_w, up_w, down_w))
    x, normed, q, kv, context, hidden, normed2_all, gate, up = kept
    operands, _ = backward_start(cotangent_in)
    dhidden, _, dq, dkv, _ = attention_backward(*operands)
    dout = rear(dkv, dq, cosine, sine, qkv_w, x, gain1, dhidden, cotangent_in)
    operands, mlp_operands = backward_start(dout)
    dinput, *parts = tail(*operands, *mlp_operands, cosine, sine, qkv_w, x, gain1, normed, context)
    grad_gate, grad_up, grad_down, grad_qkv, grad_out, bias, value_bias, gain1, gain2 = outputs(*parts)
    return (
        output.reshape(1, 1, 2, 64, D),
        dinput.reshape(1, 1, 2, 64, D),
        grad_qkv[None],
        bias,
        value_bias,
        grad_out[None],
        grad_gate[None],
        grad_up[None],
        grad_down[None],
        gain1,
        gain2,
    )


def solution(mesh):
    in_specs = (
        P("replica", None, "group", None),
        P("replica", None, "group", None),
        P("replica", None),
        P("section", "group", None),
        P("section", "group"),
        P("section", "group", None),
        P("section", "group", None),
        P("section", "group", None),
        P("section", "group", None),
        P("section", "group"),
        P("section", "group"),
    )
    out_specs = (
        P("section", "replica", None, "group", None),
        P("section", "replica", None, "group", None),
        P("section", "group", None),
        P("section", "group"),
        P("section", "group"),
        P("section", "group", None),
        P("section", "group", None),
        P("section", "group", None),
        P("section", "group", None),
        P("section", "group"),
        P("section", "group"),
    )
    return jax.shard_map(body, mesh=mesh, in_specs=in_specs, out_specs=out_specs, check_vma=False)
```
